32 devices in a mesh: dp: 4 (over y, x), row: 2 (over core), col: 4 (over z).
Axes of the slice: x: 2, y: 2, z: 4, core: 2. Of those that a mesh axis runs over, the one named last changes fastest.
Arguments:
- tokens: bfloat16 [64, 196, 1280], P(('dp', 'row', 'col')), may hold values from -72 to 72
- valid_mask: int32 [64, 196], P(('dp', 'row', 'col')), may hold values from 0 to 1, as said below
- out_grad: bfloat16 [64, 196, 1280], P(('dp', 'row', 'col')), may hold values from -6 to 6
- first_gain: float32 [1280], replicated, may hold values from 0.5 to 1.5
- first_shift: float32 [1280], replicated, may hold values from -1 to 1
- qkv_weight: bfloat16 [1280, 3, 1280], P('row', None, 'col'), may hold values from -1 to 1
- qkv_bias: float32 [2, 1280], P(None, 'col'), may hold values from -1 to 1
- rel_height: float32 [27, 80], replicated, may hold values from -0.9 to 0.9
- rel_width: float32 [27, 80], replicated, may hold values from -0.9 to 0.9
- proj_weight: bfloat16 [1280, 1280], P('col', 'row'), may hold values from -0.625 to 0.625
- proj_bias: float32 [1280], replicated, may hold values from -1 to 1
- second_gain: float32 [1280], replicated, may hold values from 0.5 to 1.5
- second_shift: float32 [1280], replicated, may hold values from -1 to 1
- expand_weight: bfloat16 [1280, 5120], P('row', 'col'), may hold values from -1 to 1
- expand_bias: float32 [5120], P('col'), may hold values from -1 to 1
- shrink_weight: bfloat16 [5120, 1280], P('col', 'row'), may hold values from -0.078125 to 0.078125
- shrink_bias: float32 [1280], replicated, may hold values from -1 to 1
Outputs:
- block_out: bfloat16 [64, 196, 1280], P(('dp', 'row', 'col'))
- input_grad: float32 [64, 196, 1280], P(('dp', 'row', 'col'))
- first_gain_grad: float32 [1280], replicated
- first_shift_grad: float32 [1280], replicated
- qkv_weight_grad: float32 [1280, 3, 1280], P('row', None, 'col')
- qkv_bias_grad: float32 [2, 1280], P(None, 'col')
- rel_height_grad: float32 [27, 80], replicated
- rel_width_grad: float32 [27, 80], replicated
- proj_weight_grad: float32 [1280, 1280], P('col', 'row')
- proj_bias_grad: float32 [1280], replicated
- second_gain_grad: float32 [1280], replicated
- second_shift_grad: float32 [1280], replicated
- expand_weight_grad: float32 [1280, 5120], P('row', 'col')
- expand_bias_grad: float32 [5120], P('col')
- shrink_weight_grad: float32 [5120, 1280], P('col', 'row')
- shrink_bias_grad: float32 [1280], replicated
- rms: float32 [5], replicated
The draws below stay inside these ranges and needn't reach their ends.
Inputs may be any that keep to these rules, and one draw needn't show every extreme that they name: `valid_mask`: windows come 25 to an image, 5 by 5 windows of 14 by 14 tokens in row-major order, the last image possibly incomplete; 1 marks tokens inside the image content, a rectangle at the top left that is 64 tokens along one side and at least half of that along the other.
All inputs are finite; a program needn't handle non-finite values.
Results may differ from the reference program's by a relative error of at most 0.012.
Values may be sent and summed in bfloat16 or wider, within the bound.
A program may use at most 256 MiB of HBM per device.

```python
import jax
import jax.numpy as jnp
from jax import lax

D = 1280
HEADS = 16
HEAD_DIM = 80
FF = 5120
WIN = 14
GRID_WIN = 5
IMG = 64
WIN_DEV = 2
WINDOWS = 64
WTOK = 196
RPOS = 27
N_COL = 4


def draw_tokens(key, part):
    key = jax.random.fold_in(key, 11)
    base_key, row_key, col_key = jax.random.split(key, 3)
    ramp = jnp.exp(jnp.log(3.0) * jnp.arange(WINDOWS, dtype=jnp.float32) / max(WINDOWS - 1, 1))
    row_scale = jnp.exp(jax.random.uniform(row_key, (WINDOWS, WTOK), minval=0.0, maxval=jnp.log(3.0)))
    col_scale = jnp.exp(jax.random.uniform(col_key, (D,), minval=jnp.log(0.5), maxval=jnp.log(2.0)))
    base = jnp.clip(jax.random.normal(base_key, (WINDOWS, WTOK, D)), -4.0, 4.0)
    return (base * (ramp[:, None] * row_scale)[:, :, None] * col_scale).astype(jnp.bfloat16)


def draw_valid_mask(key, part):
    key = jax.random.fold_in(key, 23)
    short_key, side_key = jax.random.split(key)
    per_image = GRID_WIN * GRID_WIN
    images = (WINDOWS + per_image - 1) // per_image
    short = jax.random.randint(short_key, (images,), IMG // 2, IMG + 1)
    side = jax.random.randint(side_key, (images,), 0, 2)
    height = jnp.where(side == 0, short, IMG)
    breadth = jnp.where(side == 0, IMG, short)
    window_ids = jnp.arange(WINDOWS)
    image_ids = window_ids // per_image
    slot = window_ids % per_image
    positions = jnp.arange(WTOK)
    grid_row = (slot // GRID_WIN)[:, None] * WIN + (positions // WIN)[None, :]
    grid_col = (slot % GRID_WIN)[:, None] * WIN + (positions % WIN)[None, :]
    inside = (grid_row < height[image_ids][:, None]) & (grid_col < breadth[image_ids][:, None])
    return inside.astype(jnp.int32)


def draw_qkv_weight(key, part):
    key = jax.random.fold_in(key, 37)
    base_key = jax.random.fold_in(key, 0)
    base = jnp.clip(jax.random.normal(base_key, (D, 3, D)), -4.0, 4.0)
    return (base * D ** (-0.5)).astype(jnp.bfloat16)


def draw_expand_weight(key, part):
    key = jax.random.fold_in(key, 41)
    base_key = jax.random.fold_in(key, 0)
    base = jnp.clip(jax.random.normal(base_key, (D, FF)), -4.0, 4.0)
    return (base * D ** (-0.5)).astype(jnp.bfloat16)


def strengthened(entries, key, source, target, shards_of, factor):
    def block_of(axis_at):
        return (jnp.arange(entries.shape[axis_at]) // (entries.shape[axis_at] // shards_of)).reshape((-1,) + (1,) * (entries.ndim - 1 - axis_at))

    one_side = jax.random.permutation(key, shards_of)[block_of(target)]
    far = (block_of(target) + shards_of // 2) % shards_of
    return jnp.where((block_of(source) == one_side) | (block_of(source) == far), factor * entries, entries)


def shard_levels(own_key, dims, cuts, smallest, largest):
    loudness, own = 1.0, jax.random.fold_in(own_key, 6)
    for axis_at, parts in cuts:
        heights = jnp.exp(jax.random.uniform(jax.random.fold_in(own, axis_at), (parts,), jnp.float32, smallest / len(cuts), largest / len(cuts)))
        loudness = loudness * jnp.repeat(heights, dims[axis_at] // parts).reshape([-1 if axis == axis_at else 1 for axis in range(len(dims))])
    return loudness


def centred(stream_key, dims, width, bound, cuts=(), held_as=jnp.bfloat16):
    loudness = shard_levels(stream_key, dims, cuts, -0.22, 0.18) if cuts else 1.0
    drawn = jax.random.normal(stream_key, dims, jnp.float32) * width * loudness
    return jnp.minimum(jnp.maximum(drawn, -bound), bound).astype(held_as)


def bell_draw_with(stream_key, dims, width, reach, cuts, heavy, kind=jnp.bfloat16):
    entries = width * jax.random.normal(stream_key, dims, jnp.float32)
    if cuts:
        entries = entries * shard_levels(stream_key, dims, cuts, -0.22, 0.18)
    return jnp.clip(strengthened(entries, jax.random.fold_in(stream_key, 3), *heavy), -reach, reach).astype(kind)


def setup_inputs(seed: int = 0) -> dict:
    key_list = jax.random.split(jax.random.key(seed), 18)
    tokens = draw_tokens(jax.random.fold_in(key_list[17], 71), 0)
    valid_mask = draw_valid_mask(jax.random.fold_in(key_list[17], 71), 0)
    out_grad = bell_draw_with(key_list[2], (WINDOWS, WTOK, D), 1.0, 6.0, ((0, 32),), (0, 2, 32, 2.75))
    first_gain = jnp.clip(1.0 + 0.1 * jax.random.normal(key_list[3], (D,), jnp.float32), 0.5, 1.5)
    first_shift = centred(key_list[4], (D,), 0.2, 1.0, (), jnp.float32)
    qkv_weight = draw_qkv_weight(jax.random.fold_in(key_list[17], 71), 0)
    qkv_bias = centred(key_list[6], (2, D), 0.2, 1.0, ((1, 4),), jnp.float32)
    rel_height = centred(key_list[7], (RPOS, HEAD_DIM), 0.15, 0.9, (), jnp.float32)
    rel_width = centred(key_list[8], (RPOS, HEAD_DIM), 0.15, 0.9, (), jnp.float32)
    proj_weight = centred(key_list[9], (D, D), (D // WIN) ** -0.5, 0.625, ((0, 4), (1, 2)))
    proj_bias = centred(key_list[10], (D,), 0.2, 1.0, (), jnp.float32)
    second_gain = jnp.clip(1.0 + 0.1 * jax.random.normal(key_list[11], (D,), jnp.float32), 0.5, 1.5)
    second_shift = centred(key_list[12], (D,), 0.2, 1.0, (), jnp.float32)
    expand_weight = draw_expand_weight(jax.random.fold_in(key_list[17], 71), 0)
    expand_bias = centred(key_list[14], (FF,), 0.2, 1.0, ((0, 4),), jnp.float32)
    shrink_weight = centred(key_list[15], (FF, D), FF ** -0.5, 0.078125, ((0, 4), (1, 2)))
    shrink_bias = centred(key_list[16], (D,), 0.2, 1.0, (), jnp.float32)
    return dict(tokens=tokens, valid_mask=valid_mask, out_grad=out_grad, first_gain=first_gain, first_shift=first_shift, qkv_weight=qkv_weight, qkv_bias=qkv_bias, rel_height=rel_height, rel_width=rel_width, proj_weight=proj_weight, proj_bias=proj_bias, second_gain=second_gain, second_shift=second_shift, expand_weight=expand_weight, expand_bias=expand_bias, shrink_weight=shrink_weight, shrink_bias=shrink_bias)


epsilon = 1e-06
highest = lax.Precision.HIGHEST

@jax.custom_vjp
def low(v):
    return lax.optimization_barrier(v.astype(jnp.bfloat16)).astype(jnp.float32)

@jax.custom_vjp
def low_back(v):
    return v

def low_keep(v):
    return (low(v), None)

def low_pass(kept, grad):
    return (grad,)

def back_keep(v):
    return (v, None)

def back_low(kept, grad):
    return (low(grad),)
low.defvjp(low_keep, low_pass)
low_back.defvjp(back_keep, back_low)

def layer_norm(values, norm_gain, norm_shift):
    center = values - lax.optimization_barrier(jnp.mean(values, axis=-1, keepdims=True))
    spread = lax.optimization_barrier(jnp.mean(center * center, axis=-1, keepdims=True))
    return center * lax.rsqrt(spread + epsilon) * norm_gain + norm_shift

def offset_table(span_size):
    positions = jnp.arange(span_size)
    offset = positions[:, None] - positions[None, :] + span_size - 1
    return (offset[:, :, None] == jnp.arange(2 * span_size - 1)[None, None, :]).astype(jnp.float32)

def attention_scores(query_rows, key_rows, rel_rows_table, rel_cols_table, onehot_table, span_size, scaling):
    window_count, tokens_per, head_count, head_size = query_rows.shape
    rel_count = 2 * span_size - 1
    direct = jnp.einsum('bthc,buhc->bhtu', query_rows, key_rows, precision=highest) * scaling
    along_rows = jnp.einsum('bthc,jc->bhtj', query_rows, rel_rows_table, precision=highest)
    along_cols = jnp.einsum('bthc,jc->bhtj', query_rows, rel_cols_table, precision=highest)
    grid_rows = along_rows.reshape(window_count, head_count, span_size, span_size, rel_count)
    grid_cols = along_cols.reshape(window_count, head_count, span_size, span_size, rel_count)
    rel_rows = jnp.einsum('bhxyj,xkj->bhxyk', grid_rows, onehot_table, precision=highest)
    rel_cols = jnp.einsum('bhxyj,ywj->bhxyw', grid_cols, onehot_table, precision=highest)
    score_sum = direct.reshape(window_count, head_count, span_size, span_size, span_size, span_size)
    score_sum = score_sum + rel_rows[:, :, :, :, :, None] + rel_cols[:, :, :, :, None, :]
    return score_sum.reshape(window_count, head_count, tokens_per, tokens_per)

def reference(tokens, valid_mask, out_grad, first_gain, first_shift, qkv_weight, qkv_bias, rel_height, rel_width, proj_weight, proj_bias, second_gain, second_shift, expand_weight, expand_bias, shrink_weight, shrink_bias):
    block_windows = WIN_DEV * N_COL
    block_total = WINDOWS // block_windows
    onehot_table = offset_table(WIN)
    scaling = HEAD_DIM ** (-0.5)
    keep_mask = valid_mask.astype(jnp.float32)[:, :, None]
    inputs = tokens.astype(jnp.float32)
    weights_in = tuple((item.astype(jnp.float32) for item in (first_gain, first_shift, qkv_weight, qkv_bias, rel_height, rel_width, proj_weight, proj_bias, second_gain, second_shift, expand_weight, expand_bias, shrink_weight, shrink_bias)))

    def forward(values, *weight_list):
        gain_one, shift_one, qkv_mat, qkv_add, rows_table, cols_table, proj_mat, proj_add, gain_two, shift_two, expand_mat, expand_add, shrink_mat, shrink_add = weight_list
        bias_rows = jnp.stack([qkv_add[0], jnp.zeros_like(qkv_add[0]), qkv_add[1]])

        def block_step(pair):
            block_in, block_keep = pair
            normed_one = low(layer_norm(block_in, gain_one, shift_one) * block_keep)
            projected = jnp.einsum('btd,dsk->btsk', normed_one, qkv_mat, precision=highest) + bias_rows
            projected = low(low_back(projected))
            head_shape = (block_windows, WTOK, HEADS, HEAD_DIM)
            query_rows = projected[:, :, 0].reshape(head_shape)
            key_rows = projected[:, :, 1].reshape(head_shape)
            value_rows = projected[:, :, 2].reshape(head_shape)
            scores = low_back(attention_scores(query_rows, key_rows, rows_table, cols_table, onehot_table, WIN, scaling))
            probs = low(jax.nn.softmax(scores, axis=-1))
            attended = jnp.einsum('bhtu,buhc->bthc', probs, value_rows, precision=highest).reshape(block_windows, WTOK, D)
            attended = low(low_back(attended))
            attn_out = low_back(jnp.einsum('btk,kd->btd', attended, proj_mat, precision=highest) + proj_add)
            middle = block_in + attn_out
            normed_two = low(layer_norm(middle, gain_two, shift_two))
            hidden_pre = low_back(jnp.einsum('btd,df->btf', normed_two, expand_mat, precision=highest) + expand_add)
            active = low(jax.nn.gelu(hidden_pre, approximate=False))
            mlp_out = low_back(jnp.einsum('btf,fd->btd', active, shrink_mat, precision=highest) + shrink_add)
            result = middle + mlp_out
            block_stats = jnp.stack([jnp.sum(block_keep * block_in * block_in), jnp.sum(block_keep * middle * middle), jnp.sum(block_keep * result * result), jnp.sum(block_keep * attn_out * attn_out), jnp.sum(block_keep * mlp_out * mlp_out)])
            return (result, block_stats)
        stacked_in = values.reshape(block_total, block_windows, WTOK, D)
        stacked_keep = keep_mask.reshape(block_total, block_windows, WTOK, 1)
        block_results, block_stats = lax.map(jax.checkpoint(block_step), (stacked_in, stacked_keep))
        return (block_results.reshape(WINDOWS, WTOK, D), lax.optimization_barrier(jnp.sum(block_stats, axis=0)))
    result, back_fn, stat_total = jax.vjp(forward, inputs, *weights_in, has_aux=True)
    gradients = back_fn(out_grad.astype(jnp.float32))
    rms = jnp.sqrt(stat_total / (jnp.sum(keep_mask) * D))
    return (result.astype(jnp.bfloat16), gradients[0], gradients[1], gradients[2], gradients[3], gradients[4], gradients[5], gradients[6], gradients[7], gradients[8], gradients[9], gradients[10], gradients[11], gradients[12], gradients[13], gradients[14], rms)
```

```python
import functools

import jax
import jax.numpy as jnp
from jax import lax
from jax.experimental import pallas as pl
from jax.experimental.pallas import tpu as pltpu
from jax.sharding import PartitionSpec as P

BF = jnp.bfloat16
F32 = jnp.float32
LANES = 128
SIDE = 14
SIDE_PAD = 16
WROWS = SIDE * SIDE_PAD
HEAD = 80
AT_H = HEAD
AT_W = HEAD + SIDE
AT_MASK = HEAD + 2 * SIDE
COL_W = 64


def dot(a, b):
    return jnp.dot(a, b, preferred_element_type=F32)


def dot_nt(a, b):
    return lax.dot_general(a, b, (((1,), (1,)), ((), ())), preferred_element_type=F32)


def dot_tn(a, b):
    return lax.dot_general(a, b, (((0,), (0,)), ((), ())), preferred_element_type=F32)


def lane_ids():
    return lax.broadcasted_iota(jnp.int32, (WROWS, LANES), 1)


def row_ids():
    return lax.broadcasted_iota(jnp.int32, (WROWS, LANES), 0)


def key_codes():
    u = jnp.arange(WROWS)[:, None]
    lane = jnp.arange(LANES)[None, :]
    k, l = u // SIDE_PAD, u % SIDE_PAD
    height = lane - AT_H == k
    width = (lane - AT_W == l) & (l < SIDE)
    width_back = (AT_W + SIDE - 1 - lane == l) & (l < SIDE)
    plain = jnp.where(height | width, 1.0, 0.0)
    masked = jnp.where((lane == AT_MASK) & (l >= SIDE), -1e30, plain)
    back = jnp.where(height | width_back, 1.0, 0.0)
    return jnp.stack([masked, plain, back]).astype(BF)


def split_low(values):
    high = values.astype(BF)
    return high, (values - high.astype(F32)).astype(BF)


def relative_tables(rel_height, rel_width):
    count = rel_height.shape[0]
    forward = jnp.zeros((LANES, LANES), F32)
    forward = forward.at[:HEAD, :count].set(rel_height[::-1].T)
    forward = forward.at[:HEAD, COL_W : COL_W + count].set(rel_width[::-1].T)
    high, rest = split_low(forward * (HEAD**0.5))
    back = jnp.zeros((LANES, LANES), F32)
    back = back.at[:count, :HEAD].set(rel_height[::-1])
    back = back.at[COL_W : COL_W + count, :HEAD].set(rel_width)
    back_high, back_rest = split_low(back)
    return jnp.concatenate([high, rest]), jnp.concatenate([back_high, back_high, back_rest])


def query_codes(query, rel_query):
    full = dot(jnp.concatenate([query, query], axis=1), rel_query)
    tiles = full.reshape(SIDE, SIDE_PAD, LANES)
    heights = jnp.concatenate(
        [pltpu.roll(tiles[i], AT_H - (SIDE - 1 - i), 1) for i in range(SIDE)], axis=0
    )
    widths = pltpu.roll(
        tiles, AT_W - COL_W - (SIDE - 1), 2, stride=1, stride_axis=1
    ).reshape(WROWS, LANES)
    lane = lane_ids()
    codes = jnp.where(
        (lane >= AT_H) & (lane < AT_W),
        heights,
        jnp.where((lane >= AT_W) & (lane < AT_MASK), widths, 0.0),
    )
    high, rest = split_low(codes)
    first = query + high + jnp.where(lane == AT_MASK, 1.0, 0.0).astype(BF)
    return jnp.concatenate([first, rest], axis=1)


def softmax_rows(query, key, rel_query, codes_ref):
    left = query_codes(query, rel_query)
    right = jnp.concatenate([key + codes_ref[0], codes_ref[1]], axis=1)
    scores = dot_nt(left, right)
    top = jnp.max(scores, axis=1, keepdims=True)
    weights = jnp.exp((scores - top) * (HEAD**-0.5))
    return weights / jnp.sum(weights, axis=1, keepdims=True)


def attend(query, key, value, rel_query, codes_ref):
    probs = softmax_rows(query, key, rel_query, codes_ref)
    return dot(probs.astype(BF), value)


def attend_back(query, key, value, grad, rel_query, rel_back, codes_ref):
    probs = softmax_rows(query, key, rel_query, codes_ref)
    prob_grad = dot_nt(grad, value)
    inner = jnp.sum(probs * prob_grad, axis=1, keepdims=True)
    score_low = (probs * (prob_grad - inner)).astype(BF)
    value_grad = dot_tn(probs.astype(BF), grad)
    key_grad = dot_tn(score_low, query) * (HEAD**-0.5)
    mixed = dot(score_low, key + codes_ref[2])
    tiles = mixed.reshape(SIDE, SIDE_PAD, LANES)
    heights = jnp.concatenate(
        [pltpu.roll(tiles[i], (SIDE - 1 - i - AT_H) % LANES, 1) for i in range(SIDE)], axis=0
    )
    widths = pltpu.roll(
        tiles, (COL_W - AT_W) % LANES, 2, stride=1, stride_axis=1
    ).reshape(WROWS, LANES)
    lane, row = lane_ids(), row_ids()
    first_h = SIDE - 1 - row // SIDE_PAD
    first_w = COL_W + row % SIDE_PAD
    offsets = jnp.where(
        (lane >= first_h) & (lane < first_h + SIDE),
        heights,
        jnp.where((lane >= first_w) & (lane < first_w + SIDE), widths, 0.0),
    )
    high, rest = split_low(offsets)
    query_grad = jnp.where(lane < HEAD, mixed, 0.0) * (HEAD**-0.5) + dot(
        jnp.concatenate([high, rest, high], axis=1), rel_back
    )
    rel_grad = dot_tn(jnp.concatenate([high, rest], axis=1), query)
    return query_grad, key_grad, value_grad, rel_grad


def pad_head(piece):
    return jnp.concatenate([piece, jnp.zeros((piece.shape[0], LANES - HEAD), piece.dtype)], axis=1)


def qkv_low(s, rows, h1, wq, bias, half):
    return (dot(h1[rows, :half], block(wq, s, 0)) + dot(h1[rows, half:], block(wq, s, 1)) + bias).astype(BF)


def head_of(low, part, heads, hh):
    at = (part * heads + hh) * HEAD
    return pad_head(low[:, at : at + HEAD])


def attention_slab(s, h1, wq, wp, bias, rel_query, codes, attended, total, heads, half):
    @pl.loop(0, h1.shape[0] // WROWS)
    def _(m):
        rows = pl.ds(pl.multiple_of(m * WROWS, WROWS), WROWS)
        low = qkv_low(s, rows, h1, wq, bias, half)
        outs = []
        for hh in range(heads):
            query, key, value = (head_of(low, part, heads, hh) for part in range(3))
            outs.append(attend(query, key, value, rel_query[...], codes)[:, :HEAD])
        out_low = jnp.concatenate(outs, axis=1).astype(BF)
        attended[s, rows] = out_low
        total[rows, :half] += dot(out_low, block(wp, s, 0))
        total[rows, half:] += dot(out_low, block(wp, s, 1))


SQRT_HALF = 0.5**0.5
PDF_SCALE = 0.3989422804014327


def mlp_rows(s, m, h2, gm, we, ws, bias, act, gpre, total, back, bias_grad, half):
    count = h2.shape[0] // 4

    @pl.loop(0, 2)
    def _(step):
        rows = pl.ds(pl.multiple_of((2 * m + step) * count, count), count)
        pre = dot(h2[rows, :half], block(we, s, 0)) + dot(h2[rows, half:], block(we, s, 1)) + bias
        cdf = 0.5 + 0.5 * lax.erf(pre * SQRT_HALF)
        slope = cdf + pre * (PDF_SCALE * jnp.exp(-0.5 * pre * pre))
        act_low = (pre * cdf).astype(BF)
        act[rows, :] = act_low
        hidden = dot_nt(gm[rows, :half], block(ws, s, 0)) + dot_nt(gm[rows, half:], block(ws, s, 1))
        gpre_low = (hidden * slope).astype(BF)
        gpre[rows, :] = gpre_low
        bias_grad[s] += jnp.sum(gpre_low.astype(F32), axis=0, keepdims=True)
        total[rows, :half] += dot(act_low, block(ws, s, 0))
        total[rows, half:] += dot(act_low, block(ws, s, 1))
        back[rows, :half] += dot_nt(gpre_low, block(we, s, 0))
        back[rows, half:] += dot_nt(gpre_low, block(we, s, 1))


def attention_back_slab(
    s, h1, ga, wq, wp, bias, rel_query, rel_back, codes, gqkv, back, bias_grad, rel_grad, heads, half
):
    @pl.loop(0, h1.shape[0] // WROWS)
    def _(m):
        rows = pl.ds(pl.multiple_of(m * WROWS, WROWS), WROWS)
        low = qkv_low(s, rows, h1, wq, bias, half)
        grad = (dot_nt(ga[rows, :half], block(wp, s, 0)) + dot_nt(ga[rows, half:], block(wp, s, 1))).astype(BF)
        parts = [[], [], []]
        for hh in range(heads):
            query, key, value = (head_of(low, part, heads, hh) for part in range(3))
            got = attend_back(
                query, key, value, head_of(grad, 0, heads, hh), rel_query[...], rel_back[...], codes
            )
            for part in range(3):
                parts[part].append(got[part][:, :HEAD])
            rel_grad[...] += got[3]
        grad_low = jnp.concatenate(parts[0] + parts[1] + parts[2], axis=1).astype(BF)
        gqkv[rows, :] = grad_low
        bias_grad[s] += jnp.sum(grad_low.astype(F32), axis=0, keepdims=True)
        back[rows, :half] += dot_nt(grad_low, block(wq, s, 0))
        back[rows, half:] += dot_nt(grad_low, block(wq, s, 1))


MESH_ID = pl.DeviceIdType.MESH
ARRAYS = ("qkv", "proj", "expand", "shrink")
CHUNK = 64
EPS = 1e-06
SMALL_ROWS = 24
SPARE = 4


def halves(rows):
    first = (rows // 2 + 15) // 16 * 16
    return first, rows - first


def flip(index, k):
    return ((index // 2 + k // 2) % 2) * 2 + (index % 2 + k % 2) % 2


def block(ref, slab, half):
    value = ref[slab, half]
    return value.reshape(value.shape[0] * value.shape[1], value.shape[2])


def add_low(target, index, extra):
    target[index] = (target[index].astype(F32) + extra.astype(F32)).astype(BF)


def kernel(
    tokens, keep, out_grad, vectors, biases, codes, rel_query, rel_back,
    qkv_src, proj_src, expand_src, shrink_src,
    block_out, input_grad, qkv_out, proj_out, expand_out, shrink_out, small_out, rel_out,
    rxq, rxp, rxe, rxs, ryq, ryp, rye, rys, rx2q, rx2p, rx2e, rx2s, ry2q, ry2p, ry2e, ry2s, rzq, rzp, rze, rzs,
    wq, wp, we, ws, h1, gm, h2, attended, total, back, xr, xr2, middle, act, gpre, gqkv, tmp, tmpq,
    bias_all, small, small_got, rel, rel_got, bias_e, bias_q, rel_acc,
    gsend, grecv, rsend, rrecv, fsend, frecv, csend, crecv, zsend, zrecv, local,
):
    d, r, z = lax.axis_index("dp"), lax.axis_index("row"), lax.axis_index("col")
    h, b = d // 2, d % 2
    own = tokens.shape[0]
    width = tokens.shape[1]
    half = width // 2
    heads = 2
    bufs = (wq, wp, we, ws)
    outs = (qkv_out, proj_out, expand_out, shrink_out)
    rx, ry = (rxq, rxp, rxe, rxs), (ryq, ryp, rye, rys)
    rx2, ry2 = (rx2q, rx2p, rx2e, rx2s), (ry2q, ry2p, ry2e, ry2s)
    rz = (rzq, rzp, rze, rzs)
    parts = [halves(buf.shape[3]) for buf in bufs]
    attn, mlp = (0, 1), (2, 3)

    along_x = (h * 2 + 1 - b, r, z)
    along_y = ((1 - h) * 2 + b, r, z)
    partner = (d, 1 - r, z)

    def along_z(k):
        return (d, r, flip(z, k))

    def remote(src, dst, sems, recvs, index, device):
        return pltpu.make_async_remote_copy(
            src_ref=src,
            dst_ref=dst,
            send_sem=sems.at[index],
            recv_sem=recvs.at[index],
            device_id=device,
            device_id_type=MESH_ID,
        )

    def first_part(a):
        return pl.ds(0, parts[a][0])

    def second_part(a):
        return pl.ds(parts[a][0], parts[a][1])

    def gather_z(a, k, arriving=False):
        at = bufs[a].at[flip(z, k) if arriving else z, h, b]
        return remote(at, at, gsend, grecv, (a, k, 0), along_z(k))

    def ring(a, slab, sends, recvs, index, kind, arriving):
        buf = bufs[a]
        if kind == 1:
            at, device = (buf.at[slab, h, 1 - b] if arriving else buf.at[slab, h, b]), along_x
        elif kind == 2:
            at, device = (buf.at[slab, 1 - h, b] if arriving else buf.at[slab, h, b]), along_y
        elif kind == 3:
            at = buf.at[slab, 1 - h if arriving else h, 1 - b, first_part(a)]
            device = along_y
        else:
            at = buf.at[slab, 1 - h, 1 - b if arriving else b, second_part(a)]
            device = along_x
        return remote(at, at, sends, recvs, index, device)

    def gather(a, k, kind, arriving=False):
        return ring(a, flip(z, k), gsend, grecv, (a, k, kind), kind, arriving)

    def spread(a, kind, arriving=False):
        return ring(a, 3 - z, fsend, frecv, (a, kind), kind, arriving)

    def start_z(group, k):
        for a in group:
            gather_z(a, k).start()

    def pass_xy(group, k):
        for a in group:
            gather_z(a, k, True).wait_recv()
            gather(a, k, 1).start()
            gather(a, k, 2).start()

    def pass_diagonal(group, k):
        for a in group:
            gather(a, k, 1, True).wait_recv()
            gather(a, k, 3).start()
            gather(a, k, 2, True).wait_recv()
            gather(a, k, 4).start()

    def finish_slab(group, k):
        for a in group:
            gather(a, k, 3, True).wait_recv()
            gather(a, k, 4, True).wait_recv()

    def sent_z(group):
        for a in group:
            for k in (1, 2, 3):
                gather_z(a, k).wait_send()

    def sent_xy(group, k):
        for a in group:
            for kind in (1, 2, 3, 4):
                gather(a, k, kind).wait_send()

    def slot(k):
        first = (4 - k) // 4
        return first * SPARE + (1 - first) * flip(z, k - 1 + first)

    def reduce_copy(a, k, kind):
        buf, g = bufs[a], slot(k)
        if kind == 0:
            src, dst, device = buf.at[g, :, 1 - b, first_part(a)], rx[a].at[k], along_x
        elif kind == 1:
            src, dst, device = buf.at[g, 1 - h, :, second_part(a)], ry[a].at[k], along_y
        elif kind == 2:
            src, dst, device = buf.at[g, 1 - h, b, first_part(a)], ry2[a].at[k], along_y
        elif kind == 3:
            src, dst, device = buf.at[g, h, 1 - b, second_part(a)], rx2[a].at[k], along_x
        else:
            src, dst, device = buf.at[g, h, b], rz[a].at[k], along_z(k)
        return remote(src, dst, rsend, rrecv, (a, k, kind), device)

    def reduce_one(group, k):
        for a in group:
            reduce_copy(a, k, 0).start()
            reduce_copy(a, k, 1).start()

    def scratch(a, place):
        if a == 0:
            return tmpq.at[place]
        return tmp.at[place + (2 if a == 3 else 0)]

    def reduce_two(group, k):
        loads = []
        for a in group:
            reduce_copy(a, k, 0).wait_recv()
            reduce_copy(a, k, 1).wait_recv()
            for place, got in enumerate((rx[a], ry[a])):
                to = scratch(a, place).at[:, pl.ds(0, parts[a][place])]
                loads.append(pltpu.make_async_copy(got.at[k], to, local.at[a * 2 + place]))
                loads[-1].start()
        g = slot(k)
        for i, a in enumerate(group):
            first, second = parts[a]
            loads[2 * i].wait()
            for side in range(2):
                add_low(bufs[a], (g, side, b, first_part(a)), scratch(a, 0)[side, :first])
            reduce_copy(a, k, 2).start()
            loads[2 * i + 1].wait()
            for side in range(2):
                add_low(bufs[a], (g, h, side, second_part(a)), scratch(a, 1)[side, :second])
            reduce_copy(a, k, 3).start()

    def reduce_three(group, k):
        loads = []
        for a in group:
            reduce_copy(a, k, 2).wait_recv()
            reduce_copy(a, k, 3).wait_recv()
            for place, got in enumerate((ry2[a], rx2[a])):
                to = scratch(a, place).at[0, pl.ds(0, parts[a][place])]
                loads.append(pltpu.make_async_copy(got.at[k], to, local.at[a * 2 + place]))
                loads[-1].start()
        g = slot(k)
        for i, a in enumerate(group):
            first, second = parts[a]
            loads[2 * i].wait()
            add_low(bufs[a], (g, h, b, first_part(a)), scratch(a, 0)[0, :first])
            loads[2 * i + 1].wait()
            add_low(bufs[a], (g, h, b, second_part(a)), scratch(a, 1)[0, :second])

            @pl.when(k > 0)
            def _():
                reduce_copy(a, k, 4).start()

    def reduce_four(group):
        for a in group:
            rows = bufs[a].shape[3]
            hold = gqkv if a == 0 else act
            loads = []
            for k in (1, 2, 3):
                got = remote(bufs[a].at[slot(k), h, b], rz[a].at[k], rsend, rrecv, (a, k, 4), along_z(k))
                got.wait_recv()
                loads.append(
                    pltpu.make_async_copy(rz[a].at[k], hold.at[pl.ds((k - 1) * rows, rows)], local.at[k])
                )
                loads[-1].start()
            for load in loads:
                load.wait()
            value = bufs[a][SPARE, h, b].astype(F32)
            for k in range(3):
                value = value + hold[k * rows : (k + 1) * rows].astype(F32)
            bufs[a][3 - z, h, b] = value.astype(BF)
            spread(a, 1).start()
            spread(a, 2).start()

    def reduce_five(group):
        for a in group:
            spread(a, 1, True).wait_recv()
            spread(a, 3).start()
            spread(a, 2, True).wait_recv()
            spread(a, 4).start()

    def swap_out(a):
        return remote(bufs[a].at[3 - z, 1 - r], outs[a].at[r], fsend, frecv, (a, 0), partner)

    def keep_out(a):
        return pltpu.make_async_copy(bufs[a].at[3 - z, r], outs[a].at[r], local.at[a])

    def reduce_six(group):
        for a in group:
            spread(a, 3, True).wait_recv()
            spread(a, 4, True).wait_recv()
            swap_out(a).start()
            keep_out(a).start()

    def exchange(index, src, dst):
        return remote(src, dst, csend, crecv, index, partner)

    rows_own, rows_other = pl.ds(0, own), pl.ds(own, own)
    sources = (
        lambda side: qkv_src.at[side],
        lambda side: proj_src.at[side],
        lambda side: expand_src.at[:, :, pl.ds(pl.multiple_of(side * half, half), half)],
        lambda side: shrink_src.at[side],
    )

    def source_swap(a):
        return exchange(a, sources[a](1 - r), bufs[a].at[z, r])

    def source_keep(a):
        return pltpu.make_async_copy(sources[a](r), bufs[a].at[z, r], local.at[a])

    grad_load = pltpu.make_async_copy(out_grad, gm.at[rows_own], local.at[4])
    swap_grad = exchange(4, out_grad, gm.at[rows_other])
    swap_h1 = exchange(5, h1.at[rows_own], h1.at[rows_other])
    swap_attn = exchange(6, total.at[rows_other], xr)
    swap_h2 = exchange(7, h2.at[rows_own], h2.at[rows_other])
    swap_mlp = exchange(8, total.at[rows_other], xr)
    swap_gh2 = exchange(9, back.at[rows_other], xr2)
    swap_ga = exchange(10, gm.at[rows_own], gm.at[rows_other])
    swap_gh1 = exchange(11, back.at[rows_other], xr)

    def bias_copy(k, arriving=False):
        at = bias_all.at[flip(z, k) if arriving else z]
        return remote(at, at, zsend, zrecv, k, along_z(k))

    barrier = pltpu.get_barrier_semaphore()
    peers = [partner, along_x, along_y, along_z(1), along_z(2), along_z(3)]
    for peer in peers:
        pl.semaphore_signal(barrier, inc=1, device_id=peer, device_id_type=MESH_ID)
    pl.semaphore_wait(barrier, len(peers))

    for a in range(4):
        source_swap(a).start()
        source_keep(a).start()
    bias_load = pltpu.make_async_copy(biases, bias_all.at[z], local.at[5])
    bias_load.start()
    grad_load.start()
    swap_grad.start()
    bias_load.wait()
    for k in (1, 2, 3):
        bias_copy(k).start()
    for a in attn:
        source_swap(a).wait()
        source_keep(a).wait()
    for k in (1, 2, 3):
        start_z(attn, k)

    gain_one, shift_one = vectors[0:1, :], vectors[1:2, :]
    gain_two, shift_two = vectors[2:3, :], vectors[3:4, :]
    proj_bias, shrink_bias = vectors[4:5, :], vectors[5:6, :]

    def over_rows(body):
        @pl.loop(0, own // CHUNK)
        def _(m):
            body(pl.ds(pl.multiple_of(m * CHUNK, CHUNK), CHUNK))

    def column_sum(value):
        return jnp.sum(value, axis=0, keepdims=True)

    def normalize(value):
        center = value - jnp.mean(value, axis=1, keepdims=True)
        inverse = lax.rsqrt(jnp.mean(center * center, axis=1, keepdims=True) + EPS)
        return center * inverse, inverse

    def norm_back(grad, gain, xhat, inverse):
        scaled = grad * gain
        mean = jnp.mean(scaled, axis=1, keepdims=True)
        along = jnp.mean(scaled * xhat, axis=1, keepdims=True)
        return (scaled - mean - xhat * along) * inverse

    small[...] = jnp.zeros_like(small)

    def first_rows(rows):
        value = tokens[rows].astype(F32)
        valid = keep[rows]
        xhat, _ = normalize(value)
        h1[rows] = ((xhat * gain_one + shift_one) * valid).astype(BF)
        small[0:1, :] += column_sum(valid * value * value)
        small[5:6, :] += jnp.broadcast_to(column_sum(valid), (1, width))

    over_rows(first_rows)
    swap_h1.start()
    total[...] = jnp.zeros_like(total)
    for k in (1, 2, 3):
        bias_copy(k, True).wait_recv()
    swap_h1.wait_recv()

    def bias_q_of(s):
        return bias_all[s, 0:1, half : half + wq.shape[4]]

    def bias_e_of(s):
        return bias_all[s, 0:1, :half]

    @pl.loop(0, 4)
    def _(k):
        s = flip(z, k)

        @pl.when(k > 0)
        def _():
            pass_diagonal(attn, k)
            finish_slab(attn, k)

        attention_slab(
            s, h1, wq, wp, bias_q_of(s), rel_query, codes, attended, total, heads, half
        )

        @pl.when(k == 0)
        def _():
            pass_xy(attn, 1)
            for a in mlp:
                source_swap(a).wait()
                source_keep(a).wait()
            start_z(mlp, 1)

        @pl.when(k < 2)
        def _():
            pass_xy(attn, k + 2)
            start_z(mlp, k + 2)

        @pl.when(k >= 2)
        def _():
            pass_xy(mlp, k - 1)

    swap_attn.start()
    swap_attn.wait()

    def middle_rows(rows):
        value = tokens[rows].astype(F32)
        valid = keep[rows]
        attn_out = total[rows] + xr[rows] + proj_bias
        mid = value + attn_out
        middle[rows] = mid
        xhat, _ = normalize(mid)
        h2[rows] = (xhat * gain_two + shift_two).astype(BF)
        small[1:2, :] += column_sum(valid * mid * mid)
        small[3:4, :] += column_sum(valid * attn_out * attn_out)

    over_rows(middle_rows)
    swap_h2.start()
    total[...] = jnp.zeros_like(total)
    back[...] = jnp.zeros_like(back)
    bias_e[...] = jnp.zeros_like(bias_e)
    bias_q[...] = jnp.zeros_like(bias_q)
    rel_acc[...] = jnp.zeros_like(rel_acc)
    grad_load.wait()
    swap_grad.wait()
    swap_h2.wait()

    @pl.loop(0, 4)
    def _(k):
        s = flip(z, k)
        g = slot(k)

        @pl.when(k > 0)
        def _():
            finish_slab(mlp, k)

        mlp_rows(s, 0, h2, gm, we, ws, bias_e_of(s), act, gpre, total, back, bias_e, half)

        @pl.when(k < 3)
        def _():
            pass_diagonal(mlp, k + 1)

        mlp_rows(s, 1, h2, gm, we, ws, bias_e_of(s), act, gpre, total, back, bias_e, half)

        @pl.when(k == 1)
        def _():
            sent_z(mlp)

        @pl.when(k > 1)
        def _():
            sent_xy(mlp, k - 1)

        @pl.when(k == 3)
        def _():
            sent_xy(mlp, 3)

        for side in range(2):
            columns = slice(side * half, side * half + half)
            we[g, side] = dot_tn(h2[:, columns], gpre[...]).astype(BF).reshape(we.shape[2:])
            ws[g, side] = dot_tn(act[: 2 * own], gm[:, columns]).astype(BF).reshape(ws.shape[2:])
        reduce_one(mlp, k)

        @pl.when(k == 1)
        def _():
            pass_xy(mlp, 3)

        @pl.when(k > 0)
        def _():
            reduce_two(mlp, k - 1)

    swap_mlp.start()
    swap_gh2.start()
    reduce_two(mlp, 3)
    swap_mlp.wait()
    swap_gh2.wait()

    def result_rows(rows):
        valid = keep[rows]
        mid = middle[rows]
        mlp_out = total[rows] + xr[rows] + shrink_bias
        result = mid + mlp_out
        h2[rows] = result.astype(BF)
        small[2:3, :] += column_sum(valid * result * result)
        small[4:5, :] += column_sum(valid * mlp_out * mlp_out)
        grad_out = gm[rows].astype(F32)
        small[11:12, :] += column_sum(grad_out)
        grad = back[rows] + xr2[rows]
        xhat, inverse = normalize(mid)
        small[8:9, :] += column_sum(grad * xhat)
        small[9:10, :] += column_sum(grad)
        grad_mid = grad_out + norm_back(grad, gain_two, xhat, inverse)
        middle[rows] = grad_mid
        low = grad_mid.astype(BF)
        gm[rows] = low
        small[10:11, :] += column_sum(low.astype(F32))

    over_rows(result_rows)
    swap_ga.start()
    result_store = pltpu.make_async_copy(h2.at[rows_own], block_out, local.at[8])
    result_store.start()
    back[...] = jnp.zeros_like(back)
    swap_ga.wait()

    @pl.loop(0, 4)
    def _(k):
        s = flip(z, k)
        g = slot(k)
        attention_back_slab(
            s, h1, gm, wq, wp, bias_q_of(s), rel_query, rel_back, codes, gqkv, back, bias_q, rel_acc, heads, half
        )

        @pl.when(k == 1)
        def _():
            sent_z(attn)

        @pl.when(k > 1)
        def _():
            sent_xy(attn, k - 1)

        @pl.when(k == 3)
        def _():
            sent_xy(attn, 3)

        for side in range(2):
            columns = slice(side * half, side * half + half)
            wq[g, side] = dot_tn(h1[:, columns], gqkv[: 2 * own]).astype(BF).reshape(wq.shape[2:])
            wp[g, side] = dot_tn(attended[s], gm[:, columns]).astype(BF).reshape(wp.shape[2:])
        reduce_one(attn, k)
        reduce_three(mlp, k)

        @pl.when(k > 0)
        def _():
            reduce_two(attn, k - 1)

    swap_gh1.start()
    reduce_two(attn, 3)
    reduce_four(mlp)
    swap_gh1.wait()

    def input_rows(rows):
        value = tokens[rows].astype(F32)
        grad = (back[rows] + xr[rows]) * keep[rows]
        xhat, inverse = normalize(value)
        small[6:7, :] += column_sum(grad * xhat)
        small[7:8, :] += column_sum(grad)
        middle[rows] = middle[rows] + norm_back(grad, gain_one, xhat, inverse)

    over_rows(input_rows)
    input_store = pltpu.make_async_copy(middle, input_grad, local.at[9])
    input_store.start()

    for s in range(4):
        at = SMALL_ROWS - 8 + s
        for side in range(2):

            @pl.when(r == side)
            def _():
                small[at + 4 * side : at + 4 * side + 1, :half] = bias_e[s]
                small[at + 4 * side : at + 4 * side + 1, half : half + bias_q.shape[2]] = bias_q[s]

    rel[...] = rel_acc[:LANES] + rel_acc[LANES:]

    def small_step(step, device):
        first = remote(small, small_got.at[step], csend, crecv, 12 + 2 * step, device)
        second = remote(rel, rel_got.at[step], csend, crecv, 13 + 2 * step, device)
        first.start()
        second.start()

        def finish():
            first.wait()
            second.wait()
            small[...] += small_got[step]
            rel[...] += rel_got[step]

        return finish

    finish = small_step(0, partner)
    reduce_three(attn, 0)
    finish()
    finish = small_step(1, along_x)
    reduce_three(attn, 1)
    reduce_three(attn, 2)
    finish()
    finish = small_step(2, along_y)
    reduce_three(attn, 3)
    reduce_five(mlp)
    finish()
    finish = small_step(3, along_z(1))
    reduce_four(attn)
    finish()
    finish = small_step(4, along_z(2))
    reduce_six(mlp)
    reduce_five(attn)
    finish()
    small_store = pltpu.make_async_copy(small, small_out, local.at[6])
    rel_store = pltpu.make_async_copy(rel, rel_out, local.at[7])
    small_store.start()
    rel_store.start()
    reduce_six(attn)

    swap_h1.wait_send()
    for k in (1, 2, 3):
        bias_copy(k).wait_send()
    for a in range(4):
        swap_out(a).wait()
        keep_out(a).wait()
        for kind in (1, 2, 3, 4):
            spread(a, kind).wait_send()
        for k in range(4):
            for kind in range(4):
                reduce_copy(a, k, kind).wait_send()
            if k > 0:
                reduce_copy(a, k, 4).wait_send()
    small_store.wait()
    rel_store.wait()
    result_store.wait()
    input_store.wait()


def run_kernel(
    tokens, keep, out_grad, vectors, biases, codes, rel_query, rel_back, qkv_src, proj_src, expand_src, shrink_src
):
    own, width = tokens.shape
    sources = (qkv_src, proj_src, expand_src, shrink_src)
    rows = [qkv_src.shape[2], proj_src.shape[2], expand_src.shape[1], shrink_src.shape[2]]
    lanes = [qkv_src.shape[3], proj_src.shape[3], width // 2, shrink_src.shape[3]]
    sds = jax.ShapeDtypeStruct
    any_spec = pl.BlockSpec(memory_space=pl.ANY)
    vmem_spec = pl.BlockSpec(memory_space=pltpu.VMEM)
    out_shape = [sds((own, width), BF), sds((own, width), F32)]
    out_shape += [sds((2, 2, n, l), BF) for n, l in zip(rows, lanes)]
    out_shape += [sds((SMALL_ROWS, width), F32), sds((LANES, LANES), F32)]
    first, second = zip(*[halves(n) for n in rows])
    out_shape += [sds((4, 2, n, l), BF) for n, l in zip(first, lanes)]
    out_shape += [sds((4, 2, n, l), BF) for n, l in zip(second, lanes)]
    out_shape += [sds((4, n, l), BF) for n, l in zip(second, lanes)]
    out_shape += [sds((4, n, l), BF) for n, l in zip(first, lanes)]
    out_shape += [sds((4, n, l), BF) for n, l in zip(rows, lanes)]
    both = 2 * own
    vmem, dma = pltpu.VMEM, pltpu.SemaphoreType.DMA
    hidden, qkv_width = lanes[3], lanes[0]
    scratch = [vmem((5, 2, 2, n, l), BF) for n, l in zip(rows, lanes)]
    scratch += [vmem((both, width), BF)] * 3
    scratch += [vmem((4, both, qkv_width // 3), BF)]
    scratch += [vmem((both, width), F32)] * 2
    scratch += [vmem((own, width), F32)] * 3
    deep = max(both, 3 * rows[2])
    scratch += [vmem((deep, hidden), BF), vmem((both, hidden), BF), vmem((deep, qkv_width), BF)]
    scratch += [vmem((4, 2, first[2], hidden), BF), vmem((2, 2, first[0], qkv_width), BF)]
    scratch += [vmem((4, 8, width), F32), vmem((SMALL_ROWS, width), F32), vmem((5, SMALL_ROWS, width), F32)]
    scratch += [vmem((LANES, LANES), F32), vmem((5, LANES, LANES), F32)]
    scratch += [vmem((4, 1, hidden), F32), vmem((4, 1, qkv_width), F32), vmem((2 * LANES, LANES), F32)]
    scratch += [dma((4, 4, 5))] * 4 + [dma((4, 5))] * 2 + [dma((22,))] * 2 + [dma((4,))] * 2 + [dma((10,))]
    got = pl.pallas_call(
        kernel,
        out_shape=out_shape,
        in_specs=[vmem_spec, vmem_spec, any_spec, vmem_spec, any_spec] + [vmem_spec] * 3 + [any_spec] * 4,
        out_specs=[any_spec] * len(out_shape),
        scratch_shapes=scratch,
        compiler_params=pltpu.CompilerParams(
            collective_id=0, has_side_effects=True, vmem_limit_bytes=VMEM_LIMIT
        ),
        name="block_step",
    )(tokens, keep, out_grad, vectors, biases, codes, rel_query, rel_back, *sources)
    return got[:8]


VMEM_LIMIT = 64 * 1024 * 1024 - 512 * 1024


def over_chips(
    tokens, valid_mask, out_grad, first_gain, first_shift, qkv_weight, qkv_bias, rel_height, rel_width,
    proj_weight, proj_bias, second_gain, second_shift, expand_weight, expand_bias, shrink_weight, shrink_bias,
):
    windows, per, width = tokens.shape
    side = (rel_height.shape[0] + 1) // 2
    count, head = rel_height.shape
    r = lax.axis_index("row")

    def padded(value):
        grid = value.reshape(windows, side, side, -1)
        grid = jnp.pad(grid, ((0, 0), (0, 0), (0, SIDE_PAD - side), (0, 0)))
        return grid.reshape(windows * side * SIDE_PAD, -1)

    def cut(value):
        grid = value.reshape(windows, side, SIDE_PAD, -1)[:, :, :side]
        return grid.reshape(windows, per, -1)

    rows, _, local_width = qkv_weight.shape
    part = local_width // 2
    hidden = expand_weight.shape[1] // 2
    qkv_src = qkv_weight.reshape(rows, 3, 2, part).transpose(2, 0, 1, 3).reshape(2, 2, rows // 2, 3 * part)
    proj_src = proj_weight.reshape(2, 2, part // 2, proj_weight.shape[1])
    expand_src = expand_weight.reshape(2, rows // 2, 2 * hidden)
    shrink_src = shrink_weight.reshape(2, 2, hidden // 2, shrink_weight.shape[1])
    zeros = jnp.zeros((part,), F32)
    query_bias, value_bias = (lax.dynamic_slice_in_dim(qkv_bias[i], r * part, part) for i in range(2))
    bias = jnp.concatenate(
        [lax.dynamic_slice_in_dim(expand_bias, r * hidden, hidden), query_bias, zeros, value_bias]
    )
    biases = jnp.pad(bias[None], ((0, 7), (0, width - bias.shape[0])))
    vectors = jnp.stack([first_gain, first_shift, second_gain, second_shift, proj_bias, shrink_bias])
    vectors = jnp.pad(vectors, ((0, 2), (0, 0)))
    rel_query, rel_back = relative_tables(rel_height, rel_width)
    keep = padded(valid_mask.astype(F32))
    got = run_kernel(
        padded(tokens), keep, padded(out_grad), vectors, biases, key_codes(), rel_query, rel_back,
        qkv_src, proj_src, expand_src, shrink_src,
    )
    block_low, grad, qkv_got, proj_got, expand_got, shrink_got, small, rel = got
    qkv_sum = qkv_got.astype(F32).reshape(2, rows, 3, part).transpose(1, 2, 0, 3).reshape(rows, 3, 2 * part)
    proj_sum = proj_got.astype(F32).reshape(2 * part, -1)
    expand_sum = expand_got.astype(F32).reshape(2, rows, hidden).transpose(1, 0, 2).reshape(rows, 2 * hidden)
    shrink_sum = shrink_got.astype(F32).reshape(2 * hidden, -1)
    rms = jnp.sqrt(jnp.sum(small[:5], axis=1) / (small[5, 0] * width))
    slabs = small[SMALL_ROWS - 8 :].reshape(2, 4, width)
    mine = lax.dynamic_index_in_dim(slabs, lax.axis_index("col"), axis=1, keepdims=False)
    expand_bias_sum = mine[:, :hidden].reshape(-1)
    qkv_bias_sum = mine[:, hidden : hidden + 3 * part].reshape(2, 3, part)[:, 0::2].transpose(1, 0, 2).reshape(2, -1)
    height_sum = rel[:count, :head][::-1]
    width_sum = rel[COL_W : COL_W + count, :head]
    return (
        cut(block_low),
        cut(grad),
        small[6],
        small[7],
        qkv_sum,
        qkv_bias_sum,
        height_sum,
        width_sum,
        proj_sum,
        small[10],
        small[8],
        small[9],
        expand_sum,
        expand_bias_sum,
        shrink_sum,
        small[11],
        rms,
    )


epsilon = 1e-06
highest = lax.Precision.HIGHEST


def layer_norm(values, norm_gain, norm_shift):
    center = values - jnp.mean(values, axis=-1, keepdims=True)
    spread = jnp.mean(center * center, axis=-1, keepdims=True)
    return center * lax.rsqrt(spread + epsilon) * norm_gain + norm_shift


def offset_table(span_size):
    positions = jnp.arange(span_size)
    offset = positions[:, None] - positions[None, :] + span_size - 1
    return (offset[:, :, None] == jnp.arange(2 * span_size - 1)[None, None, :]).astype(jnp.float32)


def attention_scores(
    query_rows, key_rows, rel_rows_table, rel_cols_table, onehot_table, span_size, scaling
):
    window_count, tokens_per, head_count, head_size = query_rows.shape
    rel_count = 2 * span_size - 1
    direct = (
        jnp.einsum("bthc,buhc->bhtu", query_rows, key_rows, preferred_element_type=jnp.float32)
        * scaling
    )
    query_float = query_rows.astype(jnp.float32)
    along_rows = jnp.einsum("bthc,jc->bhtj", query_float, rel_rows_table, precision=highest)
    along_cols = jnp.einsum("bthc,jc->bhtj", query_float, rel_cols_table, precision=highest)
    grid_rows = along_rows.reshape(window_count, head_count, span_size, span_size, rel_count)
    grid_cols = along_cols.reshape(window_count, head_count, span_size, span_size, rel_count)
    rel_rows = jnp.einsum("bhxyj,xkj->bhxyk", grid_rows, onehot_table, precision=highest)
    rel_cols = jnp.einsum("bhxyj,ywj->bhxyw", grid_cols, onehot_table, precision=highest)
    score_sum = direct.reshape(window_count, head_count, span_size, span_size, span_size, span_size)
    score_sum = score_sum + rel_rows[:, :, :, :, :, None] + rel_cols[:, :, :, :, None, :]
    return score_sum.reshape(window_count, head_count, tokens_per, tokens_per)


def relative_back(score_float, onehot_table, span_size):
    window_count, head_count, tokens_per, other_tokens = score_float.shape
    grid = score_float.reshape(window_count, head_count, span_size, span_size, span_size, span_size)
    rows_part = jnp.einsum("bhxykw,xkj->bhxyj", grid, onehot_table, precision=highest)
    cols_part = jnp.einsum("bhxykw,ywj->bhxyj", grid, onehot_table, precision=highest)
    return (
        rows_part.reshape(window_count, head_count, tokens_per, -1),
        cols_part.reshape(window_count, head_count, tokens_per, -1),
    )


def gather_weights(qkv_weight, proj_weight, expand_weight, shrink_weight):
    return (
        lax.all_gather(qkv_weight, "row", axis=0, tiled=True),
        lax.all_gather(proj_weight, "row", axis=1, tiled=True),
        lax.all_gather(expand_weight, "row", axis=0, tiled=True),
        lax.all_gather(shrink_weight, "row", axis=1, tiled=True),
    )


def gather_tokens(normed):
    return lax.all_gather(normed, "col", axis=0, tiled=True)


def gather_grads(grad_low):
    return lax.all_gather(grad_low, "col", axis=0, tiled=True)


def sum_branch(inputs_low, weight_full, own_windows):

    def term(first_row, row_count):
        return jnp.einsum(
            "btk,kd->btd", inputs_low, weight_full, preferred_element_type=jnp.float32
        )

    return lax.psum_scatter(
        term(jnp.int32(0), own_windows * lax.axis_size("col")),
        "col",
        scatter_dimension=0,
        tiled=True,
    )


def sum_input(grads_low, weight_full, own_windows):

    def term(first_row, row_count):
        return jnp.einsum("btk,dk->btd", grads_low, weight_full, preferred_element_type=jnp.float32)

    return lax.psum_scatter(
        term(jnp.int32(0), own_windows * lax.axis_size("col")),
        "col",
        scatter_dimension=0,
        tiled=True,
    )


def activate(values):
    return jax.nn.gelu(values, approximate=False)


def per_device(
    tokens,
    valid_mask,
    out_grad,
    first_gain,
    first_shift,
    qkv_weight,
    qkv_bias,
    rel_height,
    rel_width,
    proj_weight,
    proj_bias,
    second_gain,
    second_shift,
    expand_weight,
    expand_bias,
    shrink_weight,
    shrink_bias,
):
    span_size = (rel_height.shape[0] + 1) // 2
    head_size = rel_height.shape[1]
    local_width = qkv_weight.shape[2]
    head_count = local_width // head_size
    own_windows = tokens.shape[0]
    tokens_per = tokens.shape[1]
    model_width = tokens.shape[2]
    scaling = head_size ** (-0.5)
    onehot_table = offset_table(span_size)
    inputs = tokens.astype(jnp.float32)
    keep_mask = valid_mask.astype(jnp.float32)[:, :, None]

    def first_norm(values, norm_gain, norm_shift):
        return layer_norm(values, norm_gain, norm_shift) * keep_mask

    qkv_full, proj_full, expand_full, shrink_full = gather_weights(
        qkv_weight, proj_weight, expand_weight, shrink_weight
    )
    normed_first, first_back = jax.vjp(first_norm, inputs, first_gain, first_shift)
    first_all = gather_tokens(normed_first.astype(jnp.bfloat16))
    all_windows = first_all.shape[0]
    bias_rows = jnp.stack([qkv_bias[0], jnp.zeros_like(qkv_bias[0]), qkv_bias[1]])
    projected = (
        jnp.einsum("btd,dsk->btsk", first_all, qkv_full, preferred_element_type=jnp.float32)
        + bias_rows
    )
    projected = projected.astype(jnp.bfloat16)
    head_shape = (all_windows, tokens_per, head_count, head_size)
    query_low = projected[:, :, 0].reshape(head_shape)
    key_low = projected[:, :, 1].reshape(head_shape)
    value_low = projected[:, :, 2].reshape(head_shape)
    scores = attention_scores(
        query_low, key_low, rel_height, rel_width, onehot_table, span_size, scaling
    )
    top_score = jnp.max(scores, axis=-1, keepdims=True)
    log_total = top_score + jnp.log(jnp.sum(jnp.exp(scores - top_score), axis=-1, keepdims=True))
    probs_low = jnp.exp(scores - log_total).astype(jnp.bfloat16)
    attended = jnp.einsum(
        "bhtu,buhc->bthc", probs_low, value_low, preferred_element_type=jnp.float32
    )
    attended_low = attended.reshape(all_windows, tokens_per, local_width).astype(jnp.bfloat16)
    attn_out = sum_branch(attended_low, proj_full, own_windows) + proj_bias
    middle = inputs + attn_out
    normed_second, second_back = jax.vjp(layer_norm, middle, second_gain, second_shift)
    second_all = gather_tokens(normed_second.astype(jnp.bfloat16))
    hidden_pre = (
        jnp.einsum("btd,df->btf", second_all, expand_full, preferred_element_type=jnp.float32)
        + expand_bias
    )
    active_value, active_back = jax.vjp(activate, hidden_pre)
    hidden_low = active_value.astype(jnp.bfloat16)
    mlp_out = sum_branch(hidden_low, shrink_full, own_windows) + shrink_bias
    result = middle + mlp_out
    stat_terms = jnp.stack(
        [
            jnp.sum(keep_mask * inputs * inputs),
            jnp.sum(keep_mask * middle * middle),
            jnp.sum(keep_mask * result * result),
            jnp.sum(keep_mask * attn_out * attn_out),
            jnp.sum(keep_mask * mlp_out * mlp_out),
        ]
    )
    valid_count = jnp.sum(keep_mask)
    stat_total, count_total = lax.psum((stat_terms, valid_count), ("dp", "row", "col"))
    out_float = out_grad.astype(jnp.float32)
    qkv_full, proj_full, expand_full, shrink_full = gather_weights(
        qkv_weight, proj_weight, expand_weight, shrink_weight
    )
    mlp_grad_low = out_float.astype(jnp.bfloat16)
    shrink_bias_grad = jnp.sum(mlp_grad_low, axis=(0, 1), dtype=jnp.float32)
    mlp_grad_all = gather_grads(mlp_grad_low)
    shrink_grad_full = jnp.einsum(
        "btf,btd->fd", hidden_low, mlp_grad_all, preferred_element_type=jnp.float32
    )
    hidden_grad = jnp.einsum(
        "btd,fd->btf", mlp_grad_all, shrink_full, preferred_element_type=jnp.float32
    )
    pre_grad_low = active_back(hidden_grad)[0].astype(jnp.bfloat16)
    expand_bias_grad = jnp.sum(pre_grad_low, axis=(0, 1), dtype=jnp.float32)
    expand_grad_full = jnp.einsum(
        "btd,btf->df", second_all, pre_grad_low, preferred_element_type=jnp.float32
    )
    second_grad = sum_input(pre_grad_low, expand_full, own_windows)
    middle_part, second_gain_grad, second_shift_grad = second_back(second_grad)
    middle_grad = out_float + middle_part
    attn_grad_low = middle_grad.astype(jnp.bfloat16)
    proj_bias_grad = jnp.sum(attn_grad_low, axis=(0, 1), dtype=jnp.float32)
    attn_grad_all = gather_grads(attn_grad_low)
    proj_grad_full = jnp.einsum(
        "btk,btd->kd", attended_low, attn_grad_all, preferred_element_type=jnp.float32
    )
    attended_grad = jnp.einsum(
        "btd,kd->btk", attn_grad_all, proj_full, preferred_element_type=jnp.float32
    )
    attended_grad = attended_grad.astype(jnp.bfloat16).reshape(head_shape)
    scores_again = attention_scores(
        query_low, key_low, rel_height, rel_width, onehot_table, span_size, scaling
    )
    probs_float = jnp.exp(scores_again - log_total)
    probs_again = probs_float.astype(jnp.bfloat16)
    prob_grad = jnp.einsum(
        "bthc,buhc->bhtu", attended_grad, value_low, preferred_element_type=jnp.float32
    )
    value_grad = jnp.einsum(
        "bhtu,bthc->buhc", probs_again, attended_grad, preferred_element_type=jnp.float32
    )
    score_grad = probs_float * (
        prob_grad - jnp.sum(probs_float * prob_grad, axis=-1, keepdims=True)
    )
    score_low = score_grad.astype(jnp.bfloat16)
    rows_grad, cols_grad = relative_back(score_low.astype(jnp.float32), onehot_table, span_size)
    query_float = query_low.astype(jnp.float32)
    query_grad = (
        jnp.einsum("bhtu,buhc->bthc", score_low, key_low, preferred_element_type=jnp.float32)
        * scaling
    )
    query_grad = query_grad + jnp.einsum("bhtj,jc->bthc", rows_grad, rel_height, precision=highest)
    query_grad = query_grad + jnp.einsum("bhtj,jc->bthc", cols_grad, rel_width, precision=highest)
    key_grad = (
        jnp.einsum("bhtu,bthc->buhc", score_low, query_low, preferred_element_type=jnp.float32)
        * scaling
    )
    rel_height_grad = jnp.einsum("bhtj,bthc->jc", rows_grad, query_float, precision=highest)
    rel_width_grad = jnp.einsum("bhtj,bthc->jc", cols_grad, query_float, precision=highest)
    flat_shape = (all_windows, tokens_per, local_width)
    qkv_grad_low = jnp.stack(
        [
            query_grad.reshape(flat_shape),
            key_grad.reshape(flat_shape),
            value_grad.reshape(flat_shape),
        ],
        axis=2,
    ).astype(jnp.bfloat16)
    qkv_bias_grad = jnp.sum(qkv_grad_low[:, :, 0::2], axis=(0, 1), dtype=jnp.float32)
    qkv_grad_full = jnp.einsum(
        "btd,btsk->dsk", first_all, qkv_grad_low, preferred_element_type=jnp.float32
    )
    first_grad = sum_input(
        qkv_grad_low.reshape(all_windows, tokens_per, 3 * local_width),
        qkv_full.reshape(qkv_full.shape[0], 3 * local_width),
        own_windows,
    )
    input_part, first_gain_grad, first_shift_grad = first_back(first_grad)
    input_grad = middle_grad + input_part
    qkv_rows, proj_rows, expand_rows, shrink_rows = (
        lax.psum_scatter(qkv_grad_full, "row", scatter_dimension=0, tiled=True),
        lax.psum_scatter(proj_grad_full, "row", scatter_dimension=1, tiled=True),
        lax.psum_scatter(expand_grad_full, "row", scatter_dimension=0, tiled=True),
        lax.psum_scatter(shrink_grad_full, "row", scatter_dimension=1, tiled=True),
    )
    qkv_sum, proj_sum, expand_sum, shrink_sum = lax.psum(
        (qkv_rows, proj_rows, expand_rows, shrink_rows), "dp"
    )
    qkv_bias_sum, expand_bias_sum = lax.psum((qkv_bias_grad, expand_bias_grad), ("dp", "row"))
    (
        gain_one_sum,
        shift_one_sum,
        gain_two_sum,
        shift_two_sum,
        proj_bias_sum,
        shrink_bias_sum,
        height_sum,
        width_sum,
    ) = lax.psum(
        (
            first_gain_grad,
            first_shift_grad,
            second_gain_grad,
            second_shift_grad,
            proj_bias_grad,
            shrink_bias_grad,
            rel_height_grad,
            rel_width_grad,
        ),
        ("dp", "row", "col"),
    )
    rms = jnp.sqrt(stat_total / (count_total * model_width))
    return (
        result.astype(jnp.bfloat16),
        input_grad,
        gain_one_sum,
        shift_one_sum,
        qkv_sum,
        qkv_bias_sum,
        height_sum,
        width_sum,
        proj_sum,
        proj_bias_sum,
        gain_two_sum,
        shift_two_sum,
        expand_sum,
        expand_bias_sum,
        shrink_sum,
        shrink_bias_sum,
        rms,
    )


def choose(mesh):
    fits = tuple(mesh.shape[name] for name in ("dp", "row", "col")) == (4, 2, 4)
    return over_chips if fits else per_device


def solution(mesh):
    in_specs = (
        P(("dp", "row", "col"), None, None),
        P(("dp", "row", "col"), None),
        P(("dp", "row", "col"), None, None),
        P(),
        P(),
        P("row", None, "col"),
        P(None, "col"),
        P(),
        P(),
        P("col", "row"),
        P(),
        P(),
        P(),
        P("row", "col"),
        P("col"),
        P("col", "row"),
        P(),
    )
    out_specs = (
        P(("dp", "row", "col"), None, None),
        P(("dp", "row", "col"), None, None),
        P(),
        P(),
        P("row", None, "col"),
        P(None, "col"),
        P(),
        P(),
        P("col", "row"),
        P(),
        P(),
        P(),
        P("row", "col"),
        P("col"),
        P("col", "row"),
        P(),
        P(),
    )
    return jax.shard_map(
        choose(mesh), mesh=mesh, in_specs=in_specs, out_specs=out_specs, check_vma=False
    )
```

```python
import functools

import jax
import jax.numpy as jnp
import numpy as np
from jax import lax
from jax.experimental import pallas as pl
from jax.experimental.pallas import tpu as pltpu
from jax.sharding import PartitionSpec as P

BF = jnp.bfloat16
F32 = jnp.float32
LANES = 128
SIDE = 14
SIDE_PAD = 16
WROWS = SIDE * SIDE_PAD
HEAD = 80
AT_H = HEAD
AT_W = HEAD + SIDE
AT_MASK = HEAD + 2 * SIDE
COL_W = 64


def dot(a, b):
    return jnp.dot(a, b, preferred_element_type=F32)


def dot_nt(a, b):
    return lax.dot_general(a, b, (((1,), (1,)), ((), ())), preferred_element_type=F32)


def dot_tn(a, b):
    return lax.dot_general(a, b, (((0,), (0,)), ((), ())), preferred_element_type=F32)


def lane_ids():
    return lax.broadcasted_iota(jnp.int32, (WROWS, LANES), 1)


def row_ids():
    return lax.broadcasted_iota(jnp.int32, (WROWS, LANES), 0)


def key_codes():
    u = np.arange(WROWS)[:, None]
    lane = np.arange(LANES)[None, :]
    k, l = u // SIDE_PAD, u % SIDE_PAD
    height = lane - AT_H == k
    width = (lane - AT_W == l) & (l < SIDE)
    width_back = (AT_W + SIDE - 1 - lane == l) & (l < SIDE)
    plain = np.where(height | width, 1.0, 0.0)
    masked = np.where((lane == AT_MASK) & (l >= SIDE), -1e30, plain)
    back = np.where(height | width_back, 1.0, 0.0)
    return np.stack([masked, plain, back]).astype(BF)


def split_low(values):
    high = values.astype(BF)
    return high, (values - high.astype(F32)).astype(BF)


def relative_tables(rel_h, rel_w, rel_query, rel_back):
    count, rows = 2 * SIDE - 1, rel_h.shape[0]
    offset = lax.broadcasted_iota(jnp.int32, (rows, LANES), 0)
    lane = lax.broadcasted_iota(jnp.int32, (rows, LANES), 1)

    def places(first, step):
        return jnp.where((lane == first + step * offset) & (offset < count), 1.0, 0.0).astype(BF)

    heights, widths = places(count - 1, -1), places(COL_W + count - 1, -1)
    widths_back = places(COL_W, 1)
    tall, wide = rel_h[...], rel_w[...]
    rel_query[...] = jnp.zeros_like(rel_query)
    rel_back[...] = jnp.zeros_like(rel_back)
    for part, (a, b) in enumerate(zip(split_low(tall * HEAD**0.5), split_low(wide * HEAD**0.5))):
        at = part * LANES
        rel_query[at : at + HEAD] = (dot_tn(a, heights) + dot_tn(b, widths)).astype(BF)
    for part, (a, b) in enumerate(zip(split_low(tall), split_low(wide))):
        table = (dot_tn(heights, a) + dot_tn(widths_back, b)).astype(BF)
        for place in ((0, 1), (2,))[part]:
            rel_back[place * LANES : (place + 1) * LANES, :HEAD] = table


def query_codes(query, rel_query):
    full = dot(jnp.concatenate([query, query], axis=1), rel_query)
    tiles = full.reshape(SIDE, SIDE_PAD, LANES)
    heights = jnp.concatenate(
        [pltpu.roll(tiles[i], AT_H - (SIDE - 1 - i), 1) for i in range(SIDE)], axis=0
    )
    widths = pltpu.roll(
        tiles, AT_W - COL_W - (SIDE - 1), 2, stride=1, stride_axis=1
    ).reshape(WROWS, LANES)
    lane = lane_ids()
    codes = jnp.where(
        (lane >= AT_H) & (lane < AT_W),
        heights,
        jnp.where((lane >= AT_W) & (lane < AT_MASK), widths, 0.0),
    )
    high, rest = split_low(codes)
    first = query + high + jnp.where(lane == AT_MASK, 1.0, 0.0).astype(BF)
    return jnp.concatenate([first, rest], axis=1)


def softmax_rows(query, key, rel_query, codes_ref):
    left = query_codes(query, rel_query)
    right = jnp.concatenate([key + codes_ref[0], codes_ref[1]], axis=1)
    scores = dot_nt(left, right)
    top = jnp.max(scores, axis=1, keepdims=True)
    weights = jnp.exp((scores - top) * (HEAD**-0.5))
    return weights / jnp.sum(weights, axis=1, keepdims=True)


def attend(query, key, value, rel_query, codes_ref):
    probs = softmax_rows(query, key, rel_query, codes_ref)
    return dot(probs.astype(BF), value)


def attend_back(query, key, value, grad, rel_query, rel_back, codes_ref):
    probs = softmax_rows(query, key, rel_query, codes_ref)
    prob_grad = dot_nt(grad, value)
    inner = jnp.sum(probs * prob_grad, axis=1, keepdims=True)
    score_low = (probs * (prob_grad - inner)).astype(BF)
    value_grad = dot_tn(probs.astype(BF), grad)
    key_grad = dot_tn(score_low, query) * (HEAD**-0.5)
    mixed = dot(score_low, key + codes_ref[2])
    tiles = mixed.reshape(SIDE, SIDE_PAD, LANES)
    heights = jnp.concatenate(
        [pltpu.roll(tiles[i], (SIDE - 1 - i - AT_H) % LANES, 1) for i in range(SIDE)], axis=0
    )
    widths = pltpu.roll(
        tiles, (COL_W - AT_W) % LANES, 2, stride=1, stride_axis=1
    ).reshape(WROWS, LANES)
    lane, row = lane_ids(), row_ids()
    first_h = SIDE - 1 - row // SIDE_PAD
    first_w = COL_W + row % SIDE_PAD
    offsets = jnp.where(
        (lane >= first_h) & (lane < first_h + SIDE),
        heights,
        jnp.where((lane >= first_w) & (lane < first_w + SIDE), widths, 0.0),
    )
    high, rest = split_low(offsets)
    query_grad = jnp.where(lane < HEAD, mixed, 0.0) * (HEAD**-0.5) + dot(
        jnp.concatenate([high, rest, high], axis=1), rel_back
    )
    rel_grad = dot_tn(jnp.concatenate([high, rest], axis=1), query)
    return query_grad, key_grad, value_grad, rel_grad


def pad_head(piece):
    return jnp.concatenate([piece, jnp.zeros((piece.shape[0], LANES - HEAD), piece.dtype)], axis=1)


def qkv_low(s, rows, h1, wq, bias, half):
    return (dot_nt(h1[rows, :half], block(wq, s, 0)) + dot_nt(h1[rows, half:], block(wq, s, 1)) + bias).astype(BF)


def head_of(low, part, heads, hh):
    at = (part * heads + hh) * HEAD
    return pad_head(low[:, at : at + HEAD])


def attention_slab(s, h1, wq, wp, bias, rel_query, codes, attended, total, heads, half):
    @pl.loop(0, h1.shape[0] // WROWS)
    def _(m):
        rows = pl.ds(pl.multiple_of(m * WROWS, WROWS), WROWS)
        low = qkv_low(s, rows, h1, wq, bias, half)
        outs = []
        for hh in range(heads):
            query, key, value = (head_of(low, part, heads, hh) for part in range(3))
            outs.append(attend(query, key, value, rel_query[...], codes)[:, :HEAD])
        out_low = jnp.concatenate(outs, axis=1).astype(BF)
        attended[s, rows] = out_low
        total[rows, :half] += dot(out_low, block(wp, s, 0))
        total[rows, half:] += dot(out_low, block(wp, s, 1))


SQRT_HALF = 0.5**0.5
PDF_SCALE = 0.3989422804014327


def mlp_rows(s, m, h2, gm, we, ws, bias, act, gpre, total, back, bias_grad, half):
    count = h2.shape[0] // 4

    @pl.loop(0, 2)
    def _(step):
        rows = pl.ds(pl.multiple_of((2 * m + step) * count, count), count)
        pre = dot(h2[rows, :half], block(we, s, 0)) + dot(h2[rows, half:], block(we, s, 1)) + bias
        cdf = 0.5 + 0.5 * lax.erf(pre * SQRT_HALF)
        slope = cdf + pre * (PDF_SCALE * jnp.exp(-0.5 * pre * pre))
        act_low = (pre * cdf).astype(BF)
        act[rows, :] = act_low
        hidden = dot_nt(gm[rows, :half], block(ws, s, 0)) + dot_nt(gm[rows, half:], block(ws, s, 1))
        gpre_low = (hidden * slope).astype(BF)
        gpre[rows, :] = gpre_low
        bias_grad[s] += jnp.sum(gpre_low.astype(F32), axis=0, keepdims=True)
        total[rows, :half] += dot(act_low, block(ws, s, 0))
        total[rows, half:] += dot(act_low, block(ws, s, 1))
        back[rows, :half] += dot_nt(gpre_low, block(we, s, 0))
        back[rows, half:] += dot_nt(gpre_low, block(we, s, 1))


def attention_back_slab(
    s, h1, ga, wq, wp, bias, rel_query, rel_back, codes, gqkv, back, bias_grad, rel_grad, heads, half
):
    @pl.loop(0, h1.shape[0] // WROWS)
    def _(m):
        rows = pl.ds(pl.multiple_of(m * WROWS, WROWS), WROWS)
        low = qkv_low(s, rows, h1, wq, bias, half)
        grad = (dot_nt(ga[rows, :half], block(wp, s, 0)) + dot_nt(ga[rows, half:], block(wp, s, 1))).astype(BF)
        parts = [[], [], []]
        for hh in range(heads):
            query, key, value = (head_of(low, part, heads, hh) for part in range(3))
            got = attend_back(
                query, key, value, head_of(grad, 0, heads, hh), rel_query[...], rel_back[...], codes
            )
            for part in range(3):
                parts[part].append(got[part][:, :HEAD])
            rel_grad[...] += got[3]
        grad_low = jnp.concatenate(parts[0] + parts[1] + parts[2], axis=1).astype(BF)
        gqkv[rows, :] = grad_low
        bias_grad[s] += jnp.sum(grad_low.astype(F32), axis=0, keepdims=True)
        back[rows, :half] += dot(grad_low, block(wq, s, 0))
        back[rows, half:] += dot(grad_low, block(wq, s, 1))


MESH_ID = pl.DeviceIdType.MESH
ARRAYS = ("qkv", "proj", "expand", "shrink")
CHUNK = 64
EPS = 1e-06
SMALL_ROWS = 24
SPARE = 4


def halves(rows):
    first = (rows // 2 + 15) // 16 * 16
    return first, rows - first


def flip(index, k):
    return ((index // 2 + k // 2) % 2) * 2 + (index % 2 + k % 2) % 2


def block(ref, slab, half):
    value = ref[slab, half]
    return value.reshape(value.shape[0] * value.shape[1], value.shape[2])


def add_low(target, index, extra):
    target[index] = (target[index].astype(F32) + extra.astype(F32)).astype(BF)


def kernel(
    tokens, keep, out_grad, gain_one_in, shift_one_in, gain_two_in, shift_two_in, proj_bias_in, shrink_bias_in,
    qkv_bias_in, expand_bias_in, rel_h_in, rel_w_in, codes, qkv_src, proj_src, expand_src, shrink_src,
    block_out, input_grad, qkv_out, proj_out, expand_out, shrink_out, small_out, rel_out,
    rxq, rxp, rxe, rxs, ryq, ryp, rye, rys, rx2q, rx2p, rx2e, rx2s, ry2q, ry2p, ry2e, ry2s, rzq, rzp, rze, rzs,
    wq, wp, we, ws, h1, gm, h2, attended, total, back, xr, xr2, middle, act, gpre, gqkv, tmp,
    bias_all, small, small_got, rel, rel_got, bias_e, bias_q, rel_acc, rel_query, rel_back, rel_pad,
    gsend, grecv, rsend, rrecv, fsend, frecv, csend, crecv, zsend, zrecv, qsend, qrecv, local, qlocal,
):
    d, r, z = lax.axis_index("dp"), lax.axis_index("row"), lax.axis_index("col")
    h, b = d // 2, d % 2
    own = tokens.shape[0]
    width = tokens.shape[1]
    half = width // 2
    heads = 2
    bufs = (wq, wp, we, ws)
    outs = (qkv_out, proj_out, expand_out, shrink_out)
    rx, ry = (rxq, rxp, rxe, rxs), (ryq, ryp, rye, rys)
    rx2, ry2 = (rx2q, rx2p, rx2e, rx2s), (ry2q, ry2p, ry2e, ry2s)
    rz = (rzq, rzp, rze, rzs)
    parts = [halves(buf.shape[3]) for buf in bufs]
    attn, mlp, whole, shrink = (0, 1), (2, 3), (2,), (3,)

    along_x = (h * 2 + 1 - b, r, z)
    along_y = ((1 - h) * 2 + b, r, z)
    partner = (d, 1 - r, z)

    def along_z(k):
        return (d, r, flip(z, k))

    def remote(src, dst, sems, recvs, index, device, got=None):
        return pltpu.make_async_remote_copy(
            src_ref=src,
            dst_ref=dst,
            send_sem=sems.at[index],
            recv_sem=recvs.at[index if got is None else got],
            device_id=device,
            device_id_type=MESH_ID,
        )

    up = z // 2
    is_end = (z + 1) // 2 % 2 == 0
    is_inner = (z + 1) // 2 % 2 == 1

    def slab_of(i):
        far = i // 2
        return (1 - far) * flip(z, i) + far * ((1 - up) * i + up * (3 - i))

    def first_part(a):
        return pl.ds(0, parts[a][0])

    def second_part(a):
        return pl.ds(parts[a][0], parts[a][1])

    def gather_z(a, s, step):
        at = bufs[a].at[s] if a in whole else bufs[a].at[s, h, b]
        return remote(at, at, gsend, grecv, (a, s, 0 if step < 0 else 5), (d, r, z + step), (a, s, 0))

    def ring(a, slab, sends, recvs, index, kind, arriving):
        buf = bufs[a]
        if kind == 1:
            at, device = (buf.at[slab, h, 1 - b] if arriving else buf.at[slab, h, b]), along_x
        elif kind == 2:
            at, device = (buf.at[slab, 1 - h, b] if arriving else buf.at[slab, h, b]), along_y
        elif kind == 3:
            at = buf.at[slab, 1 - h if arriving else h, 1 - b, first_part(a)]
            device = along_y
        else:
            at = buf.at[slab, 1 - h, 1 - b if arriving else b, second_part(a)]
            device = along_x
        return remote(at, at, sends, recvs, index, device)

    def gather(a, s, kind, arriving=False):
        return ring(a, s, gsend, grecv, (a, s, kind), kind, arriving)

    def spread(a, kind, arriving=False):
        return ring(a, last_slab(a), fsend, frecv, (a, kind), kind, arriving)

    def sends_along_z(group, s, act_on):
        for a in group:

            @pl.when((s >= z) & (z > 0))
            def _():
                act_on(gather_z(a, s, -1))

            @pl.when((s <= z) & (z < 3))
            def _():
                act_on(gather_z(a, s, 1))

    def start_z(group):
        sends_along_z(group, z, lambda copy: copy.start())

    def arrive(group, i):
        s = slab_of(i)
        for a in group:
            gather_z(a, s, 1).wait_recv()
            sends_along_z((a,), s, lambda copy: copy.start())
            if a not in whole:
                gather(a, s, 1).start()
                gather(a, s, 2).start()

    def pass_diagonal(group, i):
        s = slab_of(i)
        for a in group:
            gather(a, s, 1, True).wait_recv()
            gather(a, s, 3).start()
            gather(a, s, 2, True).wait_recv()
            gather(a, s, 4).start()

    def finish_slab(group, i):
        s = slab_of(i)
        for a in group:
            gather(a, s, 3, True).wait_recv()
            gather(a, s, 4, True).wait_recv()

    def sent_slab(group, i):
        s = slab_of(i)
        sends_along_z(group, s, lambda copy: copy.wait_send())
        for a in group:
            if a not in whole:

                @pl.when(i > 0)
                def _():
                    for kind in (1, 2, 3, 4):
                        gather(a, s, kind).wait_send()

    def step_slab(a, n):
        return slab_of(n if a in mlp else 3 - n)

    def last_slab(a):
        return step_slab(a, 3)

    def slot(a, n):
        first = (4 - n) // 4
        return first * SPARE + (1 - first) * step_slab(a, n - 1 + first)

    def reduce_copy(a, n, kind):
        buf, g = bufs[a], slot(a, n)
        got = None
        if kind == 0:
            src, dst, device = buf.at[g, :, 1 - b, first_part(a)], rx[a].at[n], along_x
        elif kind == 1:
            src, dst, device = buf.at[g, 1 - h, :, second_part(a)], ry[a].at[n], along_y
        elif kind == 2:
            src, dst, device = buf.at[g, 1 - h, b, first_part(a)], ry2[a].at[n], along_y
        elif kind == 3:
            src, dst, device = buf.at[g, h, 1 - b, second_part(a)], rx2[a].at[n], along_x
        else:
            s = step_slab(a, n)
            src, dst, device = buf.at[g, h, b], rz[a].at[z], (d, r, s)
            got = (a, z, 4)
        return remote(src, dst, rsend, rrecv, (a, n, kind), device, got)

    def reduce_one(group, n):
        for a in group:
            reduce_copy(a, n, 0).start()
            reduce_copy(a, n, 1).start()

    def scratch(a, place):
        return tmp.at[place + (2 if a % 2 else 0)]

    def reduce_two(group, n):
        loads = []
        for a in group:
            reduce_copy(a, n, 0).wait_recv()
            reduce_copy(a, n, 1).wait_recv()
            for place, got in enumerate((rx[a], ry[a])):
                to = scratch(a, place).at[:, pl.ds(0, parts[a][place])]
                loads.append(pltpu.make_async_copy(got.at[n], to, local.at[a * 2 + place]))
                loads[-1].start()
        for i, a in enumerate(group):
            g = slot(a, n)
            first, second = parts[a]
            loads[2 * i].wait()
            for side in range(2):
                add_low(bufs[a], (g, side, b, first_part(a)), scratch(a, 0)[side, :first])
            reduce_copy(a, n, 2).start()
            loads[2 * i + 1].wait()
            for side in range(2):
                add_low(bufs[a], (g, h, side, second_part(a)), scratch(a, 1)[side, :second])
            reduce_copy(a, n, 3).start()

    def reduce_three(group, n):
        loads = []
        for a in group:
            reduce_copy(a, n, 2).wait_recv()
            reduce_copy(a, n, 3).wait_recv()
            for place, got in enumerate((ry2[a], rx2[a])):
                to = scratch(a, place).at[0, pl.ds(0, parts[a][place])]
                loads.append(pltpu.make_async_copy(got.at[n], to, local.at[a * 2 + place]))
                loads[-1].start()
        for i, a in enumerate(group):
            g = slot(a, n)
            first, second = parts[a]
            loads[2 * i].wait()
            add_low(bufs[a], (g, h, b, first_part(a)), scratch(a, 0)[0, :first])
            loads[2 * i + 1].wait()
            add_low(bufs[a], (g, h, b, second_part(a)), scratch(a, 1)[0, :second])

            @pl.when(step_slab(a, n) != z)
            def _():
                reduce_copy(a, n, 4).start()

    def reduce_four(group):
        for a in group:
            rows = bufs[a].shape[3]
            loads = []
            for k in (1, 2, 3):
                other = flip(z, k)
                at = rz[a].at[other]
                remote(at, at, rsend, rrecv, (a, k, 4), along_z(k), (a, other, 4)).wait_recv()
                loads.append(pltpu.make_async_copy(at, act.at[pl.ds((k - 1) * rows, rows)], local.at[k]))
                loads[-1].start()
            for load in loads:
                load.wait()
            value = bufs[a][slot(a, 0 if a in mlp else 3), h, b].astype(F32)
            for k in range(3):
                value = value + act[k * rows : (k + 1) * rows].astype(F32)
            bufs[a][last_slab(a), h, b] = value.astype(BF)
            spread(a, 1).start()
            spread(a, 2).start()

    def reduce_five(group):
        for a in group:
            spread(a, 1, True).wait_recv()
            spread(a, 3).start()
            spread(a, 2, True).wait_recv()
            spread(a, 4).start()

    def qkv_pieces(matrix, side, flat):
        rows = flat.shape[1]
        part = matrix.shape[2]
        cut = rows - part
        return (
            (matrix.at[0, side], flat.at[0, pl.ds(0, part)]),
            (matrix.at[1, side, pl.ds(0, cut)], flat.at[0, pl.ds(part, cut)]),
            (matrix.at[1, side, pl.ds(cut, part - cut)], flat.at[1, pl.ds(0, part - cut)]),
            (matrix.at[2, side], flat.at[1, pl.ds(part - cut, part)]),
        )

    def swap_out(a):
        mine = bufs[a].at[last_slab(a), 1 - r]
        if a == 0:
            pairs = qkv_pieces(outs[a], r, mine)
            return [remote(src, dst, qsend, qrecv, 4 + i, partner) for i, (dst, src) in enumerate(pairs)]
        to = outs[a].at[:, :, half_lanes(r)] if a == 2 else outs[a].at[r]
        return [remote(mine, to, fsend, frecv, (a, 0), partner)]

    def keep_out(a):
        mine = bufs[a].at[last_slab(a), r]
        if a == 0:
            pairs = qkv_pieces(outs[a], r, mine)
            return [pltpu.make_async_copy(src, dst, qlocal.at[i]) for i, (dst, src) in enumerate(pairs)]
        to = outs[a].at[:, :, half_lanes(r)] if a == 2 else outs[a].at[r]
        return [pltpu.make_async_copy(mine, to, local.at[a])]

    def reduce_six(group):
        for a in group:
            spread(a, 3, True).wait_recv()
            spread(a, 4, True).wait_recv()
            for copy in swap_out(a) + keep_out(a):
                copy.start()

    def half_lanes(side):
        return pl.ds(pl.multiple_of(side * half, half), half)

    def exchange(index, src, dst):
        return remote(src, dst, csend, crecv, index, partner)

    rows_own, rows_other = pl.ds(0, own), pl.ds(own, own)
    def source(a, side):
        if a == 2:
            return expand_src.at[:, :, half_lanes(side)]
        return (qkv_src, proj_src, expand_src, shrink_src)[a].at[side]

    def source_swap(a):
        to = bufs[a].at[z, r]
        if a == 0:
            pairs = qkv_pieces(qkv_src, 1 - r, to)
            return [remote(src, dst, qsend, qrecv, i, partner) for i, (src, dst) in enumerate(pairs)]
        return [exchange(a, source(a, 1 - r), to)]

    def source_keep(a):
        to = bufs[a].at[z, r]
        if a == 0:
            pairs = qkv_pieces(qkv_src, r, to)
            return [pltpu.make_async_copy(src, dst, qlocal.at[i]) for i, (src, dst) in enumerate(pairs)]
        return [pltpu.make_async_copy(source(a, r), to, local.at[a])]

    def start_source(group):
        for a in group:
            for copy in source_swap(a) + source_keep(a):
                copy.start()

    def finish_source(group):
        for a in group:
            for copy in source_swap(a) + source_keep(a):
                copy.wait()

    grad_load = pltpu.make_async_copy(out_grad, gm.at[rows_own], local.at[4])
    swap_grad = exchange(4, out_grad, gm.at[rows_other])
    swap_h1 = exchange(5, h1.at[rows_own], h1.at[rows_other])
    swap_attn = exchange(6, total.at[rows_other], xr)
    swap_h2 = exchange(7, h2.at[rows_own], h2.at[rows_other])
    swap_mlp = exchange(8, total.at[rows_other], xr)
    swap_gh2 = exchange(9, back.at[rows_other], xr2)
    swap_ga = exchange(10, gm.at[rows_own], gm.at[rows_other])
    swap_gh1 = exchange(11, back.at[rows_other], xr)

    def bias_copy(k, arriving=False):
        at = bias_all.at[flip(z, k) if arriving else z]
        return remote(at, at, zsend, zrecv, k, along_z(k))

    barrier = pltpu.get_barrier_semaphore()
    peers = [partner, along_x, along_y, along_z(1), along_z(2), along_z(3)]
    for peer in peers:
        pl.semaphore_signal(barrier, inc=1, device_id=peer, device_id_type=MESH_ID)
    pl.semaphore_wait(barrier, len(peers))

    start_source(attn)
    grad_load.start()
    bias_all[z] = jnp.zeros(bias_all.shape[1:], F32)
    part = qkv_bias_in.shape[1] // 2
    for side in range(2):

        @pl.when(r == side)
        def _():
            bias_all[z, 0:1, :half] = expand_bias_in[side * half : (side + 1) * half].reshape(1, half)
            for i in range(2):
                at = half + 2 * i * part
                bias_all[z, 0:1, at : at + part] = qkv_bias_in[i : i + 1, side * part : (side + 1) * part]

    finish_source(attn)
    start_z(attn)
    for k in (1, 2, 3):
        bias_copy(k).start()

    def as_row(ref):
        return ref[...].reshape(1, width)

    gain_one, shift_one, gain_two, shift_two, proj_bias, shrink_bias = (
        as_row(ref) for ref in (gain_one_in, shift_one_in, gain_two_in, shift_two_in, proj_bias_in, shrink_bias_in)
    )

    def over_rows(body):
        @pl.loop(0, own // CHUNK)
        def _(m):
            body(pl.ds(pl.multiple_of(m * CHUNK, CHUNK), CHUNK))

    def column_sum(value):
        return jnp.sum(value, axis=0, keepdims=True)

    def normalize(value):
        center = value - jnp.mean(value, axis=1, keepdims=True)
        inverse = lax.rsqrt(jnp.mean(center * center, axis=1, keepdims=True) + EPS)
        return center * inverse, inverse

    def norm_back(grad, gain, xhat, inverse):
        scaled = grad * gain
        mean = jnp.mean(scaled, axis=1, keepdims=True)
        along = jnp.mean(scaled * xhat, axis=1, keepdims=True)
        return (scaled - mean - xhat * along) * inverse

    small[...] = jnp.zeros_like(small)

    def first_rows(rows):
        value = tokens[rows].astype(F32)
        valid = keep[rows]
        xhat, _ = normalize(value)
        h1[rows] = ((xhat * gain_one + shift_one) * valid).astype(BF)
        small[0:1, :] += column_sum(valid * value * value)
        small[5:6, :] += jnp.broadcast_to(column_sum(valid), (1, width))

    over_rows(first_rows)
    swap_h1.start()
    start_source(mlp)
    swap_grad.start()
    rel_pad[...] = jnp.zeros_like(rel_pad)
    rel_pad[0, : rel_h_in.shape[0]] = rel_h_in[...]
    rel_pad[1, : rel_w_in.shape[0]] = rel_w_in[...]
    relative_tables(rel_pad.at[0], rel_pad.at[1], rel_query, rel_back)
    total[...] = jnp.zeros_like(total)
    swap_h1.wait_recv()

    def bias_q_of(s):
        return bias_all[s, 0:1, half : half + gqkv.shape[1]]

    def bias_e_of(s):
        return bias_all[s, 0:1, :half]

    @pl.loop(0, 4)
    def _(i):
        @pl.when(i == 1)
        def _():
            for k in (1, 2, 3):
                bias_copy(k, True).wait_recv()
            for n in (1, 2, 3):
                arrive(attn, n)
            finish_source(mlp)
            start_z((3, 2))
            for n in (1, 2, 3):
                pass_diagonal(attn, n)

        @pl.when(i > 0)
        def _():
            finish_slab(attn, i)

        s = slab_of(i)
        attention_slab(
            s, h1, wq, wp, bias_q_of(s), rel_query, codes, attended, total, heads, half
        )

    arrive(shrink, 1)

    @pl.when(is_inner)
    def _():
        arrive(shrink, 2)

    swap_attn.start()
    swap_attn.wait()

    def middle_rows(rows):
        value = tokens[rows].astype(F32)
        valid = keep[rows]
        attn_out = total[rows] + xr[rows] + proj_bias
        mid = value + attn_out
        middle[rows] = mid
        xhat, _ = normalize(mid)
        h2[rows] = (xhat * gain_two + shift_two).astype(BF)
        small[1:2, :] += column_sum(valid * mid * mid)
        small[3:4, :] += column_sum(valid * attn_out * attn_out)

    over_rows(middle_rows)
    swap_h2.start()
    total[...] = jnp.zeros_like(total)
    back[...] = jnp.zeros_like(back)
    bias_e[...] = jnp.zeros_like(bias_e)
    bias_q[...] = jnp.zeros_like(bias_q)
    rel_acc[...] = jnp.zeros_like(rel_acc)
    grad_load.wait()
    swap_grad.wait()
    swap_h2.wait()

    @pl.loop(0, 4)
    def _(n):
        s = slab_of(n)
        g = slot(2, n)

        @pl.when(n > 0)
        def _():
            finish_slab(shrink, n)

        mlp_rows(s, 0, h2, gm, we, ws, bias_e_of(s), act, gpre, total, back, bias_e, half)

        @pl.when(n == 0)
        def _():
            arrive(whole, 1)
            pass_diagonal(shrink, 1)

            @pl.when(is_inner)
            def _():
                arrive(whole, 2)
                pass_diagonal(shrink, 2)

        @pl.when((n == 1) | ((n == 2) & is_end))
        def _():
            arrive(shrink, n + 1 + (z + 1) // 2 % 2)

        mlp_rows(s, 1, h2, gm, we, ws, bias_e_of(s), act, gpre, total, back, bias_e, half)

        @pl.when(n > 0)
        def _():
            sent_slab(mlp, n - 1)

        @pl.when(n == 3)
        def _():
            sent_slab(mlp, 3)

        for side in range(2):
            columns = slice(side * half, side * half + half)
            we[g, side] = dot_tn(h2[:, columns], gpre[...]).astype(BF).reshape(we.shape[2:])
            ws[g, side] = dot_tn(act[: 2 * own], gm[:, columns]).astype(BF).reshape(ws.shape[2:])

        more = (n == 1) | ((n == 2) & is_end)

        @pl.when(more)
        def _():
            pass_diagonal(shrink, n + 1 + (z + 1) // 2 % 2)

        reduce_one(mlp, n)

        @pl.when(n > 0)
        def _():
            reduce_two(mlp, n - 1)

        @pl.when(n > 1)
        def _():
            reduce_three(mlp, n - 2)

        @pl.when(more)
        def _():
            arrive(whole, n + 1 + (z + 1) // 2 % 2)

    swap_mlp.start()
    swap_gh2.start()
    reduce_three(mlp, 2)
    swap_mlp.wait()
    swap_gh2.wait()

    def result_rows(rows):
        valid = keep[rows]
        mid = middle[rows]
        mlp_out = total[rows] + xr[rows] + shrink_bias
        result = mid + mlp_out
        h2[rows] = result.astype(BF)
        small[2:3, :] += column_sum(valid * result * result)
        small[4:5, :] += column_sum(valid * mlp_out * mlp_out)
        grad_out = gm[rows].astype(F32)
        small[11:12, :] += column_sum(grad_out)
        grad = back[rows] + xr2[rows]
        xhat, inverse = normalize(mid)
        small[8:9, :] += column_sum(grad * xhat)
        small[9:10, :] += column_sum(grad)
        grad_mid = grad_out + norm_back(grad, gain_two, xhat, inverse)
        middle[rows] = grad_mid
        low = grad_mid.astype(BF)
        gm[rows] = low
        small[10:11, :] += column_sum(low.astype(F32))

    over_rows(result_rows)
    swap_ga.start()
    result_store = pltpu.make_async_copy(h2.at[rows_own], block_out, local.at[8])
    result_store.start()
    back[...] = jnp.zeros_like(back)
    swap_ga.wait()

    reduce_two(mlp, 3)
    for i in range(4):
        sent_slab(attn, i)

    @pl.loop(0, 4)
    def _(n):
        s = slab_of(3 - n)
        g = slot(0, n)
        attention_back_slab(
            s, h1, gm, wq, wp, bias_q_of(s), rel_query, rel_back, codes, gqkv, back, bias_q, rel_acc, heads, half
        )
        for side in range(2):
            columns = slice(side * half, side * half + half)
            wq[g, side] = dot_tn(gqkv[...], h1[:, columns]).astype(BF).reshape(wq.shape[2:])
            wp[g, side] = dot_tn(attended[s], gm[:, columns]).astype(BF).reshape(wp.shape[2:])
        reduce_one(attn, n)

        @pl.when(n == 0)
        def _():
            reduce_three(mlp, 3)

        @pl.when(n > 0)
        def _():
            reduce_two(attn, n - 1)

        @pl.when(n > 1)
        def _():
            reduce_three(attn, n - 2)

    swap_gh1.start()
    reduce_four((2,))
    reduce_three(attn, 2)
    reduce_two(attn, 3)
    reduce_four((3,))
    swap_gh1.wait()

    def input_rows(rows):
        value = tokens[rows].astype(F32)
        grad = (back[rows] + xr[rows]) * keep[rows]
        xhat, inverse = normalize(value)
        small[6:7, :] += column_sum(grad * xhat)
        small[7:8, :] += column_sum(grad)
        middle[rows] = middle[rows] + norm_back(grad, gain_one, xhat, inverse)

    over_rows(input_rows)
    input_store = pltpu.make_async_copy(middle, input_grad, local.at[9])
    input_store.start()

    for s in range(4):
        at = SMALL_ROWS - 8 + s
        for side in range(2):

            @pl.when(r == side)
            def _():
                small[at + 4 * side : at + 4 * side + 1, :half] = bias_e[s]
                small[at + 4 * side : at + 4 * side + 1, half : half + bias_q.shape[2]] = bias_q[s]

    rel[...] = rel_acc[:LANES] + rel_acc[LANES:]

    def small_step(step, device):
        first = remote(small, small_got.at[step], csend, crecv, 12 + 2 * step, device)
        second = remote(rel, rel_got.at[step], csend, crecv, 13 + 2 * step, device)
        first.start()
        second.start()

        def finish():
            first.wait()
            second.wait()
            small[...] += small_got[step]
            rel[...] += rel_got[step]

        return finish

    finish = small_step(0, partner)
    reduce_three(attn, 3)
    finish()
    finish = small_step(1, along_x)
    reduce_four(attn)
    finish()
    finish = small_step(2, along_y)
    reduce_five(mlp)
    finish()
    finish = small_step(3, along_z(1))
    reduce_five(attn)
    finish()
    finish = small_step(4, along_z(2))
    reduce_six(mlp)
    finish()
    small_store = pltpu.make_async_copy(small, small_out, local.at[6])
    rel_store = pltpu.make_async_copy(rel, rel_out, local.at[7])
    small_store.start()
    rel_store.start()
    reduce_six(attn)

    swap_h1.wait_send()
    for k in (1, 2, 3):
        bias_copy(k).wait_send()
    for a in range(4):
        for copy in swap_out(a) + keep_out(a):
            copy.wait()
        for kind in (1, 2, 3, 4):
            spread(a, kind).wait_send()
        for n in range(4):
            for kind in range(4):
                reduce_copy(a, n, kind).wait_send()

            @pl.when(step_slab(a, n) != z)
            def _():
                reduce_copy(a, n, 4).wait_send()

    small_store.wait()
    rel_store.wait()
    result_store.wait()
    input_store.wait()


def run_kernel(tokens, keep, out_grad, vectors, qkv_bias, expand_bias, rel_height, rel_width, sources):
    own, width = tokens.shape
    half = width // 2
    rows = [source.shape[-2] for source in sources]
    rows[0] = 3 * rows[0] // 2
    sds = jax.ShapeDtypeStruct
    any_spec = pl.BlockSpec(memory_space=pl.ANY)
    vmem_spec = pl.BlockSpec(memory_space=pltpu.VMEM)
    out_shape = [sds((own, width), BF), sds((own, width), F32)]
    out_shape += [sds(source.shape, BF) for source in sources]
    out_shape += [sds((SMALL_ROWS, width), F32), sds((LANES, LANES), F32)]
    first, second = zip(*[halves(n) for n in rows])
    out_shape += [sds((4, 2, n, half), BF) for n in first]
    out_shape += [sds((4, 2, n, half), BF) for n in second]
    out_shape += [sds((4, n, half), BF) for n in second]
    out_shape += [sds((4, n, half), BF) for n in first]
    out_shape += [sds((4, n, half), BF) for n in rows]
    both = 2 * own
    vmem, dma = pltpu.VMEM, pltpu.SemaphoreType.DMA
    qkv_width = 2 * rows[0]
    scratch = [vmem((5, 2, 2, n, half), BF) for n in rows]
    scratch += [vmem((both, width), BF)] * 3
    scratch += [vmem((4, both, qkv_width // 3), BF)]
    scratch += [vmem((both, width), F32)] * 2
    scratch += [vmem((own, width), F32)] * 3
    scratch += [vmem((max(both, 3 * rows[2]), half), BF), vmem((both, half), BF), vmem((both, qkv_width), BF)]
    scratch += [vmem((4, 2, first[2], half), BF)]
    scratch += [vmem((4, 8, width), F32), vmem((SMALL_ROWS, width), F32), vmem((5, SMALL_ROWS, width), F32)]
    scratch += [vmem((LANES, LANES), F32), vmem((5, LANES, LANES), F32)]
    scratch += [vmem((4, 1, half), F32), vmem((4, 1, qkv_width), F32), vmem((2 * LANES, LANES), F32)]
    scratch += [vmem((2 * LANES, LANES), BF), vmem((3 * LANES, LANES), BF), vmem((2, 32, HEAD), F32)]
    scratch += [dma((4, 4, 6))] * 2 + [dma((4, 4, 5))] * 2 + [dma((4, 5))] * 2 + [dma((22,))] * 2
    scratch += [dma((4,))] * 2 + [dma((8,))] * 2 + [dma((10,)), dma((4,))]
    got = pl.pallas_call(
        kernel,
        out_shape=out_shape,
        in_specs=[vmem_spec, vmem_spec, any_spec] + [vmem_spec] * 11 + [any_spec] * 4,
        out_specs=[any_spec] * len(out_shape),
        scratch_shapes=scratch,
        compiler_params=pltpu.CompilerParams(
            collective_id=0, has_side_effects=True, vmem_limit_bytes=VMEM_LIMIT
        ),
        name="block_step",
    )(tokens, keep, out_grad, *vectors, qkv_bias, expand_bias, rel_height, rel_width, key_codes(), *sources)
    return got[:8]


VMEM_LIMIT = 64 * 1024 * 1024 - 512 * 1024


def over_chips(
    tokens, valid_mask, out_grad, first_gain, first_shift, qkv_weight, qkv_bias, rel_height, rel_width,
    proj_weight, proj_bias, second_gain, second_shift, expand_weight, expand_bias, shrink_weight, shrink_bias,
):
    windows, per, width = tokens.shape
    side = (rel_height.shape[0] + 1) // 2
    count, head = rel_height.shape

    def padded(value):
        grid = value.reshape(windows, side, side, -1)
        grid = jnp.pad(grid, ((0, 0), (0, 0), (0, SIDE_PAD - side), (0, 0)))
        return grid.reshape(windows * side * SIDE_PAD, -1)

    def cut(value):
        grid = value.reshape(windows, side, SIDE_PAD, -1)[:, :, :side]
        return grid.reshape(windows, per, -1)

    rows, _, local_width = qkv_weight.shape
    part = local_width // 2
    hidden = expand_weight.shape[1] // 2
    qkv_src = qkv_weight.transpose(1, 2, 0).reshape(3, 2, part, rows)
    proj_src = proj_weight.reshape(2, 2, part // 2, proj_weight.shape[1])
    expand_src = expand_weight.reshape(2, rows // 2, 2 * hidden)
    shrink_src = shrink_weight.reshape(2, 2, hidden // 2, shrink_weight.shape[1])
    vectors = (first_gain, first_shift, second_gain, second_shift, proj_bias, shrink_bias)
    keep = padded(valid_mask.astype(F32))
    got = run_kernel(
        padded(tokens), keep, padded(out_grad), vectors, qkv_bias, expand_bias, rel_height, rel_width,
        (qkv_src, proj_src, expand_src, shrink_src),
    )
    block_low, grad, qkv_got, proj_got, expand_got, shrink_got, small, rel = got
    qkv_sum = qkv_got.astype(F32).reshape(3, local_width, rows).transpose(2, 0, 1)
    proj_sum = proj_got.astype(F32).reshape(proj_weight.shape)
    expand_sum = expand_got.astype(F32).reshape(expand_weight.shape)
    shrink_sum = shrink_got.astype(F32).reshape(shrink_weight.shape)
    rms = jnp.sqrt(jnp.sum(small[:5], axis=1) / (small[5, 0] * width))
    slabs = small[SMALL_ROWS - 8 :].reshape(2, 4, width)
    mine = lax.dynamic_index_in_dim(slabs, lax.axis_index("col"), axis=1, keepdims=False)
    expand_bias_sum = mine[:, :hidden].reshape(-1)
    qkv_bias_sum = mine[:, hidden : hidden + 3 * part].reshape(2, 3, part)[:, 0::2].transpose(1, 0, 2).reshape(2, -1)
    height_sum = rel[:count, :head][::-1]
    width_sum = rel[COL_W : COL_W + count, :head]
    return (
        cut(block_low),
        cut(grad),
        small[6],
        small[7],
        qkv_sum,
        qkv_bias_sum,
        height_sum,
        width_sum,
        proj_sum,
        small[10],
        small[8],
        small[9],
        expand_sum,
        expand_bias_sum,
        shrink_sum,
        small[11],
        rms,
    )


epsilon = 1e-06
highest = lax.Precision.HIGHEST


def layer_norm(values, norm_gain, norm_shift):
    center = values - jnp.mean(values, axis=-1, keepdims=True)
    spread = jnp.mean(center * center, axis=-1, keepdims=True)
    return center * lax.rsqrt(spread + epsilon) * norm_gain + norm_shift


def offset_table(span_size):
    positions = jnp.arange(span_size)
    offset = positions[:, None] - positions[None, :] + span_size - 1
    return (offset[:, :, None] == jnp.arange(2 * span_size - 1)[None, None, :]).astype(jnp.float32)


def attention_scores(
    query_rows, key_rows, rel_rows_table, rel_cols_table, onehot_table, span_size, scaling
):
    window_count, tokens_per, head_count, head_size = query_rows.shape
    rel_count = 2 * span_size - 1
    direct = (
        jnp.einsum("bthc,buhc->bhtu", query_rows, key_rows, preferred_element_type=jnp.float32)
        * scaling
    )
    query_float = query_rows.astype(jnp.float32)
    along_rows = jnp.einsum("bthc,jc->bhtj", query_float, rel_rows_table, precision=highest)
    along_cols = jnp.einsum("bthc,jc->bhtj", query_float, rel_cols_table, precision=highest)
    grid_rows = along_rows.reshape(window_count, head_count, span_size, span_size, rel_count)
    grid_cols = along_cols.reshape(window_count, head_count, span_size, span_size, rel_count)
    rel_rows = jnp.einsum("bhxyj,xkj->bhxyk", grid_rows, onehot_table, precision=highest)
    rel_cols = jnp.einsum("bhxyj,ywj->bhxyw", grid_cols, onehot_table, precision=highest)
    score_sum = direct.reshape(window_count, head_count, span_size, span_size, span_size, span_size)
    score_sum = score_sum + rel_rows[:, :, :, :, :, None] + rel_cols[:, :, :, :, None, :]
    return score_sum.reshape(window_count, head_count, tokens_per, tokens_per)


def relative_back(score_float, onehot_table, span_size):
    window_count, head_count, tokens_per, other_tokens = score_float.shape
    grid = score_float.reshape(window_count, head_count, span_size, span_size, span_size, span_size)
    rows_part = jnp.einsum("bhxykw,xkj->bhxyj", grid, onehot_table, precision=highest)
    cols_part = jnp.einsum("bhxykw,ywj->bhxyj", grid, onehot_table, precision=highest)
    return (
        rows_part.reshape(window_count, head_count, tokens_per, -1),
        cols_part.reshape(window_count, head_count, tokens_per, -1),
    )


def gather_weights(qkv_weight, proj_weight, expand_weight, shrink_weight):
    return (
        lax.all_gather(qkv_weight, "row", axis=0, tiled=True),
        lax.all_gather(proj_weight, "row", axis=1, tiled=True),
        lax.all_gather(expand_weight, "row", axis=0, tiled=True),
        lax.all_gather(shrink_weight, "row", axis=1, tiled=True),
    )


def gather_tokens(normed):
    return lax.all_gather(normed, "col", axis=0, tiled=True)


def gather_grads(grad_low):
    return lax.all_gather(grad_low, "col", axis=0, tiled=True)


def sum_branch(inputs_low, weight_full, own_windows):

    def term(first_row, row_count):
        return jnp.einsum(
            "btk,kd->btd", inputs_low, weight_full, preferred_element_type=jnp.float32
        )

    return lax.psum_scatter(
        term(jnp.int32(0), own_windows * lax.axis_size("col")),
        "col",
        scatter_dimension=0,
        tiled=True,
    )


def sum_input(grads_low, weight_full, own_windows):

    def term(first_row, row_count):
        return jnp.einsum("btk,dk->btd", grads_low, weight_full, preferred_element_type=jnp.float32)

    return lax.psum_scatter(
        term(jnp.int32(0), own_windows * lax.axis_size("col")),
        "col",
        scatter_dimension=0,
        tiled=True,
    )


def activate(values):
    return jax.nn.gelu(values, approximate=False)


def per_device(
    tokens,
    valid_mask,
    out_grad,
    first_gain,
    first_shift,
    qkv_weight,
    qkv_bias,
    rel_height,
    rel_width,
    proj_weight,
    proj_bias,
    second_gain,
    second_shift,
    expand_weight,
    expand_bias,
    shrink_weight,
    shrink_bias,
):
    span_size = (rel_height.shape[0] + 1) // 2
    head_size = rel_height.shape[1]
    local_width = qkv_weight.shape[2]
    head_count = local_width // head_size
    own_windows = tokens.shape[0]
    tokens_per = tokens.shape[1]
    model_width = tokens.shape[2]
    scaling = head_size ** (-0.5)
    onehot_table = offset_table(span_size)
    inputs = tokens.astype(jnp.float32)
    keep_mask = valid_mask.astype(jnp.float32)[:, :, None]

    def first_norm(values, norm_gain, norm_shift):
        return layer_norm(values, norm_gain, norm_shift) * keep_mask

    qkv_full, proj_full, expand_full, shrink_full = gather_weights(
        qkv_weight, proj_weight, expand_weight, shrink_weight
    )
    normed_first, first_back = jax.vjp(first_norm, inputs, first_gain, first_shift)
    first_all = gather_tokens(normed_first.astype(jnp.bfloat16))
    all_windows = first_all.shape[0]
    bias_rows = jnp.stack([qkv_bias[0], jnp.zeros_like(qkv_bias[0]), qkv_bias[1]])
    projected = (
        jnp.einsum("btd,dsk->btsk", first_all, qkv_full, preferred_element_type=jnp.float32)
        + bias_rows
    )
    projected = projected.astype(jnp.bfloat16)
    head_shape = (all_windows, tokens_per, head_count, head_size)
    query_low = projected[:, :, 0].reshape(head_shape)
    key_low = projected[:, :, 1].reshape(head_shape)
    value_low = projected[:, :, 2].reshape(head_shape)
    scores = attention_scores(
        query_low, key_low, rel_height, rel_width, onehot_table, span_size, scaling
    )
    top_score = jnp.max(scores, axis=-1, keepdims=True)
    log_total = top_score + jnp.log(jnp.sum(jnp.exp(scores - top_score), axis=-1, keepdims=True))
    probs_low = jnp.exp(scores - log_total).astype(jnp.bfloat16)
    attended = jnp.einsum(
        "bhtu,buhc->bthc", probs_low, value_low, preferred_element_type=jnp.float32
    )
    attended_low = attended.reshape(all_windows, tokens_per, local_width).astype(jnp.bfloat16)
    attn_out = sum_branch(attended_low, proj_full, own_windows) + proj_bias
    middle = inputs + attn_out
    normed_second, second_back = jax.vjp(layer_norm, middle, second_gain, second_shift)
    second_all = gather_tokens(normed_second.astype(jnp.bfloat16))
    hidden_pre = (
        jnp.einsum("btd,df->btf", second_all, expand_full, preferred_element_type=jnp.float32)
        + expand_bias
    )
    active_value, active_back = jax.vjp(activate, hidden_pre)
    hidden_low = active_value.astype(jnp.bfloat16)
    mlp_out = sum_branch(hidden_low, shrink_full, own_windows) + shrink_bias
    result = middle + mlp_out
    stat_terms = jnp.stack(
        [
            jnp.sum(keep_mask * inputs * inputs),
            jnp.sum(keep_mask * middle * middle),
            jnp.sum(keep_mask * result * result),
            jnp.sum(keep_mask * attn_out * attn_out),
            jnp.sum(keep_mask * mlp_out * mlp_out),
        ]
    )
    valid_count = jnp.sum(keep_mask)
    stat_total, count_total = lax.psum((stat_terms, valid_count), ("dp", "row", "col"))
    out_float = out_grad.astype(jnp.float32)
    qkv_full, proj_full, expand_full, shrink_full = gather_weights(
        qkv_weight, proj_weight, expand_weight, shrink_weight
    )
    mlp_grad_low = out_float.astype(jnp.bfloat16)
    shrink_bias_grad = jnp.sum(mlp_grad_low, axis=(0, 1), dtype=jnp.float32)
    mlp_grad_all = gather_grads(mlp_grad_low)
    shrink_grad_full = jnp.einsum(
        "btf,btd->fd", hidden_low, mlp_grad_all, preferred_element_type=jnp.float32
    )
    hidden_grad = jnp.einsum(
        "btd,fd->btf", mlp_grad_all, shrink_full, preferred_element_type=jnp.float32
    )
    pre_grad_low = active_back(hidden_grad)[0].astype(jnp.bfloat16)
    expand_bias_grad = jnp.sum(pre_grad_low, axis=(0, 1), dtype=jnp.float32)
    expand_grad_full = jnp.einsum(
        "btd,btf->df", second_all, pre_grad_low, preferred_element_type=jnp.float32
    )
    second_grad = sum_input(pre_grad_low, expand_full, own_windows)
    middle_part, second_gain_grad, second_shift_grad = second_back(second_grad)
    middle_grad = out_float + middle_part
    attn_grad_low = middle_grad.astype(jnp.bfloat16)
    proj_bias_grad = jnp.sum(attn_grad_low, axis=(0, 1), dtype=jnp.float32)
    attn_grad_all = gather_grads(attn_grad_low)
    proj_grad_full = jnp.einsum(
        "btk,btd->kd", attended_low, attn_grad_all, preferred_element_type=jnp.float32
    )
    attended_grad = jnp.einsum(
        "btd,kd->btk", attn_grad_all, proj_full, preferred_element_type=jnp.float32
    )
    attended_grad = attended_grad.astype(jnp.bfloat16).reshape(head_shape)
    scores_again = attention_scores(
        query_low, key_low, rel_height, rel_width, onehot_table, span_size, scaling
    )
    probs_float = jnp.exp(scores_again - log_total)
    probs_again = probs_float.astype(jnp.bfloat16)
    prob_grad = jnp.einsum(
        "bthc,buhc->bhtu", attended_grad, value_low, preferred_element_type=jnp.float32
    )
    value_grad = jnp.einsum(
        "bhtu,bthc->buhc", probs_again, attended_grad, preferred_element_type=jnp.float32
    )
    score_grad = probs_float * (
        prob_grad - jnp.sum(probs_float * prob_grad, axis=-1, keepdims=True)
    )
    score_low = score_grad.astype(jnp.bfloat16)
    rows_grad, cols_grad = relative_back(score_low.astype(jnp.float32), onehot_table, span_size)
    query_float = query_low.astype(jnp.float32)
    query_grad = (
        jnp.einsum("bhtu,buhc->bthc", score_low, key_low, preferred_element_type=jnp.float32)
        * scaling
    )
    query_grad = query_grad + jnp.einsum("bhtj,jc->bthc", rows_grad, rel_height, precision=highest)
    query_grad = query_grad + jnp.einsum("bhtj,jc->bthc", cols_grad, rel_width, precision=highest)
    key_grad = (
        jnp.einsum("bhtu,bthc->buhc", score_low, query_low, preferred_element_type=jnp.float32)
        * scaling
    )
    rel_height_grad = jnp.einsum("bhtj,bthc->jc", rows_grad, query_float, precision=highest)
    rel_width_grad = jnp.einsum("bhtj,bthc->jc", cols_grad, query_float, precision=highest)
    flat_shape = (all_windows, tokens_per, local_width)
    qkv_grad_low = jnp.stack(
        [
            query_grad.reshape(flat_shape),
            key_grad.reshape(flat_shape),
            value_grad.reshape(flat_shape),
        ],
        axis=2,
    ).astype(jnp.bfloat16)
    qkv_bias_grad = jnp.sum(qkv_grad_low[:, :, 0::2], axis=(0, 1), dtype=jnp.float32)
    qkv_grad_full = jnp.einsum(
        "btd,btsk->dsk", first_all, qkv_grad_low, preferred_element_type=jnp.float32
    )
    first_grad = sum_input(
        qkv_grad_low.reshape(all_windows, tokens_per, 3 * local_width),
        qkv_full.reshape(qkv_full.shape[0], 3 * local_width),
        own_windows,
    )
    input_part, first_gain_grad, first_shift_grad = first_back(first_grad)
    input_grad = middle_grad + input_part
    qkv_rows, proj_rows, expand_rows, shrink_rows = (
        lax.psum_scatter(qkv_grad_full, "row", scatter_dimension=0, tiled=True),
        lax.psum_scatter(proj_grad_full, "row", scatter_dimension=1, tiled=True),
        lax.psum_scatter(expand_grad_full, "row", scatter_dimension=0, tiled=True),
        lax.psum_scatter(shrink_grad_full, "row", scatter_dimension=1, tiled=True),
    )
    qkv_sum, proj_sum, expand_sum, shrink_sum = lax.psum(
        (qkv_rows, proj_rows, expand_rows, shrink_rows), "dp"
    )
    qkv_bias_sum, expand_bias_sum = lax.psum((qkv_bias_grad, expand_bias_grad), ("dp", "row"))
    (
        gain_one_sum,
        shift_one_sum,
        gain_two_sum,
        shift_two_sum,
        proj_bias_sum,
        shrink_bias_sum,
        height_sum,
        width_sum,
    ) = lax.psum(
        (
            first_gain_grad,
            first_shift_grad,
            second_gain_grad,
            second_shift_grad,
            proj_bias_grad,
            shrink_bias_grad,
            rel_height_grad,
            rel_width_grad,
        ),
        ("dp", "row", "col"),
    )
    rms = jnp.sqrt(stat_total / (count_total * model_width))
    return (
        result.astype(jnp.bfloat16),
        input_grad,
        gain_one_sum,
        shift_one_sum,
        qkv_sum,
        qkv_bias_sum,
        height_sum,
        width_sum,
        proj_sum,
        proj_bias_sum,
        gain_two_sum,
        shift_two_sum,
        expand_sum,
        expand_bias_sum,
        shrink_sum,
        shrink_bias_sum,
        rms,
    )


def choose(mesh):
    fits = tuple(mesh.shape[name] for name in ("dp", "row", "col")) == (4, 2, 4)
    return over_chips if fits else per_device


def solution(mesh):
    in_specs = (
        P(("dp", "row", "col"), None, None),
        P(("dp", "row", "col"), None),
        P(("dp", "row", "col"), None, None),
        P(),
        P(),
        P("row", None, "col"),
        P(None, "col"),
        P(),
        P(),
        P("col", "row"),
        P(),
        P(),
        P(),
        P("row", "col"),
        P("col"),
        P("col", "row"),
        P(),
    )
    out_specs = (
        P(("dp", "row", "col"), None, None),
        P(("dp", "row", "col"), None, None),
        P(),
        P(),
        P("row", None, "col"),
        P(None, "col"),
        P(),
        P(),
        P("col", "row"),
        P(),
        P(),
        P(),
        P("row", "col"),
        P("col"),
        P("col", "row"),
        P(),
        P(),
    )
    return jax.shard_map(
        choose(mesh), mesh=mesh, in_specs=in_specs, out_specs=out_specs, check_vma=False
    )
```

```python
import functools

import jax
import jax.numpy as jnp
import numpy as np
from jax import lax
from jax.experimental import pallas as pl
from jax.experimental.pallas import tpu as pltpu
from jax.sharding import PartitionSpec as P

BF = jnp.bfloat16
F32 = jnp.float32
LANES = 128
SIDE = 14
SIDE_PAD = 16
WROWS = SIDE * SIDE_PAD
HEAD = 80
AT_H = HEAD
AT_W = HEAD + SIDE
AT_MASK = HEAD + 2 * SIDE
COL_W = 64


def dot(a, b):
    return jnp.dot(a, b, preferred_element_type=F32)


def dot_nt(a, b):
    return lax.dot_general(a, b, (((1,), (1,)), ((), ())), preferred_element_type=F32)


def dot_tn(a, b):
    return lax.dot_general(a, b, (((0,), (0,)), ((), ())), preferred_element_type=F32)


def lane_ids():
    return lax.broadcasted_iota(jnp.int32, (WROWS, LANES), 1)


def row_ids():
    return lax.broadcasted_iota(jnp.int32, (WROWS, LANES), 0)


def key_codes():
    u = np.arange(WROWS)[:, None]
    lane = np.arange(LANES)[None, :]
    k, l = u // SIDE_PAD, u % SIDE_PAD
    height = lane - AT_H == k
    width = (lane - AT_W == l) & (l < SIDE)
    width_back = (AT_W + SIDE - 1 - lane == l) & (l < SIDE)
    plain = np.where(height | width, 1.0, 0.0)
    masked = np.where((lane == AT_MASK) & (l >= SIDE), -1e30, plain)
    back = np.where(height | width_back, 1.0, 0.0)
    return np.stack([masked, plain, back]).astype(BF)


def split_low(values):
    high = values.astype(BF)
    return high, (values - high.astype(F32)).astype(BF)


def relative_tables(rel_h, rel_w, rel_query, rel_back):
    count, rows = 2 * SIDE - 1, rel_h.shape[0]
    offset = lax.broadcasted_iota(jnp.int32, (rows, LANES), 0)
    lane = lax.broadcasted_iota(jnp.int32, (rows, LANES), 1)

    def places(first, step):
        return jnp.where((lane == first + step * offset) & (offset < count), 1.0, 0.0).astype(BF)

    heights, widths = places(count - 1, -1), places(COL_W + count - 1, -1)
    widths_back = places(COL_W, 1)
    tall, wide = rel_h[...], rel_w[...]
    rel_query[...] = jnp.zeros_like(rel_query)
    rel_back[...] = jnp.zeros_like(rel_back)
    for part, (a, b) in enumerate(zip(split_low(tall * HEAD**0.5), split_low(wide * HEAD**0.5))):
        at = part * LANES
        rel_query[at : at + HEAD] = (dot_tn(a, heights) + dot_tn(b, widths)).astype(BF)
    for part, (a, b) in enumerate(zip(split_low(tall), split_low(wide))):
        table = (dot_tn(heights, a) + dot_tn(widths_back, b)).astype(BF)
        for place in ((0, 1), (2,))[part]:
            rel_back[place * LANES : (place + 1) * LANES, :HEAD] = table


def query_codes(query, rel_query):
    full = dot(jnp.concatenate([query, query], axis=1), rel_query)
    tiles = full.reshape(SIDE, SIDE_PAD, LANES)
    heights = jnp.concatenate(
        [pltpu.roll(tiles[i], AT_H - (SIDE - 1 - i), 1) for i in range(SIDE)], axis=0
    )
    widths = pltpu.roll(
        tiles, AT_W - COL_W - (SIDE - 1), 2, stride=1, stride_axis=1
    ).reshape(WROWS, LANES)
    lane = lane_ids()
    codes = jnp.where(
        (lane >= AT_H) & (lane < AT_W),
        heights,
        jnp.where((lane >= AT_W) & (lane < AT_MASK), widths, 0.0),
    )
    high, rest = split_low(codes)
    first = query + high + jnp.where(lane == AT_MASK, 1.0, 0.0).astype(BF)
    return jnp.concatenate([first, rest], axis=1)


def softmax_rows(query, key, rel_query, codes_ref):
    left = query_codes(query, rel_query)
    right = jnp.concatenate([key + codes_ref[0], codes_ref[1]], axis=1)
    scores = dot_nt(left, right)
    top = jnp.max(scores, axis=1, keepdims=True)
    weights = jnp.exp((scores - top) * (HEAD**-0.5))
    return weights / jnp.sum(weights, axis=1, keepdims=True)


def attend(query, key, value, rel_query, codes_ref):
    probs = softmax_rows(query, key, rel_query, codes_ref)
    return dot(probs.astype(BF), value)


def attend_back(query, key, value, grad, rel_query, rel_back, codes_ref):
    probs = softmax_rows(query, key, rel_query, codes_ref)
    prob_grad = dot_nt(grad, value)
    inner = jnp.sum(probs * prob_grad, axis=1, keepdims=True)
    score_low = (probs * (prob_grad - inner)).astype(BF)
    value_grad = dot_tn(probs.astype(BF), grad)
    key_grad = dot_tn(score_low, query) * (HEAD**-0.5)
    mixed = dot(score_low, key + codes_ref[2])
    tiles = mixed.reshape(SIDE, SIDE_PAD, LANES)
    heights = jnp.concatenate(
        [pltpu.roll(tiles[i], (SIDE - 1 - i - AT_H) % LANES, 1) for i in range(SIDE)], axis=0
    )
    widths = pltpu.roll(
        tiles, (COL_W - AT_W) % LANES, 2, stride=1, stride_axis=1
    ).reshape(WROWS, LANES)
    lane, row = lane_ids(), row_ids()
    first_h = SIDE - 1 - row // SIDE_PAD
    first_w = COL_W + row % SIDE_PAD
    offsets = jnp.where(
        (lane >= first_h) & (lane < first_h + SIDE),
        heights,
        jnp.where((lane >= first_w) & (lane < first_w + SIDE), widths, 0.0),
    )
    high, rest = split_low(offsets)
    query_grad = jnp.where(lane < HEAD, mixed, 0.0) * (HEAD**-0.5) + dot(
        jnp.concatenate([high, rest, high], axis=1), rel_back
    )
    rel_grad = dot_tn(jnp.concatenate([high, rest], axis=1), query)
    return query_grad, key_grad, value_grad, rel_grad


def pad_head(piece):
    return jnp.concatenate([piece, jnp.zeros((piece.shape[0], LANES - HEAD), piece.dtype)], axis=1)


def qkv_low(s, rows, h1, wq, bias, half):
    return (dot_nt(h1[rows, :half], block(wq, s, 0)) + dot_nt(h1[rows, half:], block(wq, s, 1)) + bias).astype(BF)


def head_of(low, part, heads, hh):
    at = (part * heads + hh) * HEAD
    return pad_head(low[:, at : at + HEAD])


def attention_slab(s, h1, wq, wp, bias, rel_query, codes, attended, total, heads, half):
    @pl.loop(0, h1.shape[0] // WROWS)
    def _(m):
        rows = pl.ds(pl.multiple_of(m * WROWS, WROWS), WROWS)
        low = qkv_low(s, rows, h1, wq, bias, half)
        outs = []
        for hh in range(heads):
            query, key, value = (head_of(low, part, heads, hh) for part in range(3))
            outs.append(attend(query, key, value, rel_query[...], codes)[:, :HEAD])
        out_low = jnp.concatenate(outs, axis=1).astype(BF)
        attended[s, rows] = out_low
        total[rows, :half] += dot(out_low, block(wp, s, 0))
        total[rows, half:] += dot(out_low, block(wp, s, 1))


SQRT_HALF = 0.5**0.5
PDF_SCALE = 0.3989422804014327


def mlp_rows(s, m, h2, gm, we, ws, bias, act, gpre, total, back, bias_grad, half):
    count = h2.shape[0] // 4

    @pl.loop(0, 2)
    def _(step):
        rows = pl.ds(pl.multiple_of((2 * m + step) * count, count), count)
        pre = dot(h2[rows, :half], block(we, s, 0)) + dot(h2[rows, half:], block(we, s, 1)) + bias
        cdf = 0.5 + 0.5 * lax.erf(pre * SQRT_HALF)
        slope = cdf + pre * (PDF_SCALE * jnp.exp(-0.5 * pre * pre))
        act_low = (pre * cdf).astype(BF)
        act[rows, :] = act_low
        hidden = dot_nt(gm[rows, :half], block(ws, s, 0)) + dot_nt(gm[rows, half:], block(ws, s, 1))
        gpre_low = (hidden * slope).astype(BF)
        gpre[rows, :] = gpre_low
        bias_grad[s] += jnp.sum(gpre_low.astype(F32), axis=0, keepdims=True)
        total[rows, :half] += dot(act_low, block(ws, s, 0))
        total[rows, half:] += dot(act_low, block(ws, s, 1))
        back[rows, :half] += dot_nt(gpre_low, block(we, s, 0))
        back[rows, half:] += dot_nt(gpre_low, block(we, s, 1))


def attention_back_slab(
    s, first, h1, ga, wq, wp, bias, rel_query, rel_back, codes, gqkv, back, bias_grad, rel_grad, heads, half
):
    count = h1.shape[0] // WROWS // 2

    @pl.loop(0, count)
    def _(m):
        rows = pl.ds(pl.multiple_of((first * count + m) * WROWS, WROWS), WROWS)
        low = qkv_low(s, rows, h1, wq, bias, half)
        grad = (dot_nt(ga[rows, :half], block(wp, s, 0)) + dot_nt(ga[rows, half:], block(wp, s, 1))).astype(BF)
        parts = [[], [], []]
        for hh in range(heads):
            query, key, value = (head_of(low, part, heads, hh) for part in range(3))
            got = attend_back(
                query, key, value, head_of(grad, 0, heads, hh), rel_query[...], rel_back[...], codes
            )
            for part in range(3):
                parts[part].append(got[part][:, :HEAD])
            rel_grad[...] += got[3]
        grad_low = jnp.concatenate(parts[0] + parts[1] + parts[2], axis=1).astype(BF)
        gqkv[rows, :] = grad_low
        bias_grad[s] += jnp.sum(grad_low.astype(F32), axis=0, keepdims=True)
        back[rows, :half] += dot(grad_low, block(wq, s, 0))
        back[rows, half:] += dot(grad_low, block(wq, s, 1))


MESH_ID = pl.DeviceIdType.MESH
ARRAYS = ("qkv", "proj", "expand", "shrink")
CHUNK = 64
EPS = 1e-06
SPARE = 4


def halves(rows):
    first = (rows // 2 + 15) // 16 * 16
    return first, rows - first


def flip(index, k):
    return ((index // 2 + k // 2) % 2) * 2 + (index % 2 + k % 2) % 2


def block(ref, slab, half):
    value = ref[slab, half]
    return value.reshape(value.shape[0] * value.shape[1], value.shape[2])


def add_low(target, index, extra):
    target[index] = (target[index].astype(F32) + extra.astype(F32)).astype(BF)


def kernel(
    tokens, keep, out_grad, gain_one_in, shift_one_in, gain_two_in, shift_two_in, proj_bias_in, shrink_bias_in,
    qkv_bias_in, expand_bias_in, rel_h_in, rel_w_in, codes, qkv_src, proj_src, expand_src, shrink_src,
    block_out, input_grad, qkv_out, proj_out, expand_out, shrink_out, early_out, late_out, rel_out,
    rxq, rxp, rxe, rxs, ryq, ryp, rye, rys, rx2q, rx2p, rx2e, rx2s, ry2q, ry2p, ry2e, ry2s, rzq, rzp, rze, rzs,
    wq, wp, we, ws, h1, gm, h2, attended, total, back, xr, xr2, middle, act, gpre, gqkv, tmp,
    bias_all, early, early_got, late, late_got, rel, rel_got, bias_e, bias_q, rel_acc, rel_query, rel_back, rel_pad,
    gsend, grecv, rsend, rrecv, fsend, frecv, csend, crecv, zsend, zrecv, qsend, qrecv, local, qlocal,
):
    d, r, z = lax.axis_index("dp"), lax.axis_index("row"), lax.axis_index("col")
    h, b = d // 2, d % 2
    own = tokens.shape[0]
    width = tokens.shape[1]
    half = width // 2
    heads = 2
    bufs = (wq, wp, we, ws)
    outs = (qkv_out, proj_out, expand_out, shrink_out)
    rx, ry = (rxq, rxp, rxe, rxs), (ryq, ryp, rye, rys)
    rx2, ry2 = (rx2q, rx2p, rx2e, rx2s), (ry2q, ry2p, ry2e, ry2s)
    rz = (rzq, rzp, rze, rzs)
    parts = [halves(buf.shape[3]) for buf in bufs]
    attn, mlp, whole, shrink = (0, 1), (2, 3), (2,), (3,)

    along_x = (h * 2 + 1 - b, r, z)
    along_y = ((1 - h) * 2 + b, r, z)
    across = ((1 - h) * 2 + 1 - b, r, z)
    partner = (d, 1 - r, z)

    def along_z(k):
        return (d, r, flip(z, k))

    def remote(src, dst, sems, recvs, index, device, got=None):
        return pltpu.make_async_remote_copy(
            src_ref=src,
            dst_ref=dst,
            send_sem=sems.at[index],
            recv_sem=recvs.at[index if got is None else got],
            device_id=device,
            device_id_type=MESH_ID,
        )

    up = z // 2
    is_end = (z + 1) // 2 % 2 == 0
    is_inner = (z + 1) // 2 % 2 == 1

    def slab_of(i):
        far = i // 2
        return (1 - far) * flip(z, i) + far * ((1 - up) * i + up * (3 - i))

    def first_part(a):
        return pl.ds(0, parts[a][0])

    def second_part(a):
        return pl.ds(parts[a][0], parts[a][1])

    def gather_z(a, s, step):
        at = bufs[a].at[s] if a in whole else bufs[a].at[s, h, b]
        return remote(at, at, gsend, grecv, (a, s, 0 if step < 0 else 5), (d, r, z + step), (a, s, 0))

    def ring(a, slab, sends, recvs, index, kind, arriving):
        buf = bufs[a]
        if kind == 1:
            at, device = (buf.at[slab, h, 1 - b] if arriving else buf.at[slab, h, b]), along_x
        elif kind == 2:
            at, device = (buf.at[slab, 1 - h, b] if arriving else buf.at[slab, h, b]), along_y
        elif kind == 3:
            at = buf.at[slab, 1 - h if arriving else h, 1 - b, first_part(a)]
            device = along_y
        else:
            at = buf.at[slab, 1 - h, 1 - b if arriving else b, second_part(a)]
            device = along_x
        return remote(at, at, sends, recvs, index, device)

    def gather(a, s, kind, arriving=False):
        return ring(a, s, gsend, grecv, (a, s, kind), kind, arriving)

    def spread(a, kind, arriving=False):
        return ring(a, last_slab(a), fsend, frecv, (a, kind), kind, arriving)

    def sends_along_z(group, s, act_on):
        for a in group:

            @pl.when((s >= z) & (z > 0))
            def _():
                act_on(gather_z(a, s, -1))

            @pl.when((s <= z) & (z < 3))
            def _():
                act_on(gather_z(a, s, 1))

    def start_z(group):
        sends_along_z(group, z, lambda copy: copy.start())

    def relay(group, i):
        s = slab_of(i)
        for a in group:
            gather_z(a, s, 1).wait_recv()
            sends_along_z((a,), s, lambda copy: copy.start())

    def share(group, i):
        s = slab_of(i)
        for a in group:
            gather(a, s, 1).start()
            gather(a, s, 2).start()

    def pass_diagonal(group, i):
        s = slab_of(i)
        for a in group:
            gather(a, s, 1, True).wait_recv()
            gather(a, s, 3).start()
            gather(a, s, 2, True).wait_recv()
            gather(a, s, 4).start()

    def finish_slab(group, i):
        s = slab_of(i)
        for a in group:
            gather(a, s, 3, True).wait_recv()
            gather(a, s, 4, True).wait_recv()

    def sent_slab(group, i):
        s = slab_of(i)
        sends_along_z(group, s, lambda copy: copy.wait_send())
        for a in group:
            if a not in whole:

                @pl.when(i > 0)
                def _():
                    for kind in (1, 2, 3, 4):
                        gather(a, s, kind).wait_send()

    def arrival(a, n):
        return n if a in mlp else 3 - n

    def step_slab(a, n):
        return slab_of(arrival(a, n))

    def last_slab(a):
        return step_slab(a, 3)

    def slot(a, n):
        first = (4 - n) // 4
        return first * SPARE + (1 - first) * step_slab(a, n - 1 + first)

    def reduce_copy(a, n, kind):
        buf, g = bufs[a], slot(a, n)
        got = None
        if kind == 0:
            src, dst, device = buf.at[g, :, 1 - b, first_part(a)], rx[a].at[n], along_x
        elif kind == 1:
            src, dst, device = buf.at[g, 1 - h, :, second_part(a)], ry[a].at[n], along_y
        elif kind == 2:
            src, dst, device = buf.at[g, 1 - h, b, first_part(a)], ry2[a].at[n], along_y
        elif kind == 3:
            src, dst, device = buf.at[g, h, 1 - b, second_part(a)], rx2[a].at[n], along_x
        elif kind == 4:
            s = step_slab(a, n)
            src, dst, device = buf.at[g, h, b], rz[a].at[z], (d, r, s)
            got = (a, z, 4)
        else:
            i = arrival(a, n)
            src, dst, device = buf.at[g, h, b], rz[a].at[2 + i], (d, r, slab_of(1))
            got = (a, i, 5)
        return remote(src, dst, rsend, rrecv, (a, n, min(kind, 4)), device, got)

    def reduce_z(a, n, act_on):
        i = arrival(a, n)

        @pl.when((i > 0) & (is_inner | (i == 1)))
        def _():
            act_on(reduce_copy(a, n, 4))

        @pl.when(is_end & (i > 1))
        def _():
            act_on(reduce_copy(a, n, 5))

    def reduce_one(group, n):
        for a in group:
            reduce_copy(a, n, 0).start()
            reduce_copy(a, n, 1).start()

    def scratch(a, place):
        return tmp.at[place + (2 if a % 2 else 0)]

    def reduce_two(group, n):
        loads = []
        for a in group:
            reduce_copy(a, n, 0).wait_recv()
            reduce_copy(a, n, 1).wait_recv()
            for place, got in enumerate((rx[a], ry[a])):
                to = scratch(a, place).at[:, pl.ds(0, parts[a][place])]
                loads.append(pltpu.make_async_copy(got.at[n], to, local.at[a * 2 + place]))
                loads[-1].start()
        for i, a in enumerate(group):
            g = slot(a, n)
            first, second = parts[a]
            loads[2 * i].wait()
            for side in range(2):
                add_low(bufs[a], (g, side, b, first_part(a)), scratch(a, 0)[side, :first])
            reduce_copy(a, n, 2).start()
            loads[2 * i + 1].wait()
            for side in range(2):
                add_low(bufs[a], (g, h, side, second_part(a)), scratch(a, 1)[side, :second])
            reduce_copy(a, n, 3).start()

    def reduce_three(group, n):
        loads = []
        for a in group:
            reduce_copy(a, n, 2).wait_recv()
            reduce_copy(a, n, 3).wait_recv()
            for place, got in enumerate((ry2[a], rx2[a])):
                to = scratch(a, place).at[0, pl.ds(0, parts[a][place])]
                loads.append(pltpu.make_async_copy(got.at[n], to, local.at[a * 2 + place]))
                loads[-1].start()
        for i, a in enumerate(group):
            g = slot(a, n)
            first, second = parts[a]
            loads[2 * i].wait()
            add_low(bufs[a], (g, h, b, first_part(a)), scratch(a, 0)[0, :first])
            loads[2 * i + 1].wait()
            add_low(bufs[a], (g, h, b, second_part(a)), scratch(a, 1)[0, :second])

            i = arrival(a, n)

            @pl.when(is_inner & (i > 1))
            def _():
                at = rz[a].at[2 + i]
                remote(at, at, rsend, rrecv, (a, n, 4), (d, r, slab_of(1)), (a, i, 5)).wait_recv()
                pieces = ((0, first, first_part(a)), (1, second, second_part(a)))
                copies = [
                    pltpu.make_async_copy(at.at[part], scratch(a, 0).at[side, pl.ds(0, count)], local.at[a * 2 + side])
                    for side, count, part in pieces
                ]
                for copy in copies:
                    copy.start()
                for copy, (side, count, part) in zip(copies, pieces):
                    copy.wait()
                    add_low(bufs[a], (g, h, b, part), scratch(a, 0)[side, :count])

            reduce_z(a, n, lambda copy: copy.start())

    def reduce_four(group):
        for a in group:
            rows = bufs[a].shape[3]
            loads = []
            for k in (1, 2):
                other = slab_of(k)
                at = rz[a].at[other]
                remote(at, at, rsend, rrecv, (a, k, 4), (d, r, other), (a, other, 4)).wait_recv()
                loads.append(pltpu.make_async_copy(at, act.at[pl.ds((k - 1) * rows, rows)], local.at[k]))
                loads[-1].start()
            for load in loads:
                load.wait()
            value = bufs[a][slot(a, 0 if a in mlp else 3), h, b].astype(F32)
            for k in range(2):
                value = value + act[k * rows : (k + 1) * rows].astype(F32)
            bufs[a][last_slab(a), h, b] = value.astype(BF)
            spread(a, 1).start()
            spread(a, 2).start()

    def reduce_five(group):
        for a in group:
            spread(a, 1, True).wait_recv()
            spread(a, 3).start()
            spread(a, 2, True).wait_recv()
            spread(a, 4).start()

    def qkv_pieces(matrix, side, flat):
        rows = flat.shape[1]
        part = matrix.shape[2]
        cut = rows - part
        return (
            (matrix.at[0, side], flat.at[0, pl.ds(0, part)]),
            (matrix.at[1, side, pl.ds(0, cut)], flat.at[0, pl.ds(part, cut)]),
            (matrix.at[1, side, pl.ds(cut, part - cut)], flat.at[1, pl.ds(0, part - cut)]),
            (matrix.at[2, side], flat.at[1, pl.ds(part - cut, part)]),
        )

    def swap_out(a):
        mine = bufs[a].at[last_slab(a), 1 - r]
        if a == 0:
            pairs = qkv_pieces(outs[a], r, mine)
            return [remote(src, dst, qsend, qrecv, 4 + i, partner) for i, (dst, src) in enumerate(pairs)]
        to = outs[a].at[:, :, half_lanes(r)] if a == 2 else outs[a].at[r]
        return [remote(mine, to, fsend, frecv, (a, 0), partner)]

    def keep_out(a):
        mine = bufs[a].at[last_slab(a), r]
        if a == 0:
            pairs = qkv_pieces(outs[a], r, mine)
            return [pltpu.make_async_copy(src, dst, qlocal.at[i]) for i, (dst, src) in enumerate(pairs)]
        to = outs[a].at[:, :, half_lanes(r)] if a == 2 else outs[a].at[r]
        return [pltpu.make_async_copy(mine, to, local.at[a])]

    def reduce_six(group):
        for a in group:
            spread(a, 3, True).wait_recv()
            spread(a, 4, True).wait_recv()
            for copy in swap_out(a) + keep_out(a):
                copy.start()

    def half_lanes(side):
        return pl.ds(pl.multiple_of(side * half, half), half)

    def exchange(index, src, dst):
        return remote(src, dst, csend, crecv, index, partner)

    rows_own, rows_other = pl.ds(0, own), pl.ds(own, own)
    def source(a, side):
        if a == 2:
            return expand_src.at[:, :, half_lanes(side)]
        return (qkv_src, proj_src, expand_src, shrink_src)[a].at[side]

    def source_swap(a):
        to = bufs[a].at[z, r]
        if a == 0:
            pairs = qkv_pieces(qkv_src, 1 - r, to)
            return [remote(src, dst, qsend, qrecv, i, partner) for i, (src, dst) in enumerate(pairs)]
        return [exchange(a, source(a, 1 - r), to)]

    def source_keep(a):
        to = bufs[a].at[z, r]
        if a == 0:
            pairs = qkv_pieces(qkv_src, r, to)
            return [pltpu.make_async_copy(src, dst, qlocal.at[i]) for i, (src, dst) in enumerate(pairs)]
        return [pltpu.make_async_copy(source(a, r), to, local.at[a])]

    def start_source(group):
        for a in group:
            for copy in source_swap(a) + source_keep(a):
                copy.start()

    def finish_source(group):
        for a in group:
            for copy in source_swap(a) + source_keep(a):
                copy.wait()

    grad_load = pltpu.make_async_copy(out_grad, gm.at[rows_own], local.at[4])
    swap_grad = exchange(4, out_grad, gm.at[rows_other])
    swap_h1 = exchange(5, h1.at[rows_own], h1.at[rows_other])
    swap_attn = exchange(6, total.at[rows_other], xr)
    swap_h2 = exchange(7, h2.at[rows_own], h2.at[rows_other])
    swap_mlp = exchange(8, total.at[rows_other], xr)
    swap_gh2 = exchange(9, back.at[rows_other], xr2)
    swap_ga = exchange(10, gm.at[rows_own], gm.at[rows_other])
    swap_gh1 = exchange(11, back.at[rows_other], xr)

    def bias_copy(k, arriving=False):
        at = bias_all.at[flip(z, k) if arriving else z]
        return remote(at, at, zsend, zrecv, k, along_z(k))

    barrier = pltpu.get_barrier_semaphore()
    peers = [partner, along_x, along_y, across, along_z(1), along_z(2), along_z(3)]
    for peer in peers:
        pl.semaphore_signal(barrier, inc=1, device_id=peer, device_id_type=MESH_ID)
    pl.semaphore_wait(barrier, len(peers))

    start_source(attn)
    grad_load.start()
    bias_all[z] = jnp.zeros(bias_all.shape[1:], F32)
    part = qkv_bias_in.shape[1] // 2
    for side in range(2):

        @pl.when(r == side)
        def _():
            bias_all[z, 0:1, :half] = expand_bias_in[side * half : (side + 1) * half].reshape(1, half)
            for i in range(2):
                at = half + 2 * i * part
                bias_all[z, 0:1, at : at + part] = qkv_bias_in[i : i + 1, side * part : (side + 1) * part]

    finish_source(attn)
    start_z(attn)
    for k in (1, 2, 3):
        bias_copy(k).start()
    start_source(mlp)

    def as_row(ref):
        return ref[...].reshape(1, width)

    gain_one, shift_one, gain_two, shift_two, proj_bias, shrink_bias = (
        as_row(ref) for ref in (gain_one_in, shift_one_in, gain_two_in, shift_two_in, proj_bias_in, shrink_bias_in)
    )

    def over_rows(body):
        @pl.loop(0, own // CHUNK)
        def _(m):
            body(pl.ds(pl.multiple_of(m * CHUNK, CHUNK), CHUNK))

    def column_sum(value):
        return jnp.sum(value, axis=0, keepdims=True)

    def normalize(value):
        center = value - jnp.mean(value, axis=1, keepdims=True)
        inverse = lax.rsqrt(jnp.mean(center * center, axis=1, keepdims=True) + EPS)
        return center * inverse, inverse

    def norm_back(grad, gain, xhat, inverse):
        scaled = grad * gain
        mean = jnp.mean(scaled, axis=1, keepdims=True)
        along = jnp.mean(scaled * xhat, axis=1, keepdims=True)
        return (scaled - mean - xhat * along) * inverse

    early[...] = jnp.zeros_like(early)
    late[...] = jnp.zeros_like(late)

    def first_rows(rows):
        value = tokens[rows].astype(F32)
        valid = keep[rows]
        xhat, _ = normalize(value)
        h1[rows] = ((xhat * gain_one + shift_one) * valid).astype(BF)
        early[0:1, :] += column_sum(valid * value * value)
        early[5:6, :] += jnp.broadcast_to(column_sum(valid), (1, width))

    over_rows(first_rows)
    swap_h1.start()
    swap_grad.start()
    rel_pad[...] = jnp.zeros_like(rel_pad)
    rel_pad[0, : rel_h_in.shape[0]] = rel_h_in[...]
    rel_pad[1, : rel_w_in.shape[0]] = rel_w_in[...]
    relative_tables(rel_pad.at[0], rel_pad.at[1], rel_query, rel_back)
    total[...] = jnp.zeros_like(total)
    swap_h1.wait_recv()

    def bias_q_of(s):
        return bias_all[s, 0:1, half : half + gqkv.shape[1]]

    def bias_e_of(s):
        return bias_all[s, 0:1, :half]

    finish_source(mlp)

    @pl.when(is_end)
    def _():
        start_z((3, 2))

    relay(attn, 1)
    share(attn, 1)

    @pl.loop(0, 4)
    def _(i):
        @pl.when(i == 1)
        def _():
            relay(attn, 2)
            share(attn, 2)
            relay(attn, 3)

            @pl.when(is_inner)
            def _():
                start_z(shrink)
                relay(shrink, 1)

            pass_diagonal(attn, 1)
            share(attn, 3)
            pass_diagonal(attn, 2)
            for k in (1, 2, 3):
                bias_copy(k, True).wait_recv()

            @pl.when(is_inner)
            def _():
                relay(shrink, 2)

        @pl.when(i > 0)
        def _():
            finish_slab(attn, i)

        @pl.when(i == 2)
        def _():
            pass_diagonal(attn, 3)

        @pl.when((i == 1) & is_inner)
        def _():
            relay(shrink, 3)
            start_z(whole)

        @pl.when((i > 0) & is_end)
        def _():
            relay(shrink, i)

        @pl.when((i == 3) & is_inner)
        def _():
            relay(whole, 1)

        @pl.when(i > 0)
        def _():
            share(shrink, i)

        @pl.when(i == 3)
        def _():
            pass_diagonal(shrink, 1)

        s = slab_of(i)
        attention_slab(
            s, h1, wq, wp, bias_q_of(s), rel_query, codes, attended, total, heads, half
        )

    pass_diagonal(shrink, 2)
    swap_attn.start()
    swap_attn.wait()

    def middle_rows(rows):
        value = tokens[rows].astype(F32)
        valid = keep[rows]
        attn_out = total[rows] + xr[rows] + proj_bias
        mid = value + attn_out
        middle[rows] = mid
        xhat, _ = normalize(mid)
        h2[rows] = (xhat * gain_two + shift_two).astype(BF)
        early[1:2, :] += column_sum(valid * mid * mid)
        early[3:4, :] += column_sum(valid * attn_out * attn_out)

    over_rows(middle_rows)
    swap_h2.start()
    total[...] = jnp.zeros_like(total)
    back[...] = jnp.zeros_like(back)
    bias_e[...] = jnp.zeros_like(bias_e)
    bias_q[...] = jnp.zeros_like(bias_q)
    rel_acc[...] = jnp.zeros_like(rel_acc)
    grad_load.wait()
    swap_grad.wait()
    swap_h2.wait()

    @pl.loop(0, 4)
    def _(n):
        s = slab_of(n)
        g = slot(2, n)

        @pl.when(n > 0)
        def _():
            finish_slab(shrink, n)

        @pl.when((n > 0) & is_end)
        def _():
            relay(whole, n)

        @pl.when((n == 0) & is_inner)
        def _():
            relay(whole, 2)

        @pl.when((n > 1) & is_end)
        def _():
            reduce_two(mlp, n - 1)

        mlp_rows(s, 0, h2, gm, we, ws, bias_e_of(s), act, gpre, total, back, bias_e, half)

        @pl.when(n == 0)
        def _():
            pass_diagonal(shrink, 3)

        @pl.when((n == 1) & is_inner)
        def _():
            relay(whole, 3)

        mlp_rows(s, 1, h2, gm, we, ws, bias_e_of(s), act, gpre, total, back, bias_e, half)

        @pl.when(n > 0)
        def _():
            sent_slab(mlp, n - 1)

        @pl.when(n == 3)
        def _():
            sent_slab(mlp, 3)

        for side in range(2):
            columns = slice(side * half, side * half + half)
            we[g, side] = dot_tn(h2[:, columns], gpre[...]).astype(BF).reshape(we.shape[2:])
            ws[g, side] = dot_tn(act[: 2 * own], gm[:, columns]).astype(BF).reshape(ws.shape[2:])

        reduce_one(mlp, n)

        @pl.when(n == 1)
        def _():
            reduce_two(mlp, 0)

        @pl.when((n > 1) & is_inner)
        def _():
            reduce_two(mlp, n - 1)

        @pl.when(n == 2)
        def _():
            reduce_three(mlp, 0)

        @pl.when((n == 3) | ((n == 2) & is_end))
        def _():
            reduce_three(mlp, n - 1 - (z + 1) // 2 % 2)


    swap_mlp.start()
    swap_gh2.start()
    swap_mlp.wait()
    swap_gh2.wait()

    def result_rows(rows):
        valid = keep[rows]
        mid = middle[rows]
        mlp_out = total[rows] + xr[rows] + shrink_bias
        result = mid + mlp_out
        h2[rows] = result.astype(BF)
        early[2:3, :] += column_sum(valid * result * result)
        early[4:5, :] += column_sum(valid * mlp_out * mlp_out)
        grad_out = gm[rows].astype(F32)
        early[9:10, :] += column_sum(grad_out)
        grad = back[rows] + xr2[rows]
        xhat, inverse = normalize(mid)
        early[6:7, :] += column_sum(grad * xhat)
        early[7:8, :] += column_sum(grad)
        grad_mid = grad_out + norm_back(grad, gain_two, xhat, inverse)
        middle[rows] = grad_mid
        low = grad_mid.astype(BF)
        gm[rows] = low
        early[8:9, :] += column_sum(low.astype(F32))

    over_rows(result_rows)
    swap_ga.start()
    result_store = pltpu.make_async_copy(h2.at[rows_own], block_out, local.at[8])
    result_store.start()
    back[...] = jnp.zeros_like(back)
    swap_ga.wait()

    reduce_two(mlp, 3)
    for i in range(4):
        sent_slab(attn, i)

    stages = ((partner,), (along_z(1), along_z(2), along_z(3)), (along_x, along_y, across))
    early_sums = (((early, early_got),), 12)
    late_sums = (((late, late_got), (rel, rel_got)), 19)

    def small_copies(sums, stage):
        pairs, base = sums
        first = (0, 1, 4)[stage]
        for i, device in enumerate(stages[stage]):
            for j, (src, got) in enumerate(pairs):
                index = base + (first + i) * len(pairs) + j
                yield src, got, first + i, remote(src, got.at[first + i], csend, crecv, index, device)

    def small_start(sums, stage):
        for _, _, _, copy in small_copies(sums, stage):
            copy.start()

    def small_finish(sums, stage):
        copies = list(small_copies(sums, stage))
        for _, _, _, copy in copies:
            copy.wait()
        for src, got, place, _ in copies:
            src[...] += got[place]

    def on_side(act_on):
        for side in range(2):

            @pl.when(r == side)
            def _():
                act_on(side)

    def fill_early(side):
        for s in range(4):
            early[10 + s : 11 + s, side * half : (side + 1) * half] = bias_e[s]

    on_side(fill_early)
    early_store = pltpu.make_async_copy(early, early_out, local.at[9])
    small_start(early_sums, 0)

    @pl.loop(0, 4)
    def _(n):
        s = slab_of(3 - n)
        g = slot(0, n)

        def some_windows(first):
            attention_back_slab(
                s, first, h1, gm, wq, wp, bias_q_of(s), rel_query, rel_back, codes, gqkv, back, bias_q, rel_acc, heads, half
            )

        some_windows(0)

        @pl.when(((n == 0) & is_end) | ((n == 2) & is_inner))
        def _():
            reduce_three(mlp, 3)

        @pl.when((n > 1) & is_end)
        def _():
            reduce_three(attn, n - 2)

        @pl.when(n == 3)
        def _():
            reduce_four(whole)

        @pl.when(n == 0)
        def _():
            small_finish(early_sums, 0)
            small_start(early_sums, 1)

        some_windows(1)

        @pl.when(n > 0)
        def _():
            reduce_two(attn, n - 1)

        for side in range(2):
            columns = slice(side * half, side * half + half)
            wq[g, side] = dot_tn(gqkv[...], h1[:, columns]).astype(BF).reshape(wq.shape[2:])
            wp[g, side] = dot_tn(attended[s], gm[:, columns]).astype(BF).reshape(wp.shape[2:])
        reduce_one(attn, n)

        @pl.when((n == 3) & is_inner)
        def _():
            reduce_three(attn, 0)

        @pl.when((n == 0) & is_inner)
        def _():
            reduce_three(mlp, 2)

    swap_gh1.start()
    reduce_four(shrink)
    swap_gh1.wait()

    def input_rows(rows):
        value = tokens[rows].astype(F32)
        grad = (back[rows] + xr[rows]) * keep[rows]
        xhat, inverse = normalize(value)
        late[0:1, :] += column_sum(grad * xhat)
        late[1:2, :] += column_sum(grad)
        middle[rows] = middle[rows] + norm_back(grad, gain_one, xhat, inverse)

    over_rows(input_rows)
    input_store = pltpu.make_async_copy(middle, input_grad, local.at[10])
    input_store.start()

    def fill_late(side):
        lanes = bias_q.shape[2]
        for s in range(4):
            late[2 + s : 3 + s, side * lanes : (side + 1) * lanes] = bias_q[s]

    on_side(fill_late)
    for part, at in ((0, 0), (1, COL_W)):
        rows = slice(at, at + 32)
        rel[part * 32 : part * 32 + 32] = rel_acc[rows] + rel_acc[LANES + at : LANES + at + 32]

    small_start(late_sums, 0)

    @pl.when(is_inner)
    def _():
        reduce_three(attn, 1)

    reduce_three(attn, 2)
    small_finish(late_sums, 0)
    small_start(late_sums, 1)
    reduce_five(whole)
    reduce_two(attn, 3)
    reduce_five(shrink)
    small_finish(late_sums, 1)
    small_start(late_sums, 2)
    small_finish(early_sums, 1)
    small_start(early_sums, 2)
    reduce_three(attn, 3)
    reduce_four(attn)
    small_finish(late_sums, 2)
    small_finish(early_sums, 2)
    early_store.start()
    late_stores = [
        pltpu.make_async_copy(late, late_out, local.at[6]),
        pltpu.make_async_copy(rel, rel_out, local.at[7]),
    ]
    for copy in late_stores:
        copy.start()
    reduce_six(mlp)
    reduce_five(attn)
    reduce_six(attn)

    swap_h1.wait_send()
    for k in (1, 2, 3):
        bias_copy(k).wait_send()
    for a in range(4):
        for copy in swap_out(a) + keep_out(a):
            copy.wait()
        for kind in (1, 2, 3, 4):
            spread(a, kind).wait_send()
        for n in range(4):
            for kind in range(4):
                reduce_copy(a, n, kind).wait_send()

            reduce_z(a, n, lambda copy: copy.wait_send())

    for copy in late_stores:
        copy.wait()
    early_store.wait()
    result_store.wait()
    input_store.wait()


def run_kernel(tokens, keep, out_grad, vectors, qkv_bias, expand_bias, rel_height, rel_width, sources):
    own, width = tokens.shape
    half = width // 2
    rows = [source.shape[-2] for source in sources]
    rows[0] = 3 * rows[0] // 2
    sds = jax.ShapeDtypeStruct
    any_spec = pl.BlockSpec(memory_space=pl.ANY)
    vmem_spec = pl.BlockSpec(memory_space=pltpu.VMEM)
    out_shape = [sds((own, width), BF), sds((own, width), F32)]
    out_shape += [sds(source.shape, BF) for source in sources]
    out_shape += [sds((16, width), F32), sds((8, width), F32), sds((64, LANES), F32)]
    first, second = zip(*[halves(n) for n in rows])
    out_shape += [sds((4, 2, n, half), BF) for n in first]
    out_shape += [sds((4, 2, n, half), BF) for n in second]
    out_shape += [sds((4, n, half), BF) for n in second]
    out_shape += [sds((4, n, half), BF) for n in first]
    out_shape += [sds((6, n, half), BF) for n in rows]
    both = 2 * own
    vmem, dma = pltpu.VMEM, pltpu.SemaphoreType.DMA
    qkv_width = 2 * rows[0]
    scratch = [vmem((5, 2, 2, n, half), BF) for n in rows]
    scratch += [vmem((both, width), BF)] * 3
    scratch += [vmem((4, both, qkv_width // 3), BF)]
    scratch += [vmem((both, width), F32)] * 2
    scratch += [vmem((own, width), F32)] * 3
    scratch += [vmem((max(both, 3 * rows[2]), half), BF), vmem((both, half), BF), vmem((both, qkv_width), BF)]
    scratch += [vmem((4, 2, first[2], half), BF)]
    scratch += [vmem((4, 8, width), F32), vmem((16, width), F32), vmem((7, 16, width), F32)]
    scratch += [vmem((8, width), F32), vmem((7, 8, width), F32)]
    scratch += [vmem((64, LANES), F32), vmem((7, 64, LANES), F32)]
    scratch += [vmem((4, 1, half), F32), vmem((4, 1, qkv_width), F32), vmem((2 * LANES, LANES), F32)]
    scratch += [vmem((2 * LANES, LANES), BF), vmem((3 * LANES, LANES), BF), vmem((2, 32, HEAD), F32)]
    scratch += [dma((4, 4, 6))] * 2 + [dma((4, 4, 5)), dma((4, 4, 6))] + [dma((4, 5))] * 2 + [dma((33,))] * 2
    scratch += [dma((4,))] * 2 + [dma((8,))] * 2 + [dma((11,)), dma((4,))]
    got = pl.pallas_call(
        kernel,
        out_shape=out_shape,
        in_specs=[vmem_spec, vmem_spec, any_spec] + [vmem_spec] * 11 + [any_spec] * 4,
        out_specs=[any_spec] * len(out_shape),
        scratch_shapes=scratch,
        compiler_params=pltpu.CompilerParams(
            collective_id=0, has_side_effects=True, vmem_limit_bytes=VMEM_LIMIT
        ),
        name="block_step",
    )(tokens, keep, out_grad, *vectors, qkv_bias, expand_bias, rel_height, rel_width, key_codes(), *sources)
    return got[:9]


def finish_kernel(early, late, rel, *refs):
    wide, (bias_q, bias_e, height, width_out, rms), rows_out = refs[:4], refs[4:9], refs[9:15]
    outs, held, full, load, store = refs[15:19], refs[19:23], refs[23:27], refs[27], refs[28]
    z = lax.axis_index("col")
    loads = [pltpu.make_async_copy(src, to, load.at[i]) for i, (src, to) in enumerate(zip(wide, held))]
    stores = [pltpu.make_async_copy(src, to, store.at[i]) for i, (src, to) in enumerate(zip(full, outs))]
    for copy in loads:
        copy.start()
    places = ((late, 0), (late, 1), (early, 6), (early, 7), (early, 8), (early, 9))
    for ref, (source, at) in zip(rows_out, places):
        ref[...] = source[at, :]
    features = early.shape[1]
    scale = 1.0 / (early[5:6, 0:1] * features)
    rms[...] = jnp.sqrt(jnp.sum(early[:8], axis=1, keepdims=True) * scale)
    half = features // 2
    part = bias_q.shape[1] // 2
    bias_e[...] = early[pl.ds(10 + z, 1), :]
    row = late[pl.ds(2 + z, 1), :]
    for side in range(2):
        for i in range(2):
            at = (3 * side + 2 * i) * part
            bias_q[i : i + 1, side * part : (side + 1) * part] = row[:, at : at + part]
    count = height.shape[0]
    turn = lax.broadcasted_iota(jnp.int32, (32, 32), 0) + lax.broadcasted_iota(jnp.int32, (32, 32), 1) == count - 1
    turned = jnp.dot(turn.astype(F32), rel[:32], precision=lax.Precision.HIGHEST, preferred_element_type=F32)
    height[...] = turned[:count, :HEAD]
    width_out[...] = rel[32 : 32 + count, :HEAD]
    for i in range(4):
        loads[i].wait()
        rows = held[i].shape[0]
        step = rows // 5

        @pl.loop(0, 5)
        def _(m):
            at = pl.ds(pl.multiple_of(m * step, step), step)
            full[i][at] = held[i][at].astype(F32)

        stores[i].start()
    for copy in stores:
        copy.wait()


def finish_outputs(got, part):
    early, late, rel = got[6:9]
    grads = [value.reshape(-1, value.shape[-1]) for value in got[2:6]]
    width = early.shape[1]
    sds = jax.ShapeDtypeStruct
    any_spec = pl.BlockSpec(memory_space=pl.ANY)
    vmem_spec = pl.BlockSpec(memory_space=pltpu.VMEM)
    out_shape = [sds((2, 2 * part), F32), sds((1, width), F32), sds((2 * SIDE - 1, HEAD), F32)]
    out_shape += [sds((2 * SIDE - 1, HEAD), F32), sds((8, 1), F32)] + [sds((width,), F32)] * 6
    out_shape += [sds(value.shape, F32) for value in grads]
    return pl.pallas_call(
        finish_kernel,
        out_shape=out_shape,
        in_specs=[vmem_spec] * 3 + [any_spec] * 4,
        out_specs=[vmem_spec] * 11 + [any_spec] * 4,
        scratch_shapes=[pltpu.VMEM(value.shape, BF) for value in grads]
        + [pltpu.VMEM(value.shape, F32) for value in grads]
        + [pltpu.SemaphoreType.DMA((4,))] * 2,
        compiler_params=pltpu.CompilerParams(vmem_limit_bytes=VMEM_LIMIT // 2),
        name="finish",
    )(early, late, rel, *grads)


VMEM_LIMIT = 64 * 1024 * 1024 - 512 * 1024


def over_chips(
    tokens, valid_mask, out_grad, first_gain, first_shift, qkv_weight, qkv_bias, rel_height, rel_width,
    proj_weight, proj_bias, second_gain, second_shift, expand_weight, expand_bias, shrink_weight, shrink_bias,
):
    windows, per, width = tokens.shape
    side = (rel_height.shape[0] + 1) // 2
    count, head = rel_height.shape

    def padded(value):
        grid = value.reshape(windows, side, side, -1)
        grid = jnp.pad(grid, ((0, 0), (0, 0), (0, SIDE_PAD - side), (0, 0)))
        return grid.reshape(windows * side * SIDE_PAD, -1)

    def cut(value):
        grid = value.reshape(windows, side, SIDE_PAD, -1)[:, :, :side]
        return grid.reshape(windows, per, -1)

    rows, _, local_width = qkv_weight.shape
    part = local_width // 2
    hidden = expand_weight.shape[1] // 2
    qkv_src = qkv_weight.transpose(1, 2, 0).reshape(3, 2, part, rows)
    proj_src = proj_weight.reshape(2, 2, part // 2, proj_weight.shape[1])
    expand_src = expand_weight.reshape(2, rows // 2, 2 * hidden)
    shrink_src = shrink_weight.reshape(2, 2, hidden // 2, shrink_weight.shape[1])
    vectors = (first_gain, first_shift, second_gain, second_shift, proj_bias, shrink_bias)
    keep = padded(valid_mask.astype(F32))
    got = run_kernel(
        padded(tokens), keep, padded(out_grad), vectors, qkv_bias, expand_bias, rel_height, rel_width,
        (qkv_src, proj_src, expand_src, shrink_src),
    )
    outs = finish_outputs(got, part)
    qkv_bias_sum, expand_bias_sum, height_sum, width_sum, rms = outs[:5]
    gain_one, shift_one, gain_two, shift_two, proj_bias_sum, shrink_bias_sum = outs[5:11]
    qkv_sum, proj_sum, expand_sum, shrink_sum = outs[11:]
    return (
        cut(got[0]),
        cut(got[1]),
        gain_one,
        shift_one,
        qkv_sum.reshape(3, local_width, rows).transpose(2, 0, 1),
        qkv_bias_sum,
        height_sum,
        width_sum,
        proj_sum.reshape(proj_weight.shape),
        proj_bias_sum,
        gain_two,
        shift_two,
        expand_sum.reshape(expand_weight.shape),
        expand_bias_sum.reshape(-1),
        shrink_sum.reshape(shrink_weight.shape),
        shrink_bias_sum,
        rms[:5, 0],
    )


epsilon = 1e-06
highest = lax.Precision.HIGHEST


def layer_norm(values, norm_gain, norm_shift):
    center = values - jnp.mean(values, axis=-1, keepdims=True)
    spread = jnp.mean(center * center, axis=-1, keepdims=True)
    return center * lax.rsqrt(spread + epsilon) * norm_gain + norm_shift


def offset_table(span_size):
    positions = jnp.arange(span_size)
    offset = positions[:, None] - positions[None, :] + span_size - 1
    return (offset[:, :, None] == jnp.arange(2 * span_size - 1)[None, None, :]).astype(jnp.float32)


def attention_scores(
    query_rows, key_rows, rel_rows_table, rel_cols_table, onehot_table, span_size, scaling
):
    window_count, tokens_per, head_count, head_size = query_rows.shape
    rel_count = 2 * span_size - 1
    direct = (
        jnp.einsum("bthc,buhc->bhtu", query_rows, key_rows, preferred_element_type=jnp.float32)
        * scaling
    )
    query_float = query_rows.astype(jnp.float32)
    along_rows = jnp.einsum("bthc,jc->bhtj", query_float, rel_rows_table, precision=highest)
    along_cols = jnp.einsum("bthc,jc->bhtj", query_float, rel_cols_table, precision=highest)
    grid_rows = along_rows.reshape(window_count, head_count, span_size, span_size, rel_count)
    grid_cols = along_cols.reshape(window_count, head_count, span_size, span_size, rel_count)
    rel_rows = jnp.einsum("bhxyj,xkj->bhxyk", grid_rows, onehot_table, precision=highest)
    rel_cols = jnp.einsum("bhxyj,ywj->bhxyw", grid_cols, onehot_table, precision=highest)
    score_sum = direct.reshape(window_count, head_count, span_size, span_size, span_size, span_size)
    score_sum = score_sum + rel_rows[:, :, :, :, :, None] + rel_cols[:, :, :, :, None, :]
    return score_sum.reshape(window_count, head_count, tokens_per, tokens_per)


def relative_back(score_float, onehot_table, span_size):
    window_count, head_count, tokens_per, other_tokens = score_float.shape
    grid = score_float.reshape(window_count, head_count, span_size, span_size, span_size, span_size)
    rows_part = jnp.einsum("bhxykw,xkj->bhxyj", grid, onehot_table, precision=highest)
    cols_part = jnp.einsum("bhxykw,ywj->bhxyj", grid, onehot_table, precision=highest)
    return (
        rows_part.reshape(window_count, head_count, tokens_per, -1),
        cols_part.reshape(window_count, head_count, tokens_per, -1),
    )


def gather_weights(qkv_weight, proj_weight, expand_weight, shrink_weight):
    return (
        lax.all_gather(qkv_weight, "row", axis=0, tiled=True),
        lax.all_gather(proj_weight, "row", axis=1, tiled=True),
        lax.all_gather(expand_weight, "row", axis=0, tiled=True),
        lax.all_gather(shrink_weight, "row", axis=1, tiled=True),
    )


def gather_tokens(normed):
    return lax.all_gather(normed, "col", axis=0, tiled=True)


def gather_grads(grad_low):
    return lax.all_gather(grad_low, "col", axis=0, tiled=True)


def sum_branch(inputs_low, weight_full, own_windows):

    def term(first_row, row_count):
        return jnp.einsum(
            "btk,kd->btd", inputs_low, weight_full, preferred_element_type=jnp.float32
        )

    return lax.psum_scatter(
        term(jnp.int32(0), own_windows * lax.axis_size("col")),
        "col",
        scatter_dimension=0,
        tiled=True,
    )


def sum_input(grads_low, weight_full, own_windows):

    def term(first_row, row_count):
        return jnp.einsum("btk,dk->btd", grads_low, weight_full, preferred_element_type=jnp.float32)

    return lax.psum_scatter(
        term(jnp.int32(0), own_windows * lax.axis_size("col")),
        "col",
        scatter_dimension=0,
        tiled=True,
    )


def activate(values):
    return jax.nn.gelu(values, approximate=False)


def per_device(
    tokens,
    valid_mask,
    out_grad,
    first_gain,
    first_shift,
    qkv_weight,
    qkv_bias,
    rel_height,
    rel_width,
    proj_weight,
    proj_bias,
    second_gain,
    second_shift,
    expand_weight,
    expand_bias,
    shrink_weight,
    shrink_bias,
):
    span_size = (rel_height.shape[0] + 1) // 2
    head_size = rel_height.shape[1]
    local_width = qkv_weight.shape[2]
    head_count = local_width // head_size
    own_windows = tokens.shape[0]
    tokens_per = tokens.shape[1]
    model_width = tokens.shape[2]
    scaling = head_size ** (-0.5)
    onehot_table = offset_table(span_size)
    inputs = tokens.astype(jnp.float32)
    keep_mask = valid_mask.astype(jnp.float32)[:, :, None]

    def first_norm(values, norm_gain, norm_shift):
        return layer_norm(values, norm_gain, norm_shift) * keep_mask

    qkv_full, proj_full, expand_full, shrink_full = gather_weights(
        qkv_weight, proj_weight, expand_weight, shrink_weight
    )
    normed_first, first_back = jax.vjp(first_norm, inputs, first_gain, first_shift)
    first_all = gather_tokens(normed_first.astype(jnp.bfloat16))
    all_windows = first_all.shape[0]
    bias_rows = jnp.stack([qkv_bias[0], jnp.zeros_like(qkv_bias[0]), qkv_bias[1]])
    projected = (
        jnp.einsum("btd,dsk->btsk", first_all, qkv_full, preferred_element_type=jnp.float32)
        + bias_rows
    )
    projected = projected.astype(jnp.bfloat16)
    head_shape = (all_windows, tokens_per, head_count, head_size)
    query_low = projected[:, :, 0].reshape(head_shape)
    key_low = projected[:, :, 1].reshape(head_shape)
    value_low = projected[:, :, 2].reshape(head_shape)
    scores = attention_scores(
        query_low, key_low, rel_height, rel_width, onehot_table, span_size, scaling
    )
    top_score = jnp.max(scores, axis=-1, keepdims=True)
    log_total = top_score + jnp.log(jnp.sum(jnp.exp(scores - top_score), axis=-1, keepdims=True))
    probs_low = jnp.exp(scores - log_total).astype(jnp.bfloat16)
    attended = jnp.einsum(
        "bhtu,buhc->bthc", probs_low, value_low, preferred_element_type=jnp.float32
    )
    attended_low = attended.reshape(all_windows, tokens_per, local_width).astype(jnp.bfloat16)
    attn_out = sum_branch(attended_low, proj_full, own_windows) + proj_bias
    middle = inputs + attn_out
    normed_second, second_back = jax.vjp(layer_norm, middle, second_gain, second_shift)
    second_all = gather_tokens(normed_second.astype(jnp.bfloat16))
    hidden_pre = (
        jnp.einsum("btd,df->btf", second_all, expand_full, preferred_element_type=jnp.float32)
        + expand_bias
    )
    active_value, active_back = jax.vjp(activate, hidden_pre)
    hidden_low = active_value.astype(jnp.bfloat16)
    mlp_out = sum_branch(hidden_low, shrink_full, own_windows) + shrink_bias
    result = middle + mlp_out
    stat_terms = jnp.stack(
        [
            jnp.sum(keep_mask * inputs * inputs),
            jnp.sum(keep_mask * middle * middle),
            jnp.sum(keep_mask * result * result),
            jnp.sum(keep_mask * attn_out * attn_out),
            jnp.sum(keep_mask * mlp_out * mlp_out),
        ]
    )
    valid_count = jnp.sum(keep_mask)
    stat_total, count_total = lax.psum((stat_terms, valid_count), ("dp", "row", "col"))
    out_float = out_grad.astype(jnp.float32)
    qkv_full, proj_full, expand_full, shrink_full = gather_weights(
        qkv_weight, proj_weight, expand_weight, shrink_weight
    )
    mlp_grad_low = out_float.astype(jnp.bfloat16)
    shrink_bias_grad = jnp.sum(mlp_grad_low, axis=(0, 1), dtype=jnp.float32)
    mlp_grad_all = gather_grads(mlp_grad_low)
    shrink_grad_full = jnp.einsum(
        "btf,btd->fd", hidden_low, mlp_grad_all, preferred_element_type=jnp.float32
    )
    hidden_grad = jnp.einsum(
        "btd,fd->btf", mlp_grad_all, shrink_full, preferred_element_type=jnp.float32
    )
    pre_grad_low = active_back(hidden_grad)[0].astype(jnp.bfloat16)
    expand_bias_grad = jnp.sum(pre_grad_low, axis=(0, 1), dtype=jnp.float32)
    expand_grad_full = jnp.einsum(
        "btd,btf->df", second_all, pre_grad_low, preferred_element_type=jnp.float32
    )
    second_grad = sum_input(pre_grad_low, expand_full, own_windows)
    middle_part, second_gain_grad, second_shift_grad = second_back(second_grad)
    middle_grad = out_float + middle_part
    attn_grad_low = middle_grad.astype(jnp.bfloat16)
    proj_bias_grad = jnp.sum(attn_grad_low, axis=(0, 1), dtype=jnp.float32)
    attn_grad_all = gather_grads(attn_grad_low)
    proj_grad_full = jnp.einsum(
        "btk,btd->kd", attended_low, attn_grad_all, preferred_element_type=jnp.float32
    )
    attended_grad = jnp.einsum(
        "btd,kd->btk", attn_grad_all, proj_full, preferred_element_type=jnp.float32
    )
    attended_grad = attended_grad.astype(jnp.bfloat16).reshape(head_shape)
    scores_again = attention_scores(
        query_low, key_low, rel_height, rel_width, onehot_table, span_size, scaling
    )
    probs_float = jnp.exp(scores_again - log_total)
    probs_again = probs_float.astype(jnp.bfloat16)
    prob_grad = jnp.einsum(
        "bthc,buhc->bhtu", attended_grad, value_low, preferred_element_type=jnp.float32
    )
    value_grad = jnp.einsum(
        "bhtu,bthc->buhc", probs_again, attended_grad, preferred_element_type=jnp.float32
    )
    score_grad = probs_float * (
        prob_grad - jnp.sum(probs_float * prob_grad, axis=-1, keepdims=True)
    )
    score_low = score_grad.astype(jnp.bfloat16)
    rows_grad, cols_grad = relative_back(score_low.astype(jnp.float32), onehot_table, span_size)
    query_float = query_low.astype(jnp.float32)
    query_grad = (
        jnp.einsum("bhtu,buhc->bthc", score_low, key_low, preferred_element_type=jnp.float32)
        * scaling
    )
    query_grad = query_grad + jnp.einsum("bhtj,jc->bthc", rows_grad, rel_height, precision=highest)
    query_grad = query_grad + jnp.einsum("bhtj,jc->bthc", cols_grad, rel_width, precision=highest)
    key_grad = (
        jnp.einsum("bhtu,bthc->buhc", score_low, query_low, preferred_element_type=jnp.float32)
        * scaling
    )
    rel_height_grad = jnp.einsum("bhtj,bthc->jc", rows_grad, query_float, precision=highest)
    rel_width_grad = jnp.einsum("bhtj,bthc->jc", cols_grad, query_float, precision=highest)
    flat_shape = (all_windows, tokens_per, local_width)
    qkv_grad_low = jnp.stack(
        [
            query_grad.reshape(flat_shape),
            key_grad.reshape(flat_shape),
            value_grad.reshape(flat_shape),
        ],
        axis=2,
    ).astype(jnp.bfloat16)
    qkv_bias_grad = jnp.sum(qkv_grad_low[:, :, 0::2], axis=(0, 1), dtype=jnp.float32)
    qkv_grad_full = jnp.einsum(
        "btd,btsk->dsk", first_all, qkv_grad_low, preferred_element_type=jnp.float32
    )
    first_grad = sum_input(
        qkv_grad_low.reshape(all_windows, tokens_per, 3 * local_width),
        qkv_full.reshape(qkv_full.shape[0], 3 * local_width),
        own_windows,
    )
    input_part, first_gain_grad, first_shift_grad = first_back(first_grad)
    input_grad = middle_grad + input_part
    qkv_rows, proj_rows, expand_rows, shrink_rows = (
        lax.psum_scatter(qkv_grad_full, "row", scatter_dimension=0, tiled=True),
        lax.psum_scatter(proj_grad_full, "row", scatter_dimension=1, tiled=True),
        lax.psum_scatter(expand_grad_full, "row", scatter_dimension=0, tiled=True),
        lax.psum_scatter(shrink_grad_full, "row", scatter_dimension=1, tiled=True),
    )
    qkv_sum, proj_sum, expand_sum, shrink_sum = lax.psum(
        (qkv_rows, proj_rows, expand_rows, shrink_rows), "dp"
    )
    qkv_bias_sum, expand_bias_sum = lax.psum((qkv_bias_grad, expand_bias_grad), ("dp", "row"))
    (
        gain_one_sum,
        shift_one_sum,
        gain_two_sum,
        shift_two_sum,
        proj_bias_sum,
        shrink_bias_sum,
        height_sum,
        width_sum,
    ) = lax.psum(
        (
            first_gain_grad,
            first_shift_grad,
            second_gain_grad,
            second_shift_grad,
            proj_bias_grad,
            shrink_bias_grad,
            rel_height_grad,
            rel_width_grad,
        ),
        ("dp", "row", "col"),
    )
    rms = jnp.sqrt(stat_total / (count_total * model_width))
    return (
        result.astype(jnp.bfloat16),
        input_grad,
        gain_one_sum,
        shift_one_sum,
        qkv_sum,
        qkv_bias_sum,
        height_sum,
        width_sum,
        proj_sum,
        proj_bias_sum,
        gain_two_sum,
        shift_two_sum,
        expand_sum,
        expand_bias_sum,
        shrink_sum,
        shrink_bias_sum,
        rms,
    )


def choose(mesh):
    fits = tuple(mesh.shape[name] for name in ("dp", "row", "col")) == (4, 2, 4)
    return over_chips if fits else per_device


def solution(mesh):
    in_specs = (
        P(("dp", "row", "col"), None, None),
        P(("dp", "row", "col"), None),
        P(("dp", "row", "col"), None, None),
        P(),
        P(),
        P("row", None, "col"),
        P(None, "col"),
        P(),
        P(),
        P("col", "row"),
        P(),
        P(),
        P(),
        P("row", "col"),
        P("col"),
        P("col", "row"),
        P(),
    )
    out_specs = (
        P(("dp", "row", "col"), None, None),
        P(("dp", "row", "col"), None, None),
        P(),
        P(),
        P("row", None, "col"),
        P(None, "col"),
        P(),
        P(),
        P("col", "row"),
        P(),
        P(),
        P(),
        P("row", "col"),
        P("col"),
        P("col", "row"),
        P(),
        P(),
    )
    return jax.shard_map(
        choose(mesh), mesh=mesh, in_specs=in_specs, out_specs=out_specs, check_vma=False
    )
```

```python
import functools

import jax
import jax.numpy as jnp
import numpy as np
from jax import lax
from jax.experimental import pallas as pl
from jax.experimental.pallas import tpu as pltpu
from jax.sharding import PartitionSpec as P

BF = jnp.bfloat16
F32 = jnp.float32
LANES = 128
SIDE = 14
SIDE_PAD = 16
WROWS = SIDE * SIDE_PAD
HEAD = 80
AT_H = HEAD
AT_W = HEAD + SIDE
AT_MASK = HEAD + 2 * SIDE
COL_W = 64


def dot(a, b):
    return jnp.dot(a, b, preferred_element_type=F32)


def dot_nt(a, b):
    return lax.dot_general(a, b, (((1,), (1,)), ((), ())), preferred_element_type=F32)


def dot_tn(a, b):
    return lax.dot_general(a, b, (((0,), (0,)), ((), ())), preferred_element_type=F32)


def lane_ids():
    return lax.broadcasted_iota(jnp.int32, (WROWS, LANES), 1)


def row_ids():
    return lax.broadcasted_iota(jnp.int32, (WROWS, LANES), 0)


def key_codes():
    u = np.arange(WROWS)[:, None]
    lane = np.arange(LANES)[None, :]
    k, l = u // SIDE_PAD, u % SIDE_PAD
    height = lane - AT_H == k
    width = (lane - AT_W == l) & (l < SIDE)
    width_back = (AT_W + SIDE - 1 - lane == l) & (l < SIDE)
    plain = np.where(height | width, 1.0, 0.0)
    masked = np.where((lane == AT_MASK) & (l >= SIDE), -1e30, plain)
    back = np.where(height | width_back, 1.0, 0.0)
    return np.stack([masked, plain, back]).astype(BF)


def split_low(values):
    high = values.astype(BF)
    return high, (values - high.astype(F32)).astype(BF)


def relative_tables(rel_h, rel_w, rel_query, rel_back):
    count, rows = 2 * SIDE - 1, rel_h.shape[0]
    offset = lax.broadcasted_iota(jnp.int32, (rows, LANES), 0)
    lane = lax.broadcasted_iota(jnp.int32, (rows, LANES), 1)

    def places(first, step):
        return jnp.where((lane == first + step * offset) & (offset < count), 1.0, 0.0).astype(BF)

    heights, widths = places(count - 1, -1), places(COL_W + count - 1, -1)
    widths_back = places(COL_W, 1)
    tall, wide = rel_h[...], rel_w[...]
    rel_query[...] = jnp.zeros_like(rel_query)
    rel_back[...] = jnp.zeros_like(rel_back)
    for part, (a, b) in enumerate(zip(split_low(tall * HEAD**0.5), split_low(wide * HEAD**0.5))):
        at = part * LANES
        rel_query[at : at + HEAD] = (dot_tn(a, heights) + dot_tn(b, widths)).astype(BF)
    for part, (a, b) in enumerate(zip(split_low(tall), split_low(wide))):
        table = (dot_tn(heights, a) + dot_tn(widths_back, b)).astype(BF)
        for place in ((0, 1), (2,))[part]:
            rel_back[place * LANES : (place + 1) * LANES, :HEAD] = table


def query_codes(query, rel_query):
    full = dot(jnp.concatenate([query, query], axis=1), rel_query)
    tiles = full.reshape(SIDE, SIDE_PAD, LANES)
    heights = jnp.concatenate(
        [pltpu.roll(tiles[i], AT_H - (SIDE - 1 - i), 1) for i in range(SIDE)], axis=0
    )
    widths = pltpu.roll(
        tiles, AT_W - COL_W - (SIDE - 1), 2, stride=1, stride_axis=1
    ).reshape(WROWS, LANES)
    lane = lane_ids()
    codes = jnp.where(
        (lane >= AT_H) & (lane < AT_W),
        heights,
        jnp.where((lane >= AT_W) & (lane < AT_MASK), widths, 0.0),
    )
    high, rest = split_low(codes)
    first = query + high + jnp.where(lane == AT_MASK, 1.0, 0.0).astype(BF)
    return jnp.concatenate([first, rest], axis=1)


def softmax_rows(query, key, rel_query, codes_ref):
    left = query_codes(query, rel_query)
    right = jnp.concatenate([key + codes_ref[0], codes_ref[1]], axis=1)
    scores = dot_nt(left, right)
    top = jnp.max(scores, axis=1, keepdims=True)
    weights = jnp.exp((scores - top) * (HEAD**-0.5))
    return weights / jnp.sum(weights, axis=1, keepdims=True)


def attend(query, key, value, rel_query, codes_ref):
    probs = softmax_rows(query, key, rel_query, codes_ref)
    return dot(probs.astype(BF), value)


def attend_back(query, key, value, grad, rel_query, rel_back, codes_ref):
    probs = softmax_rows(query, key, rel_query, codes_ref)
    prob_grad = dot_nt(grad, value)
    inner = jnp.sum(probs * prob_grad, axis=1, keepdims=True)
    score_low = (probs * (prob_grad - inner)).astype(BF)
    value_grad = dot_tn(probs.astype(BF), grad)
    key_grad = dot_tn(score_low, query) * (HEAD**-0.5)
    mixed = dot(score_low, key + codes_ref[2])
    tiles = mixed.reshape(SIDE, SIDE_PAD, LANES)
    heights = jnp.concatenate(
        [pltpu.roll(tiles[i], (SIDE - 1 - i - AT_H) % LANES, 1) for i in range(SIDE)], axis=0
    )
    widths = pltpu.roll(
        tiles, (COL_W - AT_W) % LANES, 2, stride=1, stride_axis=1
    ).reshape(WROWS, LANES)
    lane, row = lane_ids(), row_ids()
    first_h = SIDE - 1 - row // SIDE_PAD
    first_w = COL_W + row % SIDE_PAD
    offsets = jnp.where(
        (lane >= first_h) & (lane < first_h + SIDE),
        heights,
        jnp.where((lane >= first_w) & (lane < first_w + SIDE), widths, 0.0),
    )
    high, rest = split_low(offsets)
    query_grad = jnp.where(lane < HEAD, mixed, 0.0) * (HEAD**-0.5) + dot(
        jnp.concatenate([high, rest, high], axis=1), rel_back
    )
    rel_grad = dot_tn(jnp.concatenate([high, rest], axis=1), query)
    return query_grad, key_grad, value_grad, rel_grad


def pad_head(piece):
    return jnp.concatenate([piece, jnp.zeros((piece.shape[0], LANES - HEAD), piece.dtype)], axis=1)


def qkv_low(s, rows, h1, wq, bias, half):
    return (dot_nt(h1[rows, :half], block(wq, s, 0)) + dot_nt(h1[rows, half:], block(wq, s, 1)) + bias).astype(BF)


def head_of(low, part, heads, hh):
    at = (part * heads + hh) * HEAD
    return pad_head(low[:, at : at + HEAD])


def attention_slab(s, part, h1, wq, wp, bias, rel_query, codes, attended, total, heads, half):
    count = h1.shape[0] // WROWS // 2

    @pl.loop(0, count)
    def _(m):
        rows = pl.ds(pl.multiple_of((part * count + m) * WROWS, WROWS), WROWS)
        low = qkv_low(s, rows, h1, wq, bias, half)
        outs = []
        for hh in range(heads):
            query, key, value = (head_of(low, part, heads, hh) for part in range(3))
            outs.append(attend(query, key, value, rel_query[...], codes)[:, :HEAD])
        out_low = jnp.concatenate(outs, axis=1).astype(BF)
        attended[s, rows] = out_low
        total[rows, :half] += dot(out_low, block(wp, s, 0))
        total[rows, half:] += dot(out_low, block(wp, s, 1))


SQRT_HALF = 0.5**0.5
PDF_SCALE = 0.3989422804014327


def mlp_rows(s, place, m, h2, gm, we, ws, bias, act, gpre, total, back, bias_grad, half):
    count = h2.shape[0] // 4

    @pl.loop(0, 2)
    def _(step):
        rows = pl.ds(pl.multiple_of((2 * m + step) * count, count), count)
        pre = dot(h2[rows, :half], block(we, place, 0)) + dot(h2[rows, half:], block(we, place, 1)) + bias
        cdf = 0.5 + 0.5 * lax.erf(pre * SQRT_HALF)
        slope = cdf + pre * (PDF_SCALE * jnp.exp(-0.5 * pre * pre))
        act_low = (pre * cdf).astype(BF)
        act[rows, :] = act_low
        hidden = dot_nt(gm[rows, :half], block(ws, place, 0)) + dot_nt(gm[rows, half:], block(ws, place, 1))
        gpre_low = (hidden * slope).astype(BF)
        gpre[rows, :] = gpre_low
        bias_grad[s] += jnp.sum(gpre_low.astype(F32), axis=0, keepdims=True)
        total[rows, :half] += dot(act_low, block(ws, place, 0))
        total[rows, half:] += dot(act_low, block(ws, place, 1))
        back[rows, :half] += dot_nt(gpre_low, block(we, place, 0))
        back[rows, half:] += dot_nt(gpre_low, block(we, place, 1))


def attention_back_slab(
    s, first, h1, ga, wq, wp, bias, rel_query, rel_back, codes, gqkv, back, bias_grad, rel_grad, heads, half
):
    count = h1.shape[0] // WROWS // 2

    @pl.loop(0, count)
    def _(m):
        rows = pl.ds(pl.multiple_of((first * count + m) * WROWS, WROWS), WROWS)
        low = qkv_low(s, rows, h1, wq, bias, half)
        grad = (dot_nt(ga[rows, :half], block(wp, s, 0)) + dot_nt(ga[rows, half:], block(wp, s, 1))).astype(BF)
        parts = [[], [], []]
        for hh in range(heads):
            query, key, value = (head_of(low, part, heads, hh) for part in range(3))
            got = attend_back(
                query, key, value, head_of(grad, 0, heads, hh), rel_query[...], rel_back[...], codes
            )
            for part in range(3):
                parts[part].append(got[part][:, :HEAD])
            rel_grad[...] += got[3]
        grad_low = jnp.concatenate(parts[0] + parts[1] + parts[2], axis=1).astype(BF)
        gqkv[rows, :] = grad_low
        bias_grad[s] += jnp.sum(grad_low.astype(F32), axis=0, keepdims=True)
        back[rows, :half] += dot(grad_low, block(wq, s, 0))
        back[rows, half:] += dot(grad_low, block(wq, s, 1))


MESH_ID = pl.DeviceIdType.MESH
ARRAYS = ("qkv", "proj", "expand", "shrink")
CHUNK = 64
EPS = 1e-06
SPARE = 4


def halves(rows):
    first = (rows // 2 + 15) // 16 * 16
    return first, rows - first


def flip(index, k):
    return ((index // 2 + k // 2) % 2) * 2 + (index % 2 + k % 2) % 2


def block(ref, slab, half):
    value = ref[slab, half]
    return value.reshape(value.shape[0] * value.shape[1], value.shape[2])


def add_low(target, index, extra):
    target[index] = (target[index].astype(F32) + extra.astype(F32)).astype(BF)


def kernel(
    tokens, keep, out_grad, gain_one_in, shift_one_in, gain_two_in, shift_two_in, proj_bias_in, shrink_bias_in,
    qkv_bias_in, expand_bias_in, rel_h_in, rel_w_in, codes, qkv_src, proj_src, expand_src, shrink_src,
    block_out, input_grad, qkv_out, proj_out, expand_out, shrink_out, early_out, late_out, rel_out,
    rxq, rxp, rxe, rxs, ryq, ryp, rye, rys, rx2q, rx2p, rx2e, rx2s, ry2q, ry2p, ry2e, ry2s, rzq, rzp, rze, rzs, pair_back, pair_out,
    wq, wp, we, ws, h1, gm, h2, gmz, h2z, got_low, attended, total, back, xr, xr2, middle, act, gpre, gqkv, tmp,
    bias_all, early, early_got, late, late_got, rel, rel_got, bias_e, bias_q, rel_acc, rel_query, rel_back, rel_pad,
    gsend, grecv, rsend, rrecv, fsend, frecv, csend, crecv, zsend, zrecv, qsend, qrecv, local, qlocal,
):
    d, r, z = lax.axis_index("dp"), lax.axis_index("row"), lax.axis_index("col")
    h, b = d // 2, d % 2
    own = tokens.shape[0]
    width = tokens.shape[1]
    half = width // 2
    heads = 2
    bufs = (wq, wp, we, ws)
    outs = (qkv_out, proj_out, expand_out, shrink_out)
    rx, ry = (rxq, rxp, rxe, rxs), (ryq, ryp, rye, rys)
    rx2, ry2 = (rx2q, rx2p, rx2e, rx2s), (ry2q, ry2p, ry2e, ry2s)
    rz = (rzq, rzp, rze, rzs)
    parts = [halves(buf.shape[3]) for buf in bufs]
    attn, mlp = (0, 1), (2, 3)

    along_x = (h * 2 + 1 - b, r, z)
    along_y = ((1 - h) * 2 + b, r, z)
    across = ((1 - h) * 2 + 1 - b, r, z)
    partner = (d, 1 - r, z)
    pair, remote_slab = (d, r, flip(z, 1)), flip(z, 2)

    def along_z(k):
        return (d, r, flip(z, k))

    def remote(src, dst, sems, recvs, index, device, got=None):
        return pltpu.make_async_remote_copy(
            src_ref=src,
            dst_ref=dst,
            send_sem=sems.at[index],
            recv_sem=recvs.at[index if got is None else got],
            device_id=device,
            device_id_type=MESH_ID,
        )

    up = z // 2
    is_end = (z + 1) // 2 % 2 == 0
    is_inner = (z + 1) // 2 % 2 == 1

    def slab_of(i):
        far = i // 2
        return (1 - far) * flip(z, i) + far * ((1 - up) * i + up * (3 - i))

    def first_part(a):
        return pl.ds(0, parts[a][0])

    def second_part(a):
        return pl.ds(parts[a][0], parts[a][1])

    def gather_z(a, s, step):
        at = bufs[a].at[s, h, b]
        return remote(at, at, gsend, grecv, (a, s, 0 if step < 0 else 5), (d, r, z + step), (a, s, 0))

    def gather_far(a):
        return remote(bufs[a].at[0, h, b], bufs[a].at[1, h, b], gsend, grecv, (a, 0, 0), (d, r, remote_slab))

    def ring(a, slab, sends, recvs, index, kind, arriving):
        buf = bufs[a]
        if kind == 1:
            at, device = (buf.at[slab, h, 1 - b] if arriving else buf.at[slab, h, b]), along_x
        elif kind == 2:
            at, device = (buf.at[slab, 1 - h, b] if arriving else buf.at[slab, h, b]), along_y
        elif kind == 3:
            at = buf.at[slab, 1 - h if arriving else h, 1 - b, first_part(a)]
            device = along_y
        else:
            at = buf.at[slab, 1 - h, 1 - b if arriving else b, second_part(a)]
            device = along_x
        return remote(at, at, sends, recvs, index, device)

    def gather(a, s, kind, arriving=False):
        return ring(a, s, gsend, grecv, (a, s, kind), kind, arriving)

    def spread(a, kind, arriving=False):
        return ring(a, final_slot(a), fsend, frecv, (a, kind), kind, arriving)

    def sends_along_z(group, s, act_on):
        for a in group:

            @pl.when((s >= z) & (z > 0))
            def _():
                act_on(gather_z(a, s, -1))

            @pl.when((s <= z) & (z < 3))
            def _():
                act_on(gather_z(a, s, 1))

    def start_z(group):
        sends_along_z(group, z, lambda copy: copy.start())

    def relay(group, i):
        s = slab_of(i)
        for a in group:
            gather_z(a, s, 1).wait_recv()
            sends_along_z((a,), s, lambda copy: copy.start())

    def place_of(a, i):
        return slab_of(i) if a in attn else 1

    def share(group, i):
        for a in group:
            gather(a, place_of(a, i), 1).start()
            gather(a, place_of(a, i), 2).start()

    def share_far(group):
        for a in group:
            gather_far(a).wait_recv()
            share((a,), 1)

    def pass_diagonal(group, i):
        for a in group:
            s = place_of(a, i)
            gather(a, s, 1, True).wait_recv()
            gather(a, s, 3).start()
            gather(a, s, 2, True).wait_recv()
            gather(a, s, 4).start()

    def finish_slab(group, i):
        for a in group:
            s = place_of(a, i)
            gather(a, s, 3, True).wait_recv()
            gather(a, s, 4, True).wait_recv()

    def sent_slab(group, i):
        s = slab_of(i)
        sends_along_z(group, s, lambda copy: copy.wait_send())
        for a in group:

            @pl.when(i > 0)
            def _():
                for kind in (1, 2, 3, 4):
                    gather(a, s, kind).wait_send()

    def sent_far(group):
        for a in group:
            gather_far(a).wait_send()
            for kind in (1, 2, 3, 4):
                gather(a, 1, kind).wait_send()

    def step_slab(n):
        return slab_of(3 - n)

    def final_slot(a):
        return z if a in attn else 0

    def slot(a, n):
        if a in mlp:
            return 2 + n
        first = (4 - n) // 4
        return first * SPARE + (1 - first) * step_slab(n - 1 + first)

    def reduce_copy(a, n, kind):
        buf, g = bufs[a], slot(a, n)
        got = None
        if kind == 0:
            src, dst, device = buf.at[g, :, 1 - b, first_part(a)], rx[a].at[n], along_x
        elif kind == 1:
            src, dst, device = buf.at[g, 1 - h, :, second_part(a)], ry[a].at[n], along_y
        elif kind == 2:
            src, dst, device = buf.at[g, 1 - h, b, first_part(a)], ry2[a].at[n], along_y
        elif kind == 3:
            src, dst, device = buf.at[g, h, 1 - b, second_part(a)], rx2[a].at[n], along_x
        elif kind == 4 and a in mlp:
            src, dst, device = buf.at[g, h, b], rz[a].at[0], (d, r, remote_slab)
            got = (a, 0, 4)
        elif kind == 4:
            src, dst, device = buf.at[g, h, b], rz[a].at[z], (d, r, step_slab(n))
            got = (a, z, 4)
        else:
            src, dst, device = buf.at[g, h, b], rz[a].at[5 - n], (d, r, slab_of(1))
            got = (a, 3 - n, 5)
        return remote(src, dst, rsend, rrecv, (a, n, min(kind, 4)), device, got)

    def reduce_z(a, n, act_on):
        if a in mlp:

            @pl.when(n == 1)
            def _():
                act_on(reduce_copy(a, n, 4))

        else:

            @pl.when((n < 3) & (is_inner | (n == 2)))
            def _():
                act_on(reduce_copy(a, n, 4))

            @pl.when(is_end & (n < 2))
            def _():
                act_on(reduce_copy(a, n, 5))

    def reduce_one(group, n):
        for a in group:
            reduce_copy(a, n, 0).start()
            reduce_copy(a, n, 1).start()

    def scratch(a, place):
        return tmp.at[place + (2 if a % 2 else 0)]

    def reduce_two(group, n):
        loads = []
        for a in group:
            reduce_copy(a, n, 0).wait_recv()
            reduce_copy(a, n, 1).wait_recv()
            for place, got in enumerate((rx[a], ry[a])):
                to = scratch(a, place).at[:, pl.ds(0, parts[a][place])]
                loads.append(pltpu.make_async_copy(got.at[n], to, local.at[a * 2 + place]))
                loads[-1].start()
        for i, a in enumerate(group):
            g = slot(a, n)
            first, second = parts[a]
            loads[2 * i].wait()
            for side in range(2):
                add_low(bufs[a], (g, side, b, first_part(a)), scratch(a, 0)[side, :first])
            reduce_copy(a, n, 2).start()
            loads[2 * i + 1].wait()
            for side in range(2):
                add_low(bufs[a], (g, h, side, second_part(a)), scratch(a, 1)[side, :second])
            reduce_copy(a, n, 3).start()

    def reduce_three(group, n):
        loads = []
        for a in group:
            reduce_copy(a, n, 2).wait_recv()
            reduce_copy(a, n, 3).wait_recv()
            for place, got in enumerate((ry2[a], rx2[a])):
                to = scratch(a, place).at[0, pl.ds(0, parts[a][place])]
                loads.append(pltpu.make_async_copy(got.at[n], to, local.at[a * 2 + place]))
                loads[-1].start()
        for i, a in enumerate(group):
            g = slot(a, n)
            first, second = parts[a]
            loads[2 * i].wait()
            add_low(bufs[a], (g, h, b, first_part(a)), scratch(a, 0)[0, :first])
            loads[2 * i + 1].wait()
            add_low(bufs[a], (g, h, b, second_part(a)), scratch(a, 1)[0, :second])

            @pl.when(is_inner & (n < 2) & (a in attn))
            def _():
                at = rz[a].at[5 - n]
                remote(at, at, rsend, rrecv, (a, n, 4), (d, r, slab_of(1)), (a, 3 - n, 5)).wait_recv()
                pieces = ((0, first, first_part(a)), (1, second, second_part(a)))
                copies = [
                    pltpu.make_async_copy(at.at[part], scratch(a, 0).at[side, pl.ds(0, count)], local.at[a * 2 + side])
                    for side, count, part in pieces
                ]
                for copy in copies:
                    copy.start()
                for copy, (side, count, part) in zip(copies, pieces):
                    copy.wait()
                    add_low(bufs[a], (g, h, b, part), scratch(a, 0)[side, :count])

            reduce_z(a, n, lambda copy: copy.start())

    def reduce_four(group):
        for a in group:
            rows = bufs[a].shape[3]
            loads = []
            others = ((remote_slab, 0),) if a in mlp else [(slab_of(k), slab_of(k)) for k in (1, 2)]
            for k, (other, place) in enumerate(others, 1):
                at = rz[a].at[place]
                remote(at, at, rsend, rrecv, (a, k, 4), (d, r, other), (a, place, 4)).wait_recv()
                loads.append(pltpu.make_async_copy(at, act.at[pl.ds((k - 1) * rows, rows)], local.at[k]))
                loads[-1].start()
            for load in loads:
                load.wait()
            value = bufs[a][slot(a, 0 if a in mlp else 3), h, b].astype(F32)
            for k in range(len(others)):
                value = value + act[k * rows : (k + 1) * rows].astype(F32)
            bufs[a][final_slot(a), h, b] = value.astype(BF)
            spread(a, 1).start()
            spread(a, 2).start()

    def reduce_five(group):
        for a in group:
            spread(a, 1, True).wait_recv()
            spread(a, 3).start()
            spread(a, 2, True).wait_recv()
            spread(a, 4).start()

    def qkv_pieces(matrix, side, flat):
        rows = flat.shape[1]
        part = matrix.shape[2]
        cut = rows - part
        return (
            (matrix.at[0, side], flat.at[0, pl.ds(0, part)]),
            (matrix.at[1, side, pl.ds(0, cut)], flat.at[0, pl.ds(part, cut)]),
            (matrix.at[1, side, pl.ds(cut, part - cut)], flat.at[1, pl.ds(0, part - cut)]),
            (matrix.at[2, side], flat.at[1, pl.ds(part - cut, part)]),
        )

    def swap_out(a):
        mine = bufs[a].at[final_slot(a), 1 - r]
        if a == 0:
            pairs = qkv_pieces(outs[a], r, mine)
            return [remote(src, dst, qsend, qrecv, 4 + i, partner) for i, (dst, src) in enumerate(pairs)]
        to = outs[a].at[:, :, half_lanes(r)] if a == 2 else outs[a].at[r]
        return [remote(mine, to, fsend, frecv, (a, 0), partner)]

    def keep_out(a):
        mine = bufs[a].at[final_slot(a), r]
        if a == 0:
            pairs = qkv_pieces(outs[a], r, mine)
            return [pltpu.make_async_copy(src, dst, qlocal.at[i]) for i, (dst, src) in enumerate(pairs)]
        to = outs[a].at[:, :, half_lanes(r)] if a == 2 else outs[a].at[r]
        return [pltpu.make_async_copy(mine, to, local.at[a])]

    def reduce_six(group):
        for a in group:
            spread(a, 3, True).wait_recv()
            spread(a, 4, True).wait_recv()
            for copy in swap_out(a) + keep_out(a):
                copy.start()

    def half_lanes(side):
        return pl.ds(pl.multiple_of(side * half, half), half)

    def exchange(index, src, dst):
        return remote(src, dst, csend, crecv, index, partner)

    rows_own, rows_other = pl.ds(0, own), pl.ds(own, own)
    def source(a, side):
        if a == 2:
            return expand_src.at[:, :, half_lanes(side)]
        return (qkv_src, proj_src, expand_src, shrink_src)[a].at[side]

    def source_swap(a):
        to = bufs[a].at[z if a in attn else 0, r]
        if a == 0:
            pairs = qkv_pieces(qkv_src, 1 - r, to)
            return [remote(src, dst, qsend, qrecv, i, partner) for i, (src, dst) in enumerate(pairs)]
        return [exchange(a, source(a, 1 - r), to)]

    def source_keep(a):
        to = bufs[a].at[z if a in attn else 0, r]
        if a == 0:
            pairs = qkv_pieces(qkv_src, r, to)
            return [pltpu.make_async_copy(src, dst, qlocal.at[i]) for i, (src, dst) in enumerate(pairs)]
        return [pltpu.make_async_copy(source(a, r), to, local.at[a])]

    def start_source(group):
        for a in group:
            for copy in source_swap(a) + source_keep(a):
                copy.start()

    def finish_source(group):
        for a in group:
            for copy in source_swap(a) + source_keep(a):
                copy.wait()

    grad_load = pltpu.make_async_copy(out_grad, gm.at[rows_own], local.at[4])
    swap_grad = exchange(4, out_grad, gm.at[rows_other])
    swap_h1 = exchange(5, h1.at[rows_own], h1.at[rows_other])
    swap_attn = exchange(6, total.at[rows_other], xr)
    swap_h2 = exchange(7, h2.at[rows_own], h2.at[rows_other])
    swap_mlp = exchange(8, total.at[rows_other], xr)
    swap_gh2 = exchange(9, back.at[rows_other], xr2)
    swap_ga = exchange(10, gm.at[rows_own], gm.at[rows_other])
    swap_gh1 = exchange(11, back.at[rows_other], total.at[rows_other])
    pair_gm = remote(out_grad, gmz.at[rows_own], csend, crecv, 12, pair)
    swap_gmz = exchange(13, gmz.at[rows_own], gmz.at[rows_other])
    pair_h2 = remote(h2.at[rows_own], h2z.at[rows_own], csend, crecv, 14, pair)
    swap_h2z = exchange(15, h2z.at[rows_own], h2z.at[rows_other])
    swap_back_low = exchange(16, h2.at[rows_own], got_low.at[rows_own])
    swap_out_low = exchange(17, h2.at[rows_other], got_low.at[rows_other])
    send_back = remote(h2.at[rows_own], pair_back, csend, crecv, 18, pair)
    send_out = remote(h2.at[rows_other], pair_out, csend, crecv, 19, pair)

    def bias_copy(k, arriving=False):
        at = bias_all.at[flip(z, k) if arriving else z]
        return remote(at, at, zsend, zrecv, k, along_z(k))

    barrier = pltpu.get_barrier_semaphore()
    peers = [partner, along_x, along_y, across, along_z(1), along_z(2), along_z(3)]
    for peer in peers:
        pl.semaphore_signal(barrier, inc=1, device_id=peer, device_id_type=MESH_ID)
    pl.semaphore_wait(barrier, len(peers))

    start_source(attn)
    grad_load.start()
    bias_all[z] = jnp.zeros(bias_all.shape[1:], F32)
    part = qkv_bias_in.shape[1] // 2
    for side in range(2):

        @pl.when(r == side)
        def _():
            bias_all[z, 0:1, :half] = expand_bias_in[side * half : (side + 1) * half].reshape(1, half)
            for i in range(2):
                at = half + 2 * i * part
                bias_all[z, 0:1, at : at + part] = qkv_bias_in[i : i + 1, side * part : (side + 1) * part]

    finish_source(attn)
    start_z(attn)
    for k in (1, 2, 3):
        bias_copy(k).start()
    start_source(mlp)

    def as_row(ref):
        return ref[...].reshape(1, width)

    gain_one, shift_one, gain_two, shift_two, proj_bias, shrink_bias = (
        as_row(ref) for ref in (gain_one_in, shift_one_in, gain_two_in, shift_two_in, proj_bias_in, shrink_bias_in)
    )

    def over_rows(body):
        @pl.loop(0, own // CHUNK)
        def _(m):
            body(pl.ds(pl.multiple_of(m * CHUNK, CHUNK), CHUNK))

    def column_sum(value):
        return jnp.sum(value, axis=0, keepdims=True)

    def normalize(value):
        center = value - jnp.mean(value, axis=1, keepdims=True)
        inverse = lax.rsqrt(jnp.mean(center * center, axis=1, keepdims=True) + EPS)
        return center * inverse, inverse

    def norm_back(grad, gain, xhat, inverse):
        scaled = grad * gain
        mean = jnp.mean(scaled, axis=1, keepdims=True)
        along = jnp.mean(scaled * xhat, axis=1, keepdims=True)
        return (scaled - mean - xhat * along) * inverse

    early[...] = jnp.zeros_like(early)
    late[...] = jnp.zeros_like(late)

    def first_rows(rows):
        value = tokens[rows].astype(F32)
        valid = keep[rows]
        xhat, _ = normalize(value)
        h1[rows] = ((xhat * gain_one + shift_one) * valid).astype(BF)
        early[0:1, :] += column_sum(valid * value * value)
        early[5:6, :] += jnp.broadcast_to(column_sum(valid), (1, width))

    over_rows(first_rows)
    swap_h1.start()
    swap_grad.start()
    rel_pad[...] = jnp.zeros_like(rel_pad)
    rel_pad[0, : rel_h_in.shape[0]] = rel_h_in[...]
    rel_pad[1, : rel_w_in.shape[0]] = rel_w_in[...]
    relative_tables(rel_pad.at[0], rel_pad.at[1], rel_query, rel_back)
    total[...] = jnp.zeros_like(total)
    swap_h1.wait_recv()

    def bias_q_of(s):
        return bias_all[s, 0:1, half : half + gqkv.shape[1]]

    def bias_e_of(s):
        return bias_all[s, 0:1, :half]

    finish_source(mlp)

    def start_far():
        for a in mlp:
            gather_far(a).start()

    @pl.loop(0, 4)
    def _(i):
        @pl.when(i == 1)
        def _():
            relay(attn, 1)
            share(attn, 1)

            relay(attn, 2)
            share(attn, 2)

            @pl.when(is_end)
            def _():
                start_far()

            relay(attn, 3)
            pass_diagonal(attn, 1)
            share(attn, 3)
            pass_diagonal(attn, 2)

            @pl.when(is_inner)
            def _():
                start_far()

            for k in (1, 2, 3):
                bias_copy(k, True).wait_recv()

        @pl.when(i > 0)
        def _():
            finish_slab(attn, i)

        @pl.when(i == 2)
        def _():
            pass_diagonal(attn, 3)
            pair_gm.start()

        @pl.when(((i == 2) & is_inner) | ((i == 3) & is_end))
        def _():
            share_far(mlp)

        s = slab_of(i)
        for part in (1, 0):
            attention_slab(
                s, part, h1, wq, wp, bias_q_of(s), rel_query, codes, attended, total, heads, half
            )
            if part == 1:

                @pl.when(i == 3)
                def _():
                    swap_attn.start()


    swap_attn.wait()

    def middle_rows(rows):
        value = tokens[rows].astype(F32)
        valid = keep[rows]
        attn_out = total[rows] + xr[rows] + proj_bias
        mid = value + attn_out
        middle[rows] = mid
        xhat, _ = normalize(mid)
        h2[rows] = (xhat * gain_two + shift_two).astype(BF)
        early[1:2, :] += column_sum(valid * mid * mid)
        early[3:4, :] += column_sum(valid * attn_out * attn_out)

    over_rows(middle_rows)
    swap_h2.start()
    pair_h2.start()
    total[...] = jnp.zeros_like(total)
    back[...] = jnp.zeros_like(back)
    bias_e[...] = jnp.zeros_like(bias_e)
    bias_q[...] = jnp.zeros_like(bias_q)
    rel_acc[...] = jnp.zeros_like(rel_acc)
    grad_load.wait()
    swap_grad.wait()

    def weight_grads(j, tokens_low, grads_low, second):
        for side in range(2):
            columns = slice(side * half, side * half + half)
            for buf, left, right in (
                (we, tokens_low[:, columns], gpre[...]),
                (ws, act[...], grads_low[:, columns]),
            ):
                value = dot_tn(left, right).reshape(buf.shape[2:])
                if second:
                    value = value + buf[2 + j, side].astype(F32)
                buf[2 + j, side] = value.astype(BF)

    def slab_rows(j, tokens_low, grads_low, part):
        s = (1 - j) * z + j * remote_slab
        mlp_rows(
            s, j, part, tokens_low, grads_low, we, ws, bias_e_of(s), act, gpre, total, back, bias_e, half
        )

    slab_rows(0, h2, gm, 0)
    pass_diagonal(mlp, 1)
    swap_h2.wait()
    slab_rows(0, h2, gm, 1)
    weight_grads(0, h2, gm, False)
    finish_slab(mlp, 1)
    pair_gm.wait_recv()
    swap_gmz.start()
    slab_rows(1, h2, gm, 1)
    swap_mlp.start()
    swap_gh2.start()
    slab_rows(1, h2, gm, 0)
    weight_grads(1, h2, gm, False)
    pair_h2.wait()
    swap_h2z.start()
    swap_mlp.wait()
    swap_gh2.wait()

    def own_rows(rows):
        xr[rows] = xr[rows] + total[rows]
        xr2[rows] = xr2[rows] + back[rows]

    over_rows(own_rows)
    total[...] = jnp.zeros_like(total)
    back[...] = jnp.zeros_like(back)
    swap_gmz.wait()
    swap_h2z.wait()

    def other_rows(rows):
        return pl.ds(pl.multiple_of(rows.start + own, CHUNK), CHUNK)

    def back_low_rows(rows):
        h2[rows] = back[other_rows(rows)].astype(BF)

    def out_low_rows(rows):
        h2[other_rows(rows)] = total[other_rows(rows)].astype(BF)

    def back_sum_rows(rows):
        h2[rows] = (back[rows] + got_low[rows].astype(F32)).astype(BF)

    def out_sum_rows(rows):
        h2[other_rows(rows)] = (total[rows] + got_low[other_rows(rows)].astype(F32)).astype(BF)

    slab_rows(0, h2z, gmz, 0)
    slab_rows(0, h2z, gmz, 1)
    weight_grads(0, h2z, gmz, True)
    reduce_one(mlp, 0)
    slab_rows(1, h2z, gmz, 1)
    over_rows(back_low_rows)
    swap_back_low.start()
    over_rows(out_low_rows)
    swap_out_low.start()
    slab_rows(1, h2z, gmz, 0)
    swap_back_low.wait()
    over_rows(back_sum_rows)
    send_back.start()
    swap_out_low.wait()
    over_rows(out_sum_rows)
    send_out.start()
    weight_grads(1, h2z, gmz, True)
    reduce_one(mlp, 1)
    sent_far(mlp)
    reduce_two(mlp, 0)
    send_back.wait_recv()
    back_load = pltpu.make_async_copy(pair_back, gmz.at[rows_own], local.at[8])
    back_load.start()
    back_load.wait()

    def middle_back_rows(rows):
        mid = middle[rows]
        grad_out = gm[rows].astype(F32)
        early[9:10, :] += column_sum(grad_out)
        grad = xr2[rows] + gmz[rows].astype(F32)
        xhat, inverse = normalize(mid)
        early[6:7, :] += column_sum(grad * xhat)
        early[7:8, :] += column_sum(grad)
        grad_mid = grad_out + norm_back(grad, gain_two, xhat, inverse)
        xr2[rows] = grad_mid
        low = grad_mid.astype(BF)
        gm[rows] = low
        early[8:9, :] += column_sum(low.astype(F32))

    over_rows(middle_back_rows)
    swap_ga.start()

    def result_rows(rows):
        valid = keep[rows]
        mlp_out = xr[rows] + gmz[other_rows(rows)].astype(F32) + shrink_bias
        result = middle[rows] + mlp_out
        h2[rows] = result.astype(BF)
        early[2:3, :] += column_sum(valid * result * result)
        early[4:5, :] += column_sum(valid * mlp_out * mlp_out)

    back[...] = jnp.zeros_like(back)
    for i in range(4):
        sent_slab(attn, i)
    reduce_two(mlp, 1)
    swap_ga.wait()

    out_load = pltpu.make_async_copy(pair_out, gmz.at[rows_other], local.at[8])
    result_store = pltpu.make_async_copy(h2.at[rows_own], block_out, local.at[8])

    def finish_result():
        send_back.wait_send()
        send_out.wait_recv()
        out_load.start()
        out_load.wait()
        over_rows(result_rows)
        result_store.start()

    stages = ((partner,), (along_z(1), along_z(2), along_z(3)), (along_x, along_y, across))
    early_sums = (((early, early_got),), 20)
    late_sums = (((late, late_got), (rel, rel_got)), 27)

    def small_copies(sums, stage):
        pairs, base = sums
        first = (0, 1, 4)[stage]
        for i, device in enumerate(stages[stage]):
            for j, (src, got) in enumerate(pairs):
                index = base + (first + i) * len(pairs) + j
                yield src, got, first + i, remote(src, got.at[first + i], csend, crecv, index, device)

    def small_start(sums, stage):
        for _, _, _, copy in small_copies(sums, stage):
            copy.start()

    def small_finish(sums, stage):
        copies = list(small_copies(sums, stage))
        for _, _, _, copy in copies:
            copy.wait()
        for src, got, place, _ in copies:
            src[...] += got[place]

    def on_side(act_on):
        for side in range(2):

            @pl.when(r == side)
            def _():
                act_on(side)

    def fill_early(side):
        for s in range(4):
            early[10 + s : 11 + s, side * half : (side + 1) * half] = bias_e[s]

    early_store = pltpu.make_async_copy(early, early_out, local.at[9])

    @pl.loop(0, 4)
    def _(n):
        s = slab_of(3 - n)
        g = slot(0, n)

        def some_windows(first):
            attention_back_slab(
                s, first, h1, gm, wq, wp, bias_q_of(s), rel_query, rel_back, codes, gqkv, back, bias_q, rel_acc, heads, half
            )

        some_windows(1)

        @pl.when(n == 0)
        def _():
            reduce_three(mlp, 0)
            reduce_three(mlp, 1)

        @pl.when(n == 2)
        def _():
            small_finish(early_sums, 0)
            small_start(early_sums, 1)

        @pl.when((n > 1) & is_end)
        def _():
            reduce_three(attn, n - 2)

        @pl.when(n == 2)
        def _():
            reduce_four(mlp)

        @pl.when(n == 3)
        def _():
            swap_gh1.start()
            small_finish(early_sums, 1)
            small_start(early_sums, 2)

        some_windows(0)

        @pl.when(n > 0)
        def _():
            reduce_two(attn, n - 1)

        for side in range(2):
            columns = slice(side * half, side * half + half)
            wq[g, side] = dot_tn(gqkv[...], h1[:, columns]).astype(BF).reshape(wq.shape[2:])
            wp[g, side] = dot_tn(attended[s], gm[:, columns]).astype(BF).reshape(wp.shape[2:])
        reduce_one(attn, n)

        @pl.when((n == 3) & is_inner)
        def _():
            reduce_three(attn, 0)

        @pl.when(n == 1)
        def _():
            finish_result()
            on_side(fill_early)
            small_start(early_sums, 0)

    swap_gh1.wait()

    def input_rows(rows):
        value = tokens[rows].astype(F32)
        grad = (back[rows] + total[other_rows(rows)]) * keep[rows]
        xhat, inverse = normalize(value)
        late[0:1, :] += column_sum(grad * xhat)
        late[1:2, :] += column_sum(grad)
        xr2[rows] = xr2[rows] + norm_back(grad, gain_one, xhat, inverse)

    over_rows(input_rows)
    input_store = pltpu.make_async_copy(xr2, input_grad, local.at[10])
    input_store.start()

    def fill_late(side):
        lanes = bias_q.shape[2]
        for s in range(4):
            late[2 + s : 3 + s, side * lanes : (side + 1) * lanes] = bias_q[s]

    on_side(fill_late)
    for part, at in ((0, 0), (1, COL_W)):
        rows = slice(at, at + 32)
        rel[part * 32 : part * 32 + 32] = rel_acc[rows] + rel_acc[LANES + at : LANES + at + 32]

    small_start(late_sums, 0)

    @pl.when(is_inner)
    def _():
        reduce_three(attn, 1)

    reduce_three(attn, 2)
    small_finish(late_sums, 0)
    small_start(late_sums, 1)
    reduce_two(attn, 3)
    reduce_five(mlp)
    small_finish(late_sums, 1)
    small_start(late_sums, 2)
    reduce_three(attn, 3)
    reduce_four(attn)
    small_finish(late_sums, 2)
    small_finish(early_sums, 2)
    early_store.start()
    late_stores = [
        pltpu.make_async_copy(late, late_out, local.at[6]),
        pltpu.make_async_copy(rel, rel_out, local.at[7]),
    ]
    for copy in late_stores:
        copy.start()
    reduce_six(mlp)
    reduce_five(attn)
    reduce_six(attn)

    swap_h1.wait_send()
    pair_gm.wait_send()
    send_out.wait_send()
    for k in (1, 2, 3):
        bias_copy(k).wait_send()
    for a in range(4):
        for copy in swap_out(a) + keep_out(a):
            copy.wait()
        for kind in (1, 2, 3, 4):
            spread(a, kind).wait_send()
        for n in range(4 if a in attn else 2):
            for kind in range(4):
                reduce_copy(a, n, kind).wait_send()
            reduce_z(a, n, lambda copy: copy.wait_send())

    for copy in late_stores:
        copy.wait()
    early_store.wait()
    result_store.wait()
    input_store.wait()


def run_kernel(tokens, keep, out_grad, vectors, qkv_bias, expand_bias, rel_height, rel_width, sources):
    own, width = tokens.shape
    half = width // 2
    rows = [source.shape[-2] for source in sources]
    rows[0] = 3 * rows[0] // 2
    sds = jax.ShapeDtypeStruct
    any_spec = pl.BlockSpec(memory_space=pl.ANY)
    vmem_spec = pl.BlockSpec(memory_space=pltpu.VMEM)
    out_shape = [sds((own, width), BF), sds((own, width), F32)]
    out_shape += [sds(source.shape, BF) for source in sources]
    out_shape += [sds((16, width), F32), sds((8, width), F32), sds((64, LANES), F32)]
    first, second = zip(*[halves(n) for n in rows])
    out_shape += [sds((4, 2, n, half), BF) for n in first]
    out_shape += [sds((4, 2, n, half), BF) for n in second]
    out_shape += [sds((4, n, half), BF) for n in second]
    out_shape += [sds((4, n, half), BF) for n in first]
    out_shape += [sds((6, n, half), BF) for n in rows]
    out_shape += [sds((own, width), BF)] * 2
    both = 2 * own
    vmem, dma = pltpu.VMEM, pltpu.SemaphoreType.DMA
    qkv_width = 2 * rows[0]
    scratch = [vmem((count, 2, 2, n, half), BF) for count, n in zip((5, 5, 4, 4), rows)]
    scratch += [vmem((both, width), BF)] * 6
    scratch += [vmem((4, both, qkv_width // 3), BF)]
    scratch += [vmem((both, width), F32)] * 2
    scratch += [vmem((own, width), F32)] * 3
    scratch += [vmem((both, half), BF), vmem((both, half), BF), vmem((both, qkv_width), BF)]
    scratch += [vmem((4, 2, first[2], half), BF)]
    scratch += [vmem((4, 8, width), F32), vmem((16, width), F32), vmem((7, 16, width), F32)]
    scratch += [vmem((8, width), F32), vmem((7, 8, width), F32)]
    scratch += [vmem((64, LANES), F32), vmem((7, 64, LANES), F32)]
    scratch += [vmem((4, 1, half), F32), vmem((4, 1, qkv_width), F32), vmem((2 * LANES, LANES), F32)]
    scratch += [vmem((2 * LANES, LANES), BF), vmem((3 * LANES, LANES), BF), vmem((2, 32, HEAD), F32)]
    scratch += [dma((4, 4, 6))] * 2 + [dma((4, 4, 5)), dma((4, 4, 6))] + [dma((4, 5))] * 2 + [dma((41,))] * 2
    scratch += [dma((4,))] * 2 + [dma((8,))] * 2 + [dma((11,)), dma((4,))]
    got = pl.pallas_call(
        kernel,
        out_shape=out_shape,
        in_specs=[vmem_spec, vmem_spec, any_spec] + [vmem_spec] * 11 + [any_spec] * 4,
        out_specs=[any_spec] * len(out_shape),
        scratch_shapes=scratch,
        compiler_params=pltpu.CompilerParams(
            collective_id=0, has_side_effects=True, vmem_limit_bytes=VMEM_LIMIT
        ),
        name="block_step",
    )(tokens, keep, out_grad, *vectors, qkv_bias, expand_bias, rel_height, rel_width, key_codes(), *sources)
    return got[:9]


def finish_kernel(early, late, rel, *refs):
    wide, (bias_q, bias_e, height, width_out, rms), rows_out = refs[:4], refs[4:9], refs[9:15]
    outs, held, full, load, store = refs[15:19], refs[19:23], refs[23:27], refs[27], refs[28]
    z = lax.axis_index("col")
    loads = [pltpu.make_async_copy(src, to, load.at[i]) for i, (src, to) in enumerate(zip(wide, held))]
    stores = [pltpu.make_async_copy(src, to, store.at[i]) for i, (src, to) in enumerate(zip(full, outs))]
    for copy in loads:
        copy.start()
    places = ((late, 0), (late, 1), (early, 6), (early, 7), (early, 8), (early, 9))
    for ref, (source, at) in zip(rows_out, places):
        ref[...] = source[at, :]
    features = early.shape[1]
    scale = 1.0 / (early[5:6, 0:1] * features)
    rms[...] = jnp.sqrt(jnp.sum(early[:8], axis=1, keepdims=True) * scale)
    half = features // 2
    part = bias_q.shape[1] // 2
    bias_e[...] = early[pl.ds(10 + z, 1), :]
    row = late[pl.ds(2 + z, 1), :]
    for side in range(2):
        for i in range(2):
            at = (3 * side + 2 * i) * part
            bias_q[i : i + 1, side * part : (side + 1) * part] = row[:, at : at + part]
    count = height.shape[0]
    turn = lax.broadcasted_iota(jnp.int32, (32, 32), 0) + lax.broadcasted_iota(jnp.int32, (32, 32), 1) == count - 1
    turned = jnp.dot(turn.astype(F32), rel[:32], precision=lax.Precision.HIGHEST, preferred_element_type=F32)
    height[...] = turned[:count, :HEAD]
    width_out[...] = rel[32 : 32 + count, :HEAD]
    for i in range(4):
        loads[i].wait()
        rows = held[i].shape[0]
        step = rows // 5

        @pl.loop(0, 5)
        def _(m):
            at = pl.ds(pl.multiple_of(m * step, step), step)
            full[i][at] = held[i][at].astype(F32)

        stores[i].start()
    for copy in stores:
        copy.wait()


def finish_outputs(got, part):
    early, late, rel = got[6:9]
    grads = [value.reshape(-1, value.shape[-1]) for value in got[2:6]]
    width = early.shape[1]
    sds = jax.ShapeDtypeStruct
    any_spec = pl.BlockSpec(memory_space=pl.ANY)
    vmem_spec = pl.BlockSpec(memory_space=pltpu.VMEM)
    out_shape = [sds((2, 2 * part), F32), sds((1, width), F32), sds((2 * SIDE - 1, HEAD), F32)]
    out_shape += [sds((2 * SIDE - 1, HEAD), F32), sds((8, 1), F32)] + [sds((width,), F32)] * 6
    out_shape += [sds(value.shape, F32) for value in grads]
    return pl.pallas_call(
        finish_kernel,
        out_shape=out_shape,
        in_specs=[vmem_spec] * 3 + [any_spec] * 4,
        out_specs=[vmem_spec] * 11 + [any_spec] * 4,
        scratch_shapes=[pltpu.VMEM(value.shape, BF) for value in grads]
        + [pltpu.VMEM(value.shape, F32) for value in grads]
        + [pltpu.SemaphoreType.DMA((4,))] * 2,
        compiler_params=pltpu.CompilerParams(vmem_limit_bytes=VMEM_LIMIT // 2),
        name="finish",
    )(early, late, rel, *grads)


VMEM_LIMIT = 64 * 1024 * 1024 - 512 * 1024


def over_chips(
    tokens, valid_mask, out_grad, first_gain, first_shift, qkv_weight, qkv_bias, rel_height, rel_width,
    proj_weight, proj_bias, second_gain, second_shift, expand_weight, expand_bias, shrink_weight, shrink_bias,
):
    windows, per, width = tokens.shape
    side = (rel_height.shape[0] + 1) // 2
    count, head = rel_height.shape

    def padded(value):
        grid = value.reshape(windows, side, side, -1)
        grid = jnp.pad(grid, ((0, 0), (0, 0), (0, SIDE_PAD - side), (0, 0)))
        return grid.reshape(windows * side * SIDE_PAD, -1)

    def cut(value):
        grid = value.reshape(windows, side, SIDE_PAD, -1)[:, :, :side]
        return grid.reshape(windows, per, -1)

    rows, _, local_width = qkv_weight.shape
    part = local_width // 2
    hidden = expand_weight.shape[1] // 2
    qkv_src = qkv_weight.transpose(1, 2, 0).reshape(3, 2, part, rows)
    proj_src = proj_weight.reshape(2, 2, part // 2, proj_weight.shape[1])
    expand_src = expand_weight.reshape(2, rows // 2, 2 * hidden)
    shrink_src = shrink_weight.reshape(2, 2, hidden // 2, shrink_weight.shape[1])
    vectors = (first_gain, first_shift, second_gain, second_shift, proj_bias, shrink_bias)
    keep = padded(valid_mask.astype(F32))
    got = run_kernel(
        padded(tokens), keep, padded(out_grad), vectors, qkv_bias, expand_bias, rel_height, rel_width,
        (qkv_src, proj_src, expand_src, shrink_src),
    )
    outs = finish_outputs(got, part)
    qkv_bias_sum, expand_bias_sum, height_sum, width_sum, rms = outs[:5]
    gain_one, shift_one, gain_two, shift_two, proj_bias_sum, shrink_bias_sum = outs[5:11]
    qkv_sum, proj_sum, expand_sum, shrink_sum = outs[11:]
    return (
        cut(got[0]),
        cut(got[1]),
        gain_one,
        shift_one,
        qkv_sum.reshape(3, local_width, rows).transpose(2, 0, 1),
        qkv_bias_sum,
        height_sum,
        width_sum,
        proj_sum.reshape(proj_weight.shape),
        proj_bias_sum,
        gain_two,
        shift_two,
        expand_sum.reshape(expand_weight.shape),
        expand_bias_sum.reshape(-1),
        shrink_sum.reshape(shrink_weight.shape),
        shrink_bias_sum,
        rms[:5, 0],
    )


epsilon = 1e-06
highest = lax.Precision.HIGHEST


def layer_norm(values, norm_gain, norm_shift):
    center = values - jnp.mean(values, axis=-1, keepdims=True)
    spread = jnp.mean(center * center, axis=-1, keepdims=True)
    return center * lax.rsqrt(spread + epsilon) * norm_gain + norm_shift


def offset_table(span_size):
    positions = jnp.arange(span_size)
    offset = positions[:, None] - positions[None, :] + span_size - 1
    return (offset[:, :, None] == jnp.arange(2 * span_size - 1)[None, None, :]).astype(jnp.float32)


def attention_scores(
    query_rows, key_rows, rel_rows_table, rel_cols_table, onehot_table, span_size, scaling
):
    window_count, tokens_per, head_count, head_size = query_rows.shape
    rel_count = 2 * span_size - 1
    direct = (
        jnp.einsum("bthc,buhc->bhtu", query_rows, key_rows, preferred_element_type=jnp.float32)
        * scaling
    )
    query_float = query_rows.astype(jnp.float32)
    along_rows = jnp.einsum("bthc,jc->bhtj", query_float, rel_rows_table, precision=highest)
    along_cols = jnp.einsum("bthc,jc->bhtj", query_float, rel_cols_table, precision=highest)
    grid_rows = along_rows.reshape(window_count, head_count, span_size, span_size, rel_count)
    grid_cols = along_cols.reshape(window_count, head_count, span_size, span_size, rel_count)
    rel_rows = jnp.einsum("bhxyj,xkj->bhxyk", grid_rows, onehot_table, precision=highest)
    rel_cols = jnp.einsum("bhxyj,ywj->bhxyw", grid_cols, onehot_table, precision=highest)
    score_sum = direct.reshape(window_count, head_count, span_size, span_size, span_size, span_size)
    score_sum = score_sum + rel_rows[:, :, :, :, :, None] + rel_cols[:, :, :, :, None, :]
    return score_sum.reshape(window_count, head_count, tokens_per, tokens_per)


def relative_back(score_float, onehot_table, span_size):
    window_count, head_count, tokens_per, other_tokens = score_float.shape
    grid = score_float.reshape(window_count, head_count, span_size, span_size, span_size, span_size)
    rows_part = jnp.einsum("bhxykw,xkj->bhxyj", grid, onehot_table, precision=highest)
    cols_part = jnp.einsum("bhxykw,ywj->bhxyj", grid, onehot_table, precision=highest)
    return (
        rows_part.reshape(window_count, head_count, tokens_per, -1),
        cols_part.reshape(window_count, head_count, tokens_per, -1),
    )


def gather_weights(qkv_weight, proj_weight, expand_weight, shrink_weight):
    return (
        lax.all_gather(qkv_weight, "row", axis=0, tiled=True),
        lax.all_gather(proj_weight, "row", axis=1, tiled=True),
        lax.all_gather(expand_weight, "row", axis=0, tiled=True),
        lax.all_gather(shrink_weight, "row", axis=1, tiled=True),
    )


def gather_tokens(normed):
    return lax.all_gather(normed, "col", axis=0, tiled=True)


def gather_grads(grad_low):
    return lax.all_gather(grad_low, "col", axis=0, tiled=True)


def sum_branch(inputs_low, weight_full, own_windows):

    def term(first_row, row_count):
        return jnp.einsum(
            "btk,kd->btd", inputs_low, weight_full, preferred_element_type=jnp.float32
        )

    return lax.psum_scatter(
        term(jnp.int32(0), own_windows * lax.axis_size("col")),
        "col",
        scatter_dimension=0,
        tiled=True,
    )


def sum_input(grads_low, weight_full, own_windows):

    def term(first_row, row_count):
        return jnp.einsum("btk,dk->btd", grads_low, weight_full, preferred_element_type=jnp.float32)

    return lax.psum_scatter(
        term(jnp.int32(0), own_windows * lax.axis_size("col")),
        "col",
        scatter_dimension=0,
        tiled=True,
    )


def activate(values):
    return jax.nn.gelu(values, approximate=False)


def per_device(
    tokens,
    valid_mask,
    out_grad,
    first_gain,
    first_shift,
    qkv_weight,
    qkv_bias,
    rel_height,
    rel_width,
    proj_weight,
    proj_bias,
    second_gain,
    second_shift,
    expand_weight,
    expand_bias,
    shrink_weight,
    shrink_bias,
):
    span_size = (rel_height.shape[0] + 1) // 2
    head_size = rel_height.shape[1]
    local_width = qkv_weight.shape[2]
    head_count = local_width // head_size
    own_windows = tokens.shape[0]
    tokens_per = tokens.shape[1]
    model_width = tokens.shape[2]
    scaling = head_size ** (-0.5)
    onehot_table = offset_table(span_size)
    inputs = tokens.astype(jnp.float32)
    keep_mask = valid_mask.astype(jnp.float32)[:, :, None]

    def first_norm(values, norm_gain, norm_shift):
        return layer_norm(values, norm_gain, norm_shift) * keep_mask

    qkv_full, proj_full, expand_full, shrink_full = gather_weights(
        qkv_weight, proj_weight, expand_weight, shrink_weight
    )
    normed_first, first_back = jax.vjp(first_norm, inputs, first_gain, first_shift)
    first_all = gather_tokens(normed_first.astype(jnp.bfloat16))
    all_windows = first_all.shape[0]
    bias_rows = jnp.stack([qkv_bias[0], jnp.zeros_like(qkv_bias[0]), qkv_bias[1]])
    projected = (
        jnp.einsum("btd,dsk->btsk", first_all, qkv_full, preferred_element_type=jnp.float32)
        + bias_rows
    )
    projected = projected.astype(jnp.bfloat16)
    head_shape = (all_windows, tokens_per, head_count, head_size)
    query_low = projected[:, :, 0].reshape(head_shape)
    key_low = projected[:, :, 1].reshape(head_shape)
    value_low = projected[:, :, 2].reshape(head_shape)
    scores = attention_scores(
        query_low, key_low, rel_height, rel_width, onehot_table, span_size, scaling
    )
    top_score = jnp.max(scores, axis=-1, keepdims=True)
    log_total = top_score + jnp.log(jnp.sum(jnp.exp(scores - top_score), axis=-1, keepdims=True))
    probs_low = jnp.exp(scores - log_total).astype(jnp.bfloat16)
    attended = jnp.einsum(
        "bhtu,buhc->bthc", probs_low, value_low, preferred_element_type=jnp.float32
    )
    attended_low = attended.reshape(all_windows, tokens_per, local_width).astype(jnp.bfloat16)
    attn_out = sum_branch(attended_low, proj_full, own_windows) + proj_bias
    middle = inputs + attn_out
    normed_second, second_back = jax.vjp(layer_norm, middle, second_gain, second_shift)
    second_all = gather_tokens(normed_second.astype(jnp.bfloat16))
    hidden_pre = (
        jnp.einsum("btd,df->btf", second_all, expand_full, preferred_element_type=jnp.float32)
        + expand_bias
    )
    active_value, active_back = jax.vjp(activate, hidden_pre)
    hidden_low = active_value.astype(jnp.bfloat16)
    mlp_out = sum_branch(hidden_low, shrink_full, own_windows) + shrink_bias
    result = middle + mlp_out
    stat_terms = jnp.stack(
        [
            jnp.sum(keep_mask * inputs * inputs),
            jnp.sum(keep_mask * middle * middle),
            jnp.sum(keep_mask * result * result),
            jnp.sum(keep_mask * attn_out * attn_out),
            jnp.sum(keep_mask * mlp_out * mlp_out),
        ]
    )
    valid_count = jnp.sum(keep_mask)
    stat_total, count_total = lax.psum((stat_terms, valid_count), ("dp", "row", "col"))
    out_float = out_grad.astype(jnp.float32)
    qkv_full, proj_full, expand_full, shrink_full = gather_weights(
        qkv_weight, proj_weight, expand_weight, shrink_weight
    )
    mlp_grad_low = out_float.astype(jnp.bfloat16)
    shrink_bias_grad = jnp.sum(mlp_grad_low, axis=(0, 1), dtype=jnp.float32)
    mlp_grad_all = gather_grads(mlp_grad_low)
    shrink_grad_full = jnp.einsum(
        "btf,btd->fd", hidden_low, mlp_grad_all, preferred_element_type=jnp.float32
    )
    hidden_grad = jnp.einsum(
        "btd,fd->btf", mlp_grad_all, shrink_full, preferred_element_type=jnp.float32
    )
    pre_grad_low = active_back(hidden_grad)[0].astype(jnp.bfloat16)
    expand_bias_grad = jnp.sum(pre_grad_low, axis=(0, 1), dtype=jnp.float32)
    expand_grad_full = jnp.einsum(
        "btd,btf->df", second_all, pre_grad_low, preferred_element_type=jnp.float32
    )
    second_grad = sum_input(pre_grad_low, expand_full, own_windows)
    middle_part, second_gain_grad, second_shift_grad = second_back(second_grad)
    middle_grad = out_float + middle_part
    attn_grad_low = middle_grad.astype(jnp.bfloat16)
    proj_bias_grad = jnp.sum(attn_grad_low, axis=(0, 1), dtype=jnp.float32)
    attn_grad_all = gather_grads(attn_grad_low)
    proj_grad_full = jnp.einsum(
        "btk,btd->kd", attended_low, attn_grad_all, preferred_element_type=jnp.float32
    )
    attended_grad = jnp.einsum(
        "btd,kd->btk", attn_grad_all, proj_full, preferred_element_type=jnp.float32
    )
    attended_grad = attended_grad.astype(jnp.bfloat16).reshape(head_shape)
    scores_again = attention_scores(
        query_low, key_low, rel_height, rel_width, onehot_table, span_size, scaling
    )
    probs_float = jnp.exp(scores_again - log_total)
    probs_again = probs_float.astype(jnp.bfloat16)
    prob_grad = jnp.einsum(
        "bthc,buhc->bhtu", attended_grad, value_low, preferred_element_type=jnp.float32
    )
    value_grad = jnp.einsum(
        "bhtu,bthc->buhc", probs_again, attended_grad, preferred_element_type=jnp.float32
    )
    score_grad = probs_float * (
        prob_grad - jnp.sum(probs_float * prob_grad, axis=-1, keepdims=True)
    )
    score_low = score_grad.astype(jnp.bfloat16)
    rows_grad, cols_grad = relative_back(score_low.astype(jnp.float32), onehot_table, span_size)
    query_float = query_low.astype(jnp.float32)
    query_grad = (
        jnp.einsum("bhtu,buhc->bthc", score_low, key_low, preferred_element_type=jnp.float32)
        * scaling
    )
    query_grad = query_grad + jnp.einsum("bhtj,jc->bthc", rows_grad, rel_height, precision=highest)
    query_grad = query_grad + jnp.einsum("bhtj,jc->bthc", cols_grad, rel_width, precision=highest)
    key_grad = (
        jnp.einsum("bhtu,bthc->buhc", score_low, query_low, preferred_element_type=jnp.float32)
        * scaling
    )
    rel_height_grad = jnp.einsum("bhtj,bthc->jc", rows_grad, query_float, precision=highest)
    rel_width_grad = jnp.einsum("bhtj,bthc->jc", cols_grad, query_float, precision=highest)
    flat_shape = (all_windows, tokens_per, local_width)
    qkv_grad_low = jnp.stack(
        [
            query_grad.reshape(flat_shape),
            key_grad.reshape(flat_shape),
            value_grad.reshape(flat_shape),
        ],
        axis=2,
    ).astype(jnp.bfloat16)
    qkv_bias_grad = jnp.sum(qkv_grad_low[:, :, 0::2], axis=(0, 1), dtype=jnp.float32)
    qkv_grad_full = jnp.einsum(
        "btd,btsk->dsk", first_all, qkv_grad_low, preferred_element_type=jnp.float32
    )
    first_grad = sum_input(
        qkv_grad_low.reshape(all_windows, tokens_per, 3 * local_width),
        qkv_full.reshape(qkv_full.shape[0], 3 * local_width),
        own_windows,
    )
    input_part, first_gain_grad, first_shift_grad = first_back(first_grad)
    input_grad = middle_grad + input_part
    qkv_rows, proj_rows, expand_rows, shrink_rows = (
        lax.psum_scatter(qkv_grad_full, "row", scatter_dimension=0, tiled=True),
        lax.psum_scatter(proj_grad_full, "row", scatter_dimension=1, tiled=True),
        lax.psum_scatter(expand_grad_full, "row", scatter_dimension=0, tiled=True),
        lax.psum_scatter(shrink_grad_full, "row", scatter_dimension=1, tiled=True),
    )
    qkv_sum, proj_sum, expand_sum, shrink_sum = lax.psum(
        (qkv_rows, proj_rows, expand_rows, shrink_rows), "dp"
    )
    qkv_bias_sum, expand_bias_sum = lax.psum((qkv_bias_grad, expand_bias_grad), ("dp", "row"))
    (
        gain_one_sum,
        shift_one_sum,
        gain_two_sum,
        shift_two_sum,
        proj_bias_sum,
        shrink_bias_sum,
        height_sum,
        width_sum,
    ) = lax.psum(
        (
            first_gain_grad,
            first_shift_grad,
            second_gain_grad,
            second_shift_grad,
            proj_bias_grad,
            shrink_bias_grad,
            rel_height_grad,
            rel_width_grad,
        ),
        ("dp", "row", "col"),
    )
    rms = jnp.sqrt(stat_total / (count_total * model_width))
    return (
        result.astype(jnp.bfloat16),
        input_grad,
        gain_one_sum,
        shift_one_sum,
        qkv_sum,
        qkv_bias_sum,
        height_sum,
        width_sum,
        proj_sum,
        proj_bias_sum,
        gain_two_sum,
        shift_two_sum,
        expand_sum,
        expand_bias_sum,
        shrink_sum,
        shrink_bias_sum,
        rms,
    )


def choose(mesh):
    fits = tuple(mesh.shape[name] for name in ("dp", "row", "col")) == (4, 2, 4)
    return over_chips if fits else per_device


def solution(mesh):
    in_specs = (
        P(("dp", "row", "col"), None, None),
        P(("dp", "row", "col"), None),
        P(("dp", "row", "col"), None, None),
        P(),
        P(),
        P("row", None, "col"),
        P(None, "col"),
        P(),
        P(),
        P("col", "row"),
        P(),
        P(),
        P(),
        P("row", "col"),
        P("col"),
        P("col", "row"),
        P(),
    )
    out_specs = (
        P(("dp", "row", "col"), None, None),
        P(("dp", "row", "col"), None, None),
        P(),
        P(),
        P("row", None, "col"),
        P(None, "col"),
        P(),
        P(),
        P("col", "row"),
        P(),
        P(),
        P(),
        P("row", "col"),
        P("col"),
        P("col", "row"),
        P(),
        P(),
    )
    return jax.shard_map(
        choose(mesh), mesh=mesh, in_specs=in_specs, out_specs=out_specs, check_vma=False
    )
```

```python
import functools

import jax
import jax.numpy as jnp
import numpy as np
from jax import lax
from jax.experimental import pallas as pl
from jax.experimental.pallas import tpu as pltpu
from jax.sharding import PartitionSpec as P

BF = jnp.bfloat16
F32 = jnp.float32
LANES = 128
SIDE = 14
SIDE_PAD = 16
WROWS = SIDE * SIDE_PAD
HEAD = 80
AT_H = HEAD
AT_W = HEAD + SIDE
AT_MASK = HEAD + 2 * SIDE
COL_W = 64


def dot(a, b):
    return jnp.dot(a, b, preferred_element_type=F32)


def dot_nt(a, b):
    return lax.dot_general(a, b, (((1,), (1,)), ((), ())), preferred_element_type=F32)


def dot_tn(a, b):
    return lax.dot_general(a, b, (((0,), (0,)), ((), ())), preferred_element_type=F32)


def lane_ids():
    return lax.broadcasted_iota(jnp.int32, (WROWS, LANES), 1)


def row_ids():
    return lax.broadcasted_iota(jnp.int32, (WROWS, LANES), 0)


def key_codes():
    u = np.arange(WROWS)[:, None]
    lane = np.arange(LANES)[None, :]
    k, l = u // SIDE_PAD, u % SIDE_PAD
    height = lane - AT_H == k
    width = (lane - AT_W == l) & (l < SIDE)
    width_back = (AT_W + SIDE - 1 - lane == l) & (l < SIDE)
    plain = np.where(height | width, 1.0, 0.0)
    masked = np.where((lane == AT_MASK) & (l >= SIDE), -1e30, plain)
    back = np.where(height | width_back, 1.0, 0.0)
    return np.stack([masked, plain, back]).astype(BF)


def split_low(values):
    high = values.astype(BF)
    return high, (values - high.astype(F32)).astype(BF)


def relative_tables(rel_h, rel_w, rel_query, rel_back):
    count, rows = 2 * SIDE - 1, rel_h.shape[0]
    offset = lax.broadcasted_iota(jnp.int32, (rows, LANES), 0)
    lane = lax.broadcasted_iota(jnp.int32, (rows, LANES), 1)

    def places(first, step):
        return jnp.where((lane == first + step * offset) & (offset < count), 1.0, 0.0).astype(BF)

    heights, widths = places(count - 1, -1), places(COL_W + count - 1, -1)
    widths_back = places(COL_W, 1)
    tall, wide = rel_h[...], rel_w[...]
    rel_query[...] = jnp.zeros_like(rel_query)
    rel_back[...] = jnp.zeros_like(rel_back)
    for part, (a, b) in enumerate(zip(split_low(tall * HEAD**0.5), split_low(wide * HEAD**0.5))):
        at = part * LANES
        rel_query[at : at + HEAD] = (dot_tn(a, heights) + dot_tn(b, widths)).astype(BF)
    for part, (a, b) in enumerate(zip(split_low(tall), split_low(wide))):
        table = (dot_tn(heights, a) + dot_tn(widths_back, b)).astype(BF)
        for place in ((0, 1), (2,))[part]:
            rel_back[place * LANES : (place + 1) * LANES, :HEAD] = table


def query_codes(query, rel_query):
    full = dot(jnp.concatenate([query, query], axis=1), rel_query)
    tiles = full.reshape(SIDE, SIDE_PAD, LANES)
    heights = jnp.concatenate(
        [pltpu.roll(tiles[i], AT_H - (SIDE - 1 - i), 1) for i in range(SIDE)], axis=0
    )
    widths = pltpu.roll(
        tiles, AT_W - COL_W - (SIDE - 1), 2, stride=1, stride_axis=1
    ).reshape(WROWS, LANES)
    lane = lane_ids()
    codes = jnp.where(
        (lane >= AT_H) & (lane < AT_W),
        heights,
        jnp.where((lane >= AT_W) & (lane < AT_MASK), widths, 0.0),
    )
    high, rest = split_low(codes)
    first = query + high + jnp.where(lane == AT_MASK, 1.0, 0.0).astype(BF)
    return jnp.concatenate([first, rest], axis=1)


def softmax_rows(query, key, rel_query, codes_ref):
    left = query_codes(query, rel_query)
    right = jnp.concatenate([key + codes_ref[0], codes_ref[1]], axis=1)
    scores = dot_nt(left, right)
    top = jnp.max(scores, axis=1, keepdims=True)
    weights = jnp.exp((scores - top) * (HEAD**-0.5))
    return weights / jnp.sum(weights, axis=1, keepdims=True)


def attend(query, key, value, rel_query, codes_ref):
    probs = softmax_rows(query, key, rel_query, codes_ref)
    return dot(probs.astype(BF), value)


def attend_back(query, key, value, grad, rel_query, rel_back, codes_ref):
    probs = softmax_rows(query, key, rel_query, codes_ref)
    prob_grad = dot_nt(grad, value)
    inner = jnp.sum(probs * prob_grad, axis=1, keepdims=True)
    score_low = (probs * (prob_grad - inner)).astype(BF)
    value_grad = dot_tn(probs.astype(BF), grad)
    key_grad = dot_tn(score_low, query) * (HEAD**-0.5)
    mixed = dot(score_low, key + codes_ref[2])
    tiles = mixed.reshape(SIDE, SIDE_PAD, LANES)
    heights = jnp.concatenate(
        [pltpu.roll(tiles[i], (SIDE - 1 - i - AT_H) % LANES, 1) for i in range(SIDE)], axis=0
    )
    widths = pltpu.roll(
        tiles, (COL_W - AT_W) % LANES, 2, stride=1, stride_axis=1
    ).reshape(WROWS, LANES)
    lane, row = lane_ids(), row_ids()
    first_h = SIDE - 1 - row // SIDE_PAD
    first_w = COL_W + row % SIDE_PAD
    offsets = jnp.where(
        (lane >= first_h) & (lane < first_h + SIDE),
        heights,
        jnp.where((lane >= first_w) & (lane < first_w + SIDE), widths, 0.0),
    )
    high, rest = split_low(offsets)
    query_grad = jnp.where(lane < HEAD, mixed, 0.0) * (HEAD**-0.5) + dot(
        jnp.concatenate([high, rest, high], axis=1), rel_back
    )
    rel_grad = dot_tn(jnp.concatenate([high, rest], axis=1), query)
    return query_grad, key_grad, value_grad, rel_grad


def pad_head(piece):
    return jnp.concatenate([piece, jnp.zeros((piece.shape[0], LANES - HEAD), piece.dtype)], axis=1)


def qkv_low(s, rows, h1, wq, bias, half):
    return (dot_nt(h1[rows, :half], block(wq, s, 0)) + dot_nt(h1[rows, half:], block(wq, s, 1)) + bias).astype(BF)


def head_of(low, part, heads, hh):
    at = (part * heads + hh) * HEAD
    return pad_head(low[:, at : at + HEAD])


def attention_slab(s, h1, wq, wp, bias, rel_query, codes, attended, total, heads, half, half_done):
    count = h1.shape[0] // WROWS

    @pl.loop(0, count)
    def _(m):
        rows = pl.ds(pl.multiple_of((m + count // 2) % count * WROWS, WROWS), WROWS)
        low = qkv_low(s, rows, h1, wq, bias, half)
        outs = []
        for hh in range(heads):
            query, key, value = (head_of(low, part, heads, hh) for part in range(3))
            outs.append(attend(query, key, value, rel_query[...], codes)[:, :HEAD])
        out_low = jnp.concatenate(outs, axis=1).astype(BF)
        attended[s, rows] = out_low
        total[rows, :half] += dot(out_low, block(wp, s, 0))
        total[rows, half:] += dot(out_low, block(wp, s, 1))

        @pl.when(m == count // 2 - 1)
        def _():
            half_done()


SQRT_HALF = 0.5**0.5
PDF_SCALE = 0.3989422804014327


def mlp_rows(s, place, m, h2, gm, we, ws, bias, act, gpre, total, back, bias_grad, half):
    count = h2.shape[0] // 2

    @pl.loop(0, 1)
    def _(step):
        rows = pl.ds(pl.multiple_of((m + step) * count, count), count)
        pre = dot(h2[rows, :half], block(we, place, 0)) + dot(h2[rows, half:], block(we, place, 1)) + bias
        cdf = 0.5 + 0.5 * lax.erf(pre * SQRT_HALF)
        slope = cdf + pre * (PDF_SCALE * jnp.exp(-0.5 * pre * pre))
        act_low = (pre * cdf).astype(BF)
        act[rows, :] = act_low
        hidden = dot_nt(gm[rows, :half], block(ws, place, 0)) + dot_nt(gm[rows, half:], block(ws, place, 1))
        gpre_low = (hidden * slope).astype(BF)
        gpre[rows, :] = gpre_low
        bias_grad[s] += jnp.sum(gpre_low.astype(F32), axis=0, keepdims=True)
        total[rows, :half] += dot(act_low, block(ws, place, 0))
        total[rows, half:] += dot(act_low, block(ws, place, 1))
        back[rows, :half] += dot_nt(gpre_low, block(we, place, 0))
        back[rows, half:] += dot_nt(gpre_low, block(we, place, 1))


def attention_back_slab(
    s, h1, ga, wq, wp, bias, rel_query, rel_back, codes, gqkv, back, bias_grad, rel_grad, heads, half, half_done
):
    count = h1.shape[0] // WROWS

    @pl.loop(0, count)
    def _(m):
        rows = pl.ds(pl.multiple_of((m + count // 2) % count * WROWS, WROWS), WROWS)
        low = qkv_low(s, rows, h1, wq, bias, half)
        grad = (dot_nt(ga[rows, :half], block(wp, s, 0)) + dot_nt(ga[rows, half:], block(wp, s, 1))).astype(BF)
        parts = [[], [], []]
        for hh in range(heads):
            query, key, value = (head_of(low, part, heads, hh) for part in range(3))
            got = attend_back(
                query, key, value, head_of(grad, 0, heads, hh), rel_query[...], rel_back[...], codes
            )
            for part in range(3):
                parts[part].append(got[part][:, :HEAD])
            rel_grad[...] += got[3]
        grad_low = jnp.concatenate(parts[0] + parts[1] + parts[2], axis=1).astype(BF)
        gqkv[rows, : grad_low.shape[1]] = grad_low
        bias_grad[s] += jnp.sum(grad_low.astype(F32), axis=0, keepdims=True)
        back[rows, :half] += dot(grad_low, block(wq, s, 0))
        back[rows, half:] += dot(grad_low, block(wq, s, 1))

        @pl.when(m == count // 2 - 1)
        def _():
            half_done()


MESH_ID = pl.DeviceIdType.MESH
ARRAYS = ("qkv", "proj", "expand", "shrink")
CHUNK = 64
EPS = 1e-06
SPARE = 4


def halves(rows):
    first = (rows // 2 + 15) // 16 * 16
    return first, rows - first


def flip(index, k):
    return ((index // 2 + k // 2) % 2) * 2 + (index % 2 + k % 2) % 2


def block(ref, slab, half):
    value = ref[slab, half]
    return value.reshape(value.shape[0] * value.shape[1], value.shape[2])


def add_low(target, index, extra):
    target[index] = (target[index].astype(F32) + extra.astype(F32)).astype(BF)


def kernel(
    tokens_in, mask_in, out_grad_in, gain_one_in, shift_one_in, gain_two_in, shift_two_in, proj_bias_in, shrink_bias_in,
    qkv_bias_in, expand_bias_in, rel_h_in, rel_w_in, codes, qkv_src, proj_src, expand_src, shrink_src,
    block_out, input_grad, qkv_out, proj_out, expand_out, shrink_out, early_out, late_out, rel_out,
    rxq, rxp, rxe, rxs, ryq, ryp, rye, rys, rx2q, rx2p, rx2e, rx2s, ry2q, ry2p, ry2e, ry2s, rzq, rzp, rze, rzs, pair_back, pair_out,
    wq, wp, we, ws, tokens, keep, h1, grads, normed, got_low, attended, total, back, xr, xr2, middle, act, gpre,
    bias_all, early, early_got, late, late_got, rel, rel_got, bias_e, bias_q, rel_acc, rel_query, rel_back, rel_pad,
    gsend, grecv, rsend, rrecv, fsend, frecv, csend, crecv, zsend, zrecv, qsend, qrecv, local, qlocal,
):
    d, r, z = lax.axis_index("dp"), lax.axis_index("row"), lax.axis_index("col")
    h, b = d // 2, d % 2
    own = tokens.shape[0]
    width = tokens.shape[1]
    half = width // 2
    heads = 2
    bufs = (wq, wp, we, ws)
    outs = (qkv_out, proj_out, expand_out, shrink_out)
    rx, ry = (rxq, rxp, rxe, rxs), (ryq, ryp, rye, rys)
    rx2, ry2 = (rx2q, rx2p, rx2e, rx2s), (ry2q, ry2p, ry2e, ry2s)
    rz = (rzq, rzp, rze, rzs)
    parts = [halves(buf.shape[3]) for buf in bufs]
    attn, mlp = (0, 1), (2, 3)
    qkv_width = 3 * attended.shape[2]

    along_x = (h * 2 + 1 - b, r, z)
    along_y = ((1 - h) * 2 + b, r, z)
    across = ((1 - h) * 2 + 1 - b, r, z)
    partner = (d, 1 - r, z)
    pair, remote_slab = (d, r, flip(z, 1)), flip(z, 2)
    gm, gmz, h2, h2z = grads.at[0], grads.at[1], normed.at[0], normed.at[1]

    def along_z(k):
        return (d, r, flip(z, k))

    def remote(src, dst, sems, recvs, index, device, got=None):
        return pltpu.make_async_remote_copy(
            src_ref=src,
            dst_ref=dst,
            send_sem=sems.at[index],
            recv_sem=recvs.at[index if got is None else got],
            device_id=device,
            device_id_type=MESH_ID,
        )

    up = z // 2
    is_end = (z + 1) // 2 % 2 == 0
    is_inner = (z + 1) // 2 % 2 == 1

    def slab_of(i):
        far = i // 2
        return (1 - far) * flip(z, i) + far * ((1 - up) * i + up * (3 - i))

    def first_part(a):
        return pl.ds(0, parts[a][0])

    def second_part(a):
        return pl.ds(parts[a][0], parts[a][1])

    def gather_z(a, s, step):
        at = bufs[a].at[s, h, b]
        return remote(at, at, gsend, grecv, (a, s, 0 if step < 0 else 5), (d, r, z + step), (a, s, 0))

    def gather_far(a):
        return remote(bufs[a].at[0, h, b], bufs[a].at[1, h, b], gsend, grecv, (a, 0, 0), (d, r, remote_slab))

    def ring(a, slab, sends, recvs, index, kind, arriving):
        buf = bufs[a]
        if kind == 1:
            at, device = (buf.at[slab, h, 1 - b] if arriving else buf.at[slab, h, b]), along_x
        elif kind == 2:
            at, device = (buf.at[slab, 1 - h, b] if arriving else buf.at[slab, h, b]), along_y
        elif kind == 3:
            at = buf.at[slab, 1 - h if arriving else h, 1 - b, first_part(a)]
            device = along_y
        else:
            at = buf.at[slab, 1 - h, 1 - b if arriving else b, second_part(a)]
            device = along_x
        return remote(at, at, sends, recvs, index, device)

    def gather(a, s, kind, arriving=False):
        return ring(a, s, gsend, grecv, (a, s, kind), kind, arriving)

    def spread(a, kind, arriving=False):
        return ring(a, final_slot(a), fsend, frecv, (a, kind), kind, arriving)

    def sends_along_z(group, s, act_on):
        for a in group:

            @pl.when((s >= z) & (z > 0))
            def _():
                act_on(gather_z(a, s, -1))

            @pl.when((s <= z) & (z < 3))
            def _():
                act_on(gather_z(a, s, 1))

    def start_z(group):
        sends_along_z(group, z, lambda copy: copy.start())

    def relay(group, i):
        s = slab_of(i)
        for a in group:
            gather_z(a, s, 1).wait_recv()
            sends_along_z((a,), s, lambda copy: copy.start())

    def place_of(a, i):
        return slab_of(i) if a in attn else 1

    def share(group, i):
        for a in group:
            gather(a, place_of(a, i), 1).start()
            gather(a, place_of(a, i), 2).start()

    def share_far(group):
        for a in group:
            gather_far(a).wait_recv()
            share((a,), 1)

    def pass_diagonal(group, i):
        for a in group:
            s = place_of(a, i)
            gather(a, s, 1, True).wait_recv()
            gather(a, s, 3).start()
            gather(a, s, 2, True).wait_recv()
            gather(a, s, 4).start()

    def finish_slab(group, i):
        for a in group:
            s = place_of(a, i)
            gather(a, s, 3, True).wait_recv()
            gather(a, s, 4, True).wait_recv()

    def sent_slab(group, i):
        s = slab_of(i)
        sends_along_z(group, s, lambda copy: copy.wait_send())
        for a in group:

            @pl.when(i > 0)
            def _():
                for kind in (1, 2, 3, 4):
                    gather(a, s, kind).wait_send()

    def sent_far(group):
        for a in group:
            gather_far(a).wait_send()
            for kind in (1, 2, 3, 4):
                gather(a, 1, kind).wait_send()

    def step_slab(n):
        return slab_of(3 - n)

    def final_slot(a):
        return z if a in attn else 0

    def slot(a, n):
        if a in mlp:
            return 2 + n
        first = (4 - n) // 4
        return first * SPARE + (1 - first) * step_slab(n - 1 + first)

    def reduce_copy(a, n, kind):
        buf, g = bufs[a], slot(a, n)
        got = None
        if kind == 0:
            src, dst, device = buf.at[g, :, 1 - b, first_part(a)], rx[a].at[n], along_x
        elif kind == 1:
            src, dst, device = buf.at[g, 1 - h, :, second_part(a)], ry[a].at[n], along_y
        elif kind == 2:
            src, dst, device = buf.at[g, 1 - h, b, first_part(a)], ry2[a].at[n], along_y
        elif kind == 3:
            src, dst, device = buf.at[g, h, 1 - b, second_part(a)], rx2[a].at[n], along_x
        elif kind == 4 and a in mlp:
            src, dst, device = buf.at[g, h, b], rz[a].at[0], (d, r, remote_slab)
            got = (a, 0, 4)
        elif kind == 4:
            src, dst, device = buf.at[g, h, b], rz[a].at[z], (d, r, step_slab(n))
            got = (a, z, 4)
        else:
            src, dst, device = buf.at[g, h, b], rz[a].at[5 - n], (d, r, slab_of(1))
            got = (a, 3 - n, 5)
        return remote(src, dst, rsend, rrecv, (a, n, min(kind, 4)), device, got)

    def reduce_z(a, n, act_on):
        if a in mlp:

            @pl.when(n == 1)
            def _():
                act_on(reduce_copy(a, n, 4))

        else:

            @pl.when((n < 3) & (is_inner | (n == 2)))
            def _():
                act_on(reduce_copy(a, n, 4))

            @pl.when(is_end & (n < 2))
            def _():
                act_on(reduce_copy(a, n, 5))

    def reduce_one(group, n):
        for a in group:
            reduce_copy(a, n, 0).start()
            reduce_copy(a, n, 1).start()

    def with_room(body):
        def run(group, n):
            shape = (2 * len(group), 2, halves(max(bufs[a].shape[3] for a in group))[0], half)
            pl.run_scoped(
                lambda room: body(group, n, lambda a, place: room.at[2 * group.index(a) + place]),
                pltpu.VMEM(shape, BF),
            )

        return run

    def reduce_two_body(group, n, scratch):
        loads = []
        for a in group:
            reduce_copy(a, n, 0).wait_recv()
            reduce_copy(a, n, 1).wait_recv()
            for place, got in enumerate((rx[a], ry[a])):
                to = scratch(a, place).at[:, pl.ds(0, parts[a][place])]
                loads.append(pltpu.make_async_copy(got.at[n], to, local.at[a * 2 + place]))
                loads[-1].start()
        for i, a in enumerate(group):
            g = slot(a, n)
            first, second = parts[a]
            loads[2 * i].wait()
            for side in range(2):
                add_low(bufs[a], (g, side, b, first_part(a)), scratch(a, 0)[side, :first])
            reduce_copy(a, n, 2).start()
            loads[2 * i + 1].wait()
            for side in range(2):
                add_low(bufs[a], (g, h, side, second_part(a)), scratch(a, 1)[side, :second])
            reduce_copy(a, n, 3).start()

    def reduce_three_body(group, n, scratch):
        loads = []
        for a in group:
            reduce_copy(a, n, 2).wait_recv()
            reduce_copy(a, n, 3).wait_recv()
            for place, got in enumerate((ry2[a], rx2[a])):
                to = scratch(a, place).at[0, pl.ds(0, parts[a][place])]
                loads.append(pltpu.make_async_copy(got.at[n], to, local.at[a * 2 + place]))
                loads[-1].start()
        for i, a in enumerate(group):
            g = slot(a, n)
            first, second = parts[a]
            loads[2 * i].wait()
            add_low(bufs[a], (g, h, b, first_part(a)), scratch(a, 0)[0, :first])
            loads[2 * i + 1].wait()
            add_low(bufs[a], (g, h, b, second_part(a)), scratch(a, 1)[0, :second])

            @pl.when(is_inner & (n < 2) & (a in attn))
            def _():
                at = rz[a].at[5 - n]
                remote(at, at, rsend, rrecv, (a, n, 4), (d, r, slab_of(1)), (a, 3 - n, 5)).wait_recv()
                pieces = ((0, first, first_part(a)), (1, second, second_part(a)))
                copies = [
                    pltpu.make_async_copy(at.at[part], scratch(a, 0).at[side, pl.ds(0, count)], local.at[a * 2 + side])
                    for side, count, part in pieces
                ]
                for copy in copies:
                    copy.start()
                for copy, (side, count, part) in zip(copies, pieces):
                    copy.wait()
                    add_low(bufs[a], (g, h, b, part), scratch(a, 0)[side, :count])

            reduce_z(a, n, lambda copy: copy.start())

    def reduce_two(group, n):
        with_room(reduce_two_body)(group, n)

    def reduce_three(group, n):
        with_room(reduce_three_body)(group, n)

    def reduce_four(group):
        for a in group:
            rows = bufs[a].shape[3]
            loads = []
            others = ((remote_slab, 0),) if a in mlp else [(slab_of(k), slab_of(k)) for k in (1, 2)]
            for k, (other, place) in enumerate(others, 1):
                at = rz[a].at[place]
                remote(at, at, rsend, rrecv, (a, k, 4), (d, r, other), (a, place, 4)).wait_recv()
                loads.append(pltpu.make_async_copy(at, gpre.at[pl.ds((k - 1) * rows, rows)], local.at[k]))
                loads[-1].start()
            for load in loads:
                load.wait()
            value = bufs[a][slot(a, 0 if a in mlp else 3), h, b].astype(F32)
            for k in range(len(others)):
                value = value + gpre[k * rows : (k + 1) * rows].astype(F32)
            bufs[a][final_slot(a), h, b] = value.astype(BF)
            spread(a, 1).start()
            spread(a, 2).start()

    def reduce_five(group):
        for a in group:
            spread(a, 1, True).wait_recv()
            spread(a, 3).start()
            spread(a, 2, True).wait_recv()
            spread(a, 4).start()

    def qkv_pieces(matrix, side, flat):
        rows = flat.shape[1]
        part = matrix.shape[2]
        cut = rows - part
        return (
            (matrix.at[0, side], flat.at[0, pl.ds(0, part)]),
            (matrix.at[1, side, pl.ds(0, cut)], flat.at[0, pl.ds(part, cut)]),
            (matrix.at[1, side, pl.ds(cut, part - cut)], flat.at[1, pl.ds(0, part - cut)]),
            (matrix.at[2, side], flat.at[1, pl.ds(part - cut, part)]),
        )

    def swap_out(a):
        mine = bufs[a].at[final_slot(a), 1 - r]
        if a == 0:
            pairs = qkv_pieces(outs[a], r, mine)
            return [remote(src, dst, qsend, qrecv, 4 + i, partner) for i, (dst, src) in enumerate(pairs)]
        to = outs[a].at[:, :, half_lanes(r)] if a == 2 else outs[a].at[r]
        return [remote(mine, to, fsend, frecv, (a, 0), partner)]

    def keep_out(a):
        mine = bufs[a].at[final_slot(a), r]
        if a == 0:
            pairs = qkv_pieces(outs[a], r, mine)
            return [pltpu.make_async_copy(src, dst, qlocal.at[i]) for i, (dst, src) in enumerate(pairs)]
        to = outs[a].at[:, :, half_lanes(r)] if a == 2 else outs[a].at[r]
        return [pltpu.make_async_copy(mine, to, local.at[a])]

    def reduce_six(group):
        for a in group:
            spread(a, 3, True).wait_recv()
            spread(a, 4, True).wait_recv()
            for copy in swap_out(a) + keep_out(a):
                copy.start()

    def half_lanes(side):
        return pl.ds(pl.multiple_of(side * half, half), half)

    def exchange(index, src, dst):
        return remote(src, dst, csend, crecv, index, partner)

    rows_own, rows_other = pl.ds(0, own), pl.ds(own, own)
    def source(a, side):
        if a == 2:
            return expand_src.at[:, :, half_lanes(side)]
        return (qkv_src, proj_src, expand_src, shrink_src)[a].at[side]

    def source_swap(a):
        to = bufs[a].at[z if a in attn else 0, r]
        if a == 0:
            pairs = qkv_pieces(qkv_src, 1 - r, to)
            return [remote(src, dst, qsend, qrecv, i, partner) for i, (src, dst) in enumerate(pairs)]
        return [exchange(a, source(a, 1 - r), to)]

    def source_keep(a):
        to = bufs[a].at[z if a in attn else 0, r]
        if a == 0:
            pairs = qkv_pieces(qkv_src, r, to)
            return [pltpu.make_async_copy(src, dst, qlocal.at[i]) for i, (src, dst) in enumerate(pairs)]
        return [pltpu.make_async_copy(source(a, r), to, local.at[a])]

    def start_source(group):
        for a in group:
            for copy in source_swap(a) + source_keep(a):
                copy.start()

    def finish_source(group):
        for a in group:
            for copy in source_swap(a) + source_keep(a):
                copy.wait()

    swap_grad = exchange(4, gm.at[rows_own], gm.at[rows_other])
    swap_h1 = exchange(5, h1.at[rows_own], h1.at[rows_other])
    swap_attn = exchange(6, total.at[rows_other], xr)
    swap_h2 = exchange(7, h2.at[rows_own], h2.at[rows_other])
    swap_mlp = exchange(8, total.at[rows_other], xr)
    swap_gh2 = exchange(9, back.at[rows_other], xr2)
    swap_ga = exchange(10, gm.at[rows_own], gm.at[rows_other])
    swap_gh1 = exchange(11, back.at[rows_other], total.at[rows_other])
    pair_gm = remote(gm.at[rows_own], gmz.at[rows_own], csend, crecv, 12, pair)
    swap_gmz = exchange(13, gmz.at[rows_own], gmz.at[rows_other])
    pair_h2 = remote(h2.at[rows_own], h2z.at[rows_own], csend, crecv, 14, pair)
    swap_h2z = exchange(15, h2z.at[rows_own], h2z.at[rows_other])
    swap_back_low = exchange(16, h2.at[rows_own], got_low.at[rows_own])
    swap_out_low = exchange(17, h2.at[rows_other], got_low.at[rows_other])
    send_back = remote(h2.at[rows_own], pair_back, csend, crecv, 18, pair)
    send_out = remote(h2.at[rows_other], pair_out, csend, crecv, 19, pair)

    def bias_copy(k, arriving=False):
        at = bias_all.at[flip(z, k) if arriving else z]
        return remote(at, at, zsend, zrecv, k, along_z(k))

    barrier = pltpu.get_barrier_semaphore()
    peers = [partner, along_x, along_y, across, along_z(1), along_z(2), along_z(3)]
    for peer in peers:
        pl.semaphore_signal(barrier, inc=1, device_id=peer, device_id_type=MESH_ID)
    pl.semaphore_wait(barrier, len(peers))

    start_source(attn)
    bias_all[z] = jnp.zeros(bias_all.shape[1:], F32)
    part = qkv_bias_in.shape[1] // 2
    for side in range(2):

        @pl.when(r == side)
        def _():
            bias_all[z, 0:1, :half] = expand_bias_in[side * half : (side + 1) * half].reshape(1, half)
            for i in range(2):
                at = half + 2 * i * part
                bias_all[z, 0:1, at : at + part] = qkv_bias_in[i : i + 1, side * part : (side + 1) * part]

    finish_source(attn)
    start_z(attn)
    for k in (1, 2, 3):
        bias_copy(k).start()
    start_source(mlp)

    def as_row(ref):
        return ref[...].reshape(1, width)

    gain_one, shift_one, gain_two, shift_two, proj_bias, shrink_bias = (
        as_row(ref) for ref in (gain_one_in, shift_one_in, gain_two_in, shift_two_in, proj_bias_in, shrink_bias_in)
    )

    def over_rows(body):
        @pl.loop(0, own // CHUNK)
        def _(m):
            body(pl.ds(pl.multiple_of(m * CHUNK, CHUNK), CHUNK))

    def column_sum(value):
        return jnp.sum(value, axis=0, keepdims=True)

    def normalize(value):
        center = value - jnp.mean(value, axis=1, keepdims=True)
        inverse = lax.rsqrt(jnp.mean(center * center, axis=1, keepdims=True) + EPS)
        return center * inverse, inverse

    def norm_back(grad, gain, xhat, inverse):
        scaled = grad * gain
        mean = jnp.mean(scaled, axis=1, keepdims=True)
        along = jnp.mean(scaled * xhat, axis=1, keepdims=True)
        return (scaled - mean - xhat * along) * inverse

    early[...] = jnp.zeros_like(early)
    late[...] = jnp.zeros_like(late)

    def spread_rows(source, target):
        def move(stage):
            load = pltpu.make_async_copy(source, stage, local.at[8])
            load.start()
            load.wait()

            @pl.loop(0, SIDE)
            def _(i):
                both = stage[pl.ds(i * SIDE, SIDE)].astype(F32)
                for w in range(both.shape[1]):
                    some = jnp.concatenate([both[:, w], jnp.zeros((SIDE_PAD - SIDE, width), F32)], axis=0)
                    at = pl.multiple_of(w * WROWS + i * SIDE_PAD, SIDE_PAD)
                    target[pl.ds(at, SIDE_PAD)] = some.astype(BF)

        pl.run_scoped(move, pltpu.VMEM(source.shape, BF))

    spread_rows(tokens_in, tokens)
    count = mask_in.shape[0]
    mask = jnp.concatenate([mask_in[...].astype(F32), jnp.zeros((count, 2 * LANES - SIDE * SIDE), F32)], axis=1)
    mask = jnp.concatenate([mask, jnp.zeros((8 - count, 2 * LANES), F32)], axis=0).T
    keep[...] = jnp.zeros_like(keep)
    for i in range(SIDE):
        for w in range(count):
            at = w * WROWS + i * SIDE_PAD
            keep[at : at + SIDE] = mask[i * SIDE : (i + 1) * SIDE, w : w + 1]

    def first_rows(rows):
        value = tokens[rows].astype(F32)
        valid = keep[rows]
        xhat, _ = normalize(value)
        h1[rows] = ((xhat * gain_one + shift_one) * valid).astype(BF)
        early[0:1, :] += column_sum(valid * value * value)
        early[5:6, :] += jnp.broadcast_to(column_sum(valid), (1, width))

    over_rows(first_rows)
    swap_h1.start()
    spread_rows(out_grad_in, gm)
    swap_grad.start()
    rel_pad[...] = jnp.zeros_like(rel_pad)
    rel_pad[0, : rel_h_in.shape[0]] = rel_h_in[...]
    rel_pad[1, : rel_w_in.shape[0]] = rel_w_in[...]
    relative_tables(rel_pad.at[0], rel_pad.at[1], rel_query, rel_back)
    total[...] = jnp.zeros_like(total)
    swap_h1.wait_recv()

    def bias_q_of(s):
        return bias_all[s, 0:1, half : half + qkv_width]

    def bias_e_of(s):
        return bias_all[s, 0:1, :half]

    finish_source(mlp)

    def start_far():
        for a in mlp:
            gather_far(a).start()
        pair_gm.start()

    @pl.loop(0, 4)
    def _(i):
        @pl.when(i == 1)
        def _():
            relay(attn, 1)
            share(attn, 1)

            relay(attn, 2)
            share(attn, 2)

            @pl.when(is_end)
            def _():
                start_far()

            relay(attn, 3)
            pass_diagonal(attn, 1)
            share(attn, 3)
            pass_diagonal(attn, 2)

            @pl.when(is_inner)
            def _():
                start_far()

            for k in (1, 2, 3):
                bias_copy(k, True).wait_recv()

        @pl.when(i > 0)
        def _():
            finish_slab(attn, i)

        @pl.when(i == 2)
        def _():
            pass_diagonal(attn, 3)

        @pl.when(((i == 2) & is_inner) | ((i == 3) & is_end))
        def _():
            share_far(mlp)

        s = slab_of(i)

        def half_done():
            @pl.when(i == 3)
            def _():
                swap_attn.start()

        attention_slab(
            s, h1, wq, wp, bias_q_of(s), rel_query, codes, attended, total, heads, half, half_done
        )


    swap_attn.wait()

    def middle_rows(rows):
        value = tokens[rows].astype(F32)
        valid = keep[rows]
        attn_out = total[rows] + xr[rows] + proj_bias
        mid = value + attn_out
        middle[rows] = mid
        xhat, _ = normalize(mid)
        h2[rows] = (xhat * gain_two + shift_two).astype(BF)
        early[1:2, :] += column_sum(valid * mid * mid)
        early[3:4, :] += column_sum(valid * attn_out * attn_out)

    over_rows(middle_rows)
    swap_h2.start()
    pair_h2.start()
    total[...] = jnp.zeros_like(total)
    back[...] = jnp.zeros_like(back)
    bias_e[...] = jnp.zeros_like(bias_e)
    bias_q[...] = jnp.zeros_like(bias_q)
    rel_acc[...] = jnp.zeros_like(rel_acc)
    swap_grad.wait()

    def weight_grads(p, j):
        for side in range(2):
            columns = slice(side * half, side * half + half)
            for buf, left, right in (
                (we, normed[p, :, columns], gpre[...]),
                (ws, act[...], grads[p, :, columns]),
            ):
                value = dot_tn(left, right).reshape(buf.shape[2:])
                value = value + jnp.where(p > 0, buf[2 + j, side].astype(F32), 0.0)
                buf[2 + j, side] = value.astype(BF)

    def own_rows(rows):
        xr[rows] = xr[rows] + total[rows]
        xr2[rows] = xr2[rows] + back[rows]

    def other_rows(rows):
        return pl.ds(pl.multiple_of(rows.start + own, CHUNK), CHUNK)

    def back_low_rows(rows):
        h2[rows] = back[other_rows(rows)].astype(BF)

    def out_low_rows(rows):
        h2[other_rows(rows)] = total[other_rows(rows)].astype(BF)

    def back_sum_rows(rows):
        h2[rows] = (back[rows] + got_low[rows].astype(F32)).astype(BF)

    def out_sum_rows(rows):
        h2[other_rows(rows)] = (total[rows] + got_low[other_rows(rows)].astype(F32)).astype(BF)

    def between_passes():
        pair_h2.wait()
        swap_h2z.start()
        swap_mlp.wait()
        swap_gh2.wait()
        over_rows(own_rows)
        total[...] = jnp.zeros_like(total)
        back[...] = jnp.zeros_like(back)
        swap_gmz.wait()
        swap_h2z.wait()

    def start_pair_sums():
        over_rows(back_low_rows)
        swap_back_low.start()
        over_rows(out_low_rows)
        swap_out_low.start()

    def send_pair_sums():
        swap_back_low.wait()
        over_rows(back_sum_rows)
        send_back.start()
        swap_out_low.wait()
        over_rows(out_sum_rows)
        send_out.start()

    @pl.loop(0, 8)
    def _(t):
        p, j = t // 4, t // 2 % 2
        s = (1 - j) * z + j * remote_slab

        @pl.when(t == 1)
        def _():
            pass_diagonal(mlp, 1)
            swap_h2.wait()

        @pl.when(t == 2)
        def _():
            finish_slab(mlp, 1)
            pair_gm.wait_recv()
            swap_gmz.start()

        @pl.when(t == 3)
        def _():
            swap_mlp.start()
            swap_gh2.start()

        @pl.when(t == 4)
        def _():
            between_passes()

        @pl.when(t == 7)
        def _():
            start_pair_sums()

        mlp_rows(
            s, j, (t + j) % 2, normed.at[p], grads.at[p], we, ws, bias_e_of(s), act, gpre, total, back, bias_e, half
        )

        @pl.when(t == 7)
        def _():
            send_pair_sums()

        @pl.when(t % 2 == 1)
        def _():
            weight_grads(p, j)

            @pl.when(p == 1)
            def _():
                reduce_one(mlp, j)

    sent_far(mlp)
    reduce_two(mlp, 0)
    send_back.wait_recv()
    back_load = pltpu.make_async_copy(pair_back, gmz.at[rows_own], local.at[8])
    back_load.start()
    back_load.wait()

    pair_gm.wait_send()

    def middle_back_rows(rows):
        mid = middle[rows]
        grad_out = gm[rows].astype(F32)
        early[9:10, :] += column_sum(grad_out)
        grad = xr2[rows] + gmz[rows].astype(F32)
        xhat, inverse = normalize(mid)
        early[6:7, :] += column_sum(grad * xhat)
        early[7:8, :] += column_sum(grad)
        grad_mid = grad_out + norm_back(grad, gain_two, xhat, inverse)
        xr2[rows] = grad_mid
        low = grad_mid.astype(BF)
        gm[rows] = low
        early[8:9, :] += column_sum(low.astype(F32))

    over_rows(middle_back_rows)
    swap_ga.start()

    def result_rows(rows):
        valid = keep[rows]
        mlp_out = xr[rows] + gmz[other_rows(rows)].astype(F32) + shrink_bias
        result = middle[rows] + mlp_out
        h2[rows] = result.astype(BF)
        early[2:3, :] += column_sum(valid * result * result)
        early[4:5, :] += column_sum(valid * mlp_out * mlp_out)

    back[...] = jnp.zeros_like(back)
    for i in range(4):
        sent_slab(attn, i)
    reduce_two(mlp, 1)
    swap_ga.wait()

    out_load = pltpu.make_async_copy(pair_out, gmz.at[rows_other], local.at[8])
    result_store = pltpu.make_async_copy(h2.at[rows_own], block_out, local.at[8])

    def finish_result():
        send_back.wait_send()
        send_out.wait_recv()
        out_load.start()
        out_load.wait()
        over_rows(result_rows)
        result_store.start()

    stages = ((partner,), (along_z(1), along_z(2), along_z(3)), (along_x, along_y, across))
    early_sums = (((early, early_got),), 20)
    late_sums = (((late, late_got), (rel, rel_got)), 27)

    def small_copies(sums, stage):
        pairs, base = sums
        first = (0, 1, 4)[stage]
        for i, device in enumerate(stages[stage]):
            for j, (src, got) in enumerate(pairs):
                index = base + (first + i) * len(pairs) + j
                yield src, got, first + i, remote(src, got.at[first + i], csend, crecv, index, device)

    def small_start(sums, stage):
        for _, _, _, copy in small_copies(sums, stage):
            copy.start()

    def small_finish(sums, stage):
        copies = list(small_copies(sums, stage))
        for _, _, _, copy in copies:
            copy.wait()
        for src, got, place, _ in copies:
            src[...] += got[place]

    def on_side(act_on):
        for side in range(2):

            @pl.when(r == side)
            def _():
                act_on(side)

    def fill_early(side):
        for s in range(4):
            early[10 + s : 11 + s, side * half : (side + 1) * half] = bias_e[s]

    early_store = pltpu.make_async_copy(early, early_out, local.at[9])

    @pl.loop(0, 4)
    def _(n):
        s = slab_of(3 - n)
        g = slot(0, n)

        def half_done():
            @pl.when(n == 0)
            def _():
                reduce_three(mlp, 0)

            @pl.when(n == 2)
            def _():
                small_finish(early_sums, 0)
                small_start(early_sums, 1)
                reduce_four((2,))

            @pl.when(n == 3)
            def _():
                swap_gh1.start()
                small_finish(early_sums, 1)
                small_start(early_sums, 2)
                reduce_four((3,))

        attention_back_slab(
            s, h1, gm, wq, wp, bias_q_of(s), rel_query, rel_back, codes, act, back, bias_q, rel_acc, heads, half, half_done
        )

        @pl.when(n > 0)
        def _():
            reduce_two(attn, n - 1)

        for side in range(2):
            columns = slice(side * half, side * half + half)
            wq[g, side] = dot_tn(act[:, :qkv_width], h1[:, columns]).astype(BF).reshape(wq.shape[2:])
            wp[g, side] = dot_tn(attended[s], gm[:, columns]).astype(BF).reshape(wp.shape[2:])
        reduce_one(attn, n)

        @pl.when((n > 1) & is_end)
        def _():
            reduce_three(attn, n - 2)

        @pl.when((n == 3) & is_inner)
        def _():
            reduce_three(attn, 0)

        @pl.when(n == 0)
        def _():
            reduce_three(mlp, 1)

        @pl.when(n == 1)
        def _():
            finish_result()
            on_side(fill_early)
            small_start(early_sums, 0)

    swap_gh1.wait()

    def input_rows(rows):
        value = tokens[rows].astype(F32)
        grad = (back[rows] + total[other_rows(rows)]) * keep[rows]
        xhat, inverse = normalize(value)
        late[0:1, :] += column_sum(grad * xhat)
        late[1:2, :] += column_sum(grad)
        xr2[rows] = xr2[rows] + norm_back(grad, gain_one, xhat, inverse)

    over_rows(input_rows)
    input_store = pltpu.make_async_copy(xr2, input_grad, local.at[10])
    input_store.start()

    def fill_late(side):
        lanes = bias_q.shape[2]
        for s in range(4):
            late[2 + s : 3 + s, side * lanes : (side + 1) * lanes] = bias_q[s]

    on_side(fill_late)
    for part, at in ((0, 0), (1, COL_W)):
        rows = slice(at, at + 32)
        rel[part * 32 : part * 32 + 32] = rel_acc[rows] + rel_acc[LANES + at : LANES + at + 32]

    small_start(late_sums, 0)

    @pl.when(is_inner)
    def _():
        reduce_three(attn, 1)

    reduce_three(attn, 2)
    small_finish(late_sums, 0)
    small_start(late_sums, 1)
    reduce_two(attn, 3)
    reduce_five(mlp)
    reduce_three(attn, 3)
    reduce_four(attn)
    small_finish(late_sums, 1)
    small_start(late_sums, 2)
    small_finish(early_sums, 2)
    early_store.start()
    reduce_six(mlp)
    reduce_five(attn)
    small_finish(late_sums, 2)
    late_stores = [
        pltpu.make_async_copy(late, late_out, local.at[6]),
        pltpu.make_async_copy(rel, rel_out, local.at[7]),
    ]
    for copy in late_stores:
        copy.start()
    reduce_six(attn)

    swap_h1.wait_send()
    send_out.wait_send()
    for k in (1, 2, 3):
        bias_copy(k).wait_send()
    for a in range(4):
        for copy in swap_out(a) + keep_out(a):
            copy.wait()
        for kind in (1, 2, 3, 4):
            spread(a, kind).wait_send()
        for n in range(4 if a in attn else 2):
            for kind in range(4):
                reduce_copy(a, n, kind).wait_send()
            reduce_z(a, n, lambda copy: copy.wait_send())

    for copy in late_stores:
        copy.wait()
    early_store.wait()
    result_store.wait()
    input_store.wait()


def run_kernel(tokens, mask, out_grad, vectors, qkv_bias, expand_bias, rel_height, rel_width, sources):
    own, width = tokens.shape[1] * WROWS, tokens.shape[2]
    half = width // 2
    rows = [source.shape[-2] for source in sources]
    rows[0] = 3 * rows[0] // 2
    sds = jax.ShapeDtypeStruct
    any_spec = pl.BlockSpec(memory_space=pl.ANY)
    vmem_spec = pl.BlockSpec(memory_space=pltpu.VMEM)
    out_shape = [sds((own, width), BF), sds((own, width), F32)]
    out_shape += [sds(source.shape, BF) for source in sources]
    out_shape += [sds((16, width), F32), sds((8, width), F32), sds((64, LANES), F32)]
    first, second = zip(*[halves(n) for n in rows])
    out_shape += [sds((4, 2, n, half), BF) for n in first]
    out_shape += [sds((4, 2, n, half), BF) for n in second]
    out_shape += [sds((4, n, half), BF) for n in second]
    out_shape += [sds((4, n, half), BF) for n in first]
    out_shape += [sds((6, n, half), BF) for n in rows]
    out_shape += [sds((own, width), BF)] * 2
    both = 2 * own
    vmem, dma = pltpu.VMEM, pltpu.SemaphoreType.DMA
    qkv_width = 2 * rows[0]
    scratch = [vmem((count, 2, 2, n, half), BF) for count, n in zip((5, 5, 4, 4), rows)]
    scratch += [vmem((own, width), BF), vmem((own, 1), F32)]
    scratch += [vmem((both, width), BF)] + [vmem((2, both, width), BF)] * 2 + [vmem((both, width), BF)]
    scratch += [vmem((4, both, qkv_width // 3), BF)]
    scratch += [vmem((both, width), F32)] * 2
    scratch += [vmem((own, width), F32)] * 3
    scratch += [vmem((both, half), BF), vmem((both, half), BF)]
    scratch += [vmem((4, 8, width), F32), vmem((16, width), F32), vmem((7, 16, width), F32)]
    scratch += [vmem((8, width), F32), vmem((7, 8, width), F32)]
    scratch += [vmem((64, LANES), F32), vmem((7, 64, LANES), F32)]
    scratch += [vmem((4, 1, half), F32), vmem((4, 1, qkv_width), F32), vmem((2 * LANES, LANES), F32)]
    scratch += [vmem((2 * LANES, LANES), BF), vmem((3 * LANES, LANES), BF), vmem((2, 32, HEAD), F32)]
    scratch += [dma((4, 4, 6))] * 2 + [dma((4, 4, 5)), dma((4, 4, 6))] + [dma((4, 5))] * 2 + [dma((41,))] * 2
    scratch += [dma((4,))] * 2 + [dma((8,))] * 2 + [dma((11,)), dma((4,))]
    got = pl.pallas_call(
        kernel,
        out_shape=out_shape,
        in_specs=[any_spec, vmem_spec, any_spec] + [vmem_spec] * 11 + [any_spec] * 4,
        out_specs=[any_spec] * len(out_shape),
        scratch_shapes=scratch,
        compiler_params=pltpu.CompilerParams(
            collective_id=0, has_side_effects=True, vmem_limit_bytes=VMEM_LIMIT
        ),
        name="block_step",
    )(tokens, mask, out_grad, *vectors, qkv_bias, expand_bias, rel_height, rel_width, key_codes(), *sources)
    return got[:9]


def finish_kernel(early, late, rel, *refs):
    wide, (bias_q, bias_e, height, width_out, rms), rows_out = refs[:6], refs[6:11], refs[11:17]
    outs, held, full, load, store = refs[17:23], refs[23:29], refs[29:35], refs[35], refs[36]
    z = lax.axis_index("col")
    loads = [pltpu.make_async_copy(src, to, load.at[i]) for i, (src, to) in enumerate(zip(wide, held))]
    stores = [pltpu.make_async_copy(src, to, store.at[i]) for i, (src, to) in enumerate(zip(full, outs))]
    for i in (3, 2, 0, 1, 5, 4):
        loads[i].start()
    places = ((late, 0), (late, 1), (early, 6), (early, 7), (early, 8), (early, 9))
    for ref, (source, at) in zip(rows_out, places):
        ref[...] = source[at, :]
    features = early.shape[1]
    lane = lax.broadcasted_iota(jnp.int32, (1, LANES), 1)
    stats = jnp.zeros((1, LANES), F32)
    for i in range(rms.shape[0]):
        stats = jnp.where(lane == i, jnp.sum(early[i : i + 1, :], axis=1, keepdims=True), stats)
    rms[...] = jnp.sqrt(stats / (early[5:6, 0:1] * features))[0, : rms.shape[0]]
    half = features // 2
    part = bias_q.shape[1] // 2
    bias_e[...] = early[pl.ds(10 + z, 1), :].reshape(features)
    row = late[pl.ds(2 + z, 1), :]
    for side in range(2):
        for i in range(2):
            at = (3 * side + 2 * i) * part
            bias_q[i : i + 1, side * part : (side + 1) * part] = row[:, at : at + part]
    count = height.shape[0]
    turn = lax.broadcasted_iota(jnp.int32, (32, 32), 0) + lax.broadcasted_iota(jnp.int32, (32, 32), 1) == count - 1
    turned = jnp.dot(turn.astype(F32), rel[:32], precision=lax.Precision.HIGHEST, preferred_element_type=F32)
    height[...] = turned[:count, :HEAD]
    width_out[...] = rel[32 : 32 + count, :HEAD]
    for i in (3, 2, 0, 1):
        loads[i].wait()
        step = held[i].shape[0] // 5

        @pl.loop(0, 5)
        def _(m):
            at = pl.ds(pl.multiple_of(m * step, step), step)
            full[i][at] = held[i][at].astype(F32)

        stores[i].start()
    loads[5].wait()

    @pl.loop(0, SIDE)
    def _(i):
        for w in range(2):
            at = pl.multiple_of(w * WROWS + i * SIDE_PAD, SIDE_PAD)
            full[5][pl.ds(i * SIDE, SIDE), w, :] = held[5][pl.ds(at, SIDE_PAD)][:SIDE]

    stores[5].start()
    loads[4].wait()

    @pl.loop(0, SIDE)
    def _(i):
        places = [pl.multiple_of(w * WROWS + i * SIDE_PAD, SIDE_PAD) for w in range(2)]
        some = [held[4][pl.ds(at, SIDE_PAD)][:SIDE].astype(F32) for at in places]
        full[4][pl.ds(i * SIDE, SIDE)] = jnp.stack(some, axis=1).astype(BF)

    stores[4].start()
    for copy in stores:
        copy.wait()


def finish_outputs(got, part):
    early, late, rel = got[6:9]
    grads = [value.reshape(-1, value.shape[-1]) for value in got[2:6]]
    width = early.shape[1]
    sds = jax.ShapeDtypeStruct
    any_spec = pl.BlockSpec(memory_space=pl.ANY)
    vmem_spec = pl.BlockSpec(memory_space=pltpu.VMEM)
    windows = got[0].shape[0] // WROWS
    out_shape = [sds((2, 2 * part), F32), sds((width,), F32), sds((2 * SIDE - 1, HEAD), F32)]
    out_shape += [sds((2 * SIDE - 1, HEAD), F32), sds((5,), F32)] + [sds((width,), F32)] * 6
    held = grads + list(got[:2])
    final = [sds(value.shape, F32) for value in grads]
    final += [sds((SIDE * SIDE, windows, width), value.dtype) for value in got[:2]]
    out_shape += final
    return pl.pallas_call(
        finish_kernel,
        out_shape=out_shape,
        in_specs=[vmem_spec] * 3 + [any_spec] * 6,
        out_specs=[vmem_spec] * 11 + [any_spec] * 6,
        scratch_shapes=[pltpu.VMEM(value.shape, value.dtype) for value in held + final]
        + [pltpu.SemaphoreType.DMA((6,))] * 2,
        compiler_params=pltpu.CompilerParams(vmem_limit_bytes=VMEM_LIMIT),
        name="finish",
    )(early, late, rel, *held)


VMEM_LIMIT = 64 * 1024 * 1024 - 512 * 1024


def over_chips(
    tokens, valid_mask, out_grad, first_gain, first_shift, qkv_weight, qkv_bias, rel_height, rel_width,
    proj_weight, proj_bias, second_gain, second_shift, expand_weight, expand_bias, shrink_weight, shrink_bias,
):
    def turned(value):
        return value.transpose(1, 0, 2)

    rows, _, local_width = qkv_weight.shape
    part = local_width // 2
    hidden = expand_weight.shape[1] // 2
    qkv_src = qkv_weight.transpose(1, 2, 0).reshape(3, 2, part, rows)
    proj_src = proj_weight.reshape(2, 2, part // 2, proj_weight.shape[1])
    expand_src = expand_weight.reshape(2, rows // 2, 2 * hidden)
    shrink_src = shrink_weight.reshape(2, 2, hidden // 2, shrink_weight.shape[1])
    vectors = (first_gain, first_shift, second_gain, second_shift, proj_bias, shrink_bias)
    got = run_kernel(
        turned(tokens), valid_mask, turned(out_grad), vectors, qkv_bias, expand_bias, rel_height, rel_width,
        (qkv_src, proj_src, expand_src, shrink_src),
    )
    outs = finish_outputs(got, part)
    qkv_bias_sum, expand_bias_sum, height_sum, width_sum, rms = outs[:5]
    gain_one, shift_one, gain_two, shift_two, proj_bias_sum, shrink_bias_sum = outs[5:11]
    qkv_sum, proj_sum, expand_sum, shrink_sum, block_out, input_grad = outs[11:]
    return (
        turned(block_out),
        turned(input_grad),
        gain_one,
        shift_one,
        qkv_sum.reshape(3, local_width, rows).transpose(2, 0, 1),
        qkv_bias_sum,
        height_sum,
        width_sum,
        proj_sum.reshape(proj_weight.shape),
        proj_bias_sum,
        gain_two,
        shift_two,
        expand_sum.reshape(expand_weight.shape),
        expand_bias_sum,
        shrink_sum.reshape(shrink_weight.shape),
        shrink_bias_sum,
        rms,
    )


epsilon = 1e-06
highest = lax.Precision.HIGHEST


def layer_norm(values, norm_gain, norm_shift):
    center = values - jnp.mean(values, axis=-1, keepdims=True)
    spread = jnp.mean(center * center, axis=-1, keepdims=True)
    return center * lax.rsqrt(spread + epsilon) * norm_gain + norm_shift


def offset_table(span_size):
    positions = jnp.arange(span_size)
    offset = positions[:, None] - positions[None, :] + span_size - 1
    return (offset[:, :, None] == jnp.arange(2 * span_size - 1)[None, None, :]).astype(jnp.float32)


def attention_scores(
    query_rows, key_rows, rel_rows_table, rel_cols_table, onehot_table, span_size, scaling
):
    window_count, tokens_per, head_count, head_size = query_rows.shape
    rel_count = 2 * span_size - 1
    direct = (
        jnp.einsum("bthc,buhc->bhtu", query_rows, key_rows, preferred_element_type=jnp.float32)
        * scaling
    )
    query_float = query_rows.astype(jnp.float32)
    along_rows = jnp.einsum("bthc,jc->bhtj", query_float, rel_rows_table, precision=highest)
    along_cols = jnp.einsum("bthc,jc->bhtj", query_float, rel_cols_table, precision=highest)
    grid_rows = along_rows.reshape(window_count, head_count, span_size, span_size, rel_count)
    grid_cols = along_cols.reshape(window_count, head_count, span_size, span_size, rel_count)
    rel_rows = jnp.einsum("bhxyj,xkj->bhxyk", grid_rows, onehot_table, precision=highest)
    rel_cols = jnp.einsum("bhxyj,ywj->bhxyw", grid_cols, onehot_table, precision=highest)
    score_sum = direct.reshape(window_count, head_count, span_size, span_size, span_size, span_size)
    score_sum = score_sum + rel_rows[:, :, :, :, :, None] + rel_cols[:, :, :, :, None, :]
    return score_sum.reshape(window_count, head_count, tokens_per, tokens_per)


def relative_back(score_float, onehot_table, span_size):
    window_count, head_count, tokens_per, other_tokens = score_float.shape
    grid = score_float.reshape(window_count, head_count, span_size, span_size, span_size, span_size)
    rows_part = jnp.einsum("bhxykw,xkj->bhxyj", grid, onehot_table, precision=highest)
    cols_part = jnp.einsum("bhxykw,ywj->bhxyj", grid, onehot_table, precision=highest)
    return (
        rows_part.reshape(window_count, head_count, tokens_per, -1),
        cols_part.reshape(window_count, head_count, tokens_per, -1),
    )


def gather_weights(qkv_weight, proj_weight, expand_weight, shrink_weight):
    return (
        lax.all_gather(qkv_weight, "row", axis=0, tiled=True),
        lax.all_gather(proj_weight, "row", axis=1, tiled=True),
        lax.all_gather(expand_weight, "row", axis=0, tiled=True),
        lax.all_gather(shrink_weight, "row", axis=1, tiled=True),
    )


def gather_tokens(normed):
    return lax.all_gather(normed, "col", axis=0, tiled=True)


def gather_grads(grad_low):
    return lax.all_gather(grad_low, "col", axis=0, tiled=True)


def sum_branch(inputs_low, weight_full, own_windows):

    def term(first_row, row_count):
        return jnp.einsum(
            "btk,kd->btd", inputs_low, weight_full, preferred_element_type=jnp.float32
        )

    return lax.psum_scatter(
        term(jnp.int32(0), own_windows * lax.axis_size("col")),
        "col",
        scatter_dimension=0,
        tiled=True,
    )


def sum_input(grads_low, weight_full, own_windows):

    def term(first_row, row_count):
        return jnp.einsum("btk,dk->btd", grads_low, weight_full, preferred_element_type=jnp.float32)

    return lax.psum_scatter(
        term(jnp.int32(0), own_windows * lax.axis_size("col")),
        "col",
        scatter_dimension=0,
        tiled=True,
    )


def activate(values):
    return jax.nn.gelu(values, approximate=False)


def per_device(
    tokens,
    valid_mask,
    out_grad,
    first_gain,
    first_shift,
    qkv_weight,
    qkv_bias,
    rel_height,
    rel_width,
    proj_weight,
    proj_bias,
    second_gain,
    second_shift,
    expand_weight,
    expand_bias,
    shrink_weight,
    shrink_bias,
):
    span_size = (rel_height.shape[0] + 1) // 2
    head_size = rel_height.shape[1]
    local_width = qkv_weight.shape[2]
    head_count = local_width // head_size
    own_windows = tokens.shape[0]
    tokens_per = tokens.shape[1]
    model_width = tokens.shape[2]
    scaling = head_size ** (-0.5)
    onehot_table = offset_table(span_size)
    inputs = tokens.astype(jnp.float32)
    keep_mask = valid_mask.astype(jnp.float32)[:, :, None]

    def first_norm(values, norm_gain, norm_shift):
        return layer_norm(values, norm_gain, norm_shift) * keep_mask

    qkv_full, proj_full, expand_full, shrink_full = gather_weights(
        qkv_weight, proj_weight, expand_weight, shrink_weight
    )
    normed_first, first_back = jax.vjp(first_norm, inputs, first_gain, first_shift)
    first_all = gather_tokens(normed_first.astype(jnp.bfloat16))
    all_windows = first_all.shape[0]
    bias_rows = jnp.stack([qkv_bias[0], jnp.zeros_like(qkv_bias[0]), qkv_bias[1]])
    projected = (
        jnp.einsum("btd,dsk->btsk", first_all, qkv_full, preferred_element_type=jnp.float32)
        + bias_rows
    )
    projected = projected.astype(jnp.bfloat16)
    head_shape = (all_windows, tokens_per, head_count, head_size)
    query_low = projected[:, :, 0].reshape(head_shape)
    key_low = projected[:, :, 1].reshape(head_shape)
    value_low = projected[:, :, 2].reshape(head_shape)
    scores = attention_scores(
        query_low, key_low, rel_height, rel_width, onehot_table, span_size, scaling
    )
    top_score = jnp.max(scores, axis=-1, keepdims=True)
    log_total = top_score + jnp.log(jnp.sum(jnp.exp(scores - top_score), axis=-1, keepdims=True))
    probs_low = jnp.exp(scores - log_total).astype(jnp.bfloat16)
    attended = jnp.einsum(
        "bhtu,buhc->bthc", probs_low, value_low, preferred_element_type=jnp.float32
    )
    attended_low = attended.reshape(all_windows, tokens_per, local_width).astype(jnp.bfloat16)
    attn_out = sum_branch(attended_low, proj_full, own_windows) + proj_bias
    middle = inputs + attn_out
    normed_second, second_back = jax.vjp(layer_norm, middle, second_gain, second_shift)
    second_all = gather_tokens(normed_second.astype(jnp.bfloat16))
    hidden_pre = (
        jnp.einsum("btd,df->btf", second_all, expand_full, preferred_element_type=jnp.float32)
        + expand_bias
    )
    active_value, active_back = jax.vjp(activate, hidden_pre)
    hidden_low = active_value.astype(jnp.bfloat16)
    mlp_out = sum_branch(hidden_low, shrink_full, own_windows) + shrink_bias
    result = middle + mlp_out
    stat_terms = jnp.stack(
        [
            jnp.sum(keep_mask * inputs * inputs),
            jnp.sum(keep_mask * middle * middle),
            jnp.sum(keep_mask * result * result),
            jnp.sum(keep_mask * attn_out * attn_out),
            jnp.sum(keep_mask * mlp_out * mlp_out),
        ]
    )
    valid_count = jnp.sum(keep_mask)
    stat_total, count_total = lax.psum((stat_terms, valid_count), ("dp", "row", "col"))
    out_float = out_grad.astype(jnp.float32)
    qkv_full, proj_full, expand_full, shrink_full = gather_weights(
        qkv_weight, proj_weight, expand_weight, shrink_weight
    )
    mlp_grad_low = out_float.astype(jnp.bfloat16)
    shrink_bias_grad = jnp.sum(mlp_grad_low, axis=(0, 1), dtype=jnp.float32)
    mlp_grad_all = gather_grads(mlp_grad_low)
    shrink_grad_full = jnp.einsum(
        "btf,btd->fd", hidden_low, mlp_grad_all, preferred_element_type=jnp.float32
    )
    hidden_grad = jnp.einsum(
        "btd,fd->btf", mlp_grad_all, shrink_full, preferred_element_type=jnp.float32
    )
    pre_grad_low = active_back(hidden_grad)[0].astype(jnp.bfloat16)
    expand_bias_grad = jnp.sum(pre_grad_low, axis=(0, 1), dtype=jnp.float32)
    expand_grad_full = jnp.einsum(
        "btd,btf->df", second_all, pre_grad_low, preferred_element_type=jnp.float32
    )
    second_grad = sum_input(pre_grad_low, expand_full, own_windows)
    middle_part, second_gain_grad, second_shift_grad = second_back(second_grad)
    middle_grad = out_float + middle_part
    attn_grad_low = middle_grad.astype(jnp.bfloat16)
    proj_bias_grad = jnp.sum(attn_grad_low, axis=(0, 1), dtype=jnp.float32)
    attn_grad_all = gather_grads(attn_grad_low)
    proj_grad_full = jnp.einsum(
        "btk,btd->kd", attended_low, attn_grad_all, preferred_element_type=jnp.float32
    )
    attended_grad = jnp.einsum(
        "btd,kd->btk", attn_grad_all, proj_full, preferred_element_type=jnp.float32
    )
    attended_grad = attended_grad.astype(jnp.bfloat16).reshape(head_shape)
    scores_again = attention_scores(
        query_low, key_low, rel_height, rel_width, onehot_table, span_size, scaling
    )
    probs_float = jnp.exp(scores_again - log_total)
    probs_again = probs_float.astype(jnp.bfloat16)
    prob_grad = jnp.einsum(
        "bthc,buhc->bhtu", attended_grad, value_low, preferred_element_type=jnp.float32
    )
    value_grad = jnp.einsum(
        "bhtu,bthc->buhc", probs_again, attended_grad, preferred_element_type=jnp.float32
    )
    score_grad = probs_float * (
        prob_grad - jnp.sum(probs_float * prob_grad, axis=-1, keepdims=True)
    )
    score_low = score_grad.astype(jnp.bfloat16)
    rows_grad, cols_grad = relative_back(score_low.astype(jnp.float32), onehot_table, span_size)
    query_float = query_low.astype(jnp.float32)
    query_grad = (
        jnp.einsum("bhtu,buhc->bthc", score_low, key_low, preferred_element_type=jnp.float32)
        * scaling
    )
    query_grad = query_grad + jnp.einsum("bhtj,jc->bthc", rows_grad, rel_height, precision=highest)
    query_grad = query_grad + jnp.einsum("bhtj,jc->bthc", cols_grad, rel_width, precision=highest)
    key_grad = (
        jnp.einsum("bhtu,bthc->buhc", score_low, query_low, preferred_element_type=jnp.float32)
        * scaling
    )
    rel_height_grad = jnp.einsum("bhtj,bthc->jc", rows_grad, query_float, precision=highest)
    rel_width_grad = jnp.einsum("bhtj,bthc->jc", cols_grad, query_float, precision=highest)
    flat_shape = (all_windows, tokens_per, local_width)
    qkv_grad_low = jnp.stack(
        [
            query_grad.reshape(flat_shape),
            key_grad.reshape(flat_shape),
            value_grad.reshape(flat_shape),
        ],
        axis=2,
    ).astype(jnp.bfloat16)
    qkv_bias_grad = jnp.sum(qkv_grad_low[:, :, 0::2], axis=(0, 1), dtype=jnp.float32)
    qkv_grad_full = jnp.einsum(
        "btd,btsk->dsk", first_all, qkv_grad_low, preferred_element_type=jnp.float32
    )
    first_grad = sum_input(
        qkv_grad_low.reshape(all_windows, tokens_per, 3 * local_width),
        qkv_full.reshape(qkv_full.shape[0], 3 * local_width),
        own_windows,
    )
    input_part, first_gain_grad, first_shift_grad = first_back(first_grad)
    input_grad = middle_grad + input_part
    qkv_rows, proj_rows, expand_rows, shrink_rows = (
        lax.psum_scatter(qkv_grad_full, "row", scatter_dimension=0, tiled=True),
        lax.psum_scatter(proj_grad_full, "row", scatter_dimension=1, tiled=True),
        lax.psum_scatter(expand_grad_full, "row", scatter_dimension=0, tiled=True),
        lax.psum_scatter(shrink_grad_full, "row", scatter_dimension=1, tiled=True),
    )
    qkv_sum, proj_sum, expand_sum, shrink_sum = lax.psum(
        (qkv_rows, proj_rows, expand_rows, shrink_rows), "dp"
    )
    qkv_bias_sum, expand_bias_sum = lax.psum((qkv_bias_grad, expand_bias_grad), ("dp", "row"))
    (
        gain_one_sum,
        shift_one_sum,
        gain_two_sum,
        shift_two_sum,
        proj_bias_sum,
        shrink_bias_sum,
        height_sum,
        width_sum,
    ) = lax.psum(
        (
            first_gain_grad,
            first_shift_grad,
            second_gain_grad,
            second_shift_grad,
            proj_bias_grad,
            shrink_bias_grad,
            rel_height_grad,
            rel_width_grad,
        ),
        ("dp", "row", "col"),
    )
    rms = jnp.sqrt(stat_total / (count_total * model_width))
    return (
        result.astype(jnp.bfloat16),
        input_grad,
        gain_one_sum,
        shift_one_sum,
        qkv_sum,
        qkv_bias_sum,
        height_sum,
        width_sum,
        proj_sum,
        proj_bias_sum,
        gain_two_sum,
        shift_two_sum,
        expand_sum,
        expand_bias_sum,
        shrink_sum,
        shrink_bias_sum,
        rms,
    )


def choose(mesh):
    fits = tuple(mesh.shape[name] for name in ("dp", "row", "col")) == (4, 2, 4)
    return over_chips if fits else per_device


def solution(mesh):
    in_specs = (
        P(("dp", "row", "col"), None, None),
        P(("dp", "row", "col"), None),
        P(("dp", "row", "col"), None, None),
        P(),
        P(),
        P("row", None, "col"),
        P(None, "col"),
        P(),
        P(),
        P("col", "row"),
        P(),
        P(),
        P(),
        P("row", "col"),
        P("col"),
        P("col", "row"),
        P(),
    )
    out_specs = (
        P(("dp", "row", "col"), None, None),
        P(("dp", "row", "col"), None, None),
        P(),
        P(),
        P("row", None, "col"),
        P(None, "col"),
        P(),
        P(),
        P("col", "row"),
        P(),
        P(),
        P(),
        P("row", "col"),
        P("col"),
        P("col", "row"),
        P(),
        P(),
    )
    return jax.shard_map(
        choose(mesh), mesh=mesh, in_specs=in_specs, out_specs=out_specs, check_vma=False
    )
```

```python
import functools

import jax
import jax.numpy as jnp
import numpy as np
from jax import lax
from jax.experimental import pallas as pl
from jax.experimental.pallas import tpu as pltpu
from jax.sharding import PartitionSpec as P

BF = jnp.bfloat16
F32 = jnp.float32
LANES = 128
SIDE = 14
SIDE_PAD = 16
WROWS = SIDE * SIDE_PAD
HEAD = 80
AT_H = HEAD
AT_W = HEAD + SIDE
AT_MASK = HEAD + 2 * SIDE
COL_W = 64


def dot(a, b):
    return jnp.dot(a, b, preferred_element_type=F32)


def dot_nt(a, b):
    return lax.dot_general(a, b, (((1,), (1,)), ((), ())), preferred_element_type=F32)


def dot_tn(a, b):
    return lax.dot_general(a, b, (((0,), (0,)), ((), ())), preferred_element_type=F32)


def lane_ids():
    return lax.broadcasted_iota(jnp.int32, (WROWS, LANES), 1)


def row_ids():
    return lax.broadcasted_iota(jnp.int32, (WROWS, LANES), 0)


def key_codes():
    u = np.arange(WROWS)[:, None]
    lane = np.arange(LANES)[None, :]
    k, l = u // SIDE_PAD, u % SIDE_PAD
    height = lane - AT_H == k
    width = (lane - AT_W == l) & (l < SIDE)
    width_back = (AT_W + SIDE - 1 - lane == l) & (l < SIDE)
    plain = np.where(height | width, 1.0, 0.0)
    masked = np.where((lane == AT_MASK) & (l >= SIDE), -1e30, plain)
    back = np.where(height | width_back, 1.0, 0.0)
    return np.stack([masked, plain, back]).astype(BF)


def split_low(values):
    high = values.astype(BF)
    return high, (values - high.astype(F32)).astype(BF)


def relative_tables(rel_h, rel_w, rel_query, rel_back):
    count, rows = 2 * SIDE - 1, rel_h.shape[0]
    offset = lax.broadcasted_iota(jnp.int32, (rows, LANES), 0)
    lane = lax.broadcasted_iota(jnp.int32, (rows, LANES), 1)

    def places(first, step):
        return jnp.where((lane == first + step * offset) & (offset < count), 1.0, 0.0).astype(BF)

    heights, widths = places(count - 1, -1), places(COL_W + count - 1, -1)
    widths_back = places(COL_W, 1)
    tall, wide = rel_h[...], rel_w[...]
    rel_query[...] = jnp.zeros_like(rel_query)
    rel_back[...] = jnp.zeros_like(rel_back)
    for part, (a, b) in enumerate(zip(split_low(tall * HEAD**0.5), split_low(wide * HEAD**0.5))):
        at = part * LANES
        rel_query[at : at + HEAD] = (dot_tn(a, heights) + dot_tn(b, widths)).astype(BF)
    for part, (a, b) in enumerate(zip(split_low(tall), split_low(wide))):
        table = (dot_tn(heights, a) + dot_tn(widths_back, b)).astype(BF)
        for place in ((0, 1), (2,))[part]:
            rel_back[place * LANES : (place + 1) * LANES, :HEAD] = table


def query_codes(query, rel_query):
    full = dot(jnp.concatenate([query, query], axis=1), rel_query)
    tiles = full.reshape(SIDE, SIDE_PAD, LANES)
    heights = jnp.concatenate(
        [pltpu.roll(tiles[i], AT_H - (SIDE - 1 - i), 1) for i in range(SIDE)], axis=0
    )
    widths = pltpu.roll(
        tiles, AT_W - COL_W - (SIDE - 1), 2, stride=1, stride_axis=1
    ).reshape(WROWS, LANES)
    lane = lane_ids()
    codes = jnp.where(
        (lane >= AT_H) & (lane < AT_W),
        heights,
        jnp.where((lane >= AT_W) & (lane < AT_MASK), widths, 0.0),
    )
    high, rest = split_low(codes)
    first = query + high + jnp.where(lane == AT_MASK, 1.0, 0.0).astype(BF)
    return jnp.concatenate([first, rest], axis=1)


def softmax_rows(query, key, rel_query, codes_ref):
    left = query_codes(query, rel_query)
    right = jnp.concatenate([key + codes_ref[0], codes_ref[1]], axis=1)
    scores = dot_nt(left, right)
    top = jnp.max(scores, axis=1, keepdims=True)
    weights = jnp.exp((scores - top) * (HEAD**-0.5))
    return weights / jnp.sum(weights, axis=1, keepdims=True)


def attend(query, key, value, rel_query, codes_ref):
    probs = softmax_rows(query, key, rel_query, codes_ref)
    return dot(probs.astype(BF), value)


def attend_back(query, key, value, grad, rel_query, rel_back, codes_ref):
    probs = softmax_rows(query, key, rel_query, codes_ref)
    prob_grad = dot_nt(grad, value)
    inner = jnp.sum(probs * prob_grad, axis=1, keepdims=True)
    score_low = (probs * (prob_grad - inner)).astype(BF)
    value_grad = dot_tn(probs.astype(BF), grad)
    key_grad = dot_tn(score_low, query) * (HEAD**-0.5)
    mixed = dot(score_low, key + codes_ref[2])
    tiles = mixed.reshape(SIDE, SIDE_PAD, LANES)
    heights = jnp.concatenate(
        [pltpu.roll(tiles[i], (SIDE - 1 - i - AT_H) % LANES, 1) for i in range(SIDE)], axis=0
    )
    widths = pltpu.roll(
        tiles, (COL_W - AT_W) % LANES, 2, stride=1, stride_axis=1
    ).reshape(WROWS, LANES)
    lane, row = lane_ids(), row_ids()
    first_h = SIDE - 1 - row // SIDE_PAD
    first_w = COL_W + row % SIDE_PAD
    offsets = jnp.where(
        (lane >= first_h) & (lane < first_h + SIDE),
        heights,
        jnp.where((lane >= first_w) & (lane < first_w + SIDE), widths, 0.0),
    )
    high, rest = split_low(offsets)
    query_grad = jnp.where(lane < HEAD, mixed, 0.0) * (HEAD**-0.5) + dot(
        jnp.concatenate([high, rest, high], axis=1), rel_back
    )
    rel_grad = dot_tn(jnp.concatenate([high, rest], axis=1), query)
    return query_grad, key_grad, value_grad, rel_grad


def pad_head(piece):
    return jnp.concatenate([piece, jnp.zeros((piece.shape[0], LANES - HEAD), piece.dtype)], axis=1)


def qkv_low(s, rows, h1, wq, bias, half):
    return (dot_nt(h1[rows, :half], block(wq, s, 0)) + dot_nt(h1[rows, half:], block(wq, s, 1)) + bias).astype(BF)


def head_of(low, part, heads, hh):
    at = (part * heads + hh) * HEAD
    return pad_head(low[:, at : at + HEAD])


def attention_slab(s, h1, wq, wp, bias, rel_query, codes, attended, total, heads, half, half_done):
    count = h1.shape[0] // WROWS

    @pl.loop(0, count)
    def _(m):
        rows = pl.ds(pl.multiple_of((m + count // 2) % count * WROWS, WROWS), WROWS)
        low = qkv_low(s, rows, h1, wq, bias, half)
        outs = []
        for hh in range(heads):
            query, key, value = (head_of(low, part, heads, hh) for part in range(3))
            outs.append(attend(query, key, value, rel_query[...], codes)[:, :HEAD])
        out_low = jnp.concatenate(outs, axis=1).astype(BF)
        attended[s, rows] = out_low
        total[rows, :half] += dot(out_low, block(wp, s, 0))
        total[rows, half:] += dot(out_low, block(wp, s, 1))

        @pl.when(m == count // 2 - 1)
        def _():
            half_done()


SQRT_HALF = 0.5**0.5
PDF_SCALE = 0.3989422804014327


def both_blocks(ref, slab):
    value = ref[slab]
    return value.reshape(4 * value.shape[2], value.shape[3])


def mlp_rows(s, place, m, h2, gm, we, ws, bias, act, gpre, total, back, bias_grad, half):
    count = h2.shape[0] // 2

    @pl.loop(0, 1)
    def _(step):
        rows = pl.ds(pl.multiple_of((m + step) * count, count), count)
        pre = dot(h2[rows, :], both_blocks(we, place)) + bias
        cdf = 0.5 + 0.5 * lax.erf(pre * SQRT_HALF)
        slope = cdf + pre * (PDF_SCALE * jnp.exp(-0.5 * pre * pre))
        act_low = (pre * cdf).astype(BF)
        act[rows, :] = act_low
        hidden = dot_nt(gm[rows, :half], block(ws, place, 0)) + dot_nt(gm[rows, half:], block(ws, place, 1))
        gpre_low = (hidden * slope).astype(BF)
        gpre[rows, :] = gpre_low
        bias_grad[s] += jnp.sum(gpre_low.astype(F32), axis=0, keepdims=True)
        total[rows, :half] += dot(act_low, block(ws, place, 0))
        total[rows, half:] += dot(act_low, block(ws, place, 1))
        back[rows, :] += dot_nt(gpre_low, both_blocks(we, place))


def attention_back_slab(
    s, h1, ga, wq, wp, bias, rel_query, rel_back, codes, gqkv, back, bias_grad, rel_grad, heads, half, half_done
):
    count = h1.shape[0] // WROWS

    @pl.loop(0, count)
    def _(m):
        rows = pl.ds(pl.multiple_of((m + count // 2) % count * WROWS, WROWS), WROWS)
        low = qkv_low(s, rows, h1, wq, bias, half)
        grad = (dot_nt(ga[rows, :half], block(wp, s, 0)) + dot_nt(ga[rows, half:], block(wp, s, 1))).astype(BF)
        parts = [[], [], []]
        for hh in range(heads):
            query, key, value = (head_of(low, part, heads, hh) for part in range(3))
            got = attend_back(
                query, key, value, head_of(grad, 0, heads, hh), rel_query[...], rel_back[...], codes
            )
            for part in range(3):
                parts[part].append(got[part][:, :HEAD])
            rel_grad[...] += got[3]
        grad_low = jnp.concatenate(parts[0] + parts[1] + parts[2], axis=1).astype(BF)
        gqkv[rows, : grad_low.shape[1]] = grad_low
        bias_grad[s] += jnp.sum(grad_low.astype(F32), axis=0, keepdims=True)
        back[rows, :half] += dot(grad_low, block(wq, s, 0))
        back[rows, half:] += dot(grad_low, block(wq, s, 1))

        @pl.when(m == count // 2 - 1)
        def _():
            half_done()


MESH_ID = pl.DeviceIdType.MESH
ARRAYS = ("qkv", "proj", "expand", "shrink")
CHUNK = 64
EPS = 1e-06
SPARE = 4


def halves(rows):
    first = (rows // 2 + 15) // 16 * 16
    return first, rows - first


def flip(index, k):
    return ((index // 2 + k // 2) % 2) * 2 + (index % 2 + k % 2) % 2


def block(ref, slab, half):
    value = ref[slab, half]
    return value.reshape(value.shape[0] * value.shape[1], value.shape[2])


def add_low(target, index, extra):
    target[index] = (target[index].astype(F32) + extra.astype(F32)).astype(BF)


def kernel(
    tokens_in, mask_in, out_grad_in, gain_one_in, shift_one_in, gain_two_in, shift_two_in, proj_bias_in, shrink_bias_in,
    qkv_bias_in, expand_bias_in, rel_h_in, rel_w_in, codes, qkv_src, proj_src, expand_src, shrink_src,
    block_out, input_grad, qkv_out, proj_out, expand_out, shrink_out, early_out, late_out, rel_out,
    rxq, rxp, rxe, rxs, ryq, ryp, rye, rys, rx2q, rx2p, rx2e, rx2s, ry2q, ry2p, ry2e, ry2s, rzq, rzp, rze, rzs, pair_back, pair_out,
    wq, wp, we, ws, tokens, keep, h1, grads, normed, got_low, attended, total, back, xr, xr2, middle, act, gpre,
    bias_all, early, early_got, late, late_got, rel, rel_got, bias_e, bias_q, rel_acc, rel_query, rel_back, rel_pad,
    gsend, grecv, rsend, rrecv, fsend, frecv, csend, crecv, zsend, zrecv, qsend, qrecv, local, qlocal,
):
    d, r, z = lax.axis_index("dp"), lax.axis_index("row"), lax.axis_index("col")
    h, b = d // 2, d % 2
    own = tokens.shape[0]
    width = tokens.shape[1]
    half = width // 2
    heads = 2
    bufs = (wq, wp, we, ws)
    outs = (qkv_out, proj_out, expand_out, shrink_out)
    rx, ry = (rxq, rxp, rxe, rxs), (ryq, ryp, rye, rys)
    rx2, ry2 = (rx2q, rx2p, rx2e, rx2s), (ry2q, ry2p, ry2e, ry2s)
    rz = (rzq, rzp, rze, rzs)
    parts = [halves(buf.shape[3]) for buf in bufs]
    attn, mlp = (0, 1), (2, 3)
    qkv_width = 3 * attended.shape[2]

    along_x = (h * 2 + 1 - b, r, z)
    along_y = ((1 - h) * 2 + b, r, z)
    across = ((1 - h) * 2 + 1 - b, r, z)
    partner = (d, 1 - r, z)
    pair, remote_slab = (d, r, flip(z, 1)), flip(z, 2)
    gm, gmz, h2, h2z = grads.at[0], grads.at[1], normed.at[0], normed.at[1]

    def along_z(k):
        return (d, r, flip(z, k))

    def remote(src, dst, sems, recvs, index, device, got=None):
        return pltpu.make_async_remote_copy(
            src_ref=src,
            dst_ref=dst,
            send_sem=sems.at[index],
            recv_sem=recvs.at[index if got is None else got],
            device_id=device,
            device_id_type=MESH_ID,
        )

    up = z // 2
    is_end = (z + 1) // 2 % 2 == 0
    is_inner = (z + 1) // 2 % 2 == 1

    def slab_of(i):
        far = i // 2
        return (1 - far) * flip(z, i) + far * ((1 - up) * i + up * (3 - i))

    def first_part(a):
        return pl.ds(0, parts[a][0])

    def second_part(a):
        return pl.ds(parts[a][0], parts[a][1])

    def gather_z(a, s, step):
        at = bufs[a].at[s, h, b]
        return remote(at, at, gsend, grecv, (a, s, 0 if step < 0 else 5), (d, r, z + step), (a, s, 0))

    def gather_far(a):
        return remote(bufs[a].at[0, h, b], bufs[a].at[1, h, b], gsend, grecv, (a, 0, 0), (d, r, remote_slab))

    def ring(a, slab, sends, recvs, index, kind, arriving):
        buf = bufs[a]
        if kind == 1:
            at, device = (buf.at[slab, h, 1 - b] if arriving else buf.at[slab, h, b]), along_x
        elif kind == 2:
            at, device = (buf.at[slab, 1 - h, b] if arriving else buf.at[slab, h, b]), along_y
        elif kind == 3:
            at = buf.at[slab, 1 - h if arriving else h, 1 - b, first_part(a)]
            device = along_y
        else:
            at = buf.at[slab, 1 - h, 1 - b if arriving else b, second_part(a)]
            device = along_x
        return remote(at, at, sends, recvs, index, device)

    def gather(a, s, kind, arriving=False):
        return ring(a, s, gsend, grecv, (a, s, kind), kind, arriving)

    def spread(a, kind, arriving=False):
        return ring(a, final_slot(a), fsend, frecv, (a, kind), kind, arriving)

    def sends_along_z(group, s, act_on):
        for a in group:

            @pl.when((s >= z) & (z > 0))
            def _():
                act_on(gather_z(a, s, -1))

            @pl.when((s <= z) & (z < 3))
            def _():
                act_on(gather_z(a, s, 1))

    def start_z(group):
        sends_along_z(group, z, lambda copy: copy.start())

    def relay(group, i):
        s = slab_of(i)
        for a in group:
            gather_z(a, s, 1).wait_recv()
            sends_along_z((a,), s, lambda copy: copy.start())

    def place_of(a, i):
        return slab_of(i) if a in attn else 1

    def share(group, i):
        for a in group:
            gather(a, place_of(a, i), 1).start()
            gather(a, place_of(a, i), 2).start()

    def share_far(group):
        for a in group:
            gather_far(a).wait_recv()
            share((a,), 1)

    def pass_diagonal(group, i):
        for a in group:
            s = place_of(a, i)
            gather(a, s, 1, True).wait_recv()
            gather(a, s, 3).start()
            gather(a, s, 2, True).wait_recv()
            gather(a, s, 4).start()

    def finish_slab(group, i):
        for a in group:
            s = place_of(a, i)
            gather(a, s, 3, True).wait_recv()
            gather(a, s, 4, True).wait_recv()

    def sent_slab(group, i):
        s = slab_of(i)
        sends_along_z(group, s, lambda copy: copy.wait_send())
        for a in group:

            @pl.when(i > 0)
            def _():
                for kind in (1, 2, 3, 4):
                    gather(a, s, kind).wait_send()

    def sent_far(group):
        for a in group:
            gather_far(a).wait_send()
            for kind in (1, 2, 3, 4):
                gather(a, 1, kind).wait_send()

    def step_slab(n):
        return slab_of(3 - n)

    def final_slot(a):
        return z if a in attn else 0

    def slot(a, n):
        if a in mlp:
            return 2 + n
        first = (4 - n) // 4
        return first * SPARE + (1 - first) * step_slab(n - 1 + first)

    def reduce_copy(a, n, kind):
        buf, g = bufs[a], slot(a, n)
        got = None
        if kind == 0:
            src, dst, device = buf.at[g, :, 1 - b, first_part(a)], rx[a].at[n], along_x
        elif kind == 1:
            src, dst, device = buf.at[g, 1 - h, :, second_part(a)], ry[a].at[n], along_y
        elif kind == 2:
            src, dst, device = buf.at[g, 1 - h, b, first_part(a)], ry2[a].at[n], along_y
        elif kind == 3:
            src, dst, device = buf.at[g, h, 1 - b, second_part(a)], rx2[a].at[n], along_x
        elif kind == 4 and a in mlp:
            src, dst, device = buf.at[g, h, b], rz[a].at[0], (d, r, remote_slab)
            got = (a, 0, 4)
        elif kind == 4:
            src, dst, device = buf.at[g, h, b], rz[a].at[z], (d, r, step_slab(n))
            got = (a, z, 4)
        else:
            src, dst, device = buf.at[g, h, b], rz[a].at[5 - n], (d, r, slab_of(1))
            got = (a, 3 - n, 5)
        return remote(src, dst, rsend, rrecv, (a, n, min(kind, 4)), device, got)

    def reduce_z(a, n, act_on):
        if a in mlp:

            @pl.when(n == 1)
            def _():
                act_on(reduce_copy(a, n, 4))

        else:

            @pl.when((n < 3) & (is_inner | (n == 2)))
            def _():
                act_on(reduce_copy(a, n, 4))

            @pl.when(is_end & (n < 2))
            def _():
                act_on(reduce_copy(a, n, 5))

    def reduce_one(group, n):
        for a in group:
            reduce_copy(a, n, 0).start()
            reduce_copy(a, n, 1).start()

    def with_room(body):
        def run(group, n):
            shape = (2 * len(group), 2, halves(max(bufs[a].shape[3] for a in group))[0], half)
            pl.run_scoped(
                lambda room: body(group, n, lambda a, place: room.at[2 * group.index(a) + place]),
                pltpu.VMEM(shape, BF),
            )

        return run

    def reduce_two_body(group, n, scratch):
        loads = []
        for a in group:
            reduce_copy(a, n, 0).wait_recv()
            reduce_copy(a, n, 1).wait_recv()
            for place, got in enumerate((rx[a], ry[a])):
                to = scratch(a, place).at[:, pl.ds(0, parts[a][place])]
                loads.append(pltpu.make_async_copy(got.at[n], to, local.at[a * 2 + place]))
                loads[-1].start()
        for i, a in enumerate(group):
            g = slot(a, n)
            first, second = parts[a]
            loads[2 * i].wait()
            for side in range(2):
                add_low(bufs[a], (g, side, b, first_part(a)), scratch(a, 0)[side, :first])
            reduce_copy(a, n, 2).start()
            loads[2 * i + 1].wait()
            for side in range(2):
                add_low(bufs[a], (g, h, side, second_part(a)), scratch(a, 1)[side, :second])
            reduce_copy(a, n, 3).start()

    def reduce_three_body(group, n, scratch):
        loads = []
        for a in group:
            reduce_copy(a, n, 2).wait_recv()
            reduce_copy(a, n, 3).wait_recv()
            for place, got in enumerate((ry2[a], rx2[a])):
                to = scratch(a, place).at[0, pl.ds(0, parts[a][place])]
                loads.append(pltpu.make_async_copy(got.at[n], to, local.at[a * 2 + place]))
                loads[-1].start()
        for i, a in enumerate(group):
            g = slot(a, n)
            first, second = parts[a]
            loads[2 * i].wait()
            add_low(bufs[a], (g, h, b, first_part(a)), scratch(a, 0)[0, :first])
            loads[2 * i + 1].wait()
            add_low(bufs[a], (g, h, b, second_part(a)), scratch(a, 1)[0, :second])

            @pl.when(is_inner & (n < 2) & (a in attn))
            def _():
                at = rz[a].at[5 - n]
                remote(at, at, rsend, rrecv, (a, n, 4), (d, r, slab_of(1)), (a, 3 - n, 5)).wait_recv()
                pieces = ((0, first, first_part(a)), (1, second, second_part(a)))
                copies = [
                    pltpu.make_async_copy(at.at[part], scratch(a, 0).at[side, pl.ds(0, count)], local.at[a * 2 + side])
                    for side, count, part in pieces
                ]
                for copy in copies:
                    copy.start()
                for copy, (side, count, part) in zip(copies, pieces):
                    copy.wait()
                    add_low(bufs[a], (g, h, b, part), scratch(a, 0)[side, :count])

            reduce_z(a, n, lambda copy: copy.start())

    def reduce_two(group, n):
        with_room(reduce_two_body)(group, n)

    def reduce_three(group, n):
        with_room(reduce_three_body)(group, n)

    def reduce_four(group):
        for a in group:
            rows = bufs[a].shape[3]
            loads = []
            others = ((remote_slab, 0),) if a in mlp else [(slab_of(k), slab_of(k)) for k in (1, 2)]
            for k, (other, place) in enumerate(others, 1):
                at = rz[a].at[place]
                remote(at, at, rsend, rrecv, (a, k, 4), (d, r, other), (a, place, 4)).wait_recv()
                loads.append(pltpu.make_async_copy(at, gpre.at[pl.ds((k - 1) * rows, rows)], local.at[k]))
                loads[-1].start()
            for load in loads:
                load.wait()
            value = bufs[a][slot(a, 0 if a in mlp else 3), h, b].astype(F32)
            for k in range(len(others)):
                value = value + gpre[k * rows : (k + 1) * rows].astype(F32)
            bufs[a][final_slot(a), h, b] = value.astype(BF)
            spread(a, 1).start()
            spread(a, 2).start()

    def reduce_five(group):
        for a in group:
            spread(a, 1, True).wait_recv()
            spread(a, 3).start()
            spread(a, 2, True).wait_recv()
            spread(a, 4).start()

    def qkv_pieces(matrix, side, flat):
        rows = flat.shape[1]
        part = matrix.shape[2]
        cut = rows - part
        return (
            (matrix.at[0, side], flat.at[0, pl.ds(0, part)]),
            (matrix.at[1, side, pl.ds(0, cut)], flat.at[0, pl.ds(part, cut)]),
            (matrix.at[1, side, pl.ds(cut, part - cut)], flat.at[1, pl.ds(0, part - cut)]),
            (matrix.at[2, side], flat.at[1, pl.ds(part - cut, part)]),
        )

    def swap_out(a):
        mine = bufs[a].at[final_slot(a), 1 - r]
        if a == 0:
            pairs = qkv_pieces(outs[a], r, mine)
            return [remote(src, dst, qsend, qrecv, 4 + i, partner) for i, (dst, src) in enumerate(pairs)]
        to = outs[a].at[:, :, half_lanes(r)] if a == 2 else outs[a].at[r]
        return [remote(mine, to, fsend, frecv, (a, 0), partner)]

    def keep_out(a):
        mine = bufs[a].at[final_slot(a), r]
        if a == 0:
            pairs = qkv_pieces(outs[a], r, mine)
            return [pltpu.make_async_copy(src, dst, qlocal.at[i]) for i, (dst, src) in enumerate(pairs)]
        to = outs[a].at[:, :, half_lanes(r)] if a == 2 else outs[a].at[r]
        return [pltpu.make_async_copy(mine, to, local.at[a])]

    def reduce_six(group):
        for a in group:
            spread(a, 3, True).wait_recv()
            spread(a, 4, True).wait_recv()
            for copy in swap_out(a) + keep_out(a):
                copy.start()

    def half_lanes(side):
        return pl.ds(pl.multiple_of(side * half, half), half)

    def exchange(index, src, dst):
        return remote(src, dst, csend, crecv, index, partner)

    rows_own, rows_other = pl.ds(0, own), pl.ds(own, own)
    def source(a, side):
        if a == 2:
            return expand_src.at[:, :, half_lanes(side)]
        return (qkv_src, proj_src, expand_src, shrink_src)[a].at[side]

    def source_swap(a):
        to = bufs[a].at[z if a in attn else 0, r]
        if a == 0:
            pairs = qkv_pieces(qkv_src, 1 - r, to)
            return [remote(src, dst, qsend, qrecv, i, partner) for i, (src, dst) in enumerate(pairs)]
        return [exchange(a, source(a, 1 - r), to)]

    def source_keep(a):
        to = bufs[a].at[z if a in attn else 0, r]
        if a == 0:
            pairs = qkv_pieces(qkv_src, r, to)
            return [pltpu.make_async_copy(src, dst, qlocal.at[i]) for i, (src, dst) in enumerate(pairs)]
        return [pltpu.make_async_copy(source(a, r), to, local.at[a])]

    def start_source(group):
        for a in group:
            for copy in source_swap(a) + source_keep(a):
                copy.start()

    def finish_source(group):
        for a in group:
            for copy in source_swap(a) + source_keep(a):
                copy.wait()

    swap_grad = exchange(4, gm.at[rows_own], gm.at[rows_other])
    swap_h1 = exchange(5, h1.at[rows_own], h1.at[rows_other])
    swap_attn = exchange(6, total.at[rows_other], xr)
    swap_h2 = exchange(7, h2.at[rows_own], h2.at[rows_other])
    swap_mlp = exchange(8, total.at[rows_other], xr)
    swap_gh2 = exchange(9, back.at[rows_other], xr2)
    swap_ga = exchange(10, gm.at[rows_own], gm.at[rows_other])
    swap_gh1 = exchange(11, back.at[rows_other], total.at[rows_other])
    pair_gm = remote(gm.at[rows_own], gmz.at[rows_own], csend, crecv, 12, pair)
    swap_gmz = exchange(13, gmz.at[rows_own], gmz.at[rows_other])
    pair_h2 = remote(h2.at[rows_own], h2z.at[rows_own], csend, crecv, 14, pair)
    swap_h2z = exchange(15, h2z.at[rows_own], h2z.at[rows_other])
    swap_back_low = exchange(16, h2.at[rows_own], got_low.at[rows_own])
    swap_out_low = exchange(17, h2.at[rows_other], got_low.at[rows_other])
    send_back = remote(h2.at[rows_own], pair_back, csend, crecv, 18, pair)
    send_out = remote(h2.at[rows_other], pair_out, csend, crecv, 19, pair)

    def bias_copy(k, arriving=False):
        at = bias_all.at[flip(z, k) if arriving else z]
        return remote(at, at, zsend, zrecv, k, along_z(k))

    barrier = pltpu.get_barrier_semaphore()
    peers = [partner, along_x, along_y, across, along_z(1), along_z(2), along_z(3)]
    for peer in peers:
        pl.semaphore_signal(barrier, inc=1, device_id=peer, device_id_type=MESH_ID)
    pl.semaphore_wait(barrier, len(peers))

    start_source(attn)
    bias_all[z] = jnp.zeros(bias_all.shape[1:], F32)
    part = qkv_bias_in.shape[1] // 2
    for side in range(2):

        @pl.when(r == side)
        def _():
            bias_all[z, 0:1, :half] = expand_bias_in[side * half : (side + 1) * half].reshape(1, half)
            for i in range(2):
                at = half + 2 * i * part
                bias_all[z, 0:1, at : at + part] = qkv_bias_in[i : i + 1, side * part : (side + 1) * part]

    finish_source(attn)
    start_z(attn)
    for k in (1, 2, 3):
        bias_copy(k).start()
    start_source(mlp)

    def as_row(ref):
        return ref[...].reshape(1, width)

    gain_one, shift_one, gain_two, shift_two, proj_bias, shrink_bias = (
        as_row(ref) for ref in (gain_one_in, shift_one_in, gain_two_in, shift_two_in, proj_bias_in, shrink_bias_in)
    )

    def over_rows(body):
        @pl.loop(0, own // CHUNK)
        def _(m):
            body(pl.ds(pl.multiple_of(m * CHUNK, CHUNK), CHUNK))

    def column_sum(value):
        return jnp.sum(value, axis=0, keepdims=True)

    def normalize(value):
        center = value - jnp.mean(value, axis=1, keepdims=True)
        inverse = lax.rsqrt(jnp.mean(center * center, axis=1, keepdims=True) + EPS)
        return center * inverse, inverse

    def norm_back(grad, gain, xhat, inverse):
        scaled = grad * gain
        mean = jnp.mean(scaled, axis=1, keepdims=True)
        along = jnp.mean(scaled * xhat, axis=1, keepdims=True)
        return (scaled - mean - xhat * along) * inverse

    early[...] = jnp.zeros_like(early)
    late[...] = jnp.zeros_like(late)

    def spread_rows(source, target):
        def move(stage):
            load = pltpu.make_async_copy(source, stage, local.at[8])
            load.start()
            load.wait()

            @pl.loop(0, SIDE)
            def _(i):
                both = stage[pl.ds(i * SIDE, SIDE)].astype(F32)
                for w in range(both.shape[1]):
                    some = jnp.concatenate([both[:, w], jnp.zeros((SIDE_PAD - SIDE, width), F32)], axis=0)
                    at = pl.multiple_of(w * WROWS + i * SIDE_PAD, SIDE_PAD)
                    target[pl.ds(at, SIDE_PAD)] = some.astype(BF)

        pl.run_scoped(move, pltpu.VMEM(source.shape, BF))

    spread_rows(tokens_in, tokens)
    count = mask_in.shape[0]
    mask = jnp.concatenate([mask_in[...].astype(F32), jnp.zeros((count, 2 * LANES - SIDE * SIDE), F32)], axis=1)
    mask = jnp.concatenate([mask, jnp.zeros((8 - count, 2 * LANES), F32)], axis=0).T
    keep[...] = jnp.zeros_like(keep)
    for i in range(SIDE):
        for w in range(count):
            at = w * WROWS + i * SIDE_PAD
            keep[at : at + SIDE] = mask[i * SIDE : (i + 1) * SIDE, w : w + 1]

    def first_rows(rows):
        value = tokens[rows].astype(F32)
        valid = keep[rows]
        xhat, _ = normalize(value)
        h1[rows] = ((xhat * gain_one + shift_one) * valid).astype(BF)
        early[0:1, :] += column_sum(valid * value * value)
        early[5:6, :] += jnp.broadcast_to(column_sum(valid), (1, width))

    over_rows(first_rows)
    swap_h1.start()
    spread_rows(out_grad_in, gm)
    swap_grad.start()
    rel_pad[...] = jnp.zeros_like(rel_pad)
    rel_pad[0, : rel_h_in.shape[0]] = rel_h_in[...]
    rel_pad[1, : rel_w_in.shape[0]] = rel_w_in[...]
    relative_tables(rel_pad.at[0], rel_pad.at[1], rel_query, rel_back)
    total[...] = jnp.zeros_like(total)
    swap_h1.wait_recv()

    def bias_q_of(s):
        return bias_all[s, 0:1, half : half + qkv_width]

    def bias_e_of(s):
        return bias_all[s, 0:1, :half]

    finish_source(mlp)

    def start_far():
        for a in mlp:
            gather_far(a).start()
        pair_gm.start()

    @pl.loop(0, 4)
    def _(i):
        @pl.when(i == 1)
        def _():
            @pl.when(is_end)
            def _():
                relay(attn, 2)
                share(attn, 2)
                start_far()

            relay(attn, 3)
            pass_diagonal(attn, 1)
            share(attn, 3)
            pass_diagonal(attn, 2)

            @pl.when(is_inner)
            def _():
                start_far()

            for k in (1, 2, 3):
                bias_copy(k, True).wait_recv()

        @pl.when(i > 0)
        def _():
            finish_slab(attn, i)

        @pl.when(i == 2)
        def _():
            pass_diagonal(attn, 3)

        @pl.when(((i == 2) & is_inner) | ((i == 3) & is_end))
        def _():
            share_far(mlp)

        s = slab_of(i)

        def half_done():
            @pl.when(i == 0)
            def _():
                relay(attn, 1)
                share(attn, 1)

                @pl.when(is_inner)
                def _():
                    relay(attn, 2)
                    share(attn, 2)

            @pl.when(i == 3)
            def _():
                swap_attn.start()

        attention_slab(
            s, h1, wq, wp, bias_q_of(s), rel_query, codes, attended, total, heads, half, half_done
        )


    swap_attn.wait()

    def middle_rows(rows):
        value = tokens[rows].astype(F32)
        valid = keep[rows]
        attn_out = total[rows] + xr[rows] + proj_bias
        mid = value + attn_out
        middle[rows] = mid
        xhat, _ = normalize(mid)
        h2[rows] = (xhat * gain_two + shift_two).astype(BF)
        early[1:2, :] += column_sum(valid * mid * mid)
        early[3:4, :] += column_sum(valid * attn_out * attn_out)

    over_rows(middle_rows)
    swap_h2.start()
    pair_h2.start()
    total[...] = jnp.zeros_like(total)
    back[...] = jnp.zeros_like(back)
    bias_e[...] = jnp.zeros_like(bias_e)
    bias_q[...] = jnp.zeros_like(bias_q)
    rel_acc[...] = jnp.zeros_like(rel_acc)
    swap_grad.wait()

    def add_grad(buf, p, j, side, value):
        value = value.reshape(buf.shape[2:]) + jnp.where(p > 0, buf[2 + j, side].astype(F32), 0.0)
        buf[2 + j, side] = value.astype(BF)

    def weight_grads(p, j, done):
        sides = [(side, slice(side * half, side * half + half)) for side in range(2)]
        for side, columns in sides:
            add_grad(we, p, j, side, dot_tn(normed[p, :, columns], gpre[...]))
        done((2,))
        for side, columns in sides:
            add_grad(ws, p, j, side, dot_tn(act[...], grads[p, :, columns]))
        done((3,))

    def own_rows(rows):
        xr[rows] = xr[rows] + total[rows]
        xr2[rows] = xr2[rows] + back[rows]

    def other_rows(rows):
        return pl.ds(pl.multiple_of(rows.start + own, CHUNK), CHUNK)

    def back_low_rows(rows):
        h2[rows] = back[other_rows(rows)].astype(BF)

    def out_low_rows(rows):
        h2[other_rows(rows)] = total[other_rows(rows)].astype(BF)

    def back_sum_rows(rows):
        h2[rows] = (back[rows] + got_low[rows].astype(F32)).astype(BF)

    def out_sum_rows(rows):
        h2[other_rows(rows)] = (total[rows] + got_low[other_rows(rows)].astype(F32)).astype(BF)

    def between_passes():
        pair_h2.wait()
        swap_h2z.start()
        swap_mlp.wait()
        swap_gh2.wait()
        over_rows(own_rows)
        total[...] = jnp.zeros_like(total)
        back[...] = jnp.zeros_like(back)
        swap_gmz.wait()
        swap_h2z.wait()

    def start_pair_sums():
        over_rows(back_low_rows)
        swap_back_low.start()
        over_rows(out_low_rows)
        swap_out_low.start()

    def send_pair_sums():
        swap_back_low.wait()
        over_rows(back_sum_rows)
        send_back.start()
        swap_out_low.wait()
        over_rows(out_sum_rows)
        send_out.start()

    @pl.loop(0, 8)
    def _(t):
        p, j = t // 4, (t // 2 + t // 4) % 2
        s = (1 - j) * z + j * remote_slab

        @pl.when(t == 1)
        def _():
            pass_diagonal(mlp, 1)
            swap_h2.wait()

        @pl.when(t == 2)
        def _():
            finish_slab(mlp, 1)
            pair_gm.wait_recv()
            swap_gmz.start()

        @pl.when(t == 3)
        def _():
            swap_mlp.start()
            swap_gh2.start()

        @pl.when(t == 4)
        def _():
            between_passes()

        @pl.when(t == 7)
        def _():
            start_pair_sums()

        mlp_rows(
            s, j, (t + t // 2) % 2, normed.at[p], grads.at[p], we, ws, bias_e_of(s), act, gpre, total, back, bias_e, half
        )

        @pl.when(t == 7)
        def _():
            send_pair_sums()

        @pl.when(t % 2 == 1)
        def _():
            def done(group):
                @pl.when(t == 5)
                def _():
                    reduce_one(group, 1)

            weight_grads(p, j, done)

    sent_far(mlp)
    reduce_two(mlp, 1)
    reduce_one(mlp, 0)
    send_back.wait_recv()
    back_load = pltpu.make_async_copy(pair_back, gmz.at[rows_own], local.at[8])
    back_load.start()
    back_load.wait()

    pair_gm.wait_send()

    def middle_back_rows(rows):
        mid = middle[rows]
        grad_out = gm[rows].astype(F32)
        early[9:10, :] += column_sum(grad_out)
        grad = xr2[rows] + gmz[rows].astype(F32)
        xhat, inverse = normalize(mid)
        early[6:7, :] += column_sum(grad * xhat)
        early[7:8, :] += column_sum(grad)
        grad_mid = grad_out + norm_back(grad, gain_two, xhat, inverse)
        xr2[rows] = grad_mid
        low = grad_mid.astype(BF)
        gm[rows] = low
        early[8:9, :] += column_sum(low.astype(F32))

    over_rows(middle_back_rows)
    swap_ga.start()

    def result_rows(rows):
        valid = keep[rows]
        mlp_out = xr[rows] + gmz[other_rows(rows)].astype(F32) + shrink_bias
        result = middle[rows] + mlp_out
        h2[rows] = result.astype(BF)
        early[2:3, :] += column_sum(valid * result * result)
        early[4:5, :] += column_sum(valid * mlp_out * mlp_out)

    back[...] = jnp.zeros_like(back)
    for i in range(4):
        sent_slab(attn, i)
    reduce_three(mlp, 1)
    swap_ga.wait()

    out_load = pltpu.make_async_copy(pair_out, gmz.at[rows_other], local.at[8])
    result_store = pltpu.make_async_copy(h2.at[rows_own], block_out, local.at[8])

    def finish_result():
        send_back.wait_send()
        send_out.wait_recv()
        out_load.start()
        out_load.wait()
        over_rows(result_rows)
        result_store.start()

    stages = ((partner,), (along_z(1), along_z(2), along_z(3)), (along_x, along_y, across))
    early_sums = (((early, early_got),), 20)
    late_sums = (((late, late_got), (rel, rel_got)), 27)

    def small_copies(sums, stage):
        pairs, base = sums
        first = (0, 1, 4)[stage]
        for i, device in enumerate(stages[stage]):
            for j, (src, got) in enumerate(pairs):
                index = base + (first + i) * len(pairs) + j
                yield src, got, first + i, remote(src, got.at[first + i], csend, crecv, index, device)

    def small_start(sums, stage):
        for _, _, _, copy in small_copies(sums, stage):
            copy.start()

    def small_finish(sums, stage):
        copies = list(small_copies(sums, stage))
        for _, _, _, copy in copies:
            copy.wait()
        for src, got, place, _ in copies:
            src[...] += got[place]

    def on_side(act_on):
        for side in range(2):

            @pl.when(r == side)
            def _():
                act_on(side)

    def fill_early(side):
        for s in range(4):
            early[10 + s : 11 + s, side * half : (side + 1) * half] = bias_e[s]

    early_store = pltpu.make_async_copy(early, early_out, local.at[9])

    @pl.loop(0, 4)
    def _(n):
        s = slab_of(3 - n)
        g = slot(0, n)

        def half_done():
            @pl.when(n == 0)
            def _():
                reduce_two(mlp, 0)

            @pl.when(n == 1)
            def _():
                reduce_four((2,))

            @pl.when(n == 2)
            def _():
                small_finish(early_sums, 0)
                small_start(early_sums, 1)
                reduce_four((3,))

            @pl.when(n == 3)
            def _():
                swap_gh1.start()

        attention_back_slab(
            s, h1, gm, wq, wp, bias_q_of(s), rel_query, rel_back, codes, act, back, bias_q, rel_acc, heads, half, half_done
        )

        @pl.when(n > 0)
        def _():
            reduce_two(attn, n - 1)

        for side in range(2):
            columns = slice(side * half, side * half + half)
            wq[g, side] = dot_tn(act[:, :qkv_width], h1[:, columns]).astype(BF).reshape(wq.shape[2:])
            wp[g, side] = dot_tn(attended[s], gm[:, columns]).astype(BF).reshape(wp.shape[2:])
        reduce_one(attn, n)

        @pl.when((n > 1) & is_end)
        def _():
            reduce_three(attn, n - 2)

        @pl.when((n == 3) & is_inner)
        def _():
            reduce_three(attn, 0)

        @pl.when(n == 0)
        def _():
            reduce_three(mlp, 0)

        @pl.when(n == 1)
        def _():
            finish_result()
            on_side(fill_early)
            small_start(early_sums, 0)

    swap_gh1.wait()

    def input_rows(rows):
        value = tokens[rows].astype(F32)
        grad = (back[rows] + total[other_rows(rows)]) * keep[rows]
        xhat, inverse = normalize(value)
        late[0:1, :] += column_sum(grad * xhat)
        late[1:2, :] += column_sum(grad)
        xr2[rows] = xr2[rows] + norm_back(grad, gain_one, xhat, inverse)

    over_rows(input_rows)
    input_store = pltpu.make_async_copy(xr2, input_grad, local.at[10])
    input_store.start()

    def fill_late(side):
        lanes = bias_q.shape[2]
        for s in range(4):
            late[2 + s : 3 + s, side * lanes : (side + 1) * lanes] = bias_q[s]

    on_side(fill_late)
    for part, at in ((0, 0), (1, COL_W)):
        rows = slice(at, at + 32)
        rel[part * 32 : part * 32 + 32] = rel_acc[rows] + rel_acc[LANES + at : LANES + at + 32]

    small_start(late_sums, 0)

    @pl.when(is_inner)
    def _():
        reduce_three(attn, 1)

    small_finish(late_sums, 0)
    small_start(late_sums, 1)
    reduce_three(attn, 2)
    reduce_five((2,))
    reduce_two(attn, 3)
    reduce_five((3,))
    small_finish(early_sums, 1)
    small_start(early_sums, 2)
    reduce_three(attn, 3)
    reduce_four(attn)
    small_finish(late_sums, 1)
    small_start(late_sums, 2)
    reduce_six(mlp)
    small_finish(early_sums, 2)
    early_store.start()
    reduce_five(attn)
    small_finish(late_sums, 2)
    late_stores = [
        pltpu.make_async_copy(late, late_out, local.at[6]),
        pltpu.make_async_copy(rel, rel_out, local.at[7]),
    ]
    for copy in late_stores:
        copy.start()
    reduce_six(attn)

    swap_h1.wait_send()
    send_out.wait_send()
    for k in (1, 2, 3):
        bias_copy(k).wait_send()
    for a in range(4):
        for copy in swap_out(a) + keep_out(a):
            copy.wait()
        for kind in (1, 2, 3, 4):
            spread(a, kind).wait_send()
        for n in range(4 if a in attn else 2):
            for kind in range(4):
                reduce_copy(a, n, kind).wait_send()
            reduce_z(a, n, lambda copy: copy.wait_send())

    for copy in late_stores:
        copy.wait()
    early_store.wait()
    result_store.wait()
    input_store.wait()


def run_kernel(tokens, mask, out_grad, vectors, qkv_bias, expand_bias, rel_height, rel_width, sources):
    own, width = tokens.shape[1] * WROWS, tokens.shape[2]
    half = width // 2
    rows = [source.shape[-2] for source in sources]
    rows[0] = 3 * rows[0] // 2
    sds = jax.ShapeDtypeStruct
    any_spec = pl.BlockSpec(memory_space=pl.ANY)
    vmem_spec = pl.BlockSpec(memory_space=pltpu.VMEM)
    out_shape = [sds((own, width), BF), sds((own, width), F32)]
    out_shape += [sds(source.shape, BF) for source in sources]
    out_shape += [sds((16, width), F32), sds((8, width), F32), sds((64, LANES), F32)]
    first, second = zip(*[halves(n) for n in rows])
    out_shape += [sds((4, 2, n, half), BF) for n in first]
    out_shape += [sds((4, 2, n, half), BF) for n in second]
    out_shape += [sds((4, n, half), BF) for n in second]
    out_shape += [sds((4, n, half), BF) for n in first]
    out_shape += [sds((6, n, half), BF) for n in rows]
    out_shape += [sds((own, width), BF)] * 2
    both = 2 * own
    vmem, dma = pltpu.VMEM, pltpu.SemaphoreType.DMA
    qkv_width = 2 * rows[0]
    scratch = [vmem((count, 2, 2, n, half), BF) for count, n in zip((5, 5, 4, 4), rows)]
    scratch += [vmem((own, width), BF), vmem((own, 1), F32)]
    scratch += [vmem((both, width), BF)] + [vmem((2, both, width), BF)] * 2 + [vmem((both, width), BF)]
    scratch += [vmem((4, both, qkv_width // 3), BF)]
    scratch += [vmem((both, width), F32)] * 2
    scratch += [vmem((own, width), F32)] * 3
    scratch += [vmem((both, half), BF), vmem((both, half), BF)]
    scratch += [vmem((4, 8, width), F32), vmem((16, width), F32), vmem((7, 16, width), F32)]
    scratch += [vmem((8, width), F32), vmem((7, 8, width), F32)]
    scratch += [vmem((64, LANES), F32), vmem((7, 64, LANES), F32)]
    scratch += [vmem((4, 1, half), F32), vmem((4, 1, qkv_width), F32), vmem((2 * LANES, LANES), F32)]
    scratch += [vmem((2 * LANES, LANES), BF), vmem((3 * LANES, LANES), BF), vmem((2, 32, HEAD), F32)]
    scratch += [dma((4, 4, 6))] * 2 + [dma((4, 4, 5)), dma((4, 4, 6))] + [dma((4, 5))] * 2 + [dma((41,))] * 2
    scratch += [dma((4,))] * 2 + [dma((8,))] * 2 + [dma((11,)), dma((4,))]
    got = pl.pallas_call(
        kernel,
        out_shape=out_shape,
        in_specs=[any_spec, vmem_spec, any_spec] + [vmem_spec] * 11 + [any_spec] * 4,
        out_specs=[any_spec] * len(out_shape),
        scratch_shapes=scratch,
        compiler_params=pltpu.CompilerParams(
            collective_id=0, has_side_effects=True, vmem_limit_bytes=VMEM_LIMIT
        ),
        name="block_step",
    )(tokens, mask, out_grad, *vectors, qkv_bias, expand_bias, rel_height, rel_width, key_codes(), *sources)
    return got[:9]


def finish_kernel(early, late, rel, *refs):
    wide, (bias_q, bias_e, height, width_out, rms), rows_out = refs[:6], refs[6:11], refs[11:17]
    outs, held, full, load, store = refs[17:23], refs[23:29], refs[29:35], refs[35], refs[36]
    z = lax.axis_index("col")
    loads = [pltpu.make_async_copy(src, to, load.at[i]) for i, (src, to) in enumerate(zip(wide, held))]
    stores = [pltpu.make_async_copy(src, to, store.at[i]) for i, (src, to) in enumerate(zip(full, outs))]
    for i in (3, 2, 0, 1, 5, 4):
        loads[i].start()
    places = ((late, 0), (late, 1), (early, 6), (early, 7), (early, 8), (early, 9))
    for ref, (source, at) in zip(rows_out, places):
        ref[...] = source[at, :]
    features = early.shape[1]
    lane = lax.broadcasted_iota(jnp.int32, (1, LANES), 1)
    stats = jnp.zeros((1, LANES), F32)
    for i in range(rms.shape[0]):
        stats = jnp.where(lane == i, jnp.sum(early[i : i + 1, :], axis=1, keepdims=True), stats)
    rms[...] = jnp.sqrt(stats / (early[5:6, 0:1] * features))[0, : rms.shape[0]]
    half = features // 2
    part = bias_q.shape[1] // 2
    bias_e[...] = early[pl.ds(10 + z, 1), :].reshape(features)
    row = late[pl.ds(2 + z, 1), :]
    for side in range(2):
        for i in range(2):
            at = (3 * side + 2 * i) * part
            bias_q[i : i + 1, side * part : (side + 1) * part] = row[:, at : at + part]
    count = height.shape[0]
    turn = lax.broadcasted_iota(jnp.int32, (32, 32), 0) + lax.broadcasted_iota(jnp.int32, (32, 32), 1) == count - 1
    turned = jnp.dot(turn.astype(F32), rel[:32], precision=lax.Precision.HIGHEST, preferred_element_type=F32)
    height[...] = turned[:count, :HEAD]
    width_out[...] = rel[32 : 32 + count, :HEAD]
    for i in (3, 2, 0, 1):
        loads[i].wait()
        step = held[i].shape[0] // 5

        @pl.loop(0, 5)
        def _(m):
            at = pl.ds(pl.multiple_of(m * step, step), step)
            full[i][at] = held[i][at].astype(F32)

        stores[i].start()
    loads[5].wait()

    @pl.loop(0, SIDE)
    def _(i):
        for w in range(2):
            at = pl.multiple_of(w * WROWS + i * SIDE_PAD, SIDE_PAD)
            full[5][pl.ds(i * SIDE, SIDE), w, :] = held[5][pl.ds(at, SIDE_PAD)][:SIDE]

    stores[5].start()
    loads[4].wait()

    @pl.loop(0, SIDE)
    def _(i):
        places = [pl.multiple_of(w * WROWS + i * SIDE_PAD, SIDE_PAD) for w in range(2)]
        some = [held[4][pl.ds(at, SIDE_PAD)][:SIDE].astype(F32) for at in places]
        full[4][pl.ds(i * SIDE, SIDE)] = jnp.stack(some, axis=1).astype(BF)

    stores[4].start()
    for copy in stores:
        copy.wait()


def finish_outputs(got, part):
    early, late, rel = got[6:9]
    grads = [value.reshape(-1, value.shape[-1]) for value in got[2:6]]
    width = early.shape[1]
    sds = jax.ShapeDtypeStruct
    any_spec = pl.BlockSpec(memory_space=pl.ANY)
    vmem_spec = pl.BlockSpec(memory_space=pltpu.VMEM)
    windows = got[0].shape[0] // WROWS
    out_shape = [sds((2, 2 * part), F32), sds((width,), F32), sds((2 * SIDE - 1, HEAD), F32)]
    out_shape += [sds((2 * SIDE - 1, HEAD), F32), sds((5,), F32)] + [sds((width,), F32)] * 6
    held = grads + list(got[:2])
    final = [sds(value.shape, F32) for value in grads]
    final += [sds((SIDE * SIDE, windows, width), value.dtype) for value in got[:2]]
    out_shape += final
    return pl.pallas_call(
        finish_kernel,
        out_shape=out_shape,
        in_specs=[vmem_spec] * 3 + [any_spec] * 6,
        out_specs=[vmem_spec] * 11 + [any_spec] * 6,
        scratch_shapes=[pltpu.VMEM(value.shape, value.dtype) for value in held + final]
        + [pltpu.SemaphoreType.DMA((6,))] * 2,
        compiler_params=pltpu.CompilerParams(vmem_limit_bytes=VMEM_LIMIT),
        name="finish",
    )(early, late, rel, *held)


VMEM_LIMIT = 64 * 1024 * 1024 - 512 * 1024


def over_chips(
    tokens, valid_mask, out_grad, first_gain, first_shift, qkv_weight, qkv_bias, rel_height, rel_width,
    proj_weight, proj_bias, second_gain, second_shift, expand_weight, expand_bias, shrink_weight, shrink_bias,
):
    def turned(value):
        return value.transpose(1, 0, 2)

    rows, _, local_width = qkv_weight.shape
    part = local_width // 2
    hidden = expand_weight.shape[1] // 2
    qkv_src = qkv_weight.transpose(1, 2, 0).reshape(3, 2, part, rows)
    proj_src = proj_weight.reshape(2, 2, part // 2, proj_weight.shape[1])
    expand_src = expand_weight.reshape(2, rows // 2, 2 * hidden)
    shrink_src = shrink_weight.reshape(2, 2, hidden // 2, shrink_weight.shape[1])
    vectors = (first_gain, first_shift, second_gain, second_shift, proj_bias, shrink_bias)
    got = run_kernel(
        turned(tokens), valid_mask, turned(out_grad), vectors, qkv_bias, expand_bias, rel_height, rel_width,
        (qkv_src, proj_src, expand_src, shrink_src),
    )
    outs = finish_outputs(got, part)
    qkv_bias_sum, expand_bias_sum, height_sum, width_sum, rms = outs[:5]
    gain_one, shift_one, gain_two, shift_two, proj_bias_sum, shrink_bias_sum = outs[5:11]
    qkv_sum, proj_sum, expand_sum, shrink_sum, block_out, input_grad = outs[11:]
    return (
        turned(block_out),
        turned(input_grad),
        gain_one,
        shift_one,
        qkv_sum.reshape(3, local_width, rows).transpose(2, 0, 1),
        qkv_bias_sum,
        height_sum,
        width_sum,
        proj_sum.reshape(proj_weight.shape),
        proj_bias_sum,
        gain_two,
        shift_two,
        expand_sum.reshape(expand_weight.shape),
        expand_bias_sum,
        shrink_sum.reshape(shrink_weight.shape),
        shrink_bias_sum,
        rms,
    )


epsilon = 1e-06
highest = lax.Precision.HIGHEST


def layer_norm(values, norm_gain, norm_shift):
    center = values - jnp.mean(values, axis=-1, keepdims=True)
    spread = jnp.mean(center * center, axis=-1, keepdims=True)
    return center * lax.rsqrt(spread + epsilon) * norm_gain + norm_shift


def offset_table(span_size):
    positions = jnp.arange(span_size)
    offset = positions[:, None] - positions[None, :] + span_size - 1
    return (offset[:, :, None] == jnp.arange(2 * span_size - 1)[None, None, :]).astype(jnp.float32)


def attention_scores(
    query_rows, key_rows, rel_rows_table, rel_cols_table, onehot_table, span_size, scaling
):
    window_count, tokens_per, head_count, head_size = query_rows.shape
    rel_count = 2 * span_size - 1
    direct = (
        jnp.einsum("bthc,buhc->bhtu", query_rows, key_rows, preferred_element_type=jnp.float32)
        * scaling
    )
    query_float = query_rows.astype(jnp.float32)
    along_rows = jnp.einsum("bthc,jc->bhtj", query_float, rel_rows_table, precision=highest)
    along_cols = jnp.einsum("bthc,jc->bhtj", query_float, rel_cols_table, precision=highest)
    grid_rows = along_rows.reshape(window_count, head_count, span_size, span_size, rel_count)
    grid_cols = along_cols.reshape(window_count, head_count, span_size, span_size, rel_count)
    rel_rows = jnp.einsum("bhxyj,xkj->bhxyk", grid_rows, onehot_table, precision=highest)
    rel_cols = jnp.einsum("bhxyj,ywj->bhxyw", grid_cols, onehot_table, precision=highest)
    score_sum = direct.reshape(window_count, head_count, span_size, span_size, span_size, span_size)
    score_sum = score_sum + rel_rows[:, :, :, :, :, None] + rel_cols[:, :, :, :, None, :]
    return score_sum.reshape(window_count, head_count, tokens_per, tokens_per)


def relative_back(score_float, onehot_table, span_size):
    window_count, head_count, tokens_per, other_tokens = score_float.shape
    grid = score_float.reshape(window_count, head_count, span_size, span_size, span_size, span_size)
    rows_part = jnp.einsum("bhxykw,xkj->bhxyj", grid, onehot_table, precision=highest)
    cols_part = jnp.einsum("bhxykw,ywj->bhxyj", grid, onehot_table, precision=highest)
    return (
        rows_part.reshape(window_count, head_count, tokens_per, -1),
        cols_part.reshape(window_count, head_count, tokens_per, -1),
    )


def gather_weights(qkv_weight, proj_weight, expand_weight, shrink_weight):
    return (
        lax.all_gather(qkv_weight, "row", axis=0, tiled=True),
        lax.all_gather(proj_weight, "row", axis=1, tiled=True),
        lax.all_gather(expand_weight, "row", axis=0, tiled=True),
        lax.all_gather(shrink_weight, "row", axis=1, tiled=True),
    )


def gather_tokens(normed):
    return lax.all_gather(normed, "col", axis=0, tiled=True)


def gather_grads(grad_low):
    return lax.all_gather(grad_low, "col", axis=0, tiled=True)


def sum_branch(inputs_low, weight_full, own_windows):

    def term(first_row, row_count):
        return jnp.einsum(
            "btk,kd->btd", inputs_low, weight_full, preferred_element_type=jnp.float32
        )

    return lax.psum_scatter(
        term(jnp.int32(0), own_windows * lax.axis_size("col")),
        "col",
        scatter_dimension=0,
        tiled=True,
    )


def sum_input(grads_low, weight_full, own_windows):

    def term(first_row, row_count):
        return jnp.einsum("btk,dk->btd", grads_low, weight_full, preferred_element_type=jnp.float32)

    return lax.psum_scatter(
        term(jnp.int32(0), own_windows * lax.axis_size("col")),
        "col",
        scatter_dimension=0,
        tiled=True,
    )


def activate(values):
    return jax.nn.gelu(values, approximate=False)


def per_device(
    tokens,
    valid_mask,
    out_grad,
    first_gain,
    first_shift,
    qkv_weight,
    qkv_bias,
    rel_height,
    rel_width,
    proj_weight,
    proj_bias,
    second_gain,
    second_shift,
    expand_weight,
    expand_bias,
    shrink_weight,
    shrink_bias,
):
    span_size = (rel_height.shape[0] + 1) // 2
    head_size = rel_height.shape[1]
    local_width = qkv_weight.shape[2]
    head_count = local_width // head_size
    own_windows = tokens.shape[0]
    tokens_per = tokens.shape[1]
    model_width = tokens.shape[2]
    scaling = head_size ** (-0.5)
    onehot_table = offset_table(span_size)
    inputs = tokens.astype(jnp.float32)
    keep_mask = valid_mask.astype(jnp.float32)[:, :, None]

    def first_norm(values, norm_gain, norm_shift):
        return layer_norm(values, norm_gain, norm_shift) * keep_mask

    qkv_full, proj_full, expand_full, shrink_full = gather_weights(
        qkv_weight, proj_weight, expand_weight, shrink_weight
    )
    normed_first, first_back = jax.vjp(first_norm, inputs, first_gain, first_shift)
    first_all = gather_tokens(normed_first.astype(jnp.bfloat16))
    all_windows = first_all.shape[0]
    bias_rows = jnp.stack([qkv_bias[0], jnp.zeros_like(qkv_bias[0]), qkv_bias[1]])
    projected = (
        jnp.einsum("btd,dsk->btsk", first_all, qkv_full, preferred_element_type=jnp.float32)
        + bias_rows
    )
    projected = projected.astype(jnp.bfloat16)
    head_shape = (all_windows, tokens_per, head_count, head_size)
    query_low = projected[:, :, 0].reshape(head_shape)
    key_low = projected[:, :, 1].reshape(head_shape)
    value_low = projected[:, :, 2].reshape(head_shape)
    scores = attention_scores(
        query_low, key_low, rel_height, rel_width, onehot_table, span_size, scaling
    )
    top_score = jnp.max(scores, axis=-1, keepdims=True)
    log_total = top_score + jnp.log(jnp.sum(jnp.exp(scores - top_score), axis=-1, keepdims=True))
    probs_low = jnp.exp(scores - log_total).astype(jnp.bfloat16)
    attended = jnp.einsum(
        "bhtu,buhc->bthc", probs_low, value_low, preferred_element_type=jnp.float32
    )
    attended_low = attended.reshape(all_windows, tokens_per, local_width).astype(jnp.bfloat16)
    attn_out = sum_branch(attended_low, proj_full, own_windows) + proj_bias
    middle = inputs + attn_out
    normed_second, second_back = jax.vjp(layer_norm, middle, second_gain, second_shift)
    second_all = gather_tokens(normed_second.astype(jnp.bfloat16))
    hidden_pre = (
        jnp.einsum("btd,df->btf", second_all, expand_full, preferred_element_type=jnp.float32)
        + expand_bias
    )
    active_value, active_back = jax.vjp(activate, hidden_pre)
    hidden_low = active_value.astype(jnp.bfloat16)
    mlp_out = sum_branch(hidden_low, shrink_full, own_windows) + shrink_bias
    result = middle + mlp_out
    stat_terms = jnp.stack(
        [
            jnp.sum(keep_mask * inputs * inputs),
            jnp.sum(keep_mask * middle * middle),
            jnp.sum(keep_mask * result * result),
            jnp.sum(keep_mask * attn_out * attn_out),
            jnp.sum(keep_mask * mlp_out * mlp_out),
        ]
    )
    valid_count = jnp.sum(keep_mask)
    stat_total, count_total = lax.psum((stat_terms, valid_count), ("dp", "row", "col"))
    out_float = out_grad.astype(jnp.float32)
    qkv_full, proj_full, expand_full, shrink_full = gather_weights(
        qkv_weight, proj_weight, expand_weight, shrink_weight
    )
    mlp_grad_low = out_float.astype(jnp.bfloat16)
    shrink_bias_grad = jnp.sum(mlp_grad_low, axis=(0, 1), dtype=jnp.float32)
    mlp_grad_all = gather_grads(mlp_grad_low)
    shrink_grad_full = jnp.einsum(
        "btf,btd->fd", hidden_low, mlp_grad_all, preferred_element_type=jnp.float32
    )
    hidden_grad = jnp.einsum(
        "btd,fd->btf", mlp_grad_all, shrink_full, preferred_element_type=jnp.float32
    )
    pre_grad_low = active_back(hidden_grad)[0].astype(jnp.bfloat16)
    expand_bias_grad = jnp.sum(pre_grad_low, axis=(0, 1), dtype=jnp.float32)
    expand_grad_full = jnp.einsum(
        "btd,btf->df", second_all, pre_grad_low, preferred_element_type=jnp.float32
    )
    second_grad = sum_input(pre_grad_low, expand_full, own_windows)
    middle_part, second_gain_grad, second_shift_grad = second_back(second_grad)
    middle_grad = out_float + middle_part
    attn_grad_low = middle_grad.astype(jnp.bfloat16)
    proj_bias_grad = jnp.sum(attn_grad_low, axis=(0, 1), dtype=jnp.float32)
    attn_grad_all = gather_grads(attn_grad_low)
    proj_grad_full = jnp.einsum(
        "btk,btd->kd", attended_low, attn_grad_all, preferred_element_type=jnp.float32
    )
    attended_grad = jnp.einsum(
        "btd,kd->btk", attn_grad_all, proj_full, preferred_element_type=jnp.float32
    )
    attended_grad = attended_grad.astype(jnp.bfloat16).reshape(head_shape)
    scores_again = attention_scores(
        query_low, key_low, rel_height, rel_width, onehot_table, span_size, scaling
    )
    probs_float = jnp.exp(scores_again - log_total)
    probs_again = probs_float.astype(jnp.bfloat16)
    prob_grad = jnp.einsum(
        "bthc,buhc->bhtu", attended_grad, value_low, preferred_element_type=jnp.float32
    )
    value_grad = jnp.einsum(
        "bhtu,bthc->buhc", probs_again, attended_grad, preferred_element_type=jnp.float32
    )
    score_grad = probs_float * (
        prob_grad - jnp.sum(probs_float * prob_grad, axis=-1, keepdims=True)
    )
    score_low = score_grad.astype(jnp.bfloat16)
    rows_grad, cols_grad = relative_back(score_low.astype(jnp.float32), onehot_table, span_size)
    query_float = query_low.astype(jnp.float32)
    query_grad = (
        jnp.einsum("bhtu,buhc->bthc", score_low, key_low, preferred_element_type=jnp.float32)
        * scaling
    )
    query_grad = query_grad + jnp.einsum("bhtj,jc->bthc", rows_grad, rel_height, precision=highest)
    query_grad = query_grad + jnp.einsum("bhtj,jc->bthc", cols_grad, rel_width, precision=highest)
    key_grad = (
        jnp.einsum("bhtu,bthc->buhc", score_low, query_low, preferred_element_type=jnp.float32)
        * scaling
    )
    rel_height_grad = jnp.einsum("bhtj,bthc->jc", rows_grad, query_float, precision=highest)
    rel_width_grad = jnp.einsum("bhtj,bthc->jc", cols_grad, query_float, precision=highest)
    flat_shape = (all_windows, tokens_per, local_width)
    qkv_grad_low = jnp.stack(
        [
            query_grad.reshape(flat_shape),
            key_grad.reshape(flat_shape),
            value_grad.reshape(flat_shape),
        ],
        axis=2,
    ).astype(jnp.bfloat16)
    qkv_bias_grad = jnp.sum(qkv_grad_low[:, :, 0::2], axis=(0, 1), dtype=jnp.float32)
    qkv_grad_full = jnp.einsum(
        "btd,btsk->dsk", first_all, qkv_grad_low, preferred_element_type=jnp.float32
    )
    first_grad = sum_input(
        qkv_grad_low.reshape(all_windows, tokens_per, 3 * local_width),
        qkv_full.reshape(qkv_full.shape[0], 3 * local_width),
        own_windows,
    )
    input_part, first_gain_grad, first_shift_grad = first_back(first_grad)
    input_grad = middle_grad + input_part
    qkv_rows, proj_rows, expand_rows, shrink_rows = (
        lax.psum_scatter(qkv_grad_full, "row", scatter_dimension=0, tiled=True),
        lax.psum_scatter(proj_grad_full, "row", scatter_dimension=1, tiled=True),
        lax.psum_scatter(expand_grad_full, "row", scatter_dimension=0, tiled=True),
        lax.psum_scatter(shrink_grad_full, "row", scatter_dimension=1, tiled=True),
    )
    qkv_sum, proj_sum, expand_sum, shrink_sum = lax.psum(
        (qkv_rows, proj_rows, expand_rows, shrink_rows), "dp"
    )
    qkv_bias_sum, expand_bias_sum = lax.psum((qkv_bias_grad, expand_bias_grad), ("dp", "row"))
    (
        gain_one_sum,
        shift_one_sum,
        gain_two_sum,
        shift_two_sum,
        proj_bias_sum,
        shrink_bias_sum,
        height_sum,
        width_sum,
    ) = lax.psum(
        (
            first_gain_grad,
            first_shift_grad,
            second_gain_grad,
            second_shift_grad,
            proj_bias_grad,
            shrink_bias_grad,
            rel_height_grad,
            rel_width_grad,
        ),
        ("dp", "row", "col"),
    )
    rms = jnp.sqrt(stat_total / (count_total * model_width))
    return (
        result.astype(jnp.bfloat16),
        input_grad,
        gain_one_sum,
        shift_one_sum,
        qkv_sum,
        qkv_bias_sum,
        height_sum,
        width_sum,
        proj_sum,
        proj_bias_sum,
        gain_two_sum,
        shift_two_sum,
        expand_sum,
        expand_bias_sum,
        shrink_sum,
        shrink_bias_sum,
        rms,
    )


def choose(mesh):
    fits = tuple(mesh.shape[name] for name in ("dp", "row", "col")) == (4, 2, 4)
    return over_chips if fits else per_device


def solution(mesh):
    in_specs = (
        P(("dp", "row", "col"), None, None),
        P(("dp", "row", "col"), None),
        P(("dp", "row", "col"), None, None),
        P(),
        P(),
        P("row", None, "col"),
        P(None, "col"),
        P(),
        P(),
        P("col", "row"),
        P(),
        P(),
        P(),
        P("row", "col"),
        P("col"),
        P("col", "row"),
        P(),
    )
    out_specs = (
        P(("dp", "row", "col"), None, None),
        P(("dp", "row", "col"), None, None),
        P(),
        P(),
        P("row", None, "col"),
        P(None, "col"),
        P(),
        P(),
        P("col", "row"),
        P(),
        P(),
        P(),
        P("row", "col"),
        P("col"),
        P("col", "row"),
        P(),
        P(),
    )
    return jax.shard_map(
        choose(mesh), mesh=mesh, in_specs=in_specs, out_specs=out_specs, check_vma=False
    )
```

```python
import functools

import jax
import jax.numpy as jnp
import numpy as np
from jax import lax
from jax.experimental import pallas as pl
from jax.experimental.pallas import tpu as pltpu
from jax.sharding import PartitionSpec as P

BF = jnp.bfloat16
F32 = jnp.float32
LANES = 128
SIDE = 14
SIDE_PAD = 16
WROWS = SIDE * SIDE_PAD
HEAD = 80
AT_H = HEAD
AT_W = HEAD + SIDE
AT_MASK = HEAD + 2 * SIDE
COL_W = 64


def dot(a, b):
    return jnp.dot(a, b, preferred_element_type=F32)


def dot_nt(a, b):
    return lax.dot_general(a, b, (((1,), (1,)), ((), ())), preferred_element_type=F32)


def dot_tn(a, b):
    return lax.dot_general(a, b, (((0,), (0,)), ((), ())), preferred_element_type=F32)


def lane_ids():
    return lax.broadcasted_iota(jnp.int32, (WROWS, LANES), 1)


def row_ids():
    return lax.broadcasted_iota(jnp.int32, (WROWS, LANES), 0)


def key_codes():
    u = np.arange(WROWS)[:, None]
    lane = np.arange(LANES)[None, :]
    k, l = u // SIDE_PAD, u % SIDE_PAD
    height = lane - AT_H == k
    width = (lane - AT_W == l) & (l < SIDE)
    width_back = (AT_W + SIDE - 1 - lane == l) & (l < SIDE)
    plain = np.where(height | width, 1.0, 0.0)
    masked = np.where((lane == AT_MASK) & (l >= SIDE), -1e30, plain)
    back = np.where(height | width_back, 1.0, 0.0)
    return np.stack([masked, plain, back]).astype(BF)


def split_low(values):
    high = values.astype(BF)
    return high, (values - high.astype(F32)).astype(BF)


def relative_tables(rel_h, rel_w, rel_query, rel_back):
    count, rows = 2 * SIDE - 1, rel_h.shape[0]
    offset = lax.broadcasted_iota(jnp.int32, (rows, LANES), 0)
    lane = lax.broadcasted_iota(jnp.int32, (rows, LANES), 1)

    def places(first, step):
        return jnp.where((lane == first + step * offset) & (offset < count), 1.0, 0.0).astype(BF)

    heights, widths = places(count - 1, -1), places(COL_W + count - 1, -1)
    widths_back = places(COL_W, 1)
    tall, wide = rel_h[...], rel_w[...]
    rel_query[...] = jnp.zeros_like(rel_query)
    rel_back[...] = jnp.zeros_like(rel_back)
    for part, (a, b) in enumerate(zip(split_low(tall * HEAD**0.5), split_low(wide * HEAD**0.5))):
        at = part * LANES
        rel_query[at : at + HEAD] = (dot_tn(a, heights) + dot_tn(b, widths)).astype(BF)
    for part, (a, b) in enumerate(zip(split_low(tall), split_low(wide))):
        table = (dot_tn(heights, a) + dot_tn(widths_back, b)).astype(BF)
        for place in ((0, 1), (2,))[part]:
            rel_back[place * LANES : (place + 1) * LANES, :HEAD] = table


def query_codes(query, rel_query):
    full = dot(jnp.concatenate([query, query], axis=1), rel_query)
    tiles = full.reshape(SIDE, SIDE_PAD, LANES)
    heights = jnp.concatenate(
        [pltpu.roll(tiles[i], AT_H - (SIDE - 1 - i), 1) for i in range(SIDE)], axis=0
    )
    widths = pltpu.roll(
        tiles, AT_W - COL_W - (SIDE - 1), 2, stride=1, stride_axis=1
    ).reshape(WROWS, LANES)
    lane = lane_ids()
    codes = jnp.where(
        (lane >= AT_H) & (lane < AT_W),
        heights,
        jnp.where((lane >= AT_W) & (lane < AT_MASK), widths, 0.0),
    )
    high, rest = split_low(codes)
    first = query + high + jnp.where(lane == AT_MASK, 1.0, 0.0).astype(BF)
    return jnp.concatenate([first, rest], axis=1)


def softmax_rows(query, key, rel_query, codes_ref):
    left = query_codes(query, rel_query)
    right = jnp.concatenate([key + codes_ref[0], codes_ref[1]], axis=1)
    scores = dot_nt(left, right)
    top = jnp.max(scores, axis=1, keepdims=True)
    weights = jnp.exp((scores - top) * (HEAD**-0.5))
    return weights / jnp.sum(weights, axis=1, keepdims=True)


def attend(query, key, value, rel_query, codes_ref):
    probs = softmax_rows(query, key, rel_query, codes_ref)
    return dot(probs.astype(BF), value)


def attend_back(query, key, value, grad, rel_query, rel_back, codes_ref):
    probs = softmax_rows(query, key, rel_query, codes_ref)
    prob_grad = dot_nt(grad, value)
    inner = jnp.sum(probs * prob_grad, axis=1, keepdims=True)
    score_low = (probs * (prob_grad - inner)).astype(BF)
    value_grad = dot_tn(probs.astype(BF), grad)
    key_grad = dot_tn(score_low, query) * (HEAD**-0.5)
    mixed = dot(score_low, key + codes_ref[2])
    tiles = mixed.reshape(SIDE, SIDE_PAD, LANES)
    heights = jnp.concatenate(
        [pltpu.roll(tiles[i], (SIDE - 1 - i - AT_H) % LANES, 1) for i in range(SIDE)], axis=0
    )
    widths = pltpu.roll(
        tiles, (COL_W - AT_W) % LANES, 2, stride=1, stride_axis=1
    ).reshape(WROWS, LANES)
    lane, row = lane_ids(), row_ids()
    first_h = SIDE - 1 - row // SIDE_PAD
    first_w = COL_W + row % SIDE_PAD
    offsets = jnp.where(
        (lane >= first_h) & (lane < first_h + SIDE),
        heights,
        jnp.where((lane >= first_w) & (lane < first_w + SIDE), widths, 0.0),
    )
    high, rest = split_low(offsets)
    query_grad = jnp.where(lane < HEAD, mixed, 0.0) * (HEAD**-0.5) + dot(
        jnp.concatenate([high, rest, high], axis=1), rel_back
    )
    rel_grad = dot_tn(jnp.concatenate([high, rest], axis=1), query)
    return query_grad, key_grad, value_grad, rel_grad


def pad_head(piece):
    return jnp.concatenate([piece, jnp.zeros((piece.shape[0], LANES - HEAD), piece.dtype)], axis=1)


def qkv_low(s, rows, h1, wq, bias, half):
    return (dot_nt(h1[rows, :half], block(wq, s, 0)) + dot_nt(h1[rows, half:], block(wq, s, 1)) + bias).astype(BF)


def head_of(low, part, heads, hh):
    at = (part * heads + hh) * HEAD
    return pad_head(low[:, at : at + HEAD])


def attention_slab(s, h1, wq, wp, bias, rel_query, codes, attended, total, heads, half, half_done):
    count = h1.shape[0] // WROWS

    @pl.loop(0, count)
    def _(m):
        rows = pl.ds(pl.multiple_of((m + count // 2) % count * WROWS, WROWS), WROWS)
        low = qkv_low(s, rows, h1, wq, bias, half)
        outs = []
        for hh in range(heads):
            query, key, value = (head_of(low, part, heads, hh) for part in range(3))
            outs.append(attend(query, key, value, rel_query[...], codes)[:, :HEAD])
        out_low = jnp.concatenate(outs, axis=1).astype(BF)
        attended[s, rows] = out_low
        total[rows, :half] += dot(out_low, block(wp, s, 0))
        total[rows, half:] += dot(out_low, block(wp, s, 1))

        @pl.when(m == count // 2 - 1)
        def _():
            half_done()


SQRT_HALF = 0.5**0.5
PDF_SCALE = 0.3989422804014327


def both_blocks(ref, slab):
    value = ref[slab]
    return value.reshape(4 * value.shape[2], value.shape[3])


def mlp_rows(s, place, m, h2, gm, we, ws, bias, act, gpre, total, back, bias_grad, half):
    count = h2.shape[0] // 2

    @pl.loop(0, 1)
    def _(step):
        rows = pl.ds(pl.multiple_of((m + step) * count, count), count)
        pre = dot(h2[rows, :], both_blocks(we, place)) + bias
        cdf = 0.5 + 0.5 * lax.erf(pre * SQRT_HALF)
        slope = cdf + pre * (PDF_SCALE * jnp.exp(-0.5 * pre * pre))
        act_low = (pre * cdf).astype(BF)
        act[rows, :] = act_low
        hidden = dot_nt(gm[rows, :half], block(ws, place, 0)) + dot_nt(gm[rows, half:], block(ws, place, 1))
        gpre_low = (hidden * slope).astype(BF)
        gpre[rows, :] = gpre_low
        bias_grad[s] += jnp.sum(gpre_low.astype(F32), axis=0, keepdims=True)
        total[rows, :half] += dot(act_low, block(ws, place, 0))
        total[rows, half:] += dot(act_low, block(ws, place, 1))
        back[rows, :] += dot_nt(gpre_low, both_blocks(we, place))


def attention_back_slab(
    s, h1, ga, wq, wp, bias, rel_query, rel_back, codes, gqkv, back, bias_grad, rel_grad, heads, half, half_done
):
    count = h1.shape[0] // WROWS

    @pl.loop(0, count)
    def _(m):
        rows = pl.ds(pl.multiple_of((m + count // 2) % count * WROWS, WROWS), WROWS)
        low = qkv_low(s, rows, h1, wq, bias, half)
        grad = (dot_nt(ga[rows, :half], block(wp, s, 0)) + dot_nt(ga[rows, half:], block(wp, s, 1))).astype(BF)
        parts = [[], [], []]
        for hh in range(heads):
            query, key, value = (head_of(low, part, heads, hh) for part in range(3))
            got = attend_back(
                query, key, value, head_of(grad, 0, heads, hh), rel_query[...], rel_back[...], codes
            )
            for part in range(3):
                parts[part].append(got[part][:, :HEAD])
            rel_grad[...] += got[3]
        grad_low = jnp.concatenate(parts[0] + parts[1] + parts[2], axis=1).astype(BF)
        gqkv[rows, : grad_low.shape[1]] = grad_low
        bias_grad[s] += jnp.sum(grad_low.astype(F32), axis=0, keepdims=True)
        back[rows, :half] += dot(grad_low, block(wq, s, 0))
        back[rows, half:] += dot(grad_low, block(wq, s, 1))

        @pl.when(m == count // 2 - 1)
        def _():
            half_done()


MESH_ID = pl.DeviceIdType.MESH
ARRAYS = ("qkv", "proj", "expand", "shrink")
CHUNK = 64
EPS = 1e-06
SPARE = 4


def halves(rows):
    first = (rows // 2 + 15) // 16 * 16
    return first, rows - first


def flip(index, k):
    return ((index // 2 + k // 2) % 2) * 2 + (index % 2 + k % 2) % 2


def block(ref, slab, half):
    value = ref[slab, half]
    return value.reshape(value.shape[0] * value.shape[1], value.shape[2])


def add_low(target, index, extra):
    target[index] = (target[index].astype(F32) + extra.astype(F32)).astype(BF)


def kernel(
    tokens_in, mask_in, out_grad_in, gain_one_in, shift_one_in, gain_two_in, shift_two_in, proj_bias_in, shrink_bias_in,
    qkv_bias_in, expand_bias_in, rel_h_in, rel_w_in, codes, qkv_src, proj_src, expand_src, shrink_src,
    block_out, input_grad, qkv_out, proj_out, expand_out, shrink_out, early_out, late_out, rel_out,
    rxq, rxp, rxe, rxs, ryq, ryp, rye, rys, rx2q, rx2p, rx2e, rx2s, ry2q, ry2p, ry2e, ry2s, rzq, rzp, rze, rzs, pair_back, pair_out,
    wq, wp, we, ws, tokens, keep, h1, grads, normed, got_low, attended, total, back, xr, xr2, middle, act, gpre,
    bias_all, early, early_full, early_half, late, late_full, late_half, rel, rel_full, rel_half, bias_e, bias_q, rel_acc, rel_query, rel_back, rel_pad,
    gsend, grecv, rsend, rrecv, fsend, frecv, csend, crecv, zsend, zrecv, qsend, qrecv, local, qlocal,
):
    d, r, z = lax.axis_index("dp"), lax.axis_index("row"), lax.axis_index("col")
    h, b = d // 2, d % 2
    own = tokens.shape[0]
    width = tokens.shape[1]
    half = width // 2
    heads = 2
    bufs = (wq, wp, we, ws)
    outs = (qkv_out, proj_out, expand_out, shrink_out)
    rx, ry = (rxq, rxp, rxe, rxs), (ryq, ryp, rye, rys)
    rx2, ry2 = (rx2q, rx2p, rx2e, rx2s), (ry2q, ry2p, ry2e, ry2s)
    rz = (rzq, rzp, rze, rzs)
    parts = [halves(buf.shape[3]) for buf in bufs]
    attn, mlp = (0, 1), (2, 3)
    qkv_width = 3 * attended.shape[2]

    along_x = (h * 2 + 1 - b, r, z)
    along_y = ((1 - h) * 2 + b, r, z)
    across = ((1 - h) * 2 + 1 - b, r, z)
    partner = (d, 1 - r, z)
    pair, remote_slab = (d, r, flip(z, 1)), flip(z, 2)
    gm, gmz, h2, h2z = grads.at[0], grads.at[1], normed.at[0], normed.at[1]

    def along_z(k):
        return (d, r, flip(z, k))

    def remote(src, dst, sems, recvs, index, device, got=None):
        return pltpu.make_async_remote_copy(
            src_ref=src,
            dst_ref=dst,
            send_sem=sems.at[index],
            recv_sem=recvs.at[index if got is None else got],
            device_id=device,
            device_id_type=MESH_ID,
        )

    up = z // 2
    is_end = (z + 1) // 2 % 2 == 0
    is_inner = (z + 1) // 2 % 2 == 1

    def slab_of(i):
        far = i // 2
        return (1 - far) * flip(z, i) + far * ((1 - up) * i + up * (3 - i))

    def first_part(a):
        return pl.ds(0, parts[a][0])

    def second_part(a):
        return pl.ds(parts[a][0], parts[a][1])

    def gather_z(a, s, step):
        at = bufs[a].at[s, h, b]
        return remote(at, at, gsend, grecv, (a, s, 0 if step < 0 else 5), (d, r, z + step), (a, s, 0))

    def gather_far(a):
        return remote(bufs[a].at[0, h, b], bufs[a].at[1, h, b], gsend, grecv, (a, 0, 0), (d, r, remote_slab))

    def ring(a, slab, sends, recvs, index, kind, arriving):
        buf = bufs[a]
        if kind == 1:
            at, device = (buf.at[slab, h, 1 - b] if arriving else buf.at[slab, h, b]), along_x
        elif kind == 2:
            at, device = (buf.at[slab, 1 - h, b] if arriving else buf.at[slab, h, b]), along_y
        elif kind == 3:
            at = buf.at[slab, 1 - h if arriving else h, 1 - b, first_part(a)]
            device = along_y
        else:
            at = buf.at[slab, 1 - h, 1 - b if arriving else b, second_part(a)]
            device = along_x
        return remote(at, at, sends, recvs, index, device)

    def gather(a, s, kind, arriving=False):
        return ring(a, s, gsend, grecv, (a, s, kind), kind, arriving)

    def spread(a, kind, arriving=False):
        return ring(a, final_slot(a), fsend, frecv, (a, kind), kind, arriving)

    def sends_along_z(group, s, act_on):
        for a in group:

            @pl.when((s >= z) & (z > 0))
            def _():
                act_on(gather_z(a, s, -1))

            @pl.when((s <= z) & (z < 3))
            def _():
                act_on(gather_z(a, s, 1))

    def start_z(group):
        sends_along_z(group, z, lambda copy: copy.start())

    def relay(group, i):
        s = slab_of(i)
        for a in group:
            gather_z(a, s, 1).wait_recv()
            sends_along_z((a,), s, lambda copy: copy.start())

    def place_of(a, i):
        return slab_of(i) if a in attn else 1

    def share(group, i):
        for a in group:
            gather(a, place_of(a, i), 1).start()
            gather(a, place_of(a, i), 2).start()

    def share_far(group):
        for a in group:
            gather_far(a).wait_recv()
            share((a,), 1)

    def pass_diagonal(group, i):
        for a in group:
            s = place_of(a, i)
            gather(a, s, 1, True).wait_recv()
            gather(a, s, 3).start()
            gather(a, s, 2, True).wait_recv()
            gather(a, s, 4).start()

    def finish_slab(group, i):
        for a in group:
            s = place_of(a, i)
            gather(a, s, 3, True).wait_recv()
            gather(a, s, 4, True).wait_recv()

    def sent_slab(group, i):
        s = slab_of(i)
        sends_along_z(group, s, lambda copy: copy.wait_send())
        for a in group:

            @pl.when(i > 0)
            def _():
                for kind in (1, 2, 3, 4):
                    gather(a, s, kind).wait_send()

    def sent_far(group):
        for a in group:
            gather_far(a).wait_send()
            for kind in (1, 2, 3, 4):
                gather(a, 1, kind).wait_send()

    def step_slab(n):
        return slab_of(3 - n)

    def final_slot(a):
        return z if a in attn else 0

    def slot(a, n):
        if a in mlp:
            return 2 + n
        first = (4 - n) // 4
        return first * SPARE + (1 - first) * step_slab(n - 1 + first)

    def reduce_copy(a, n, kind):
        buf, g = bufs[a], slot(a, n)
        got = None
        if kind == 0:
            src, dst, device = buf.at[g, :, 1 - b, first_part(a)], rx[a].at[n], along_x
        elif kind == 1:
            src, dst, device = buf.at[g, 1 - h, :, second_part(a)], ry[a].at[n], along_y
        elif kind == 2:
            src, dst, device = buf.at[g, 1 - h, b, first_part(a)], ry2[a].at[n], along_y
        elif kind == 3:
            src, dst, device = buf.at[g, h, 1 - b, second_part(a)], rx2[a].at[n], along_x
        elif kind == 4 and a in mlp:
            src, dst, device = buf.at[g, h, b], rz[a].at[0], (d, r, remote_slab)
            got = (a, 0, 4)
        elif kind == 4:
            src, dst, device = buf.at[g, h, b], rz[a].at[z], (d, r, step_slab(n))
            got = (a, z, 4)
        else:
            src, dst, device = buf.at[g, h, b], rz[a].at[5 - n], (d, r, slab_of(1))
            got = (a, 3 - n, 5)
        return remote(src, dst, rsend, rrecv, (a, n, min(kind, 4)), device, got)

    def reduce_z(a, n, act_on):
        if a in mlp:

            @pl.when(n == 1)
            def _():
                act_on(reduce_copy(a, n, 4))

        else:

            @pl.when((n < 3) & (is_inner | (n == 2)))
            def _():
                act_on(reduce_copy(a, n, 4))

            @pl.when(is_end & (n < 2))
            def _():
                act_on(reduce_copy(a, n, 5))

    def reduce_one(group, n):
        for a in group:
            reduce_copy(a, n, 0).start()
            reduce_copy(a, n, 1).start()

    def with_room(body):
        def run(group, n):
            shape = (2 * len(group), 2, halves(max(bufs[a].shape[3] for a in group))[0], half)
            pl.run_scoped(
                lambda room: body(group, n, lambda a, place: room.at[2 * group.index(a) + place]),
                pltpu.VMEM(shape, BF),
            )

        return run

    def reduce_two_body(group, n, scratch):
        loads = []
        for a in group:
            reduce_copy(a, n, 0).wait_recv()
            reduce_copy(a, n, 1).wait_recv()
            for place, got in enumerate((rx[a], ry[a])):
                to = scratch(a, place).at[:, pl.ds(0, parts[a][place])]
                loads.append(pltpu.make_async_copy(got.at[n], to, local.at[a * 2 + place]))
                loads[-1].start()
        for i, a in enumerate(group):
            g = slot(a, n)
            first, second = parts[a]
            loads[2 * i].wait()
            for side in range(2):
                add_low(bufs[a], (g, side, b, first_part(a)), scratch(a, 0)[side, :first])
            reduce_copy(a, n, 2).start()
            loads[2 * i + 1].wait()
            for side in range(2):
                add_low(bufs[a], (g, h, side, second_part(a)), scratch(a, 1)[side, :second])
            reduce_copy(a, n, 3).start()

    def reduce_three_body(group, n, scratch):
        loads = []
        for a in group:
            reduce_copy(a, n, 2).wait_recv()
            reduce_copy(a, n, 3).wait_recv()
            for place, got in enumerate((ry2[a], rx2[a])):
                to = scratch(a, place).at[0, pl.ds(0, parts[a][place])]
                loads.append(pltpu.make_async_copy(got.at[n], to, local.at[a * 2 + place]))
                loads[-1].start()
        for i, a in enumerate(group):
            g = slot(a, n)
            first, second = parts[a]
            loads[2 * i].wait()
            add_low(bufs[a], (g, h, b, first_part(a)), scratch(a, 0)[0, :first])
            loads[2 * i + 1].wait()
            add_low(bufs[a], (g, h, b, second_part(a)), scratch(a, 1)[0, :second])

            @pl.when(is_inner & (n < 2) & (a in attn))
            def _():
                at = rz[a].at[5 - n]
                remote(at, at, rsend, rrecv, (a, n, 4), (d, r, slab_of(1)), (a, 3 - n, 5)).wait_recv()
                pieces = ((0, first, first_part(a)), (1, second, second_part(a)))
                copies = [
                    pltpu.make_async_copy(at.at[part], scratch(a, 0).at[side, pl.ds(0, count)], local.at[a * 2 + side])
                    for side, count, part in pieces
                ]
                for copy in copies:
                    copy.start()
                for copy, (side, count, part) in zip(copies, pieces):
                    copy.wait()
                    add_low(bufs[a], (g, h, b, part), scratch(a, 0)[side, :count])

            reduce_z(a, n, lambda copy: copy.start())

    def reduce_two(group, n):
        with_room(reduce_two_body)(group, n)

    def reduce_three(group, n):
        with_room(reduce_three_body)(group, n)

    def reduce_four(group):
        for a in group:
            rows = bufs[a].shape[3]
            loads = []
            others = ((remote_slab, 0),) if a in mlp else [(slab_of(k), slab_of(k)) for k in (1, 2)]
            for k, (other, place) in enumerate(others, 1):
                at = rz[a].at[place]
                remote(at, at, rsend, rrecv, (a, k, 4), (d, r, other), (a, place, 4)).wait_recv()
                loads.append(pltpu.make_async_copy(at, gpre.at[pl.ds((k - 1) * rows, rows)], local.at[k]))
                loads[-1].start()
            for load in loads:
                load.wait()
            value = bufs[a][slot(a, 0 if a in mlp else 3), h, b].astype(F32)
            for k in range(len(others)):
                value = value + gpre[k * rows : (k + 1) * rows].astype(F32)
            bufs[a][final_slot(a), h, b] = value.astype(BF)
            spread(a, 1).start()
            spread(a, 2).start()

    def reduce_five(group):
        for a in group:
            spread(a, 1, True).wait_recv()
            spread(a, 3).start()
            spread(a, 2, True).wait_recv()
            spread(a, 4).start()

    def qkv_pieces(matrix, side, flat):
        rows = flat.shape[1]
        part = matrix.shape[2]
        cut = rows - part
        return (
            (matrix.at[0, side], flat.at[0, pl.ds(0, part)]),
            (matrix.at[1, side, pl.ds(0, cut)], flat.at[0, pl.ds(part, cut)]),
            (matrix.at[1, side, pl.ds(cut, part - cut)], flat.at[1, pl.ds(0, part - cut)]),
            (matrix.at[2, side], flat.at[1, pl.ds(part - cut, part)]),
        )

    def swap_out(a):
        mine = bufs[a].at[final_slot(a), 1 - r]
        if a == 0:
            pairs = qkv_pieces(outs[a], r, mine)
            return [remote(src, dst, qsend, qrecv, 4 + i, partner) for i, (dst, src) in enumerate(pairs)]
        to = outs[a].at[:, :, half_lanes(r)] if a == 2 else outs[a].at[r]
        return [remote(mine, to, fsend, frecv, (a, 0), partner)]

    def keep_out(a):
        mine = bufs[a].at[final_slot(a), r]
        if a == 0:
            pairs = qkv_pieces(outs[a], r, mine)
            return [pltpu.make_async_copy(src, dst, qlocal.at[i]) for i, (dst, src) in enumerate(pairs)]
        to = outs[a].at[:, :, half_lanes(r)] if a == 2 else outs[a].at[r]
        return [pltpu.make_async_copy(mine, to, local.at[a])]

    def reduce_six(group):
        for a in group:
            spread(a, 3, True).wait_recv()
            spread(a, 4, True).wait_recv()
            for copy in swap_out(a) + keep_out(a):
                copy.start()

    def half_lanes(side):
        return pl.ds(pl.multiple_of(side * half, half), half)

    def exchange(index, src, dst):
        return remote(src, dst, csend, crecv, index, partner)

    rows_own, rows_other = pl.ds(0, own), pl.ds(own, own)
    def source(a, side):
        if a == 2:
            return expand_src.at[:, :, half_lanes(side)]
        return (qkv_src, proj_src, expand_src, shrink_src)[a].at[side]

    def source_swap(a):
        to = bufs[a].at[z if a in attn else 0, r]
        if a == 0:
            pairs = qkv_pieces(qkv_src, 1 - r, to)
            return [remote(src, dst, qsend, qrecv, i, partner) for i, (src, dst) in enumerate(pairs)]
        return [exchange(a, source(a, 1 - r), to)]

    def source_keep(a):
        to = bufs[a].at[z if a in attn else 0, r]
        if a == 0:
            pairs = qkv_pieces(qkv_src, r, to)
            return [pltpu.make_async_copy(src, dst, qlocal.at[i]) for i, (src, dst) in enumerate(pairs)]
        return [pltpu.make_async_copy(source(a, r), to, local.at[a])]

    def start_source(group):
        for a in group:
            for copy in source_swap(a) + source_keep(a):
                copy.start()

    def finish_source(group):
        for a in group:
            for copy in source_swap(a) + source_keep(a):
                copy.wait()

    swap_grad = exchange(4, gm.at[rows_own], gm.at[rows_other])
    swap_h1 = exchange(5, h1.at[rows_own], h1.at[rows_other])
    swap_attn = exchange(6, total.at[rows_other], xr)
    swap_h2 = exchange(7, h2.at[rows_own], h2.at[rows_other])
    swap_mlp = exchange(8, total.at[rows_other], xr)
    swap_gh2 = exchange(9, back.at[rows_other], xr2)
    swap_ga = exchange(10, gm.at[rows_own], gm.at[rows_other])
    swap_gh1 = exchange(11, back.at[rows_other], total.at[rows_other])
    pair_gm = remote(gm.at[rows_own], gmz.at[rows_own], csend, crecv, 12, pair)
    swap_gmz = exchange(13, gmz.at[rows_own], gmz.at[rows_other])
    pair_h2 = remote(h2.at[rows_own], h2z.at[rows_own], csend, crecv, 14, pair)
    swap_h2z = exchange(15, h2z.at[rows_own], h2z.at[rows_other])
    swap_back_low = exchange(16, h2.at[rows_own], got_low.at[rows_own])
    swap_out_low = exchange(17, h2.at[rows_other], got_low.at[rows_other])
    send_back = remote(h2.at[rows_own], pair_back, csend, crecv, 18, pair)
    send_out = remote(h2.at[rows_other], pair_out, csend, crecv, 19, pair)

    def bias_copy(k, arriving=False):
        at = bias_all.at[flip(z, k) if arriving else z]
        return remote(at, at, zsend, zrecv, k, along_z(k))

    barrier = pltpu.get_barrier_semaphore()
    peers = [partner, along_x, along_y, across, along_z(1), along_z(2), along_z(3)]
    for peer in peers:
        pl.semaphore_signal(barrier, inc=1, device_id=peer, device_id_type=MESH_ID)
    pl.semaphore_wait(barrier, len(peers))

    start_source(attn)
    bias_all[z] = jnp.zeros(bias_all.shape[1:], F32)
    part = qkv_bias_in.shape[1] // 2
    for side in range(2):

        @pl.when(r == side)
        def _():
            bias_all[z, 0:1, :half] = expand_bias_in[side * half : (side + 1) * half].reshape(1, half)
            for i in range(2):
                at = half + 2 * i * part
                bias_all[z, 0:1, at : at + part] = qkv_bias_in[i : i + 1, side * part : (side + 1) * part]

    finish_source(attn)
    start_z(attn)
    for k in (1, 2, 3):
        bias_copy(k).start()
    start_source(mlp)

    def as_row(ref):
        return ref[...].reshape(1, width)

    gain_one, shift_one, gain_two, shift_two, proj_bias, shrink_bias = (
        as_row(ref) for ref in (gain_one_in, shift_one_in, gain_two_in, shift_two_in, proj_bias_in, shrink_bias_in)
    )

    def over_rows(body):
        @pl.loop(0, own // CHUNK)
        def _(m):
            body(pl.ds(pl.multiple_of(m * CHUNK, CHUNK), CHUNK))

    def column_sum(value):
        return jnp.sum(value, axis=0, keepdims=True)

    def normalize(value):
        center = value - jnp.mean(value, axis=1, keepdims=True)
        inverse = lax.rsqrt(jnp.mean(center * center, axis=1, keepdims=True) + EPS)
        return center * inverse, inverse

    def norm_back(grad, gain, xhat, inverse):
        scaled = grad * gain
        mean = jnp.mean(scaled, axis=1, keepdims=True)
        along = jnp.mean(scaled * xhat, axis=1, keepdims=True)
        return (scaled - mean - xhat * along) * inverse

    early[...] = jnp.zeros_like(early)
    late[...] = jnp.zeros_like(late)

    def spread_rows(source, target):
        def move(stage):
            load = pltpu.make_async_copy(source, stage, local.at[8])
            load.start()
            load.wait()

            @pl.loop(0, SIDE)
            def _(i):
                both = stage[pl.ds(i * SIDE, SIDE)].astype(F32)
                for w in range(both.shape[1]):
                    some = jnp.concatenate([both[:, w], jnp.zeros((SIDE_PAD - SIDE, width), F32)], axis=0)
                    at = pl.multiple_of(w * WROWS + i * SIDE_PAD, SIDE_PAD)
                    target[pl.ds(at, SIDE_PAD)] = some.astype(BF)

        pl.run_scoped(move, pltpu.VMEM(source.shape, BF))

    spread_rows(tokens_in, tokens)
    count = mask_in.shape[0]
    mask = jnp.concatenate([mask_in[...].astype(F32), jnp.zeros((count, 2 * LANES - SIDE * SIDE), F32)], axis=1)
    mask = jnp.concatenate([mask, jnp.zeros((8 - count, 2 * LANES), F32)], axis=0).T
    keep[...] = jnp.zeros_like(keep)
    for i in range(SIDE):
        for w in range(count):
            at = w * WROWS + i * SIDE_PAD
            keep[at : at + SIDE] = mask[i * SIDE : (i + 1) * SIDE, w : w + 1]

    def first_rows(rows):
        value = tokens[rows].astype(F32)
        valid = keep[rows]
        xhat, _ = normalize(value)
        h1[rows] = ((xhat * gain_one + shift_one) * valid).astype(BF)
        early[0:1, :] += column_sum(valid * value * value)
        early[5:6, :] += jnp.broadcast_to(column_sum(valid), (1, width))

    over_rows(first_rows)
    swap_h1.start()
    spread_rows(out_grad_in, gm)
    swap_grad.start()
    rel_pad[...] = jnp.zeros_like(rel_pad)
    rel_pad[0, : rel_h_in.shape[0]] = rel_h_in[...]
    rel_pad[1, : rel_w_in.shape[0]] = rel_w_in[...]
    relative_tables(rel_pad.at[0], rel_pad.at[1], rel_query, rel_back)
    total[...] = jnp.zeros_like(total)
    swap_h1.wait_recv()

    def bias_q_of(s):
        return bias_all[s, 0:1, half : half + qkv_width]

    def bias_e_of(s):
        return bias_all[s, 0:1, :half]

    finish_source(mlp)

    def start_far():
        for a in mlp:
            gather_far(a).start()
        pair_gm.start()

    @pl.loop(0, 4)
    def _(i):
        @pl.when(i == 1)
        def _():
            @pl.when(is_end)
            def _():
                relay(attn, 2)
                share(attn, 2)
                start_far()

            relay(attn, 3)
            pass_diagonal(attn, 1)
            share(attn, 3)
            pass_diagonal(attn, 2)

            @pl.when(is_inner)
            def _():
                start_far()

            for k in (1, 2, 3):
                bias_copy(k, True).wait_recv()

        @pl.when(i > 0)
        def _():
            finish_slab(attn, i)

        @pl.when(i == 2)
        def _():
            pass_diagonal(attn, 3)

        @pl.when(((i == 2) & is_inner) | ((i == 3) & is_end))
        def _():
            share_far(mlp)

        s = slab_of(i)

        def half_done():
            @pl.when(i == 0)
            def _():
                relay(attn, 1)
                share(attn, 1)

                @pl.when(is_inner)
                def _():
                    relay(attn, 2)
                    share(attn, 2)

            @pl.when(i == 3)
            def _():
                swap_attn.start()

        attention_slab(
            s, h1, wq, wp, bias_q_of(s), rel_query, codes, attended, total, heads, half, half_done
        )


    swap_attn.wait()

    def middle_rows(rows):
        value = tokens[rows].astype(F32)
        valid = keep[rows]
        attn_out = total[rows] + xr[rows] + proj_bias
        mid = value + attn_out
        middle[rows] = mid
        xhat, _ = normalize(mid)
        h2[rows] = (xhat * gain_two + shift_two).astype(BF)
        early[1:2, :] += column_sum(valid * mid * mid)
        early[3:4, :] += column_sum(valid * attn_out * attn_out)

    over_rows(middle_rows)
    swap_h2.start()
    pair_h2.start()
    total[...] = jnp.zeros_like(total)
    back[...] = jnp.zeros_like(back)
    bias_e[...] = jnp.zeros_like(bias_e)
    bias_q[...] = jnp.zeros_like(bias_q)
    rel_acc[...] = jnp.zeros_like(rel_acc)
    swap_grad.wait()

    def add_grad(buf, p, j, side, value):
        value = value.reshape(buf.shape[2:]) + jnp.where(p > 0, buf[2 + j, side].astype(F32), 0.0)
        buf[2 + j, side] = value.astype(BF)

    def weight_grads(p, j, done):
        sides = [(side, slice(side * half, side * half + half)) for side in range(2)]
        for side, columns in sides:
            add_grad(we, p, j, side, dot_tn(normed[p, :, columns], gpre[...]))
        done((2,))
        for side, columns in sides:
            add_grad(ws, p, j, side, dot_tn(act[...], grads[p, :, columns]))
        done((3,))

    def own_rows(rows):
        xr[rows] = xr[rows] + total[rows]
        xr2[rows] = xr2[rows] + back[rows]

    def other_rows(rows):
        return pl.ds(pl.multiple_of(rows.start + own, CHUNK), CHUNK)

    def back_low_rows(rows):
        h2[rows] = back[other_rows(rows)].astype(BF)

    def out_low_rows(rows):
        h2[other_rows(rows)] = total[other_rows(rows)].astype(BF)

    def back_sum_rows(rows):
        h2[rows] = (back[rows] + got_low[rows].astype(F32)).astype(BF)

    def out_sum_rows(rows):
        h2[other_rows(rows)] = (total[rows] + got_low[other_rows(rows)].astype(F32)).astype(BF)

    def between_passes():
        pair_h2.wait()
        swap_h2z.start()
        swap_mlp.wait()
        swap_gh2.wait()
        over_rows(own_rows)
        total[...] = jnp.zeros_like(total)
        back[...] = jnp.zeros_like(back)
        swap_gmz.wait()
        swap_h2z.wait()

    def start_pair_sums():
        over_rows(back_low_rows)
        swap_back_low.start()
        over_rows(out_low_rows)
        swap_out_low.start()

    def send_pair_sums():
        swap_back_low.wait()
        over_rows(back_sum_rows)
        send_back.start()
        swap_out_low.wait()
        over_rows(out_sum_rows)
        send_out.start()

    @pl.loop(0, 8)
    def _(t):
        p, j = t // 4, (t // 2 + t // 4) % 2
        s = (1 - j) * z + j * remote_slab

        @pl.when(t == 1)
        def _():
            pass_diagonal(mlp, 1)
            swap_h2.wait()

        @pl.when(t == 2)
        def _():
            finish_slab(mlp, 1)
            pair_gm.wait_recv()
            swap_gmz.start()

        @pl.when(t == 3)
        def _():
            swap_mlp.start()
            swap_gh2.start()

        @pl.when(t == 4)
        def _():
            between_passes()

        @pl.when(t == 7)
        def _():
            start_pair_sums()

        mlp_rows(
            s, j, (t + t // 2) % 2, normed.at[p], grads.at[p], we, ws, bias_e_of(s), act, gpre, total, back, bias_e, half
        )

        @pl.when(t == 7)
        def _():
            send_pair_sums()

        @pl.when(t % 2 == 1)
        def _():
            def done(group):
                @pl.when(t == 5)
                def _():
                    reduce_one(group, 1)

            weight_grads(p, j, done)

    sent_far(mlp)
    reduce_two(mlp, 1)
    reduce_one(mlp, 0)
    send_back.wait_recv()
    back_load = pltpu.make_async_copy(pair_back, gmz.at[rows_own], local.at[8])
    back_load.start()
    back_load.wait()

    pair_gm.wait_send()

    def middle_back_rows(rows):
        mid = middle[rows]
        grad_out = gm[rows].astype(F32)
        early[9:10, :] += column_sum(grad_out)
        grad = xr2[rows] + gmz[rows].astype(F32)
        xhat, inverse = normalize(mid)
        early[6:7, :] += column_sum(grad * xhat)
        early[7:8, :] += column_sum(grad)
        grad_mid = grad_out + norm_back(grad, gain_two, xhat, inverse)
        xr2[rows] = grad_mid
        low = grad_mid.astype(BF)
        gm[rows] = low
        early[8:9, :] += column_sum(low.astype(F32))

    over_rows(middle_back_rows)
    swap_ga.start()

    def result_rows(rows):
        valid = keep[rows]
        mlp_out = xr[rows] + gmz[other_rows(rows)].astype(F32) + shrink_bias
        result = middle[rows] + mlp_out
        h2[rows] = result.astype(BF)
        early[2:3, :] += column_sum(valid * result * result)
        early[4:5, :] += column_sum(valid * mlp_out * mlp_out)

    back[...] = jnp.zeros_like(back)
    for i in range(4):
        sent_slab(attn, i)
    reduce_three(mlp, 1)
    swap_ga.wait()

    out_load = pltpu.make_async_copy(pair_out, gmz.at[rows_other], local.at[8])

    def interleave(source, target):
        def move(stage):
            @pl.loop(0, SIDE)
            def _(i):
                places = [pl.multiple_of(w * WROWS + i * SIDE_PAD, SIDE_PAD) for w in range(stage.shape[1])]
                some = [source[pl.ds(at, SIDE_PAD)][:SIDE].astype(F32) for at in places]
                stage[pl.ds(i * SIDE, SIDE)] = jnp.stack(some, axis=1).astype(stage.dtype)

            store = pltpu.make_async_copy(stage, target, local.at[8])
            store.start()
            store.wait()

        pl.run_scoped(move, pltpu.VMEM(target.shape, target.dtype))

    def finish_result():
        send_back.wait_send()
        send_out.wait_recv()
        out_load.start()
        out_load.wait()
        over_rows(result_rows)

    stages = (partner,), (along_z(1), along_z(2), along_z(3)), (along_x, along_y, across), (partner,)
    early_sums = (((early, early_full, early_half),), 20)
    late_sums = (((late, late_full, late_half), (rel, rel_full, rel_half)), 28)

    def small_copies(sums, stage):
        pairs, base = sums
        first = (0, 1, 4, 7)[stage]
        for i, device in enumerate(stages[stage]):
            for q, (src, full, part) in enumerate(pairs):
                rows = part.shape[1]
                mine = pl.ds(pl.multiple_of(r * rows, rows), rows)
                index = base + (first + i) * len(pairs) + q
                if stage == 0:
                    yield src, full, slice(None), remote(src, full, csend, crecv, index, device)
                else:
                    got = part.at[first + i - 1]
                    yield src, got, mine, remote(src.at[mine], got, csend, crecv, index, device)

    def small_start(sums, stage):
        for _, _, _, copy in small_copies(sums, stage):
            copy.start()

    def small_finish(sums, stage):
        copies = list(small_copies(sums, stage))
        for _, _, _, copy in copies:
            copy.wait()
        for src, got, rows, _ in copies:
            if stage == 3:
                count = got.shape[0]
                src[pl.ds(pl.multiple_of((1 - r) * count, count), count)] = got[...]
            else:
                src[rows] += got[...]

    def on_side(act_on):
        for side in range(2):

            @pl.when(r == side)
            def _():
                act_on(side)

    def fill_early(side):
        for s in range(4):
            early[10 + s : 11 + s, side * half : (side + 1) * half] = bias_e[s]

    early_store = pltpu.make_async_copy(early, early_out, local.at[9])

    @pl.loop(0, 4)
    def _(n):
        s = slab_of(3 - n)
        g = slot(0, n)

        def half_done():
            @pl.when(n == 0)
            def _():
                reduce_two(mlp, 0)

            @pl.when(n == 1)
            def _():
                reduce_four((2,))

            @pl.when(n == 2)
            def _():
                small_finish(early_sums, 0)
                small_start(early_sums, 1)
                reduce_four((3,))

            @pl.when(n == 3)
            def _():
                swap_gh1.start()

        attention_back_slab(
            s, h1, gm, wq, wp, bias_q_of(s), rel_query, rel_back, codes, act, back, bias_q, rel_acc, heads, half, half_done
        )

        @pl.when(n > 0)
        def _():
            reduce_two(attn, n - 1)

        for side in range(2):
            columns = slice(side * half, side * half + half)
            wq[g, side] = dot_tn(act[:, :qkv_width], h1[:, columns]).astype(BF).reshape(wq.shape[2:])
            wp[g, side] = dot_tn(attended[s], gm[:, columns]).astype(BF).reshape(wp.shape[2:])
        reduce_one(attn, n)

        @pl.when((n > 1) & is_end)
        def _():
            reduce_three(attn, n - 2)

        @pl.when((n == 3) & is_inner)
        def _():
            reduce_three(attn, 0)

        @pl.when(n == 0)
        def _():
            reduce_three(mlp, 0)

        @pl.when(n == 1)
        def _():
            finish_result()
            on_side(fill_early)
            small_start(early_sums, 0)

    swap_gh1.wait()

    def input_rows(rows):
        value = tokens[rows].astype(F32)
        grad = (back[rows] + total[other_rows(rows)]) * keep[rows]
        xhat, inverse = normalize(value)
        for place, value in ((8, column_sum(grad * xhat)), (10, column_sum(grad))):
            late[place : place + 1, :] += value[:, :half]
            late[place + 1 : place + 2, :] += value[:, half:]
        xr2[rows] = xr2[rows] + norm_back(grad, gain_one, xhat, inverse)

    over_rows(input_rows)

    def fill_late(side):
        for s in range(4):
            late[2 * s + side : 2 * s + side + 1, :qkv_width] = bias_q[s]

    on_side(fill_late)
    for part, at in ((0, 0), (1, COL_W)):
        rows = slice(at, at + 32)
        rel[part * 32 : part * 32 + 32] = rel_acc[rows] + rel_acc[LANES + at : LANES + at + 32]

    small_start(late_sums, 0)

    @pl.when(is_inner)
    def _():
        reduce_three(attn, 1)

    small_finish(late_sums, 0)
    small_start(late_sums, 1)
    reduce_three(attn, 2)
    reduce_five((2,))
    reduce_two(attn, 3)
    reduce_five((3,))
    interleave(xr2, input_grad)
    interleave(h2, block_out)
    small_finish(early_sums, 1)
    small_start(early_sums, 2)
    reduce_three(attn, 3)
    reduce_four(attn)
    small_finish(late_sums, 1)
    small_start(late_sums, 2)
    reduce_six(mlp)
    small_finish(early_sums, 2)
    small_start(early_sums, 3)
    reduce_five(attn)
    small_finish(late_sums, 2)
    small_start(late_sums, 3)
    small_finish(early_sums, 3)
    early_store.start()
    small_finish(late_sums, 3)
    late_stores = [
        pltpu.make_async_copy(late, late_out, local.at[6]),
        pltpu.make_async_copy(rel, rel_out, local.at[7]),
    ]
    for copy in late_stores:
        copy.start()
    reduce_six(attn)

    swap_h1.wait_send()
    send_out.wait_send()
    for k in (1, 2, 3):
        bias_copy(k).wait_send()
    for a in range(4):
        for copy in swap_out(a) + keep_out(a):
            copy.wait()
        for kind in (1, 2, 3, 4):
            spread(a, kind).wait_send()
        for n in range(4 if a in attn else 2):
            for kind in range(4):
                reduce_copy(a, n, kind).wait_send()
            reduce_z(a, n, lambda copy: copy.wait_send())

    for copy in late_stores:
        copy.wait()
    early_store.wait()


def run_kernel(tokens, mask, out_grad, vectors, qkv_bias, expand_bias, rel_height, rel_width, sources):
    own, width = tokens.shape[1] * WROWS, tokens.shape[2]
    half = width // 2
    rows = [source.shape[-2] for source in sources]
    rows[0] = 3 * rows[0] // 2
    sds = jax.ShapeDtypeStruct
    any_spec = pl.BlockSpec(memory_space=pl.ANY)
    vmem_spec = pl.BlockSpec(memory_space=pltpu.VMEM)
    out_shape = [sds(tokens.shape, BF), sds(tokens.shape, F32)]
    out_shape += [sds(source.shape, BF) for source in sources]
    out_shape += [sds((16, width), F32), sds((16, half), F32), sds((64, LANES), F32)]
    first, second = zip(*[halves(n) for n in rows])
    out_shape += [sds((4, 2, n, half), BF) for n in first]
    out_shape += [sds((4, 2, n, half), BF) for n in second]
    out_shape += [sds((4, n, half), BF) for n in second]
    out_shape += [sds((4, n, half), BF) for n in first]
    out_shape += [sds((6, n, half), BF) for n in rows]
    out_shape += [sds((own, width), BF)] * 2
    both = 2 * own
    vmem, dma = pltpu.VMEM, pltpu.SemaphoreType.DMA
    qkv_width = 2 * rows[0]
    scratch = [vmem((count, 2, 2, n, half), BF) for count, n in zip((5, 5, 4, 4), rows)]
    scratch += [vmem((own, width), BF), vmem((own, 1), F32)]
    scratch += [vmem((both, width), BF)] + [vmem((2, both, width), BF)] * 2 + [vmem((both, width), BF)]
    scratch += [vmem((4, both, qkv_width // 3), BF)]
    scratch += [vmem((both, width), F32)] * 2
    scratch += [vmem((own, width), F32)] * 3
    scratch += [vmem((both, half), BF), vmem((both, half), BF)]
    scratch += [vmem((4, 8, width), F32), vmem((16, width), F32), vmem((16, width), F32), vmem((7, 8, width), F32)]
    scratch += [vmem((16, half), F32), vmem((16, half), F32), vmem((7, 8, half), F32)]
    scratch += [vmem((64, LANES), F32), vmem((64, LANES), F32), vmem((7, 32, LANES), F32)]
    scratch += [vmem((4, 1, half), F32), vmem((4, 1, qkv_width), F32), vmem((2 * LANES, LANES), F32)]
    scratch += [vmem((2 * LANES, LANES), BF), vmem((3 * LANES, LANES), BF), vmem((2, 32, HEAD), F32)]
    scratch += [dma((4, 4, 6))] * 2 + [dma((4, 4, 5)), dma((4, 4, 6))] + [dma((4, 5))] * 2 + [dma((44,))] * 2
    scratch += [dma((4,))] * 2 + [dma((8,))] * 2 + [dma((11,)), dma((4,))]
    got = pl.pallas_call(
        kernel,
        out_shape=out_shape,
        in_specs=[any_spec, vmem_spec, any_spec] + [vmem_spec] * 11 + [any_spec] * 4,
        out_specs=[any_spec] * len(out_shape),
        scratch_shapes=scratch,
        compiler_params=pltpu.CompilerParams(
            collective_id=0, has_side_effects=True, vmem_limit_bytes=VMEM_LIMIT
        ),
        name="block_step",
    )(tokens, mask, out_grad, *vectors, qkv_bias, expand_bias, rel_height, rel_width, key_codes(), *sources)
    return got[:9]


def finish_kernel(early, late, rel, *refs):
    wide, (bias_q, bias_e, height, width_out, rms), rows_out = refs[:6], refs[6:11], refs[11:17]
    outs, held, full, load, store = refs[17:23], refs[23:29], refs[29:33], refs[33], refs[34]
    z = lax.axis_index("col")
    loads = [pltpu.make_async_copy(src, to, load.at[i]) for i, (src, to) in enumerate(zip(wide, held))]
    full = list(full) + list(held[4:])
    stores = [pltpu.make_async_copy(src, to, store.at[i]) for i, (src, to) in enumerate(zip(full, outs))]
    for i in (3, 2, 5, 4, 0, 1):
        loads[i].start()
    features = early.shape[1]
    half = features // 2
    for ref, at in zip(rows_out[:2], (8, 10)):
        ref[:half] = late[at, :]
        ref[half:] = late[at + 1, :]
    for ref, at in zip(rows_out[2:], (6, 7, 8, 9)):
        ref[...] = early[at, :]
    lane = lax.broadcasted_iota(jnp.int32, (1, LANES), 1)
    stats = jnp.zeros((1, LANES), F32)
    for i in range(rms.shape[0]):
        stats = jnp.where(lane == i, jnp.sum(early[i : i + 1, :], axis=1, keepdims=True), stats)
    rms[...] = jnp.sqrt(stats / (early[5:6, 0:1] * features))[0, : rms.shape[0]]
    part = bias_q.shape[1] // 2
    bias_e[...] = early[pl.ds(10 + z, 1), :].reshape(features)
    for side in range(2):
        row = late[pl.ds(2 * z + side, 1), :]
        for i in range(2):
            bias_q[i : i + 1, side * part : (side + 1) * part] = row[:, 2 * i * part : (2 * i + 1) * part]
    count = height.shape[0]
    turn = lax.broadcasted_iota(jnp.int32, (32, 32), 0) + lax.broadcasted_iota(jnp.int32, (32, 32), 1) == count - 1
    turned = jnp.dot(turn.astype(F32), rel[:32], precision=lax.Precision.HIGHEST, preferred_element_type=F32)
    height[...] = turned[:count, :HEAD]
    width_out[...] = rel[32 : 32 + count, :HEAD]
    for i in (3, 2, 0, 1):
        loads[i].wait()
        step = held[i].shape[0] // 5

        @pl.loop(0, 5)
        def _(m):
            at = pl.ds(pl.multiple_of(m * step, step), step)
            full[i][at] = held[i][at].astype(F32)

        stores[i].start()
        for j in {3: (5,), 2: (4,)}.get(i, ()):
            loads[j].wait()
            stores[j].start()
    for copy in stores:
        copy.wait()


def finish_outputs(got, part):
    early, late, rel = got[6:9]
    grads = [value.reshape(-1, value.shape[-1]) for value in got[2:6]]
    width = early.shape[1]
    sds = jax.ShapeDtypeStruct
    any_spec = pl.BlockSpec(memory_space=pl.ANY)
    vmem_spec = pl.BlockSpec(memory_space=pltpu.VMEM)
    out_shape = [sds((2, 2 * part), F32), sds((width,), F32), sds((2 * SIDE - 1, HEAD), F32)]
    out_shape += [sds((2 * SIDE - 1, HEAD), F32), sds((5,), F32)] + [sds((width,), F32)] * 6
    final = [sds(value.shape, F32) for value in grads]
    out_shape += final + [sds(value.shape, value.dtype) for value in got[:2]]
    return pl.pallas_call(
        finish_kernel,
        out_shape=out_shape,
        in_specs=[vmem_spec] * 3 + [any_spec] * 6,
        out_specs=[vmem_spec] * 11 + [any_spec] * 6,
        scratch_shapes=[pltpu.VMEM(value.shape, value.dtype) for value in grads + list(got[:2]) + final]
        + [pltpu.SemaphoreType.DMA((6,))] * 2,
        compiler_params=pltpu.CompilerParams(vmem_limit_bytes=VMEM_LIMIT),
        name="finish",
    )(early, late, rel, *grads, *got[:2])


VMEM_LIMIT = 64 * 1024 * 1024 - 512 * 1024


def over_chips(
    tokens, valid_mask, out_grad, first_gain, first_shift, qkv_weight, qkv_bias, rel_height, rel_width,
    proj_weight, proj_bias, second_gain, second_shift, expand_weight, expand_bias, shrink_weight, shrink_bias,
):
    def turned(value):
        return value.transpose(1, 0, 2)

    rows, _, local_width = qkv_weight.shape
    part = local_width // 2
    hidden = expand_weight.shape[1] // 2
    qkv_src = qkv_weight.transpose(1, 2, 0).reshape(3, 2, part, rows)
    proj_src = proj_weight.reshape(2, 2, part // 2, proj_weight.shape[1])
    expand_src = expand_weight.reshape(2, rows // 2, 2 * hidden)
    shrink_src = shrink_weight.reshape(2, 2, hidden // 2, shrink_weight.shape[1])
    vectors = (first_gain, first_shift, second_gain, second_shift, proj_bias, shrink_bias)
    got = run_kernel(
        turned(tokens), valid_mask, turned(out_grad), vectors, qkv_bias, expand_bias, rel_height, rel_width,
        (qkv_src, proj_src, expand_src, shrink_src),
    )
    outs = finish_outputs(got, part)
    qkv_bias_sum, expand_bias_sum, height_sum, width_sum, rms = outs[:5]
    gain_one, shift_one, gain_two, shift_two, proj_bias_sum, shrink_bias_sum = outs[5:11]
    qkv_sum, proj_sum, expand_sum, shrink_sum, block_out, input_grad = outs[11:]
    return (
        turned(block_out),
        turned(input_grad),
        gain_one,
        shift_one,
        qkv_sum.reshape(3, local_width, rows).transpose(2, 0, 1),
        qkv_bias_sum,
        height_sum,
        width_sum,
        proj_sum.reshape(proj_weight.shape),
        proj_bias_sum,
        gain_two,
        shift_two,
        expand_sum.reshape(expand_weight.shape),
        expand_bias_sum,
        shrink_sum.reshape(shrink_weight.shape),
        shrink_bias_sum,
        rms,
    )


epsilon = 1e-06
highest = lax.Precision.HIGHEST


def layer_norm(values, norm_gain, norm_shift):
    center = values - jnp.mean(values, axis=-1, keepdims=True)
    spread = jnp.mean(center * center, axis=-1, keepdims=True)
    return center * lax.rsqrt(spread + epsilon) * norm_gain + norm_shift


def offset_table(span_size):
    positions = jnp.arange(span_size)
    offset = positions[:, None] - positions[None, :] + span_size - 1
    return (offset[:, :, None] == jnp.arange(2 * span_size - 1)[None, None, :]).astype(jnp.float32)


def attention_scores(
    query_rows, key_rows, rel_rows_table, rel_cols_table, onehot_table, span_size, scaling
):
    window_count, tokens_per, head_count, head_size = query_rows.shape
    rel_count = 2 * span_size - 1
    direct = (
        jnp.einsum("bthc,buhc->bhtu", query_rows, key_rows, preferred_element_type=jnp.float32)
        * scaling
    )
    query_float = query_rows.astype(jnp.float32)
    along_rows = jnp.einsum("bthc,jc->bhtj", query_float, rel_rows_table, precision=highest)
    along_cols = jnp.einsum("bthc,jc->bhtj", query_float, rel_cols_table, precision=highest)
    grid_rows = along_rows.reshape(window_count, head_count, span_size, span_size, rel_count)
    grid_cols = along_cols.reshape(window_count, head_count, span_size, span_size, rel_count)
    rel_rows = jnp.einsum("bhxyj,xkj->bhxyk", grid_rows, onehot_table, precision=highest)
    rel_cols = jnp.einsum("bhxyj,ywj->bhxyw", grid_cols, onehot_table, precision=highest)
    score_sum = direct.reshape(window_count, head_count, span_size, span_size, span_size, span_size)
    score_sum = score_sum + rel_rows[:, :, :, :, :, None] + rel_cols[:, :, :, :, None, :]
    return score_sum.reshape(window_count, head_count, tokens_per, tokens_per)


def relative_back(score_float, onehot_table, span_size):
    window_count, head_count, tokens_per, other_tokens = score_float.shape
    grid = score_float.reshape(window_count, head_count, span_size, span_size, span_size, span_size)
    rows_part = jnp.einsum("bhxykw,xkj->bhxyj", grid, onehot_table, precision=highest)
    cols_part = jnp.einsum("bhxykw,ywj->bhxyj", grid, onehot_table, precision=highest)
    return (
        rows_part.reshape(window_count, head_count, tokens_per, -1),
        cols_part.reshape(window_count, head_count, tokens_per, -1),
    )


def gather_weights(qkv_weight, proj_weight, expand_weight, shrink_weight):
    return (
        lax.all_gather(qkv_weight, "row", axis=0, tiled=True),
        lax.all_gather(proj_weight, "row", axis=1, tiled=True),
        lax.all_gather(expand_weight, "row", axis=0, tiled=True),
        lax.all_gather(shrink_weight, "row", axis=1, tiled=True),
    )


def gather_tokens(normed):
    return lax.all_gather(normed, "col", axis=0, tiled=True)


def gather_grads(grad_low):
    return lax.all_gather(grad_low, "col", axis=0, tiled=True)


def sum_branch(inputs_low, weight_full, own_windows):

    def term(first_row, row_count):
        return jnp.einsum(
            "btk,kd->btd", inputs_low, weight_full, preferred_element_type=jnp.float32
        )

    return lax.psum_scatter(
        term(jnp.int32(0), own_windows * lax.axis_size("col")),
        "col",
        scatter_dimension=0,
        tiled=True,
    )


def sum_input(grads_low, weight_full, own_windows):

    def term(first_row, row_count):
        return jnp.einsum("btk,dk->btd", grads_low, weight_full, preferred_element_type=jnp.float32)

    return lax.psum_scatter(
        term(jnp.int32(0), own_windows * lax.axis_size("col")),
        "col",
        scatter_dimension=0,
        tiled=True,
    )


def activate(values):
    return jax.nn.gelu(values, approximate=False)


def per_device(
    tokens,
    valid_mask,
    out_grad,
    first_gain,
    first_shift,
    qkv_weight,
    qkv_bias,
    rel_height,
    rel_width,
    proj_weight,
    proj_bias,
    second_gain,
    second_shift,
    expand_weight,
    expand_bias,
    shrink_weight,
    shrink_bias,
):
    span_size = (rel_height.shape[0] + 1) // 2
    head_size = rel_height.shape[1]
    local_width = qkv_weight.shape[2]
    head_count = local_width // head_size
    own_windows = tokens.shape[0]
    tokens_per = tokens.shape[1]
    model_width = tokens.shape[2]
    scaling = head_size ** (-0.5)
    onehot_table = offset_table(span_size)
    inputs = tokens.astype(jnp.float32)
    keep_mask = valid_mask.astype(jnp.float32)[:, :, None]

    def first_norm(values, norm_gain, norm_shift):
        return layer_norm(values, norm_gain, norm_shift) * keep_mask

    qkv_full, proj_full, expand_full, shrink_full = gather_weights(
        qkv_weight, proj_weight, expand_weight, shrink_weight
    )
    normed_first, first_back = jax.vjp(first_norm, inputs, first_gain, first_shift)
    first_all = gather_tokens(normed_first.astype(jnp.bfloat16))
    all_windows = first_all.shape[0]
    bias_rows = jnp.stack([qkv_bias[0], jnp.zeros_like(qkv_bias[0]), qkv_bias[1]])
    projected = (
        jnp.einsum("btd,dsk->btsk", first_all, qkv_full, preferred_element_type=jnp.float32)
        + bias_rows
    )
    projected = projected.astype(jnp.bfloat16)
    head_shape = (all_windows, tokens_per, head_count, head_size)
    query_low = projected[:, :, 0].reshape(head_shape)
    key_low = projected[:, :, 1].reshape(head_shape)
    value_low = projected[:, :, 2].reshape(head_shape)
    scores = attention_scores(
        query_low, key_low, rel_height, rel_width, onehot_table, span_size, scaling
    )
    top_score = jnp.max(scores, axis=-1, keepdims=True)
    log_total = top_score + jnp.log(jnp.sum(jnp.exp(scores - top_score), axis=-1, keepdims=True))
    probs_low = jnp.exp(scores - log_total).astype(jnp.bfloat16)
    attended = jnp.einsum(
        "bhtu,buhc->bthc", probs_low, value_low, preferred_element_type=jnp.float32
    )
    attended_low = attended.reshape(all_windows, tokens_per, local_width).astype(jnp.bfloat16)
    attn_out = sum_branch(attended_low, proj_full, own_windows) + proj_bias
    middle = inputs + attn_out
    normed_second, second_back = jax.vjp(layer_norm, middle, second_gain, second_shift)
    second_all = gather_tokens(normed_second.astype(jnp.bfloat16))
    hidden_pre = (
        jnp.einsum("btd,df->btf", second_all, expand_full, preferred_element_type=jnp.float32)
        + expand_bias
    )
    active_value, active_back = jax.vjp(activate, hidden_pre)
    hidden_low = active_value.astype(jnp.bfloat16)
    mlp_out = sum_branch(hidden_low, shrink_full, own_windows) + shrink_bias
    result = middle + mlp_out
    stat_terms = jnp.stack(
        [
            jnp.sum(keep_mask * inputs * inputs),
            jnp.sum(keep_mask * middle * middle),
            jnp.sum(keep_mask * result * result),
            jnp.sum(keep_mask * attn_out * attn_out),
            jnp.sum(keep_mask * mlp_out * mlp_out),
        ]
    )
    valid_count = jnp.sum(keep_mask)
    stat_total, count_total = lax.psum((stat_terms, valid_count), ("dp", "row", "col"))
    out_float = out_grad.astype(jnp.float32)
    qkv_full, proj_full, expand_full, shrink_full = gather_weights(
        qkv_weight, proj_weight, expand_weight, shrink_weight
    )
    mlp_grad_low = out_float.astype(jnp.bfloat16)
    shrink_bias_grad = jnp.sum(mlp_grad_low, axis=(0, 1), dtype=jnp.float32)
    mlp_grad_all = gather_grads(mlp_grad_low)
    shrink_grad_full = jnp.einsum(
        "btf,btd->fd", hidden_low, mlp_grad_all, preferred_element_type=jnp.float32
    )
    hidden_grad = jnp.einsum(
        "btd,fd->btf", mlp_grad_all, shrink_full, preferred_element_type=jnp.float32
    )
    pre_grad_low = active_back(hidden_grad)[0].astype(jnp.bfloat16)
    expand_bias_grad = jnp.sum(pre_grad_low, axis=(0, 1), dtype=jnp.float32)
    expand_grad_full = jnp.einsum(
        "btd,btf->df", second_all, pre_grad_low, preferred_element_type=jnp.float32
    )
    second_grad = sum_input(pre_grad_low, expand_full, own_windows)
    middle_part, second_gain_grad, second_shift_grad = second_back(second_grad)
    middle_grad = out_float + middle_part
    attn_grad_low = middle_grad.astype(jnp.bfloat16)
    proj_bias_grad = jnp.sum(attn_grad_low, axis=(0, 1), dtype=jnp.float32)
    attn_grad_all = gather_grads(attn_grad_low)
    proj_grad_full = jnp.einsum(
        "btk,btd->kd", attended_low, attn_grad_all, preferred_element_type=jnp.float32
    )
    attended_grad = jnp.einsum(
        "btd,kd->btk", attn_grad_all, proj_full, preferred_element_type=jnp.float32
    )
    attended_grad = attended_grad.astype(jnp.bfloat16).reshape(head_shape)
    scores_again = attention_scores(
        query_low, key_low, rel_height, rel_width, onehot_table, span_size, scaling
    )
    probs_float = jnp.exp(scores_again - log_total)
    probs_again = probs_float.astype(jnp.bfloat16)
    prob_grad = jnp.einsum(
        "bthc,buhc->bhtu", attended_grad, value_low, preferred_element_type=jnp.float32
    )
    value_grad = jnp.einsum(
        "bhtu,bthc->buhc", probs_again, attended_grad, preferred_element_type=jnp.float32
    )
    score_grad = probs_float * (
        prob_grad - jnp.sum(probs_float * prob_grad, axis=-1, keepdims=True)
    )
    score_low = score_grad.astype(jnp.bfloat16)
    rows_grad, cols_grad = relative_back(score_low.astype(jnp.float32), onehot_table, span_size)
    query_float = query_low.astype(jnp.float32)
    query_grad = (
        jnp.einsum("bhtu,buhc->bthc", score_low, key_low, preferred_element_type=jnp.float32)
        * scaling
    )
    query_grad = query_grad + jnp.einsum("bhtj,jc->bthc", rows_grad, rel_height, precision=highest)
    query_grad = query_grad + jnp.einsum("bhtj,jc->bthc", cols_grad, rel_width, precision=highest)
    key_grad = (
        jnp.einsum("bhtu,bthc->buhc", score_low, query_low, preferred_element_type=jnp.float32)
        * scaling
    )
    rel_height_grad = jnp.einsum("bhtj,bthc->jc", rows_grad, query_float, precision=highest)
    rel_width_grad = jnp.einsum("bhtj,bthc->jc", cols_grad, query_float, precision=highest)
    flat_shape = (all_windows, tokens_per, local_width)
    qkv_grad_low = jnp.stack(
        [
            query_grad.reshape(flat_shape),
            key_grad.reshape(flat_shape),
            value_grad.reshape(flat_shape),
        ],
        axis=2,
    ).astype(jnp.bfloat16)
    qkv_bias_grad = jnp.sum(qkv_grad_low[:, :, 0::2], axis=(0, 1), dtype=jnp.float32)
    qkv_grad_full = jnp.einsum(
        "btd,btsk->dsk", first_all, qkv_grad_low, preferred_element_type=jnp.float32
    )
    first_grad = sum_input(
        qkv_grad_low.reshape(all_windows, tokens_per, 3 * local_width),
        qkv_full.reshape(qkv_full.shape[0], 3 * local_width),
        own_windows,
    )
    input_part, first_gain_grad, first_shift_grad = first_back(first_grad)
    input_grad = middle_grad + input_part
    qkv_rows, proj_rows, expand_rows, shrink_rows = (
        lax.psum_scatter(qkv_grad_full, "row", scatter_dimension=0, tiled=True),
        lax.psum_scatter(proj_grad_full, "row", scatter_dimension=1, tiled=True),
        lax.psum_scatter(expand_grad_full, "row", scatter_dimension=0, tiled=True),
        lax.psum_scatter(shrink_grad_full, "row", scatter_dimension=1, tiled=True),
    )
    qkv_sum, proj_sum, expand_sum, shrink_sum = lax.psum(
        (qkv_rows, proj_rows, expand_rows, shrink_rows), "dp"
    )
    qkv_bias_sum, expand_bias_sum = lax.psum((qkv_bias_grad, expand_bias_grad), ("dp", "row"))
    (
        gain_one_sum,
        shift_one_sum,
        gain_two_sum,
        shift_two_sum,
        proj_bias_sum,
        shrink_bias_sum,
        height_sum,
        width_sum,
    ) = lax.psum(
        (
            first_gain_grad,
            first_shift_grad,
            second_gain_grad,
            second_shift_grad,
            proj_bias_grad,
            shrink_bias_grad,
            rel_height_grad,
            rel_width_grad,
        ),
        ("dp", "row", "col"),
    )
    rms = jnp.sqrt(stat_total / (count_total * model_width))
    return (
        result.astype(jnp.bfloat16),
        input_grad,
        gain_one_sum,
        shift_one_sum,
        qkv_sum,
        qkv_bias_sum,
        height_sum,
        width_sum,
        proj_sum,
        proj_bias_sum,
        gain_two_sum,
        shift_two_sum,
        expand_sum,
        expand_bias_sum,
        shrink_sum,
        shrink_bias_sum,
        rms,
    )


def choose(mesh):
    fits = tuple(mesh.shape[name] for name in ("dp", "row", "col")) == (4, 2, 4)
    return over_chips if fits else per_device


def solution(mesh):
    in_specs = (
        P(("dp", "row", "col"), None, None),
        P(("dp", "row", "col"), None),
        P(("dp", "row", "col"), None, None),
        P(),
        P(),
        P("row", None, "col"),
        P(None, "col"),
        P(),
        P(),
        P("col", "row"),
        P(),
        P(),
        P(),
        P("row", "col"),
        P("col"),
        P("col", "row"),
        P(),
    )
    out_specs = (
        P(("dp", "row", "col"), None, None),
        P(("dp", "row", "col"), None, None),
        P(),
        P(),
        P("row", None, "col"),
        P(None, "col"),
        P(),
        P(),
        P("col", "row"),
        P(),
        P(),
        P(),
        P("row", "col"),
        P("col"),
        P("col", "row"),
        P(),
        P(),
    )
    return jax.shard_map(
        choose(mesh), mesh=mesh, in_specs=in_specs, out_specs=out_specs, check_vma=False
    )
```

```python
import functools

import jax
import jax.numpy as jnp
import numpy as np
from jax import lax
from jax.experimental import pallas as pl
from jax.experimental.pallas import tpu as pltpu
from jax.sharding import PartitionSpec as P

BF = jnp.bfloat16
F32 = jnp.float32
LANES = 128
SIDE = 14
SIDE_PAD = 16
WROWS = SIDE * SIDE_PAD
HEAD = 80
AT_H = HEAD
AT_W = HEAD + SIDE
AT_MASK = HEAD + 2 * SIDE
COL_W = 64


def dot(a, b):
    return jnp.dot(a, b, preferred_element_type=F32)


def dot_nt(a, b):
    return lax.dot_general(a, b, (((1,), (1,)), ((), ())), preferred_element_type=F32)


def dot_tn(a, b):
    return lax.dot_general(a, b, (((0,), (0,)), ((), ())), preferred_element_type=F32)


def lane_ids():
    return lax.broadcasted_iota(jnp.int32, (WROWS, LANES), 1)


def row_ids():
    return lax.broadcasted_iota(jnp.int32, (WROWS, LANES), 0)


def key_codes():
    u = np.arange(WROWS)[:, None]
    lane = np.arange(LANES)[None, :]
    k, l = u // SIDE_PAD, u % SIDE_PAD
    height = lane - AT_H == k
    width = (lane - AT_W == l) & (l < SIDE)
    width_back = (AT_W + SIDE - 1 - lane == l) & (l < SIDE)
    plain = np.where(height | width, 1.0, 0.0)
    masked = np.where((lane == AT_MASK) & (l >= SIDE), -1e30, plain)
    back = np.where(height | width_back, 1.0, 0.0)
    return np.stack([masked, plain, back]).astype(BF)


def split_low(values):
    high = values.astype(BF)
    return high, (values - high.astype(F32)).astype(BF)


def relative_tables(rel_h, rel_w, rel_query, rel_back):
    count, rows = 2 * SIDE - 1, rel_h.shape[0]
    offset = lax.broadcasted_iota(jnp.int32, (rows, LANES), 0)
    lane = lax.broadcasted_iota(jnp.int32, (rows, LANES), 1)

    def places(first, step):
        return jnp.where((lane == first + step * offset) & (offset < count), 1.0, 0.0).astype(BF)

    heights, widths = places(count - 1, -1), places(COL_W + count - 1, -1)
    widths_back = places(COL_W, 1)
    tall, wide = rel_h[...], rel_w[...]
    rel_query[...] = jnp.zeros_like(rel_query)
    rel_back[...] = jnp.zeros_like(rel_back)
    for part, (a, b) in enumerate(zip(split_low(tall * HEAD**0.5), split_low(wide * HEAD**0.5))):
        at = part * LANES
        rel_query[at : at + HEAD] = (dot_tn(a, heights) + dot_tn(b, widths)).astype(BF)
    for part, (a, b) in enumerate(zip(split_low(tall), split_low(wide))):
        table = (dot_tn(heights, a) + dot_tn(widths_back, b)).astype(BF)
        for place in ((0, 1), (2,))[part]:
            rel_back[place * LANES : (place + 1) * LANES, :HEAD] = table


def query_codes(query, rel_query):
    full = dot(jnp.concatenate([query, query], axis=1), rel_query)
    tiles = full.reshape(SIDE, SIDE_PAD, LANES)
    heights = jnp.concatenate(
        [pltpu.roll(tiles[i], AT_H - (SIDE - 1 - i), 1) for i in range(SIDE)], axis=0
    )
    widths = pltpu.roll(
        tiles, AT_W - COL_W - (SIDE - 1), 2, stride=1, stride_axis=1
    ).reshape(WROWS, LANES)
    lane = lane_ids()
    codes = jnp.where(
        (lane >= AT_H) & (lane < AT_W),
        heights,
        jnp.where((lane >= AT_W) & (lane < AT_MASK), widths, 0.0),
    )
    high, rest = split_low(codes)
    first = query + high + jnp.where(lane == AT_MASK, 1.0, 0.0).astype(BF)
    return jnp.concatenate([first, rest], axis=1)


def softmax_rows(query, key, rel_query, codes_ref):
    left = query_codes(query, rel_query)
    right = jnp.concatenate([key + codes_ref[0], codes_ref[1]], axis=1)
    scores = dot_nt(left, right)
    top = jnp.max(scores, axis=1, keepdims=True)
    weights = jnp.exp((scores - top) * (HEAD**-0.5))
    return weights / jnp.sum(weights, axis=1, keepdims=True)


def attend(query, key, value, rel_query, codes_ref):
    probs = softmax_rows(query, key, rel_query, codes_ref)
    return dot(probs.astype(BF), value)


def attend_back(query, key, value, grad, rel_query, rel_back, codes_ref):
    probs = softmax_rows(query, key, rel_query, codes_ref)
    prob_grad = dot_nt(grad, value)
    inner = jnp.sum(probs * prob_grad, axis=1, keepdims=True)
    score_low = (probs * (prob_grad - inner)).astype(BF)
    value_grad = dot_tn(probs.astype(BF), grad)
    key_grad = dot_tn(score_low, query) * (HEAD**-0.5)
    mixed = dot(score_low, key + codes_ref[2])
    tiles = mixed.reshape(SIDE, SIDE_PAD, LANES)
    heights = jnp.concatenate(
        [pltpu.roll(tiles[i], (SIDE - 1 - i - AT_H) % LANES, 1) for i in range(SIDE)], axis=0
    )
    widths = pltpu.roll(
        tiles, (COL_W - AT_W) % LANES, 2, stride=1, stride_axis=1
    ).reshape(WROWS, LANES)
    lane, row = lane_ids(), row_ids()
    first_h = SIDE - 1 - row // SIDE_PAD
    first_w = COL_W + row % SIDE_PAD
    offsets = jnp.where(
        (lane >= first_h) & (lane < first_h + SIDE),
        heights,
        jnp.where((lane >= first_w) & (lane < first_w + SIDE), widths, 0.0),
    )
    high, rest = split_low(offsets)
    query_grad = jnp.where(lane < HEAD, mixed, 0.0) * (HEAD**-0.5) + dot(
        jnp.concatenate([high, rest, high], axis=1), rel_back
    )
    rel_grad = dot_tn(jnp.concatenate([high, rest], axis=1), query)
    return query_grad, key_grad, value_grad, rel_grad


def pad_head(piece):
    return jnp.concatenate([piece, jnp.zeros((piece.shape[0], LANES - HEAD), piece.dtype)], axis=1)


def qkv_low(s, rows, h1, wq, bias, half):
    return (dot_nt(h1[rows, :half], block(wq, s, 0)) + dot_nt(h1[rows, half:], block(wq, s, 1)) + bias).astype(BF)


def head_of(low, part, heads, hh):
    at = (part * heads + hh) * HEAD
    return pad_head(low[:, at : at + HEAD])


def attention_slab(s, h1, wq, wp, bias, rel_query, codes, attended, total, heads, half, half_done):
    count = h1.shape[0] // WROWS

    @pl.loop(0, count)
    def _(m):
        rows = pl.ds(pl.multiple_of((m + count // 2) % count * WROWS, WROWS), WROWS)
        low = qkv_low(s, rows, h1, wq, bias, half)
        outs = []
        for hh in range(heads):
            query, key, value = (head_of(low, part, heads, hh) for part in range(3))
            outs.append(attend(query, key, value, rel_query[...], codes)[:, :HEAD])
        out_low = jnp.concatenate(outs, axis=1).astype(BF)
        attended[s, rows] = out_low
        total[rows, :half] += dot(out_low, block(wp, s, 0))
        total[rows, half:] += dot(out_low, block(wp, s, 1))

        @pl.when(m == count // 2 - 1)
        def _():
            half_done()


SQRT_HALF = 0.5**0.5
PDF_SCALE = 0.3989422804014327


def both_blocks(ref, slab):
    value = ref[slab]
    return value.reshape(4 * value.shape[2], value.shape[3])


def mlp_rows(s, place, m, h2, gm, we, ws, bias, act, gpre, total, back, bias_grad, half):
    count = h2.shape[0] // 2

    @pl.loop(0, 1)
    def _(step):
        rows = pl.ds(pl.multiple_of((m + step) * count, count), count)
        pre = dot(h2[rows, :], both_blocks(we, place)) + bias
        cdf = 0.5 + 0.5 * lax.erf(pre * SQRT_HALF)
        slope = cdf + pre * (PDF_SCALE * jnp.exp(-0.5 * pre * pre))
        act_low = (pre * cdf).astype(BF)
        act[rows, :] = act_low
        hidden = dot_nt(gm[rows, :half], block(ws, place, 0)) + dot_nt(gm[rows, half:], block(ws, place, 1))
        gpre_low = (hidden * slope).astype(BF)
        gpre[rows, :] = gpre_low
        bias_grad[s] += jnp.sum(gpre_low.astype(F32), axis=0, keepdims=True)
        total[rows, :half] += dot(act_low, block(ws, place, 0))
        total[rows, half:] += dot(act_low, block(ws, place, 1))
        back[rows, :] += dot_nt(gpre_low, both_blocks(we, place))


def attention_back_slab(
    s, h1, ga, wq, wp, bias, rel_query, rel_back, codes, gqkv, back, bias_grad, rel_grad, heads, half, half_done
):
    count = h1.shape[0] // WROWS

    @pl.loop(0, count)
    def _(m):
        rows = pl.ds(pl.multiple_of((m + count // 2) % count * WROWS, WROWS), WROWS)
        low = qkv_low(s, rows, h1, wq, bias, half)
        grad = (dot_nt(ga[rows, :half], block(wp, s, 0)) + dot_nt(ga[rows, half:], block(wp, s, 1))).astype(BF)
        parts = [[], [], []]
        for hh in range(heads):
            query, key, value = (head_of(low, part, heads, hh) for part in range(3))
            got = attend_back(
                query, key, value, head_of(grad, 0, heads, hh), rel_query[...], rel_back[...], codes
            )
            for part in range(3):
                parts[part].append(got[part][:, :HEAD])
            rel_grad[...] += got[3]
        grad_low = jnp.concatenate(parts[0] + parts[1] + parts[2], axis=1).astype(BF)
        gqkv[rows, : grad_low.shape[1]] = grad_low
        bias_grad[s] += jnp.sum(grad_low.astype(F32), axis=0, keepdims=True)
        back[rows, :half] += dot(grad_low, block(wq, s, 0))
        back[rows, half:] += dot(grad_low, block(wq, s, 1))

        @pl.when(m == count // 2 - 1)
        def _():
            half_done()


MESH_ID = pl.DeviceIdType.MESH
ARRAYS = ("qkv", "proj", "expand", "shrink")
CHUNK = 64
EPS = 1e-06
SPARE = 4


def halves(rows):
    first = (rows // 16 + 1) // 4 * 32
    return first, rows - first


def flip(index, k):
    return ((index // 2 + k // 2) % 2) * 2 + (index % 2 + k % 2) % 2


def block(ref, slab, half):
    value = ref[slab, half]
    return value.reshape(value.shape[0] * value.shape[1], value.shape[2])


def add_low(target, index, extra):
    target[index] = (target[index].astype(F32) + extra.astype(F32)).astype(BF)


def kernel(
    tokens_in, mask_in, out_grad_in, gain_one_in, shift_one_in, gain_two_in, shift_two_in, proj_bias_in, shrink_bias_in,
    qkv_bias_in, expand_bias_in, rel_h_in, rel_w_in, codes, qkv_src, proj_src, expand_src, shrink_src,
    block_out, input_grad, qkv_out, proj_out, expand_out, shrink_out, early_out, late_out, rel_out,
    rxq, rxp, rxe, rxs, ryq, ryp, rye, rys, rx2q, rx2p, rx2e, rx2s, ry2q, ry2p, ry2e, ry2s, rzq, rzp, rze, rzs, pair_back, pair_out,
    wq, wp, we, ws, tokens, keep, h1, grads, normed, got_low, attended, total, back, xr, xr2, middle, act, gpre,
    bias_all, early, early_full, early_half, late, late_full, late_half, rel, rel_full, rel_half, bias_e, bias_q, rel_acc, rel_query, rel_back, rel_pad,
    gsend, grecv, rsend, rrecv, fsend, frecv, csend, crecv, zsend, zrecv, qsend, qrecv, local, qlocal,
):
    d, r, z = lax.axis_index("dp"), lax.axis_index("row"), lax.axis_index("col")
    h, b = d // 2, d % 2
    own = tokens.shape[0]
    width = tokens.shape[1]
    half = width // 2
    heads = 2
    bufs = (wq, wp, we, ws)
    outs = (qkv_out, proj_out, expand_out, shrink_out)
    rx, ry = (rxq, rxp, rxe, rxs), (ryq, ryp, rye, rys)
    rx2, ry2 = (rx2q, rx2p, rx2e, rx2s), (ry2q, ry2p, ry2e, ry2s)
    rz = (rzq, rzp, rze, rzs)
    parts = [halves(buf.shape[3]) for buf in bufs]
    attn, mlp = (0, 1), (2, 3)
    qkv_width = 3 * attended.shape[2]

    along_x = (h * 2 + 1 - b, r, z)
    along_y = ((1 - h) * 2 + b, r, z)
    across = ((1 - h) * 2 + 1 - b, r, z)
    partner = (d, 1 - r, z)
    pair, remote_slab = (d, r, flip(z, 1)), flip(z, 2)
    gm, gmz, h2, h2z = grads.at[0], grads.at[1], normed.at[0], normed.at[1]

    def along_z(k):
        return (d, r, flip(z, k))

    def remote(src, dst, sems, recvs, index, device, got=None):
        return pltpu.make_async_remote_copy(
            src_ref=src,
            dst_ref=dst,
            send_sem=sems.at[index],
            recv_sem=recvs.at[index if got is None else got],
            device_id=device,
            device_id_type=MESH_ID,
        )

    up = z // 2
    is_end = (z + 1) // 2 % 2 == 0
    is_inner = (z + 1) // 2 % 2 == 1

    def slab_of(i):
        far = i // 2
        return (1 - far) * flip(z, i) + far * ((1 - up) * i + up * (3 - i))

    def first_part(a):
        return pl.ds(0, parts[a][0])

    def second_part(a):
        return pl.ds(parts[a][0], parts[a][1])

    def gather_z(a, s, step):
        at = bufs[a].at[s, h, b]
        return remote(at, at, gsend, grecv, (a, s, 0 if step < 0 else 5), (d, r, z + step), (a, s, 0))

    def gather_far(a):
        return remote(bufs[a].at[0, h, b], bufs[a].at[1, h, b], gsend, grecv, (a, 0, 0), (d, r, remote_slab))

    def ring(a, slab, sends, recvs, index, kind, arriving):
        buf = bufs[a]
        if kind == 1:
            at, device = (buf.at[slab, h, 1 - b] if arriving else buf.at[slab, h, b]), along_x
        elif kind == 2:
            at, device = (buf.at[slab, 1 - h, b] if arriving else buf.at[slab, h, b]), along_y
        elif kind == 3:
            at = buf.at[slab, 1 - h if arriving else h, 1 - b, first_part(a)]
            device = along_y
        else:
            at = buf.at[slab, 1 - h, 1 - b if arriving else b, second_part(a)]
            device = along_x
        return remote(at, at, sends, recvs, index, device)

    def gather(a, s, kind, arriving=False):
        return ring(a, s, gsend, grecv, (a, s, kind), kind, arriving)

    def spread(a, kind, arriving=False):
        return ring(a, final_slot(a), fsend, frecv, (a, kind), kind, arriving)

    def sends_along_z(group, s, act_on):
        for a in group:

            @pl.when((s >= z) & (z > 0))
            def _():
                act_on(gather_z(a, s, -1))

            @pl.when((s <= z) & (z < 3))
            def _():
                act_on(gather_z(a, s, 1))

    def start_z(group):
        sends_along_z(group, z, lambda copy: copy.start())

    def relay(group, i):
        s = slab_of(i)
        for a in group:
            gather_z(a, s, 1).wait_recv()
            sends_along_z((a,), s, lambda copy: copy.start())

    def place_of(a, i):
        return slab_of(i) if a in attn else 1

    def share(group, i):
        for a in group:
            gather(a, place_of(a, i), 1).start()
            gather(a, place_of(a, i), 2).start()

    def share_far(group):
        for a in group:
            gather_far(a).wait_recv()
            share((a,), 1)

    def pass_diagonal(group, i):
        for a in group:
            s = place_of(a, i)
            gather(a, s, 1, True).wait_recv()
            gather(a, s, 3).start()
            gather(a, s, 2, True).wait_recv()
            gather(a, s, 4).start()

    def finish_slab(group, i):
        for a in group:
            s = place_of(a, i)
            gather(a, s, 3, True).wait_recv()
            gather(a, s, 4, True).wait_recv()

    def sent_slab(group, i):
        s = slab_of(i)
        sends_along_z(group, s, lambda copy: copy.wait_send())
        for a in group:

            @pl.when(i > 0)
            def _():
                for kind in (1, 2, 3, 4):
                    gather(a, s, kind).wait_send()

    def sent_far(group):
        for a in group:
            gather_far(a).wait_send()
            for kind in (1, 2, 3, 4):
                gather(a, 1, kind).wait_send()

    def step_slab(n):
        return slab_of(3 - n)

    def final_slot(a):
        return z if a in attn else 0

    def slot(a, n):
        if a in mlp:
            return 2 + n
        first = (4 - n) // 4
        return first * SPARE + (1 - first) * step_slab(n - 1 + first)

    def reduce_copy(a, n, kind):
        buf, g = bufs[a], slot(a, n)
        got = None
        if kind == 0:
            src, dst, device = buf.at[g, :, 1 - b, first_part(a)], rx[a].at[n], along_x
        elif kind == 1:
            src, dst, device = buf.at[g, 1 - h, :, second_part(a)], ry[a].at[n], along_y
        elif kind == 2:
            src, dst, device = buf.at[g, 1 - h, b, first_part(a)], ry2[a].at[n], along_y
        elif kind == 3:
            src, dst, device = buf.at[g, h, 1 - b, second_part(a)], rx2[a].at[n], along_x
        elif kind == 4 and a in mlp:
            src, dst, device = buf.at[g, h, b], rz[a].at[0], (d, r, remote_slab)
            got = (a, 0, 4)
        elif kind == 4:
            src, dst, device = buf.at[g, h, b], rz[a].at[z], (d, r, step_slab(n))
            got = (a, z, 4)
        else:
            src, dst, device = buf.at[g, h, b], rz[a].at[5 - n], (d, r, slab_of(1))
            got = (a, 3 - n, 5)
        return remote(src, dst, rsend, rrecv, (a, n, min(kind, 4)), device, got)

    def reduce_z(a, n, act_on):
        if a in mlp:

            @pl.when(n == 1)
            def _():
                act_on(reduce_copy(a, n, 4))

        else:

            @pl.when((n < 3) & (is_inner | (n == 2)))
            def _():
                act_on(reduce_copy(a, n, 4))

            @pl.when(is_end & (n < 2))
            def _():
                act_on(reduce_copy(a, n, 5))

    def reduce_one(group, n):
        for a in group:
            reduce_copy(a, n, 0).start()
            reduce_copy(a, n, 1).start()

    def with_room(body):
        def run(group, n):
            shape = (2 * len(group), 2, halves(max(bufs[a].shape[3] for a in group))[0], half)
            pl.run_scoped(
                lambda room: body(group, n, lambda a, place: room.at[2 * group.index(a) + place]),
                pltpu.VMEM(shape, BF),
            )

        return run

    def reduce_two_body(group, n, scratch):
        loads = []
        for a in group:
            reduce_copy(a, n, 0).wait_recv()
            reduce_copy(a, n, 1).wait_recv()
            for place, got in enumerate((rx[a], ry[a])):
                to = scratch(a, place).at[:, pl.ds(0, parts[a][place])]
                loads.append(pltpu.make_async_copy(got.at[n], to, local.at[a * 2 + place]))
                loads[-1].start()
        for i, a in enumerate(group):
            g = slot(a, n)
            first, second = parts[a]
            loads[2 * i].wait()
            for side in range(2):
                add_low(bufs[a], (g, side, b, first_part(a)), scratch(a, 0)[side, :first])
            reduce_copy(a, n, 2).start()
            loads[2 * i + 1].wait()
            for side in range(2):
                add_low(bufs[a], (g, h, side, second_part(a)), scratch(a, 1)[side, :second])
            reduce_copy(a, n, 3).start()

    def reduce_three_body(group, n, scratch):
        loads = []
        for a in group:
            reduce_copy(a, n, 2).wait_recv()
            reduce_copy(a, n, 3).wait_recv()
            for place, got in enumerate((ry2[a], rx2[a])):
                to = scratch(a, place).at[0, pl.ds(0, parts[a][place])]
                loads.append(pltpu.make_async_copy(got.at[n], to, local.at[a * 2 + place]))
                loads[-1].start()
        for i, a in enumerate(group):
            g = slot(a, n)
            first, second = parts[a]
            loads[2 * i].wait()
            add_low(bufs[a], (g, h, b, first_part(a)), scratch(a, 0)[0, :first])
            loads[2 * i + 1].wait()
            add_low(bufs[a], (g, h, b, second_part(a)), scratch(a, 1)[0, :second])

            @pl.when(is_inner & (n < 2) & (a in attn))
            def _():
                at = rz[a].at[5 - n]
                remote(at, at, rsend, rrecv, (a, n, 4), (d, r, slab_of(1)), (a, 3 - n, 5)).wait_recv()
                pieces = ((0, first, first_part(a)), (1, second, second_part(a)))
                copies = [
                    pltpu.make_async_copy(at.at[part], scratch(a, 0).at[side, pl.ds(0, count)], local.at[a * 2 + side])
                    for side, count, part in pieces
                ]
                for copy in copies:
                    copy.start()
                for copy, (side, count, part) in zip(copies, pieces):
                    copy.wait()
                    add_low(bufs[a], (g, h, b, part), scratch(a, 0)[side, :count])

            reduce_z(a, n, lambda copy: copy.start())

    def reduce_two(group, n):
        with_room(reduce_two_body)(group, n)

    def reduce_three(group, n):
        with_room(reduce_three_body)(group, n)

    def reduce_four(group):
        for a in group:
            rows = bufs[a].shape[3]
            loads = []
            others = ((remote_slab, 0),) if a in mlp else [(slab_of(k), slab_of(k)) for k in (1, 2)]
            for k, (other, place) in enumerate(others, 1):
                at = rz[a].at[place]
                remote(at, at, rsend, rrecv, (a, k, 4), (d, r, other), (a, place, 4)).wait_recv()
                loads.append(pltpu.make_async_copy(at, gpre.at[pl.ds((k - 1) * rows, rows)], local.at[k]))
                loads[-1].start()
            for load in loads:
                load.wait()
            value = bufs[a][slot(a, 0 if a in mlp else 3), h, b].astype(F32)
            for k in range(len(others)):
                value = value + gpre[k * rows : (k + 1) * rows].astype(F32)
            bufs[a][final_slot(a), h, b] = value.astype(BF)
            spread(a, 1).start()
            spread(a, 2).start()

    def reduce_five(group):
        for a in group:
            spread(a, 1, True).wait_recv()
            spread(a, 3).start()
            spread(a, 2, True).wait_recv()
            spread(a, 4).start()

    def qkv_pieces(matrix, side, flat):
        rows = flat.shape[1]
        part = matrix.shape[2]
        cut = rows - part
        return (
            (matrix.at[0, side], flat.at[0, pl.ds(0, part)]),
            (matrix.at[1, side, pl.ds(0, cut)], flat.at[0, pl.ds(part, cut)]),
            (matrix.at[1, side, pl.ds(cut, part - cut)], flat.at[1, pl.ds(0, part - cut)]),
            (matrix.at[2, side], flat.at[1, pl.ds(part - cut, part)]),
        )

    def swap_out(a):
        mine = bufs[a].at[final_slot(a), 1 - r]
        if a == 0:
            pairs = qkv_pieces(outs[a], r, mine)
            return [remote(src, dst, qsend, qrecv, 4 + i, partner) for i, (dst, src) in enumerate(pairs)]
        to = outs[a].at[:, :, half_lanes(r)] if a == 2 else outs[a].at[r]
        return [remote(mine, to, fsend, frecv, (a, 0), partner)]

    def keep_out(a):
        mine = bufs[a].at[final_slot(a), r]
        if a == 0:
            pairs = qkv_pieces(outs[a], r, mine)
            return [pltpu.make_async_copy(src, dst, qlocal.at[i]) for i, (dst, src) in enumerate(pairs)]
        to = outs[a].at[:, :, half_lanes(r)] if a == 2 else outs[a].at[r]
        return [pltpu.make_async_copy(mine, to, local.at[a])]

    def reduce_six(group):
        for a in group:
            spread(a, 3, True).wait_recv()
            spread(a, 4, True).wait_recv()
            for copy in swap_out(a) + keep_out(a):
                copy.start()

    def half_lanes(side):
        return pl.ds(pl.multiple_of(side * half, half), half)

    def exchange(index, src, dst):
        return remote(src, dst, csend, crecv, index, partner)

    rows_own, rows_other = pl.ds(0, own), pl.ds(own, own)
    def source(a, side):
        if a == 2:
            return expand_src.at[:, :, half_lanes(side)]
        return (qkv_src, proj_src, expand_src, shrink_src)[a].at[side]

    def source_swap(a):
        to = bufs[a].at[z if a in attn else 0, r]
        if a == 0:
            pairs = qkv_pieces(qkv_src, 1 - r, to)
            return [remote(src, dst, qsend, qrecv, i, partner) for i, (src, dst) in enumerate(pairs)]
        return [exchange(a, source(a, 1 - r), to)]

    def source_keep(a):
        to = bufs[a].at[z if a in attn else 0, r]
        if a == 0:
            pairs = qkv_pieces(qkv_src, r, to)
            return [pltpu.make_async_copy(src, dst, qlocal.at[i]) for i, (src, dst) in enumerate(pairs)]
        return [pltpu.make_async_copy(source(a, r), to, local.at[a])]

    def start_source(group):
        for a in group:
            for copy in source_swap(a) + source_keep(a):
                copy.start()

    def finish_source(group):
        for a in group:
            for copy in source_swap(a) + source_keep(a):
                copy.wait()

    swap_grad = exchange(4, gm.at[rows_own], gm.at[rows_other])
    swap_h1 = exchange(5, h1.at[rows_own], h1.at[rows_other])
    swap_attn = exchange(6, total.at[rows_other], xr)
    swap_h2 = exchange(7, h2.at[rows_own], h2.at[rows_other])
    swap_mlp = exchange(8, total.at[rows_other], xr)
    swap_gh2 = exchange(9, back.at[rows_other], xr2)
    swap_ga = exchange(10, gm.at[rows_own], gm.at[rows_other])
    swap_gh1 = exchange(11, back.at[rows_other], total.at[rows_other])
    pair_gm = remote(gm.at[rows_own], gmz.at[rows_own], csend, crecv, 12, pair)
    swap_gmz = exchange(13, gmz.at[rows_own], gmz.at[rows_other])
    pair_h2 = remote(h2.at[rows_own], h2z.at[rows_own], csend, crecv, 14, pair)
    swap_h2z = exchange(15, h2z.at[rows_own], h2z.at[rows_other])
    swap_back_low = exchange(16, h2.at[rows_own], got_low.at[rows_own])
    swap_out_low = exchange(17, h2.at[rows_other], got_low.at[rows_other])
    send_back = remote(h2.at[rows_own], pair_back, csend, crecv, 18, pair)
    send_out = remote(h2.at[rows_other], pair_out, csend, crecv, 19, pair)

    def bias_copy(k, arriving=False):
        at = bias_all.at[flip(z, k) if arriving else z]
        return remote(at, at, zsend, zrecv, k, along_z(k))

    barrier = pltpu.get_barrier_semaphore()
    peers = [partner, along_x, along_y, across, along_z(1), along_z(2), along_z(3)]
    for peer in peers:
        pl.semaphore_signal(barrier, inc=1, device_id=peer, device_id_type=MESH_ID)
    pl.semaphore_wait(barrier, len(peers))

    start_source(attn)
    bias_all[z] = jnp.zeros(bias_all.shape[1:], F32)
    part = qkv_bias_in.shape[1] // 2
    for side in range(2):

        @pl.when(r == side)
        def _():
            bias_all[z, 0:1, :half] = expand_bias_in[side * half : (side + 1) * half].reshape(1, half)
            for i in range(2):
                at = half + 2 * i * part
                bias_all[z, 0:1, at : at + part] = qkv_bias_in[i : i + 1, side * part : (side + 1) * part]

    finish_source(attn)
    start_z(attn)
    for k in (1, 2, 3):
        bias_copy(k).start()
    start_source(mlp)

    def as_row(ref):
        return ref[...].reshape(1, width)

    gain_one, shift_one, gain_two, shift_two, proj_bias, shrink_bias = (
        as_row(ref) for ref in (gain_one_in, shift_one_in, gain_two_in, shift_two_in, proj_bias_in, shrink_bias_in)
    )

    def over_rows(body):
        @pl.loop(0, own // CHUNK)
        def _(m):
            body(pl.ds(pl.multiple_of(m * CHUNK, CHUNK), CHUNK))

    def column_sum(value):
        return jnp.sum(value, axis=0, keepdims=True)

    def normalize(value):
        center = value - jnp.mean(value, axis=1, keepdims=True)
        inverse = lax.rsqrt(jnp.mean(center * center, axis=1, keepdims=True) + EPS)
        return center * inverse, inverse

    def norm_back(grad, gain, xhat, inverse):
        scaled = grad * gain
        mean = jnp.mean(scaled, axis=1, keepdims=True)
        along = jnp.mean(scaled * xhat, axis=1, keepdims=True)
        return (scaled - mean - xhat * along) * inverse

    early[...] = jnp.zeros_like(early)
    late[...] = jnp.zeros_like(late)

    def spread_rows(source, target):
        def move(stage):
            load = pltpu.make_async_copy(source, stage, local.at[8])
            load.start()
            load.wait()

            @pl.loop(0, SIDE)
            def _(i):
                both = stage[pl.ds(i * SIDE, SIDE)].astype(F32)
                for w in range(both.shape[1]):
                    some = jnp.concatenate([both[:, w], jnp.zeros((SIDE_PAD - SIDE, width), F32)], axis=0)
                    at = pl.multiple_of(w * WROWS + i * SIDE_PAD, SIDE_PAD)
                    target[pl.ds(at, SIDE_PAD)] = some.astype(BF)

        pl.run_scoped(move, pltpu.VMEM(source.shape, BF))

    spread_rows(tokens_in, tokens)
    count = mask_in.shape[0]
    mask = jnp.concatenate([mask_in[...].astype(F32), jnp.zeros((count, 2 * LANES - SIDE * SIDE), F32)], axis=1)
    mask = jnp.concatenate([mask, jnp.zeros((8 - count, 2 * LANES), F32)], axis=0).T
    keep[...] = jnp.zeros_like(keep)
    for i in range(SIDE):
        for w in range(count):
            at = w * WROWS + i * SIDE_PAD
            keep[at : at + SIDE] = mask[i * SIDE : (i + 1) * SIDE, w : w + 1]

    def first_rows(rows):
        value = tokens[rows].astype(F32)
        valid = keep[rows]
        xhat, _ = normalize(value)
        h1[rows] = ((xhat * gain_one + shift_one) * valid).astype(BF)
        early[0:1, :] += column_sum(valid * value * value)
        early[5:6, :] += jnp.broadcast_to(column_sum(valid), (1, width))

    over_rows(first_rows)
    swap_h1.start()
    spread_rows(out_grad_in, gm)
    swap_grad.start()
    rel_pad[...] = jnp.zeros_like(rel_pad)
    rel_pad[0, : rel_h_in.shape[0]] = rel_h_in[...]
    rel_pad[1, : rel_w_in.shape[0]] = rel_w_in[...]
    relative_tables(rel_pad.at[0], rel_pad.at[1], rel_query, rel_back)
    total[...] = jnp.zeros_like(total)
    swap_h1.wait_recv()

    def bias_q_of(s):
        return bias_all[s, 0:1, half : half + qkv_width]

    def bias_e_of(s):
        return bias_all[s, 0:1, :half]

    finish_source(mlp)

    def start_far():
        for a in mlp:
            gather_far(a).start()
        pair_gm.start()

    @pl.loop(0, 4)
    def _(i):
        @pl.when(i == 1)
        def _():
            @pl.when(is_end)
            def _():
                relay(attn, 2)
                share(attn, 2)
                start_far()

            relay(attn, 3)
            pass_diagonal(attn, 1)
            share(attn, 3)
            pass_diagonal(attn, 2)

            @pl.when(is_inner)
            def _():
                start_far()

            for k in (1, 2, 3):
                bias_copy(k, True).wait_recv()

        @pl.when(i > 0)
        def _():
            finish_slab(attn, i)

        @pl.when(i == 2)
        def _():
            pass_diagonal(attn, 3)

        @pl.when(((i == 2) & is_inner) | ((i == 3) & is_end))
        def _():
            share_far(mlp)

        s = slab_of(i)

        def half_done():
            @pl.when(i == 0)
            def _():
                relay(attn, 1)
                share(attn, 1)

                @pl.when(is_inner)
                def _():
                    relay(attn, 2)
                    share(attn, 2)

            @pl.when(i == 3)
            def _():
                swap_attn.start()

        attention_slab(
            s, h1, wq, wp, bias_q_of(s), rel_query, codes, attended, total, heads, half, half_done
        )


    swap_attn.wait()

    def middle_rows(rows):
        value = tokens[rows].astype(F32)
        valid = keep[rows]
        attn_out = total[rows] + xr[rows] + proj_bias
        mid = value + attn_out
        middle[rows] = mid
        xhat, _ = normalize(mid)
        h2[rows] = (xhat * gain_two + shift_two).astype(BF)
        early[1:2, :] += column_sum(valid * mid * mid)
        early[3:4, :] += column_sum(valid * attn_out * attn_out)

    over_rows(middle_rows)
    swap_h2.start()
    pair_h2.start()
    total[...] = jnp.zeros_like(total)
    back[...] = jnp.zeros_like(back)
    bias_e[...] = jnp.zeros_like(bias_e)
    bias_q[...] = jnp.zeros_like(bias_q)
    rel_acc[...] = jnp.zeros_like(rel_acc)
    swap_grad.wait()

    def add_grad(buf, p, j, side, value):
        value = value.reshape(buf.shape[2:]) + jnp.where(p > 0, buf[2 + j, side].astype(F32), 0.0)
        buf[2 + j, side] = value.astype(BF)

    def weight_grads(p, j, done):
        sides = [(side, slice(side * half, side * half + half)) for side in range(2)]
        for side, columns in sides:
            add_grad(we, p, j, side, dot_tn(normed[p, :, columns], gpre[...]))
        done((2,))
        for side, columns in sides:
            add_grad(ws, p, j, side, dot_tn(act[...], grads[p, :, columns]))
        done((3,))

    def own_rows(rows):
        xr[rows] = xr[rows] + total[rows]
        xr2[rows] = xr2[rows] + back[rows]

    def other_rows(rows):
        return pl.ds(pl.multiple_of(rows.start + own, CHUNK), CHUNK)

    def back_low_rows(rows):
        h2[rows] = back[other_rows(rows)].astype(BF)

    def out_low_rows(rows):
        h2[other_rows(rows)] = total[other_rows(rows)].astype(BF)

    def back_sum_rows(rows):
        h2[rows] = (back[rows] + got_low[rows].astype(F32)).astype(BF)

    def out_sum_rows(rows):
        h2[other_rows(rows)] = (total[rows] + got_low[other_rows(rows)].astype(F32)).astype(BF)

    def between_passes():
        pair_h2.wait()
        swap_h2z.start()
        swap_mlp.wait()
        swap_gh2.wait()
        over_rows(own_rows)
        total[...] = jnp.zeros_like(total)
        back[...] = jnp.zeros_like(back)
        swap_gmz.wait()
        swap_h2z.wait()

    def start_pair_sums():
        over_rows(back_low_rows)
        swap_back_low.start()
        over_rows(out_low_rows)
        swap_out_low.start()

    def send_pair_sums():
        swap_back_low.wait()
        over_rows(back_sum_rows)
        send_back.start()
        swap_out_low.wait()
        over_rows(out_sum_rows)
        send_out.start()

    @pl.loop(0, 8)
    def _(t):
        p, j = t // 4, (t // 2 + t // 4) % 2
        s = (1 - j) * z + j * remote_slab

        @pl.when(t == 1)
        def _():
            pass_diagonal(mlp, 1)
            swap_h2.wait()

        @pl.when(t == 2)
        def _():
            finish_slab(mlp, 1)
            pair_gm.wait_recv()
            swap_gmz.start()

        @pl.when(t == 3)
        def _():
            swap_mlp.start()
            swap_gh2.start()

        @pl.when(t == 4)
        def _():
            between_passes()

        @pl.when(t == 7)
        def _():
            start_pair_sums()

        mlp_rows(
            s, j, (t + t // 2) % 2, normed.at[p], grads.at[p], we, ws, bias_e_of(s), act, gpre, total, back, bias_e, half
        )

        @pl.when(t == 7)
        def _():
            send_pair_sums()

        @pl.when(t % 2 == 1)
        def _():
            def done(group):
                @pl.when(t == 5)
                def _():
                    reduce_one(group, 1)

            weight_grads(p, j, done)

    sent_far(mlp)
    reduce_two(mlp, 1)
    reduce_one(mlp, 0)
    send_back.wait_recv()
    back_load = pltpu.make_async_copy(pair_back, gmz.at[rows_own], local.at[8])
    back_load.start()
    back_load.wait()

    pair_gm.wait_send()

    def middle_back_rows(rows):
        mid = middle[rows]
        grad_out = gm[rows].astype(F32)
        early[9:10, :] += column_sum(grad_out)
        grad = xr2[rows] + gmz[rows].astype(F32)
        xhat, inverse = normalize(mid)
        early[6:7, :] += column_sum(grad * xhat)
        early[7:8, :] += column_sum(grad)
        grad_mid = grad_out + norm_back(grad, gain_two, xhat, inverse)
        xr2[rows] = grad_mid
        low = grad_mid.astype(BF)
        gm[rows] = low
        early[8:9, :] += column_sum(low.astype(F32))

    over_rows(middle_back_rows)
    swap_ga.start()

    def result_rows(rows):
        valid = keep[rows]
        mlp_out = xr[rows] + gmz[other_rows(rows)].astype(F32) + shrink_bias
        result = middle[rows] + mlp_out
        h2[rows] = result.astype(BF)
        early[2:3, :] += column_sum(valid * result * result)
        early[4:5, :] += column_sum(valid * mlp_out * mlp_out)

    back[...] = jnp.zeros_like(back)
    for i in range(4):
        sent_slab(attn, i)
    reduce_three(mlp, 1)
    swap_ga.wait()

    out_load = pltpu.make_async_copy(pair_out, gmz.at[rows_other], local.at[8])

    def interleave(source, target):
        def move(stage):
            @pl.loop(0, SIDE)
            def _(i):
                places = [pl.multiple_of(w * WROWS + i * SIDE_PAD, SIDE_PAD) for w in range(stage.shape[1])]
                some = [source[pl.ds(at, SIDE_PAD)][:SIDE].astype(F32) for at in places]
                stage[pl.ds(i * SIDE, SIDE)] = jnp.stack(some, axis=1).astype(stage.dtype)

            store = pltpu.make_async_copy(stage, target, local.at[8])
            store.start()
            store.wait()

        pl.run_scoped(move, pltpu.VMEM(target.shape, target.dtype))

    def finish_result():
        send_back.wait_send()
        send_out.wait_recv()
        out_load.start()
        out_load.wait()
        over_rows(result_rows)

    stages = (partner,), (along_z(1), along_z(2), along_z(3)), (along_x, along_y, across), (partner,)
    early_sums = (((early, early_full, early_half),), 20)
    late_sums = (((late, late_full, late_half), (rel, rel_full, rel_half)), 28)

    def small_copies(sums, stage):
        pairs, base = sums
        first = (0, 1, 4, 7)[stage]
        for i, device in enumerate(stages[stage]):
            for q, (src, full, part) in enumerate(pairs):
                rows = part.shape[1]
                mine = pl.ds(pl.multiple_of(r * rows, rows), rows)
                index = base + (first + i) * len(pairs) + q
                if stage == 0:
                    yield src, full, slice(None), remote(src, full, csend, crecv, index, device)
                else:
                    got = part.at[first + i - 1]
                    yield src, got, mine, remote(src.at[mine], got, csend, crecv, index, device)

    def small_start(sums, stage):
        for _, _, _, copy in small_copies(sums, stage):
            copy.start()

    def small_finish(sums, stage):
        copies = list(small_copies(sums, stage))
        for _, _, _, copy in copies:
            copy.wait()
        for src, got, rows, _ in copies:
            if stage == 3:
                count = got.shape[0]
                src[pl.ds(pl.multiple_of((1 - r) * count, count), count)] = got[...]
            else:
                src[rows] += got[...]

    def on_side(act_on):
        for side in range(2):

            @pl.when(r == side)
            def _():
                act_on(side)

    def fill_early(side):
        for s in range(4):
            early[10 + s : 11 + s, side * half : (side + 1) * half] = bias_e[s]

    early_store = pltpu.make_async_copy(early, early_out, local.at[9])

    @pl.loop(0, 4)
    def _(n):
        s = slab_of(3 - n)
        g = slot(0, n)

        def half_done():
            @pl.when(n == 0)
            def _():
                reduce_two(mlp, 0)

            @pl.when(n == 1)
            def _():
                reduce_four((2,))

            @pl.when(n == 2)
            def _():
                small_finish(early_sums, 0)
                small_start(early_sums, 1)
                reduce_four((3,))

            @pl.when(n == 3)
            def _():
                swap_gh1.start()

        attention_back_slab(
            s, h1, gm, wq, wp, bias_q_of(s), rel_query, rel_back, codes, act, back, bias_q, rel_acc, heads, half, half_done
        )

        @pl.when(n > 0)
        def _():
            reduce_two(attn, n - 1)

        for side in range(2):
            columns = slice(side * half, side * half + half)
            wq[g, side] = dot_tn(act[:, :qkv_width], h1[:, columns]).astype(BF).reshape(wq.shape[2:])
            wp[g, side] = dot_tn(attended[s], gm[:, columns]).astype(BF).reshape(wp.shape[2:])
        reduce_one(attn, n)

        @pl.when((n > 1) & is_end)
        def _():
            reduce_three(attn, n - 2)

        @pl.when((n == 3) & is_inner)
        def _():
            reduce_three(attn, 0)

        @pl.when(n == 0)
        def _():
            reduce_three(mlp, 0)

        @pl.when(n == 1)
        def _():
            finish_result()
            on_side(fill_early)
            small_start(early_sums, 0)

    swap_gh1.wait()

    def input_rows(rows):
        value = tokens[rows].astype(F32)
        grad = (back[rows] + total[other_rows(rows)]) * keep[rows]
        xhat, inverse = normalize(value)
        for place, value in ((8, column_sum(grad * xhat)), (10, column_sum(grad))):
            late[place : place + 1, :] += value[:, :half]
            late[place + 1 : place + 2, :] += value[:, half:]
        xr2[rows] = xr2[rows] + norm_back(grad, gain_one, xhat, inverse)

    over_rows(input_rows)

    def fill_late(side):
        for s in range(4):
            late[2 * s + side : 2 * s + side + 1, :qkv_width] = bias_q[s]

    on_side(fill_late)
    for part, at in ((0, 0), (1, COL_W)):
        rows = slice(at, at + 32)
        rel[part * 32 : part * 32 + 32] = rel_acc[rows] + rel_acc[LANES + at : LANES + at + 32]

    small_start(late_sums, 0)

    @pl.when(is_inner)
    def _():
        reduce_three(attn, 1)

    small_finish(late_sums, 0)
    small_start(late_sums, 1)
    reduce_three(attn, 2)
    reduce_five((2,))
    reduce_two(attn, 3)
    reduce_five((3,))
    interleave(xr2, input_grad)
    interleave(h2, block_out)
    small_finish(early_sums, 1)
    small_start(early_sums, 2)
    reduce_three(attn, 3)
    reduce_four(attn)
    small_finish(late_sums, 1)
    small_start(late_sums, 2)
    reduce_six(mlp)
    small_finish(early_sums, 2)
    small_start(early_sums, 3)
    reduce_five(attn)
    small_finish(late_sums, 2)
    small_start(late_sums, 3)
    small_finish(early_sums, 3)
    early_store.start()
    small_finish(late_sums, 3)
    late_stores = [
        pltpu.make_async_copy(late, late_out, local.at[6]),
        pltpu.make_async_copy(rel, rel_out, local.at[7]),
    ]
    for copy in late_stores:
        copy.start()
    reduce_six(attn)

    swap_h1.wait_send()
    send_out.wait_send()
    for k in (1, 2, 3):
        bias_copy(k).wait_send()
    for a in range(4):
        for copy in swap_out(a) + keep_out(a):
            copy.wait()
        for kind in (1, 2, 3, 4):
            spread(a, kind).wait_send()
        for n in range(4 if a in attn else 2):
            for kind in range(4):
                reduce_copy(a, n, kind).wait_send()
            reduce_z(a, n, lambda copy: copy.wait_send())

    for copy in late_stores:
        copy.wait()
    early_store.wait()


def run_kernel(tokens, mask, out_grad, vectors, qkv_bias, expand_bias, rel_height, rel_width, sources):
    own, width = tokens.shape[1] * WROWS, tokens.shape[2]
    half = width // 2
    rows = [source.shape[-2] for source in sources]
    rows[0] = 3 * rows[0] // 2
    sds = jax.ShapeDtypeStruct
    any_spec = pl.BlockSpec(memory_space=pl.ANY)
    vmem_spec = pl.BlockSpec(memory_space=pltpu.VMEM)
    out_shape = [sds(tokens.shape, BF), sds(tokens.shape, F32)]
    out_shape += [sds(source.shape, BF) for source in sources]
    out_shape += [sds((16, width), F32), sds((16, half), F32), sds((64, LANES), F32)]
    first, second = zip(*[halves(n) for n in rows])
    out_shape += [sds((4, 2, n, half), BF) for n in first]
    out_shape += [sds((4, 2, n, half), BF) for n in second]
    out_shape += [sds((4, n, half), BF) for n in second]
    out_shape += [sds((4, n, half), BF) for n in first]
    out_shape += [sds((6, n, half), BF) for n in rows]
    out_shape += [sds((own, width), BF)] * 2
    both = 2 * own
    vmem, dma = pltpu.VMEM, pltpu.SemaphoreType.DMA
    qkv_width = 2 * rows[0]
    scratch = [vmem((count, 2, 2, n, half), BF) for count, n in zip((5, 5, 4, 4), rows)]
    scratch += [vmem((own, width), BF), vmem((own, 1), F32)]
    scratch += [vmem((both, width), BF)] + [vmem((2, both, width), BF)] * 2 + [vmem((both, width), BF)]
    scratch += [vmem((4, both, qkv_width // 3), BF)]
    scratch += [vmem((both, width), F32)] * 2
    scratch += [vmem((own, width), F32)] * 3
    scratch += [vmem((both, half), BF), vmem((both, half), BF)]
    scratch += [vmem((4, 8, width), F32), vmem((16, width), F32), vmem((16, width), F32), vmem((7, 8, width), F32)]
    scratch += [vmem((16, half), F32), vmem((16, half), F32), vmem((7, 8, half), F32)]
    scratch += [vmem((64, LANES), F32), vmem((64, LANES), F32), vmem((7, 32, LANES), F32)]
    scratch += [vmem((4, 1, half), F32), vmem((4, 1, qkv_width), F32), vmem((2 * LANES, LANES), F32)]
    scratch += [vmem((2 * LANES, LANES), BF), vmem((3 * LANES, LANES), BF), vmem((2, 32, HEAD), F32)]
    scratch += [dma((4, 4, 6))] * 2 + [dma((4, 4, 5)), dma((4, 4, 6))] + [dma((4, 5))] * 2 + [dma((44,))] * 2
    scratch += [dma((4,))] * 2 + [dma((8,))] * 2 + [dma((11,)), dma((4,))]
    got = pl.pallas_call(
        kernel,
        out_shape=out_shape,
        in_specs=[any_spec, vmem_spec, any_spec] + [vmem_spec] * 11 + [any_spec] * 4,
        out_specs=[any_spec] * len(out_shape),
        scratch_shapes=scratch,
        compiler_params=pltpu.CompilerParams(
            collective_id=0, has_side_effects=True, vmem_limit_bytes=VMEM_LIMIT
        ),
        name="block_step",
    )(tokens, mask, out_grad, *vectors, qkv_bias, expand_bias, rel_height, rel_width, key_codes(), *sources)
    return got[:9]


def finish_kernel(early, late, rel, *refs):
    wide, (bias_q, bias_e, height, width_out, rms), rows_out = refs[:6], refs[6:11], refs[11:17]
    outs, held, full, load, store = refs[17:23], refs[23:29], refs[29:33], refs[33], refs[34]
    z = lax.axis_index("col")
    loads = [pltpu.make_async_copy(src, to, load.at[i]) for i, (src, to) in enumerate(zip(wide, held))]
    full = list(full) + list(held[4:])
    stores = [pltpu.make_async_copy(src, to, store.at[i]) for i, (src, to) in enumerate(zip(full, outs))]
    for i in (3, 2, 5, 4, 0, 1):
        loads[i].start()
    features = early.shape[1]
    half = features // 2
    for ref, at in zip(rows_out[:2], (8, 10)):
        ref[:half] = late[at, :]
        ref[half:] = late[at + 1, :]
    for ref, at in zip(rows_out[2:], (6, 7, 8, 9)):
        ref[...] = early[at, :]
    lane = lax.broadcasted_iota(jnp.int32, (1, LANES), 1)
    stats = jnp.zeros((1, LANES), F32)
    for i in range(rms.shape[0]):
        stats = jnp.where(lane == i, jnp.sum(early[i : i + 1, :], axis=1, keepdims=True), stats)
    rms[...] = jnp.sqrt(stats / (early[5:6, 0:1] * features))[0, : rms.shape[0]]
    part = bias_q.shape[1] // 2
    bias_e[...] = early[pl.ds(10 + z, 1), :].reshape(features)
    for side in range(2):
        row = late[pl.ds(2 * z + side, 1), :]
        for i in range(2):
            bias_q[i : i + 1, side * part : (side + 1) * part] = row[:, 2 * i * part : (2 * i + 1) * part]
    count = height.shape[0]
    turn = lax.broadcasted_iota(jnp.int32, (32, 32), 0) + lax.broadcasted_iota(jnp.int32, (32, 32), 1) == count - 1
    turned = jnp.dot(turn.astype(F32), rel[:32], precision=lax.Precision.HIGHEST, preferred_element_type=F32)
    height[...] = turned[:count, :HEAD]
    width_out[...] = rel[32 : 32 + count, :HEAD]
    for i in (3, 2, 0, 1):
        loads[i].wait()
        step = held[i].shape[0] // 5

        @pl.loop(0, 5)
        def _(m):
            at = pl.ds(pl.multiple_of(m * step, step), step)
            full[i][at] = held[i][at].astype(F32)

        stores[i].start()
        for j in {3: (5,), 2: (4,)}.get(i, ()):
            loads[j].wait()
            stores[j].start()
    for copy in stores:
        copy.wait()


def finish_outputs(got, part):
    early, late, rel = got[6:9]
    grads = [value.reshape(-1, value.shape[-1]) for value in got[2:6]]
    width = early.shape[1]
    sds = jax.ShapeDtypeStruct
    any_spec = pl.BlockSpec(memory_space=pl.ANY)
    vmem_spec = pl.BlockSpec(memory_space=pltpu.VMEM)
    out_shape = [sds((2, 2 * part), F32), sds((width,), F32), sds((2 * SIDE - 1, HEAD), F32)]
    out_shape += [sds((2 * SIDE - 1, HEAD), F32), sds((5,), F32)] + [sds((width,), F32)] * 6
    final = [sds(value.shape, F32) for value in grads]
    out_shape += final + [sds(value.shape, value.dtype) for value in got[:2]]
    return pl.pallas_call(
        finish_kernel,
        out_shape=out_shape,
        in_specs=[vmem_spec] * 3 + [any_spec] * 6,
        out_specs=[vmem_spec] * 11 + [any_spec] * 6,
        scratch_shapes=[pltpu.VMEM(value.shape, value.dtype) for value in grads + list(got[:2]) + final]
        + [pltpu.SemaphoreType.DMA((6,))] * 2,
        compiler_params=pltpu.CompilerParams(vmem_limit_bytes=VMEM_LIMIT),
        name="finish",
    )(early, late, rel, *grads, *got[:2])


VMEM_LIMIT = 64 * 1024 * 1024 - 512 * 1024


def over_chips(
    tokens, valid_mask, out_grad, first_gain, first_shift, qkv_weight, qkv_bias, rel_height, rel_width,
    proj_weight, proj_bias, second_gain, second_shift, expand_weight, expand_bias, shrink_weight, shrink_bias,
):
    def turned(value):
        return value.transpose(1, 0, 2)

    rows, _, local_width = qkv_weight.shape
    part = local_width // 2
    hidden = expand_weight.shape[1] // 2
    qkv_src = qkv_weight.transpose(1, 2, 0).reshape(3, 2, part, rows)
    proj_src = proj_weight.reshape(2, 2, part // 2, proj_weight.shape[1])
    expand_src = expand_weight.reshape(2, rows // 2, 2 * hidden)
    shrink_src = shrink_weight.reshape(2, 2, hidden // 2, shrink_weight.shape[1])
    vectors = (first_gain, first_shift, second_gain, second_shift, proj_bias, shrink_bias)
    got = run_kernel(
        turned(tokens), valid_mask, turned(out_grad), vectors, qkv_bias, expand_bias, rel_height, rel_width,
        (qkv_src, proj_src, expand_src, shrink_src),
    )
    outs = finish_outputs(got, part)
    qkv_bias_sum, expand_bias_sum, height_sum, width_sum, rms = outs[:5]
    gain_one, shift_one, gain_two, shift_two, proj_bias_sum, shrink_bias_sum = outs[5:11]
    qkv_sum, proj_sum, expand_sum, shrink_sum, block_out, input_grad = outs[11:]
    return (
        turned(block_out),
        turned(input_grad),
        gain_one,
        shift_one,
        qkv_sum.reshape(3, local_width, rows).transpose(2, 0, 1),
        qkv_bias_sum,
        height_sum,
        width_sum,
        proj_sum.reshape(proj_weight.shape),
        proj_bias_sum,
        gain_two,
        shift_two,
        expand_sum.reshape(expand_weight.shape),
        expand_bias_sum,
        shrink_sum.reshape(shrink_weight.shape),
        shrink_bias_sum,
        rms,
    )


epsilon = 1e-06
highest = lax.Precision.HIGHEST


def layer_norm(values, norm_gain, norm_shift):
    center = values - jnp.mean(values, axis=-1, keepdims=True)
    spread = jnp.mean(center * center, axis=-1, keepdims=True)
    return center * lax.rsqrt(spread + epsilon) * norm_gain + norm_shift


def offset_table(span_size):
    positions = jnp.arange(span_size)
    offset = positions[:, None] - positions[None, :] + span_size - 1
    return (offset[:, :, None] == jnp.arange(2 * span_size - 1)[None, None, :]).astype(jnp.float32)


def attention_scores(
    query_rows, key_rows, rel_rows_table, rel_cols_table, onehot_table, span_size, scaling
):
    window_count, tokens_per, head_count, head_size = query_rows.shape
    rel_count = 2 * span_size - 1
    direct = (
        jnp.einsum("bthc,buhc->bhtu", query_rows, key_rows, preferred_element_type=jnp.float32)
        * scaling
    )
    query_float = query_rows.astype(jnp.float32)
    along_rows = jnp.einsum("bthc,jc->bhtj", query_float, rel_rows_table, precision=highest)
    along_cols = jnp.einsum("bthc,jc->bhtj", query_float, rel_cols_table, precision=highest)
    grid_rows = along_rows.reshape(window_count, head_count, span_size, span_size, rel_count)
    grid_cols = along_cols.reshape(window_count, head_count, span_size, span_size, rel_count)
    rel_rows = jnp.einsum("bhxyj,xkj->bhxyk", grid_rows, onehot_table, precision=highest)
    rel_cols = jnp.einsum("bhxyj,ywj->bhxyw", grid_cols, onehot_table, precision=highest)
    score_sum = direct.reshape(window_count, head_count, span_size, span_size, span_size, span_size)
    score_sum = score_sum + rel_rows[:, :, :, :, :, None] + rel_cols[:, :, :, :, None, :]
    return score_sum.reshape(window_count, head_count, tokens_per, tokens_per)


def relative_back(score_float, onehot_table, span_size):
    window_count, head_count, tokens_per, other_tokens = score_float.shape
    grid = score_float.reshape(window_count, head_count, span_size, span_size, span_size, span_size)
    rows_part = jnp.einsum("bhxykw,xkj->bhxyj", grid, onehot_table, precision=highest)
    cols_part = jnp.einsum("bhxykw,ywj->bhxyj", grid, onehot_table, precision=highest)
    return (
        rows_part.reshape(window_count, head_count, tokens_per, -1),
        cols_part.reshape(window_count, head_count, tokens_per, -1),
    )


def gather_weights(qkv_weight, proj_weight, expand_weight, shrink_weight):
    return (
        lax.all_gather(qkv_weight, "row", axis=0, tiled=True),
        lax.all_gather(proj_weight, "row", axis=1, tiled=True),
        lax.all_gather(expand_weight, "row", axis=0, tiled=True),
        lax.all_gather(shrink_weight, "row", axis=1, tiled=True),
    )


def gather_tokens(normed):
    return lax.all_gather(normed, "col", axis=0, tiled=True)


def gather_grads(grad_low):
    return lax.all_gather(grad_low, "col", axis=0, tiled=True)


def sum_branch(inputs_low, weight_full, own_windows):

    def term(first_row, row_count):
        return jnp.einsum(
            "btk,kd->btd", inputs_low, weight_full, preferred_element_type=jnp.float32
        )

    return lax.psum_scatter(
        term(jnp.int32(0), own_windows * lax.axis_size("col")),
        "col",
        scatter_dimension=0,
        tiled=True,
    )


def sum_input(grads_low, weight_full, own_windows):

    def term(first_row, row_count):
        return jnp.einsum("btk,dk->btd", grads_low, weight_full, preferred_element_type=jnp.float32)

    return lax.psum_scatter(
        term(jnp.int32(0), own_windows * lax.axis_size("col")),
        "col",
        scatter_dimension=0,
        tiled=True,
    )


def activate(values):
    return jax.nn.gelu(values, approximate=False)


def per_device(
    tokens,
    valid_mask,
    out_grad,
    first_gain,
    first_shift,
    qkv_weight,
    qkv_bias,
    rel_height,
    rel_width,
    proj_weight,
    proj_bias,
    second_gain,
    second_shift,
    expand_weight,
    expand_bias,
    shrink_weight,
    shrink_bias,
):
    span_size = (rel_height.shape[0] + 1) // 2
    head_size = rel_height.shape[1]
    local_width = qkv_weight.shape[2]
    head_count = local_width // head_size
    own_windows = tokens.shape[0]
    tokens_per = tokens.shape[1]
    model_width = tokens.shape[2]
    scaling = head_size ** (-0.5)
    onehot_table = offset_table(span_size)
    inputs = tokens.astype(jnp.float32)
    keep_mask = valid_mask.astype(jnp.float32)[:, :, None]

    def first_norm(values, norm_gain, norm_shift):
        return layer_norm(values, norm_gain, norm_shift) * keep_mask

    qkv_full, proj_full, expand_full, shrink_full = gather_weights(
        qkv_weight, proj_weight, expand_weight, shrink_weight
    )
    normed_first, first_back = jax.vjp(first_norm, inputs, first_gain, first_shift)
    first_all = gather_tokens(normed_first.astype(jnp.bfloat16))
    all_windows = first_all.shape[0]
    bias_rows = jnp.stack([qkv_bias[0], jnp.zeros_like(qkv_bias[0]), qkv_bias[1]])
    projected = (
        jnp.einsum("btd,dsk->btsk", first_all, qkv_full, preferred_element_type=jnp.float32)
        + bias_rows
    )
    projected = projected.astype(jnp.bfloat16)
    head_shape = (all_windows, tokens_per, head_count, head_size)
    query_low = projected[:, :, 0].reshape(head_shape)
    key_low = projected[:, :, 1].reshape(head_shape)
    value_low = projected[:, :, 2].reshape(head_shape)
    scores = attention_scores(
        query_low, key_low, rel_height, rel_width, onehot_table, span_size, scaling
    )
    top_score = jnp.max(scores, axis=-1, keepdims=True)
    log_total = top_score + jnp.log(jnp.sum(jnp.exp(scores - top_score), axis=-1, keepdims=True))
    probs_low = jnp.exp(scores - log_total).astype(jnp.bfloat16)
    attended = jnp.einsum(
        "bhtu,buhc->bthc", probs_low, value_low, preferred_element_type=jnp.float32
    )
    attended_low = attended.reshape(all_windows, tokens_per, local_width).astype(jnp.bfloat16)
    attn_out = sum_branch(attended_low, proj_full, own_windows) + proj_bias
    middle = inputs + attn_out
    normed_second, second_back = jax.vjp(layer_norm, middle, second_gain, second_shift)
    second_all = gather_tokens(normed_second.astype(jnp.bfloat16))
    hidden_pre = (
        jnp.einsum("btd,df->btf", second_all, expand_full, preferred_element_type=jnp.float32)
        + expand_bias
    )
    active_value, active_back = jax.vjp(activate, hidden_pre)
    hidden_low = active_value.astype(jnp.bfloat16)
    mlp_out = sum_branch(hidden_low, shrink_full, own_windows) + shrink_bias
    result = middle + mlp_out
    stat_terms = jnp.stack(
        [
            jnp.sum(keep_mask * inputs * inputs),
            jnp.sum(keep_mask * middle * middle),
            jnp.sum(keep_mask * result * result),
            jnp.sum(keep_mask * attn_out * attn_out),
            jnp.sum(keep_mask * mlp_out * mlp_out),
        ]
    )
    valid_count = jnp.sum(keep_mask)
    stat_total, count_total = lax.psum((stat_terms, valid_count), ("dp", "row", "col"))
    out_float = out_grad.astype(jnp.float32)
    qkv_full, proj_full, expand_full, shrink_full = gather_weights(
        qkv_weight, proj_weight, expand_weight, shrink_weight
    )
    mlp_grad_low = out_float.astype(jnp.bfloat16)
    shrink_bias_grad = jnp.sum(mlp_grad_low, axis=(0, 1), dtype=jnp.float32)
    mlp_grad_all = gather_grads(mlp_grad_low)
    shrink_grad_full = jnp.einsum(
        "btf,btd->fd", hidden_low, mlp_grad_all, preferred_element_type=jnp.float32
    )
    hidden_grad = jnp.einsum(
        "btd,fd->btf", mlp_grad_all, shrink_full, preferred_element_type=jnp.float32
    )
    pre_grad_low = active_back(hidden_grad)[0].astype(jnp.bfloat16)
    expand_bias_grad = jnp.sum(pre_grad_low, axis=(0, 1), dtype=jnp.float32)
    expand_grad_full = jnp.einsum(
        "btd,btf->df", second_all, pre_grad_low, preferred_element_type=jnp.float32
    )
    second_grad = sum_input(pre_grad_low, expand_full, own_windows)
    middle_part, second_gain_grad, second_shift_grad = second_back(second_grad)
    middle_grad = out_float + middle_part
    attn_grad_low = middle_grad.astype(jnp.bfloat16)
    proj_bias_grad = jnp.sum(attn_grad_low, axis=(0, 1), dtype=jnp.float32)
    attn_grad_all = gather_grads(attn_grad_low)
    proj_grad_full = jnp.einsum(
        "btk,btd->kd", attended_low, attn_grad_all, preferred_element_type=jnp.float32
    )
    attended_grad = jnp.einsum(
        "btd,kd->btk", attn_grad_all, proj_full, preferred_element_type=jnp.float32
    )
    attended_grad = attended_grad.astype(jnp.bfloat16).reshape(head_shape)
    scores_again = attention_scores(
        query_low, key_low, rel_height, rel_width, onehot_table, span_size, scaling
    )
    probs_float = jnp.exp(scores_again - log_total)
    probs_again = probs_float.astype(jnp.bfloat16)
    prob_grad = jnp.einsum(
        "bthc,buhc->bhtu", attended_grad, value_low, preferred_element_type=jnp.float32
    )
    value_grad = jnp.einsum(
        "bhtu,bthc->buhc", probs_again, attended_grad, preferred_element_type=jnp.float32
    )
    score_grad = probs_float * (
        prob_grad - jnp.sum(probs_float * prob_grad, axis=-1, keepdims=True)
    )
    score_low = score_grad.astype(jnp.bfloat16)
    rows_grad, cols_grad = relative_back(score_low.astype(jnp.float32), onehot_table, span_size)
    query_float = query_low.astype(jnp.float32)
    query_grad = (
        jnp.einsum("bhtu,buhc->bthc", score_low, key_low, preferred_element_type=jnp.float32)
        * scaling
    )
    query_grad = query_grad + jnp.einsum("bhtj,jc->bthc", rows_grad, rel_height, precision=highest)
    query_grad = query_grad + jnp.einsum("bhtj,jc->bthc", cols_grad, rel_width, precision=highest)
    key_grad = (
        jnp.einsum("bhtu,bthc->buhc", score_low, query_low, preferred_element_type=jnp.float32)
        * scaling
    )
    rel_height_grad = jnp.einsum("bhtj,bthc->jc", rows_grad, query_float, precision=highest)
    rel_width_grad = jnp.einsum("bhtj,bthc->jc", cols_grad, query_float, precision=highest)
    flat_shape = (all_windows, tokens_per, local_width)
    qkv_grad_low = jnp.stack(
        [
            query_grad.reshape(flat_shape),
            key_grad.reshape(flat_shape),
            value_grad.reshape(flat_shape),
        ],
        axis=2,
    ).astype(jnp.bfloat16)
    qkv_bias_grad = jnp.sum(qkv_grad_low[:, :, 0::2], axis=(0, 1), dtype=jnp.float32)
    qkv_grad_full = jnp.einsum(
        "btd,btsk->dsk", first_all, qkv_grad_low, preferred_element_type=jnp.float32
    )
    first_grad = sum_input(
        qkv_grad_low.reshape(all_windows, tokens_per, 3 * local_width),
        qkv_full.reshape(qkv_full.shape[0], 3 * local_width),
        own_windows,
    )
    input_part, first_gain_grad, first_shift_grad = first_back(first_grad)
    input_grad = middle_grad + input_part
    qkv_rows, proj_rows, expand_rows, shrink_rows = (
        lax.psum_scatter(qkv_grad_full, "row", scatter_dimension=0, tiled=True),
        lax.psum_scatter(proj_grad_full, "row", scatter_dimension=1, tiled=True),
        lax.psum_scatter(expand_grad_full, "row", scatter_dimension=0, tiled=True),
        lax.psum_scatter(shrink_grad_full, "row", scatter_dimension=1, tiled=True),
    )
    qkv_sum, proj_sum, expand_sum, shrink_sum = lax.psum(
        (qkv_rows, proj_rows, expand_rows, shrink_rows), "dp"
    )
    qkv_bias_sum, expand_bias_sum = lax.psum((qkv_bias_grad, expand_bias_grad), ("dp", "row"))
    (
        gain_one_sum,
        shift_one_sum,
        gain_two_sum,
        shift_two_sum,
        proj_bias_sum,
        shrink_bias_sum,
        height_sum,
        width_sum,
    ) = lax.psum(
        (
            first_gain_grad,
            first_shift_grad,
            second_gain_grad,
            second_shift_grad,
            proj_bias_grad,
            shrink_bias_grad,
            rel_height_grad,
            rel_width_grad,
        ),
        ("dp", "row", "col"),
    )
    rms = jnp.sqrt(stat_total / (count_total * model_width))
    return (
        result.astype(jnp.bfloat16),
        input_grad,
        gain_one_sum,
        shift_one_sum,
        qkv_sum,
        qkv_bias_sum,
        height_sum,
        width_sum,
        proj_sum,
        proj_bias_sum,
        gain_two_sum,
        shift_two_sum,
        expand_sum,
        expand_bias_sum,
        shrink_sum,
        shrink_bias_sum,
        rms,
    )


def choose(mesh):
    fits = tuple(mesh.shape[name] for name in ("dp", "row", "col")) == (4, 2, 4)
    return over_chips if fits else per_device


def solution(mesh):
    in_specs = (
        P(("dp", "row", "col"), None, None),
        P(("dp", "row", "col"), None),
        P(("dp", "row", "col"), None, None),
        P(),
        P(),
        P("row", None, "col"),
        P(None, "col"),
        P(),
        P(),
        P("col", "row"),
        P(),
        P(),
        P(),
        P("row", "col"),
        P("col"),
        P("col", "row"),
        P(),
    )
    out_specs = (
        P(("dp", "row", "col"), None, None),
        P(("dp", "row", "col"), None, None),
        P(),
        P(),
        P("row", None, "col"),
        P(None, "col"),
        P(),
        P(),
        P("col", "row"),
        P(),
        P(),
        P(),
        P("row", "col"),
        P("col"),
        P("col", "row"),
        P(),
        P(),
    )
    return jax.shard_map(
        choose(mesh), mesh=mesh, in_specs=in_specs, out_specs=out_specs, check_vma=False
    )
```

```python
import functools

import jax
import jax.numpy as jnp
import numpy as np
from jax import lax
from jax.experimental import pallas as pl
from jax.experimental.pallas import tpu as pltpu
from jax.sharding import PartitionSpec as P

BF = jnp.bfloat16
F32 = jnp.float32
LANES = 128
SIDE = 14
SIDE_PAD = 16
WROWS = SIDE * SIDE_PAD
HEAD = 80
AT_H = HEAD
AT_W = HEAD + SIDE
AT_MASK = HEAD + 2 * SIDE
COL_W = 64


def dot(a, b):
    return jnp.dot(a, b, preferred_element_type=F32)


def dot_nt(a, b):
    return lax.dot_general(a, b, (((1,), (1,)), ((), ())), preferred_element_type=F32)


def dot_tn(a, b):
    return lax.dot_general(a, b, (((0,), (0,)), ((), ())), preferred_element_type=F32)


def lane_ids():
    return lax.broadcasted_iota(jnp.int32, (WROWS, LANES), 1)


def row_ids():
    return lax.broadcasted_iota(jnp.int32, (WROWS, LANES), 0)


def key_codes():
    u = np.arange(WROWS)[:, None]
    lane = np.arange(LANES)[None, :]
    k, l = u // SIDE_PAD, u % SIDE_PAD
    height = lane - AT_H == k
    width = (lane - AT_W == l) & (l < SIDE)
    width_back = (AT_W + SIDE - 1 - lane == l) & (l < SIDE)
    plain = np.where(height | width, 1.0, 0.0)
    masked = np.where((lane == AT_MASK) & (l >= SIDE), -1e30, plain)
    back = np.where(height | width_back, 1.0, 0.0)
    return np.stack([masked, plain, back]).astype(BF)


def split_low(values):
    high = values.astype(BF)
    return high, (values - high.astype(F32)).astype(BF)


def relative_tables(rel_h, rel_w, rel_query, rel_back):
    count, rows = 2 * SIDE - 1, rel_h.shape[0]
    offset = lax.broadcasted_iota(jnp.int32, (rows, LANES), 0)
    lane = lax.broadcasted_iota(jnp.int32, (rows, LANES), 1)

    def places(first, step):
        return jnp.where((lane == first + step * offset) & (offset < count), 1.0, 0.0).astype(BF)

    heights, widths = places(count - 1, -1), places(COL_W + count - 1, -1)
    widths_back = places(COL_W, 1)
    tall, wide = rel_h[...], rel_w[...]
    rel_query[...] = jnp.zeros_like(rel_query)
    rel_back[...] = jnp.zeros_like(rel_back)
    for part, (a, b) in enumerate(zip(split_low(tall * HEAD**0.5), split_low(wide * HEAD**0.5))):
        at = part * LANES
        rel_query[at : at + HEAD] = (dot_tn(a, heights) + dot_tn(b, widths)).astype(BF)
    for part, (a, b) in enumerate(zip(split_low(tall), split_low(wide))):
        table = (dot_tn(heights, a) + dot_tn(widths_back, b)).astype(BF)
        for place in ((0, 1), (2,))[part]:
            rel_back[place * LANES : (place + 1) * LANES, :HEAD] = table


def query_codes(query, rel_query):
    full = dot(jnp.concatenate([query, query], axis=1), rel_query)
    tiles = full.reshape(SIDE, SIDE_PAD, LANES)
    heights = jnp.concatenate(
        [pltpu.roll(tiles[i], AT_H - (SIDE - 1 - i), 1) for i in range(SIDE)], axis=0
    )
    widths = pltpu.roll(
        tiles, AT_W - COL_W - (SIDE - 1), 2, stride=1, stride_axis=1
    ).reshape(WROWS, LANES)
    lane = lane_ids()
    codes = jnp.where(
        (lane >= AT_H) & (lane < AT_W),
        heights,
        jnp.where((lane >= AT_W) & (lane < AT_MASK), widths, 0.0),
    )
    high, rest = split_low(codes)
    first = query + high + jnp.where(lane == AT_MASK, 1.0, 0.0).astype(BF)
    return jnp.concatenate([first, rest], axis=1)


def softmax_rows(query, key, rel_query, codes_ref):
    left = query_codes(query, rel_query)
    right = jnp.concatenate([key + codes_ref[0], codes_ref[1]], axis=1)
    scores = dot_nt(left, right)
    top = jnp.max(scores, axis=1, keepdims=True)
    weights = jnp.exp((scores - top) * (HEAD**-0.5))
    return weights / jnp.sum(weights, axis=1, keepdims=True)


def attend(query, key, value, rel_query, codes_ref):
    probs = softmax_rows(query, key, rel_query, codes_ref)
    return dot(probs.astype(BF), value)


def attend_back(query, key, value, grad, rel_query, rel_back, codes_ref):
    probs = softmax_rows(query, key, rel_query, codes_ref)
    prob_grad = dot_nt(grad, value)
    inner = jnp.sum(probs * prob_grad, axis=1, keepdims=True)
    score_low = (probs * (prob_grad - inner)).astype(BF)
    value_grad = dot_tn(probs.astype(BF), grad)
    key_grad = dot_tn(score_low, query) * (HEAD**-0.5)
    mixed = dot(score_low, key + codes_ref[2])
    tiles = mixed.reshape(SIDE, SIDE_PAD, LANES)
    heights = jnp.concatenate(
        [pltpu.roll(tiles[i], (SIDE - 1 - i - AT_H) % LANES, 1) for i in range(SIDE)], axis=0
    )
    widths = pltpu.roll(
        tiles, (COL_W - AT_W) % LANES, 2, stride=1, stride_axis=1
    ).reshape(WROWS, LANES)
    lane, row = lane_ids(), row_ids()
    first_h = SIDE - 1 - row // SIDE_PAD
    first_w = COL_W + row % SIDE_PAD
    offsets = jnp.where(
        (lane >= first_h) & (lane < first_h + SIDE),
        heights,
        jnp.where((lane >= first_w) & (lane < first_w + SIDE), widths, 0.0),
    )
    high, rest = split_low(offsets)
    query_grad = jnp.where(lane < HEAD, mixed, 0.0) * (HEAD**-0.5) + dot(
        jnp.concatenate([high, rest, high], axis=1), rel_back
    )
    rel_grad = dot_tn(jnp.concatenate([high, rest], axis=1), query)
    return query_grad, key_grad, value_grad, rel_grad


def pad_head(piece):
    return jnp.concatenate([piece, jnp.zeros((piece.shape[0], LANES - HEAD), piece.dtype)], axis=1)


def qkv_low(s, rows, h1, wq, bias, half):
    return (dot_nt(h1[rows, :half], block(wq, s, 0)) + dot_nt(h1[rows, half:], block(wq, s, 1)) + bias).astype(BF)


def head_of(low, part, heads, hh):
    at = (part * heads + hh) * HEAD
    return pad_head(low[:, at : at + HEAD])


def attention_slab(s, h1, wq, wp, bias, rel_query, codes, attended, total, heads, half, half_done):
    count = h1.shape[0] // WROWS

    @pl.loop(0, count)
    def _(m):
        rows = pl.ds(pl.multiple_of((m + count // 2) % count * WROWS, WROWS), WROWS)
        low = qkv_low(s, rows, h1, wq, bias, half)
        outs = []
        for hh in range(heads):
            query, key, value = (head_of(low, part, heads, hh) for part in range(3))
            outs.append(attend(query, key, value, rel_query[...], codes)[:, :HEAD])
        out_low = jnp.concatenate(outs, axis=1).astype(BF)
        attended[s, rows] = out_low
        total[rows, :half] += dot(out_low, block(wp, s, 0))
        total[rows, half:] += dot(out_low, block(wp, s, 1))

        @pl.when(m == count // 2 - 1)
        def _():
            half_done()


SQRT_HALF = 0.5**0.5
PDF_SCALE = 0.3989422804014327


def both_blocks(ref, slab):
    value = ref[slab]
    return value.reshape(4 * value.shape[2], value.shape[3])


def mlp_rows(s, place, m, h2, gm, we, ws, bias, act, gpre, total, back, bias_grad, half):
    count = h2.shape[0] // 2

    @pl.loop(0, 1)
    def _(step):
        rows = pl.ds(pl.multiple_of((m + step) * count, count), count)
        pre = dot(h2[rows, :], both_blocks(we, place)) + bias
        cdf = 0.5 + 0.5 * lax.erf(pre * SQRT_HALF)
        slope = cdf + pre * (PDF_SCALE * jnp.exp(-0.5 * pre * pre))
        act_low = (pre * cdf).astype(BF)
        act[rows, :] = act_low
        hidden = dot_nt(gm[rows, :half], block(ws, place, 0)) + dot_nt(gm[rows, half:], block(ws, place, 1))
        gpre_low = (hidden * slope).astype(BF)
        gpre[rows, :] = gpre_low
        bias_grad[s] += jnp.sum(gpre_low.astype(F32), axis=0, keepdims=True)
        total[rows, :half] += dot(act_low, block(ws, place, 0))
        total[rows, half:] += dot(act_low, block(ws, place, 1))
        back[rows, :] += dot_nt(gpre_low, both_blocks(we, place))


def attention_back_slab(
    s, h1, ga, wq, wp, bias, rel_query, rel_back, codes, gqkv, back, bias_grad, rel_grad, heads, half, half_done
):
    count = h1.shape[0] // WROWS

    @pl.loop(0, count)
    def _(m):
        rows = pl.ds(pl.multiple_of((m + count // 2) % count * WROWS, WROWS), WROWS)
        low = qkv_low(s, rows, h1, wq, bias, half)
        grad = (dot_nt(ga[rows, :half], block(wp, s, 0)) + dot_nt(ga[rows, half:], block(wp, s, 1))).astype(BF)
        parts = [[], [], []]
        for hh in range(heads):
            query, key, value = (head_of(low, part, heads, hh) for part in range(3))
            got = attend_back(
                query, key, value, head_of(grad, 0, heads, hh), rel_query[...], rel_back[...], codes
            )
            for part in range(3):
                parts[part].append(got[part][:, :HEAD])
            rel_grad[...] += got[3]
        grad_low = jnp.concatenate(parts[0] + parts[1] + parts[2], axis=1).astype(BF)
        gqkv[rows, : grad_low.shape[1]] = grad_low
        bias_grad[s] += jnp.sum(grad_low.astype(F32), axis=0, keepdims=True)
        back[rows, :half] += dot(grad_low, block(wq, s, 0))
        back[rows, half:] += dot(grad_low, block(wq, s, 1))

        @pl.when(m == count // 2 - 1)
        def _():
            half_done()


MESH_ID = pl.DeviceIdType.MESH
ARRAYS = ("qkv", "proj", "expand", "shrink")
CHUNK = 64
EPS = 1e-06
SPARE = 4


def halves(rows):
    first = (rows // 16 + 1) // 4 * 32
    return first, rows - first


def flip(index, k):
    return ((index // 2 + k // 2) % 2) * 2 + (index % 2 + k % 2) % 2


def block(ref, slab, half):
    value = ref[slab, half]
    return value.reshape(value.shape[0] * value.shape[1], value.shape[2])


def add_low(target, index, extra):
    target[index] = (target[index].astype(F32) + extra.astype(F32)).astype(BF)


def kernel(
    tokens_in, mask_in, out_grad_in, gain_one_in, shift_one_in, gain_two_in, shift_two_in, proj_bias_in, shrink_bias_in,
    qkv_bias_in, expand_bias_in, rel_h_in, rel_w_in, codes, qkv_src, proj_src, expand_src, shrink_src,
    block_out, input_grad, qkv_out, proj_out, expand_out, shrink_out, early_out, late_out, rel_out,
    rxq, rxp, rxe, rxs, ryq, ryp, rye, rys, rx2q, rx2p, rx2e, rx2s, ry2q, ry2p, ry2e, ry2s, rzq, rzp, rze, rzs, pair_back, pair_out,
    wq, wp, we, ws, tokens, keep, h1, grads, normed, got_low, attended, total, back, xr, xr2, middle, act, gpre,
    bias_all, early, early_full, early_half, late, late_full, late_half, rel, rel_full, rel_half, bias_e, bias_q, rel_acc, rel_query, rel_back, rel_pad,
    gsend, grecv, rsend, rrecv, fsend, frecv, csend, crecv, zsend, zrecv, qsend, qrecv, local, qlocal,
):
    d, r, z = lax.axis_index("dp"), lax.axis_index("row"), lax.axis_index("col")
    h, b = d // 2, d % 2
    own = tokens.shape[0]
    width = tokens.shape[1]
    half = width // 2
    heads = 2
    bufs = (wq, wp, we, ws)
    outs = (qkv_out, proj_out, expand_out, shrink_out)
    rx, ry = (rxq, rxp, rxe, rxs), (ryq, ryp, rye, rys)
    rx2, ry2 = (rx2q, rx2p, rx2e, rx2s), (ry2q, ry2p, ry2e, ry2s)
    rz = (rzq, rzp, rze, rzs)
    parts = [halves(buf.shape[3]) for buf in bufs]
    attn, mlp = (0, 1), (2, 3)
    qkv_width = 3 * attended.shape[2]

    along_x = (h * 2 + 1 - b, r, z)
    along_y = ((1 - h) * 2 + b, r, z)
    across = ((1 - h) * 2 + 1 - b, r, z)
    partner = (d, 1 - r, z)
    pair, remote_slab = (d, r, flip(z, 1)), flip(z, 2)
    gm, gmz, h2, h2z = grads.at[0], grads.at[1], normed.at[0], normed.at[1]

    def along_z(k):
        return (d, r, flip(z, k))

    def remote(src, dst, sems, recvs, index, device, got=None):
        return pltpu.make_async_remote_copy(
            src_ref=src,
            dst_ref=dst,
            send_sem=sems.at[index],
            recv_sem=recvs.at[index if got is None else got],
            device_id=device,
            device_id_type=MESH_ID,
        )

    up = z // 2
    is_end = (z + 1) // 2 % 2 == 0
    is_inner = (z + 1) // 2 % 2 == 1

    def slab_of(i):
        far = i // 2
        return (1 - far) * flip(z, i) + far * ((1 - up) * i + up * (3 - i))

    def first_part(a):
        return pl.ds(0, parts[a][0])

    def second_part(a):
        return pl.ds(parts[a][0], parts[a][1])

    def gather_z(a, s, step):
        at = bufs[a].at[s, h, b]
        return remote(at, at, gsend, grecv, (a, s, 0 if step < 0 else 5), (d, r, z + step), (a, s, 0))

    def gather_far(a):
        return remote(bufs[a].at[0, h, b], bufs[a].at[1, h, b], gsend, grecv, (a, 0, 0), (d, r, remote_slab))

    def ring(a, slab, sends, recvs, index, kind, arriving):
        buf = bufs[a]
        if kind == 1:
            at, device = (buf.at[slab, h, 1 - b] if arriving else buf.at[slab, h, b]), along_x
        elif kind == 2:
            at, device = (buf.at[slab, 1 - h, b] if arriving else buf.at[slab, h, b]), along_y
        elif kind == 3:
            at = buf.at[slab, 1 - h if arriving else h, 1 - b, first_part(a)]
            device = along_y
        else:
            at = buf.at[slab, 1 - h, 1 - b if arriving else b, second_part(a)]
            device = along_x
        return remote(at, at, sends, recvs, index, device)

    def gather(a, s, kind, arriving=False):
        return ring(a, s, gsend, grecv, (a, s, kind), kind, arriving)

    def spread(a, kind, arriving=False):
        return ring(a, final_slot(a), fsend, frecv, (a, kind), kind, arriving)

    def sends_along_z(group, s, act_on):
        for a in group:

            @pl.when((s >= z) & (z > 0))
            def _():
                act_on(gather_z(a, s, -1))

            @pl.when((s <= z) & (z < 3))
            def _():
                act_on(gather_z(a, s, 1))

    def start_z(group):
        sends_along_z(group, z, lambda copy: copy.start())

    def relay(group, i):
        s = slab_of(i)
        for a in group:
            gather_z(a, s, 1).wait_recv()
            sends_along_z((a,), s, lambda copy: copy.start())

    def place_of(a, i):
        return slab_of(i) if a in attn else 1

    def share(group, i):
        for a in group:
            gather(a, place_of(a, i), 1).start()
            gather(a, place_of(a, i), 2).start()

    def share_far(group):
        for a in group:
            gather_far(a).wait_recv()
            share((a,), 1)

    def pass_diagonal(group, i):
        for a in group:
            s = place_of(a, i)
            gather(a, s, 1, True).wait_recv()
            gather(a, s, 3).start()
            gather(a, s, 2, True).wait_recv()
            gather(a, s, 4).start()

    def finish_slab(group, i):
        for a in group:
            s = place_of(a, i)
            gather(a, s, 3, True).wait_recv()
            gather(a, s, 4, True).wait_recv()

    def sent_slab(group, i):
        s = slab_of(i)
        sends_along_z(group, s, lambda copy: copy.wait_send())
        for a in group:

            @pl.when(i > 0)
            def _():
                for kind in (1, 2, 3, 4):
                    gather(a, s, kind).wait_send()

    def sent_far(group):
        for a in group:
            gather_far(a).wait_send()
            for kind in (1, 2, 3, 4):
                gather(a, 1, kind).wait_send()

    def step_slab(n):
        return slab_of(3 - n)

    def final_slot(a):
        return z if a in attn else 0

    def slot(a, n):
        if a in mlp:
            return 2 + n
        first = (4 - n) // 4
        return first * SPARE + (1 - first) * step_slab(n - 1 + first)

    def reduce_copy(a, n, kind):
        buf, g = bufs[a], slot(a, n)
        got = None
        if kind == 0:
            src, dst, device = buf.at[g, :, 1 - b, first_part(a)], rx[a].at[n], along_x
        elif kind == 1:
            src, dst, device = buf.at[g, 1 - h, :, second_part(a)], ry[a].at[n], along_y
        elif kind == 2:
            src, dst, device = buf.at[g, 1 - h, b, first_part(a)], ry2[a].at[n], along_y
        elif kind == 3:
            src, dst, device = buf.at[g, h, 1 - b, second_part(a)], rx2[a].at[n], along_x
        elif kind == 4 and a in mlp:
            src, dst, device = buf.at[g, h, b], rz[a].at[0], (d, r, remote_slab)
            got = (a, 0, 4)
        elif kind == 4:
            src, dst, device = buf.at[g, h, b], rz[a].at[z], (d, r, step_slab(n))
            got = (a, z, 4)
        else:
            src, dst, device = buf.at[g, h, b], rz[a].at[5 - n], (d, r, slab_of(1))
            got = (a, 3 - n, 5)
        return remote(src, dst, rsend, rrecv, (a, n, min(kind, 4)), device, got)

    def reduce_z(a, n, act_on):
        if a in mlp:

            @pl.when(n == 1)
            def _():
                act_on(reduce_copy(a, n, 4))

        else:

            @pl.when((n < 3) & (is_inner | (n == 2)))
            def _():
                act_on(reduce_copy(a, n, 4))

            @pl.when(is_end & (n < 2))
            def _():
                act_on(reduce_copy(a, n, 5))

    def reduce_one(group, n):
        for a in group:
            reduce_copy(a, n, 0).start()
            reduce_copy(a, n, 1).start()

    def with_room(body):
        def run(group, n):
            shape = (2 * len(group), 2, halves(max(bufs[a].shape[3] for a in group))[0], half)
            pl.run_scoped(
                lambda room: body(group, n, lambda a, place: room.at[2 * group.index(a) + place]),
                pltpu.VMEM(shape, BF),
            )

        return run

    def reduce_two_body(group, n, scratch):
        loads = []
        for a in group:
            reduce_copy(a, n, 0).wait_recv()
            reduce_copy(a, n, 1).wait_recv()
            for place, got in enumerate((rx[a], ry[a])):
                to = scratch(a, place).at[:, pl.ds(0, parts[a][place])]
                loads.append(pltpu.make_async_copy(got.at[n], to, local.at[a * 2 + place]))
                loads[-1].start()
        for i, a in enumerate(group):
            g = slot(a, n)
            first, second = parts[a]
            loads[2 * i].wait()
            for side in range(2):
                add_low(bufs[a], (g, side, b, first_part(a)), scratch(a, 0)[side, :first])
            reduce_copy(a, n, 2).start()
            loads[2 * i + 1].wait()
            for side in range(2):
                add_low(bufs[a], (g, h, side, second_part(a)), scratch(a, 1)[side, :second])
            reduce_copy(a, n, 3).start()

    def reduce_three_body(group, n, scratch):
        loads = []
        for a in group:
            reduce_copy(a, n, 2).wait_recv()
            reduce_copy(a, n, 3).wait_recv()
            for place, got in enumerate((ry2[a], rx2[a])):
                to = scratch(a, place).at[0, pl.ds(0, parts[a][place])]
                loads.append(pltpu.make_async_copy(got.at[n], to, local.at[a * 2 + place]))
                loads[-1].start()
        for i, a in enumerate(group):
            g = slot(a, n)
            first, second = parts[a]
            loads[2 * i].wait()
            add_low(bufs[a], (g, h, b, first_part(a)), scratch(a, 0)[0, :first])
            loads[2 * i + 1].wait()
            add_low(bufs[a], (g, h, b, second_part(a)), scratch(a, 1)[0, :second])

            @pl.when(is_inner & (n < 2) & (a in attn))
            def _():
                at = rz[a].at[5 - n]
                remote(at, at, rsend, rrecv, (a, n, 4), (d, r, slab_of(1)), (a, 3 - n, 5)).wait_recv()
                pieces = ((0, first, first_part(a)), (1, second, second_part(a)))
                copies = [
                    pltpu.make_async_copy(at.at[part], scratch(a, 0).at[side, pl.ds(0, count)], local.at[a * 2 + side])
                    for side, count, part in pieces
                ]
                for copy in copies:
                    copy.start()
                for copy, (side, count, part) in zip(copies, pieces):
                    copy.wait()
                    add_low(bufs[a], (g, h, b, part), scratch(a, 0)[side, :count])

            reduce_z(a, n, lambda copy: copy.start())

    def reduce_two(group, n):
        with_room(reduce_two_body)(group, n)

    def reduce_three(group, n):
        with_room(reduce_three_body)(group, n)

    def reduce_four(group):
        for a in group:
            rows = bufs[a].shape[3]
            loads = []
            others = ((remote_slab, 0),) if a in mlp else [(slab_of(k), slab_of(k)) for k in (1, 2)]
            for k, (other, place) in enumerate(others, 1):
                at = rz[a].at[place]
                remote(at, at, rsend, rrecv, (a, k, 4), (d, r, other), (a, place, 4)).wait_recv()
                loads.append(pltpu.make_async_copy(at, gpre.at[pl.ds((k - 1) * rows, rows)], local.at[k]))
                loads[-1].start()
            for load in loads:
                load.wait()
            value = bufs[a][slot(a, 0 if a in mlp else 3), h, b].astype(F32)
            for k in range(len(others)):
                value = value + gpre[k * rows : (k + 1) * rows].astype(F32)
            bufs[a][final_slot(a), h, b] = value.astype(BF)
            spread(a, 1).start()
            spread(a, 2).start()

    def reduce_five(group):
        for a in group:
            spread(a, 1, True).wait_recv()
            spread(a, 3).start()
            spread(a, 2, True).wait_recv()
            spread(a, 4).start()

    def qkv_pieces(matrix, side, flat):
        rows = flat.shape[1]
        part = matrix.shape[2]
        cut = rows - part
        return (
            (matrix.at[0, side], flat.at[0, pl.ds(0, part)]),
            (matrix.at[1, side, pl.ds(0, cut)], flat.at[0, pl.ds(part, cut)]),
            (matrix.at[1, side, pl.ds(cut, part - cut)], flat.at[1, pl.ds(0, part - cut)]),
            (matrix.at[2, side], flat.at[1, pl.ds(part - cut, part)]),
        )

    def swap_out(a):
        mine = bufs[a].at[final_slot(a), 1 - r]
        if a == 0:
            pairs = qkv_pieces(outs[a], r, mine)
            return [remote(src, dst, qsend, qrecv, 4 + i, partner) for i, (dst, src) in enumerate(pairs)]
        to = outs[a].at[:, :, half_lanes(r)] if a == 2 else outs[a].at[r]
        return [remote(mine, to, fsend, frecv, (a, 0), partner)]

    def keep_out(a):
        mine = bufs[a].at[final_slot(a), r]
        if a == 0:
            pairs = qkv_pieces(outs[a], r, mine)
            return [pltpu.make_async_copy(src, dst, qlocal.at[i]) for i, (dst, src) in enumerate(pairs)]
        to = outs[a].at[:, :, half_lanes(r)] if a == 2 else outs[a].at[r]
        return [pltpu.make_async_copy(mine, to, local.at[a])]

    def reduce_six(group):
        for a in group:
            spread(a, 3, True).wait_recv()
            spread(a, 4, True).wait_recv()
            for copy in swap_out(a) + keep_out(a):
                copy.start()

    def half_lanes(side):
        return pl.ds(pl.multiple_of(side * half, half), half)

    def exchange(index, src, dst):
        return remote(src, dst, csend, crecv, index, partner)

    rows_own, rows_other = pl.ds(0, own), pl.ds(own, own)
    def source(a, side):
        if a == 2:
            return expand_src.at[:, :, half_lanes(side)]
        return (qkv_src, proj_src, expand_src, shrink_src)[a].at[side]

    def source_swap(a):
        to = bufs[a].at[z if a in attn else 0, r]
        if a == 0:
            pairs = qkv_pieces(qkv_src, 1 - r, to)
            return [remote(src, dst, qsend, qrecv, i, partner) for i, (src, dst) in enumerate(pairs)]
        return [exchange(a, source(a, 1 - r), to)]

    def source_keep(a):
        to = bufs[a].at[z if a in attn else 0, r]
        if a == 0:
            pairs = qkv_pieces(qkv_src, r, to)
            return [pltpu.make_async_copy(src, dst, qlocal.at[i]) for i, (src, dst) in enumerate(pairs)]
        return [pltpu.make_async_copy(source(a, r), to, local.at[a])]

    def start_source(group):
        for a in group:
            for copy in source_swap(a) + source_keep(a):
                copy.start()

    def finish_source(group):
        for a in group:
            for copy in source_swap(a) + source_keep(a):
                copy.wait()

    swap_grad = exchange(4, gm.at[rows_own], gm.at[rows_other])
    swap_h1 = exchange(5, h1.at[rows_own], h1.at[rows_other])
    swap_attn = exchange(6, total.at[rows_other], xr)
    swap_h2 = exchange(7, h2.at[rows_own], h2.at[rows_other])
    swap_mlp = exchange(8, total.at[rows_other], xr)
    swap_gh2 = exchange(9, back.at[rows_other], xr2)
    swap_ga = exchange(10, gm.at[rows_own], gm.at[rows_other])
    swap_gh1 = exchange(11, back.at[rows_other], total.at[rows_other])
    pair_gm = remote(gm.at[rows_own], gmz.at[rows_own], csend, crecv, 12, pair)
    swap_gmz = exchange(13, gmz.at[rows_own], gmz.at[rows_other])
    pair_h2 = remote(h2.at[rows_own], h2z.at[rows_own], csend, crecv, 14, pair)
    swap_h2z = exchange(15, h2z.at[rows_own], h2z.at[rows_other])
    swap_back_low = exchange(16, h2.at[rows_own], got_low.at[rows_own])
    swap_out_low = exchange(17, h2.at[rows_other], got_low.at[rows_other])
    send_back = remote(h2.at[rows_own], pair_back, csend, crecv, 18, pair)
    send_out = remote(h2.at[rows_other], pair_out, csend, crecv, 19, pair)

    def bias_copy(k, arriving=False):
        at = bias_all.at[flip(z, k) if arriving else z]
        return remote(at, at, zsend, zrecv, k, along_z(k))

    barrier = pltpu.get_barrier_semaphore()
    peers = [partner, along_x, along_y, across, along_z(1), along_z(2), along_z(3)]
    for peer in peers:
        pl.semaphore_signal(barrier, inc=1, device_id=peer, device_id_type=MESH_ID)
    pl.semaphore_wait(barrier, len(peers))

    start_source(attn)
    bias_all[z] = jnp.zeros(bias_all.shape[1:], F32)
    part = qkv_bias_in.shape[1] // 2
    for side in range(2):

        @pl.when(r == side)
        def _():
            bias_all[z, 0:1, :half] = expand_bias_in[side * half : (side + 1) * half].reshape(1, half)
            for i in range(2):
                at = half + 2 * i * part
                bias_all[z, 0:1, at : at + part] = qkv_bias_in[i : i + 1, side * part : (side + 1) * part]

    finish_source(attn)
    start_z(attn)
    for k in (1, 2, 3):
        bias_copy(k).start()
    start_source(mlp)

    def as_row(ref):
        return ref[...].reshape(1, width)

    gain_one, shift_one, gain_two, shift_two, proj_bias, shrink_bias = (
        as_row(ref) for ref in (gain_one_in, shift_one_in, gain_two_in, shift_two_in, proj_bias_in, shrink_bias_in)
    )

    def over_rows(body):
        @pl.loop(0, own // CHUNK)
        def _(m):
            body(pl.ds(pl.multiple_of(m * CHUNK, CHUNK), CHUNK))

    def column_sum(value):
        return jnp.sum(value, axis=0, keepdims=True)

    def normalize(value):
        center = value - jnp.mean(value, axis=1, keepdims=True)
        inverse = lax.rsqrt(jnp.mean(center * center, axis=1, keepdims=True) + EPS)
        return center * inverse, inverse

    def norm_back(grad, gain, xhat, inverse):
        scaled = grad * gain
        mean = jnp.mean(scaled, axis=1, keepdims=True)
        along = jnp.mean(scaled * xhat, axis=1, keepdims=True)
        return (scaled - mean - xhat * along) * inverse

    early[...] = jnp.zeros_like(early)
    late[...] = jnp.zeros_like(late)

    def spread_rows(source, target):
        def move(stage):
            load = pltpu.make_async_copy(source, stage, local.at[8])
            load.start()
            load.wait()

            @pl.loop(0, SIDE)
            def _(i):
                both = stage[pl.ds(i * SIDE, SIDE)].astype(F32)
                for w in range(both.shape[1]):
                    some = jnp.concatenate([both[:, w], jnp.zeros((SIDE_PAD - SIDE, width), F32)], axis=0)
                    at = pl.multiple_of(w * WROWS + i * SIDE_PAD, SIDE_PAD)
                    target[pl.ds(at, SIDE_PAD)] = some.astype(BF)

        pl.run_scoped(move, pltpu.VMEM(source.shape, BF))

    spread_rows(tokens_in, tokens)
    count = mask_in.shape[0]
    mask = jnp.concatenate([mask_in[...].astype(F32), jnp.zeros((count, 2 * LANES - SIDE * SIDE), F32)], axis=1)
    mask = jnp.concatenate([mask, jnp.zeros((8 - count, 2 * LANES), F32)], axis=0).T
    keep[...] = jnp.zeros_like(keep)
    for i in range(SIDE):
        for w in range(count):
            at = w * WROWS + i * SIDE_PAD
            keep[at : at + SIDE] = mask[i * SIDE : (i + 1) * SIDE, w : w + 1]

    def first_rows(rows):
        value = tokens[rows].astype(F32)
        valid = keep[rows]
        xhat, _ = normalize(value)
        h1[rows] = ((xhat * gain_one + shift_one) * valid).astype(BF)
        early[0:1, :] += column_sum(valid * value * value)
        early[5:6, :] += jnp.broadcast_to(column_sum(valid), (1, width))

    over_rows(first_rows)
    swap_h1.start()
    spread_rows(out_grad_in, gm)
    swap_grad.start()
    rel_pad[...] = jnp.zeros_like(rel_pad)
    rel_pad[0, : rel_h_in.shape[0]] = rel_h_in[...]
    rel_pad[1, : rel_w_in.shape[0]] = rel_w_in[...]
    relative_tables(rel_pad.at[0], rel_pad.at[1], rel_query, rel_back)
    total[...] = jnp.zeros_like(total)
    swap_h1.wait_recv()

    def bias_q_of(s):
        return bias_all[s, 0:1, half : half + qkv_width]

    def bias_e_of(s):
        return bias_all[s, 0:1, :half]

    finish_source(mlp)

    def start_far():
        for a in mlp:
            gather_far(a).start()
        pair_gm.start()

    @pl.loop(0, 4)
    def _(i):
        @pl.when(i == 1)
        def _():
            @pl.when(is_end)
            def _():
                relay(attn, 2)
                share(attn, 2)
                start_far()

            relay(attn, 3)
            pass_diagonal(attn, 1)
            share(attn, 3)
            pass_diagonal(attn, 2)

            @pl.when(is_inner)
            def _():
                start_far()

            for k in (1, 2, 3):
                bias_copy(k, True).wait_recv()

        @pl.when(i > 0)
        def _():
            finish_slab(attn, i)

        @pl.when(i == 2)
        def _():
            pass_diagonal(attn, 3)

        @pl.when(((i == 2) & is_inner) | ((i == 3) & is_end))
        def _():
            share_far(mlp)

        s = slab_of(i)

        def half_done():
            @pl.when(i == 0)
            def _():
                relay(attn, 1)
                share(attn, 1)

                @pl.when(is_inner)
                def _():
                    relay(attn, 2)
                    share(attn, 2)

            @pl.when(i == 3)
            def _():
                swap_attn.start()

        attention_slab(
            s, h1, wq, wp, bias_q_of(s), rel_query, codes, attended, total, heads, half, half_done
        )


    swap_attn.wait()

    def middle_rows(rows):
        value = tokens[rows].astype(F32)
        valid = keep[rows]
        attn_out = total[rows] + xr[rows] + proj_bias
        mid = value + attn_out
        middle[rows] = mid
        xhat, _ = normalize(mid)
        h2[rows] = (xhat * gain_two + shift_two).astype(BF)
        early[1:2, :] += column_sum(valid * mid * mid)
        early[3:4, :] += column_sum(valid * attn_out * attn_out)

    over_rows(middle_rows)
    swap_h2.start()
    pair_h2.start()
    total[...] = jnp.zeros_like(total)
    back[...] = jnp.zeros_like(back)
    bias_e[...] = jnp.zeros_like(bias_e)
    bias_q[...] = jnp.zeros_like(bias_q)
    rel_acc[...] = jnp.zeros_like(rel_acc)
    swap_grad.wait()

    def add_grad(buf, p, j, side, value):
        value = value.reshape(buf.shape[2:]) + jnp.where(p > 0, buf[2 + j, side].astype(F32), 0.0)
        buf[2 + j, side] = value.astype(BF)

    def weight_grads(p, j, done):
        sides = [(side, slice(side * half, side * half + half)) for side in range(2)]
        for side, columns in sides:
            add_grad(we, p, j, side, dot_tn(normed[p, :, columns], gpre[...]))
        done((2,))
        for side, columns in sides:
            add_grad(ws, p, j, side, dot_tn(act[...], grads[p, :, columns]))
        done((3,))

    def own_rows(rows):
        xr[rows] = xr[rows] + total[rows]
        xr2[rows] = xr2[rows] + back[rows]

    def other_rows(rows):
        return pl.ds(pl.multiple_of(rows.start + own, CHUNK), CHUNK)

    def back_low_rows(rows):
        h2[rows] = back[other_rows(rows)].astype(BF)

    def out_low_rows(rows):
        h2[other_rows(rows)] = total[other_rows(rows)].astype(BF)

    def back_sum_rows(rows):
        h2[rows] = (back[rows] + got_low[rows].astype(F32)).astype(BF)

    def out_sum_rows(rows):
        h2[other_rows(rows)] = (total[rows] + got_low[other_rows(rows)].astype(F32)).astype(BF)

    def between_passes():
        pair_h2.wait()
        swap_h2z.start()
        swap_mlp.wait()
        swap_gh2.wait()
        over_rows(own_rows)
        total[...] = jnp.zeros_like(total)
        back[...] = jnp.zeros_like(back)
        swap_gmz.wait()
        swap_h2z.wait()

    def start_pair_sums():
        over_rows(back_low_rows)
        swap_back_low.start()
        over_rows(out_low_rows)
        swap_out_low.start()

    def send_pair_sums():
        swap_back_low.wait()
        over_rows(back_sum_rows)
        send_back.start()
        swap_out_low.wait()
        over_rows(out_sum_rows)
        send_out.start()

    @pl.loop(0, 8)
    def _(t):
        p, j = t // 4, (t // 2 + t // 4) % 2
        s = (1 - j) * z + j * remote_slab

        @pl.when(t == 1)
        def _():
            pass_diagonal(mlp, 1)
            swap_h2.wait()

        @pl.when(t == 2)
        def _():
            finish_slab(mlp, 1)
            pair_gm.wait_recv()
            swap_gmz.start()

        @pl.when(t == 3)
        def _():
            swap_mlp.start()
            swap_gh2.start()

        @pl.when(t == 4)
        def _():
            between_passes()

        @pl.when(t == 7)
        def _():
            start_pair_sums()

        mlp_rows(
            s, j, (t + t // 2) % 2, normed.at[p], grads.at[p], we, ws, bias_e_of(s), act, gpre, total, back, bias_e, half
        )

        @pl.when(t == 7)
        def _():
            send_pair_sums()

        @pl.when(t % 2 == 1)
        def _():
            def done(group):
                @pl.when(t == 5)
                def _():
                    reduce_one(group, 1)

            weight_grads(p, j, done)

    sent_far(mlp)
    reduce_two(mlp, 1)
    reduce_one(mlp, 0)
    send_back.wait_recv()
    back_load = pltpu.make_async_copy(pair_back, gmz.at[rows_own], local.at[8])
    back_load.start()
    back_load.wait()

    pair_gm.wait_send()

    def middle_back_rows(rows):
        mid = middle[rows]
        grad_out = gm[rows].astype(F32)
        early[9:10, :] += column_sum(grad_out)
        grad = xr2[rows] + gmz[rows].astype(F32)
        xhat, inverse = normalize(mid)
        early[6:7, :] += column_sum(grad * xhat)
        early[7:8, :] += column_sum(grad)
        grad_mid = grad_out + norm_back(grad, gain_two, xhat, inverse)
        xr2[rows] = grad_mid
        low = grad_mid.astype(BF)
        gm[rows] = low
        early[8:9, :] += column_sum(low.astype(F32))

    over_rows(middle_back_rows)
    swap_ga.start()

    def result_rows(rows):
        valid = keep[rows]
        mlp_out = xr[rows] + gmz[other_rows(rows)].astype(F32) + shrink_bias
        result = middle[rows] + mlp_out
        h2[rows] = result.astype(BF)
        early[2:3, :] += column_sum(valid * result * result)
        early[4:5, :] += column_sum(valid * mlp_out * mlp_out)

    back[...] = jnp.zeros_like(back)
    for i in range(4):
        sent_slab(attn, i)
    reduce_three(mlp, 1)
    swap_ga.wait()

    out_load = pltpu.make_async_copy(pair_out, gmz.at[rows_other], local.at[8])

    def interleave(source, target):
        def move(stage):
            @pl.loop(0, SIDE)
            def _(i):
                places = [pl.multiple_of(w * WROWS + i * SIDE_PAD, SIDE_PAD) for w in range(stage.shape[1])]
                some = [source[pl.ds(at, SIDE_PAD)][:SIDE].astype(F32) for at in places]
                stage[pl.ds(i * SIDE, SIDE)] = jnp.stack(some, axis=1).astype(stage.dtype)

            store = pltpu.make_async_copy(stage, target, local.at[8])
            store.start()
            store.wait()

        pl.run_scoped(move, pltpu.VMEM(target.shape, target.dtype))

    def finish_result():
        send_back.wait_send()
        send_out.wait_recv()
        out_load.start()
        out_load.wait()
        over_rows(result_rows)

    stages = (partner,), (along_z(1), along_z(2), along_z(3)), (along_x, along_y, across), (partner,)
    early_sums = (((early, early_full, early_half),), 20)
    late_sums = (((late, late_full, late_half), (rel, rel_full, rel_half)), 28)

    def small_copies(sums, stage):
        pairs, base = sums
        first = (0, 1, 4, 7)[stage]
        for i, device in enumerate(stages[stage]):
            for q, (src, full, part) in enumerate(pairs):
                rows = part.shape[1]
                mine = pl.ds(pl.multiple_of(r * rows, rows), rows)
                index = base + (first + i) * len(pairs) + q
                if stage == 0:
                    yield src, full, slice(None), remote(src, full, csend, crecv, index, device)
                else:
                    got = part.at[first + i - 1]
                    yield src, got, mine, remote(src.at[mine], got, csend, crecv, index, device)

    def small_start(sums, stage):
        for _, _, _, copy in small_copies(sums, stage):
            copy.start()

    def small_finish(sums, stage):
        copies = list(small_copies(sums, stage))
        for _, _, _, copy in copies:
            copy.wait()
        for src, got, rows, _ in copies:
            if stage == 3:
                count = got.shape[0]
                src[pl.ds(pl.multiple_of((1 - r) * count, count), count)] = got[...]
            else:
                src[rows] += got[...]

    def on_side(act_on):
        for side in range(2):

            @pl.when(r == side)
            def _():
                act_on(side)

    def fill_early(side):
        for s in range(4):
            early[10 + s : 11 + s, side * half : (side + 1) * half] = bias_e[s]

    early_store = pltpu.make_async_copy(early, early_out, local.at[9])

    @pl.loop(0, 4)
    def _(n):
        s = slab_of(3 - n)
        g = slot(0, n)

        def half_done():
            @pl.when(n == 0)
            def _():
                reduce_two(mlp, 0)

            @pl.when(n == 1)
            def _():
                reduce_four((2,))

            @pl.when(n == 2)
            def _():
                small_finish(early_sums, 0)
                small_start(early_sums, 1)
                reduce_four((3,))

            @pl.when(n == 3)
            def _():
                swap_gh1.start()
                small_finish(early_sums, 1)
                small_start(early_sums, 2)

        attention_back_slab(
            s, h1, gm, wq, wp, bias_q_of(s), rel_query, rel_back, codes, act, back, bias_q, rel_acc, heads, half, half_done
        )

        @pl.when(n > 0)
        def _():
            reduce_two(attn, n - 1)

        for side in range(2):
            columns = slice(side * half, side * half + half)
            wq[g, side] = dot_tn(act[:, :qkv_width], h1[:, columns]).astype(BF).reshape(wq.shape[2:])
            wp[g, side] = dot_tn(attended[s], gm[:, columns]).astype(BF).reshape(wp.shape[2:])
        reduce_one(attn, n)

        @pl.when((n > 1) & is_end)
        def _():
            reduce_three(attn, n - 2)

        @pl.when((n == 3) & is_inner)
        def _():
            reduce_three(attn, 0)

        @pl.when(n == 0)
        def _():
            reduce_three(mlp, 0)

        @pl.when(n == 1)
        def _():
            finish_result()
            on_side(fill_early)
            small_start(early_sums, 0)

    swap_gh1.wait()

    def input_rows(rows):
        value = tokens[rows].astype(F32)
        grad = (back[rows] + total[other_rows(rows)]) * keep[rows]
        xhat, inverse = normalize(value)
        for place, value in ((8, column_sum(grad * xhat)), (10, column_sum(grad))):
            late[place : place + 1, :] += value[:, :half]
            late[place + 1 : place + 2, :] += value[:, half:]
        xr2[rows] = xr2[rows] + norm_back(grad, gain_one, xhat, inverse)

    over_rows(input_rows)

    def fill_late(side):
        for s in range(4):
            late[2 * s + side : 2 * s + side + 1, :qkv_width] = bias_q[s]

    on_side(fill_late)
    for part, at in ((0, 0), (1, COL_W)):
        rows = slice(at, at + 32)
        rel[part * 32 : part * 32 + 32] = rel_acc[rows] + rel_acc[LANES + at : LANES + at + 32]

    small_start(late_sums, 0)

    @pl.when(is_inner)
    def _():
        reduce_three(attn, 1)

    small_finish(late_sums, 0)
    small_start(late_sums, 1)
    reduce_three(attn, 2)
    reduce_five((2,))
    reduce_two(attn, 3)
    reduce_five((3,))
    interleave(xr2, input_grad)
    interleave(h2, block_out)
    reduce_three(attn, 3)
    reduce_four(attn)
    small_finish(late_sums, 1)
    small_start(late_sums, 2)
    reduce_six(mlp)
    small_finish(early_sums, 2)
    small_start(early_sums, 3)
    reduce_five(attn)
    small_finish(late_sums, 2)
    small_start(late_sums, 3)
    small_finish(early_sums, 3)
    early_store.start()
    small_finish(late_sums, 3)
    late_stores = [
        pltpu.make_async_copy(late, late_out, local.at[6]),
        pltpu.make_async_copy(rel, rel_out, local.at[7]),
    ]
    for copy in late_stores:
        copy.start()
    reduce_six(attn)

    swap_h1.wait_send()
    send_out.wait_send()
    for k in (1, 2, 3):
        bias_copy(k).wait_send()
    for a in range(4):
        for copy in swap_out(a) + keep_out(a):
            copy.wait()
        for kind in (1, 2, 3, 4):
            spread(a, kind).wait_send()
        for n in range(4 if a in attn else 2):
            for kind in range(4):
                reduce_copy(a, n, kind).wait_send()
            reduce_z(a, n, lambda copy: copy.wait_send())

    for copy in late_stores:
        copy.wait()
    early_store.wait()


def run_kernel(tokens, mask, out_grad, vectors, qkv_bias, expand_bias, rel_height, rel_width, sources):
    own, width = tokens.shape[1] * WROWS, tokens.shape[2]
    half = width // 2
    rows = [source.shape[-2] for source in sources]
    rows[0] = 3 * rows[0] // 2
    sds = jax.ShapeDtypeStruct
    any_spec = pl.BlockSpec(memory_space=pl.ANY)
    vmem_spec = pl.BlockSpec(memory_space=pltpu.VMEM)
    out_shape = [sds(tokens.shape, BF), sds(tokens.shape, F32)]
    out_shape += [sds(source.shape, BF) for source in sources]
    out_shape += [sds((16, width), F32), sds((16, half), F32), sds((64, LANES), F32)]
    first, second = zip(*[halves(n) for n in rows])
    out_shape += [sds((4, 2, n, half), BF) for n in first]
    out_shape += [sds((4, 2, n, half), BF) for n in second]
    out_shape += [sds((4, n, half), BF) for n in second]
    out_shape += [sds((4, n, half), BF) for n in first]
    out_shape += [sds((6, n, half), BF) for n in rows]
    out_shape += [sds((own, width), BF)] * 2
    both = 2 * own
    vmem, dma = pltpu.VMEM, pltpu.SemaphoreType.DMA
    qkv_width = 2 * rows[0]
    scratch = [vmem((count, 2, 2, n, half), BF) for count, n in zip((5, 5, 4, 4), rows)]
    scratch += [vmem((own, width), BF), vmem((own, 1), F32)]
    scratch += [vmem((both, width), BF)] + [vmem((2, both, width), BF)] * 2 + [vmem((both, width), BF)]
    scratch += [vmem((4, both, qkv_width // 3), BF)]
    scratch += [vmem((both, width), F32)] * 2
    scratch += [vmem((own, width), F32)] * 3
    scratch += [vmem((both, half), BF), vmem((both, half), BF)]
    scratch += [vmem((4, 8, width), F32), vmem((16, width), F32), vmem((16, width), F32), vmem((7, 8, width), F32)]
    scratch += [vmem((16, half), F32), vmem((16, half), F32), vmem((7, 8, half), F32)]
    scratch += [vmem((64, LANES), F32), vmem((64, LANES), F32), vmem((7, 32, LANES), F32)]
    scratch += [vmem((4, 1, half), F32), vmem((4, 1, qkv_width), F32), vmem((2 * LANES, LANES), F32)]
    scratch += [vmem((2 * LANES, LANES), BF), vmem((3 * LANES, LANES), BF), vmem((2, 32, HEAD), F32)]
    scratch += [dma((4, 4, 6))] * 2 + [dma((4, 4, 5)), dma((4, 4, 6))] + [dma((4, 5))] * 2 + [dma((44,))] * 2
    scratch += [dma((4,))] * 2 + [dma((8,))] * 2 + [dma((11,)), dma((4,))]
    got = pl.pallas_call(
        kernel,
        out_shape=out_shape,
        in_specs=[any_spec, vmem_spec, any_spec] + [vmem_spec] * 11 + [any_spec] * 4,
        out_specs=[any_spec] * len(out_shape),
        scratch_shapes=scratch,
        compiler_params=pltpu.CompilerParams(
            collective_id=0, has_side_effects=True, vmem_limit_bytes=VMEM_LIMIT
        ),
        name="block_step",
    )(tokens, mask, out_grad, *vectors, qkv_bias, expand_bias, rel_height, rel_width, key_codes(), *sources)
    return got[:9]


def finish_kernel(early, late, rel, *refs):
    wide, (bias_q, bias_e, height, width_out, rms), rows_out = refs[:6], refs[6:11], refs[11:17]
    outs, held, full, load, store = refs[17:23], refs[23:29], refs[29:33], refs[33], refs[34]
    z = lax.axis_index("col")
    loads = [pltpu.make_async_copy(src, to, load.at[i]) for i, (src, to) in enumerate(zip(wide, held))]
    full = list(full) + list(held[4:])
    stores = [pltpu.make_async_copy(src, to, store.at[i]) for i, (src, to) in enumerate(zip(full, outs))]
    for i in (3, 2, 5, 4, 0, 1):
        loads[i].start()
    features = early.shape[1]
    half = features // 2
    for ref, at in zip(rows_out[:2], (8, 10)):
        ref[:half] = late[at, :]
        ref[half:] = late[at + 1, :]
    for ref, at in zip(rows_out[2:], (6, 7, 8, 9)):
        ref[...] = early[at, :]
    lane = lax.broadcasted_iota(jnp.int32, (1, LANES), 1)
    stats = jnp.zeros((1, LANES), F32)
    for i in range(rms.shape[0]):
        stats = jnp.where(lane == i, jnp.sum(early[i : i + 1, :], axis=1, keepdims=True), stats)
    rms[...] = jnp.sqrt(stats / (early[5:6, 0:1] * features))[0, : rms.shape[0]]
    part = bias_q.shape[1] // 2
    bias_e[...] = early[pl.ds(10 + z, 1), :].reshape(features)
    for side in range(2):
        row = late[pl.ds(2 * z + side, 1), :]
        for i in range(2):
            bias_q[i : i + 1, side * part : (side + 1) * part] = row[:, 2 * i * part : (2 * i + 1) * part]
    count = height.shape[0]
    turn = lax.broadcasted_iota(jnp.int32, (32, 32), 0) + lax.broadcasted_iota(jnp.int32, (32, 32), 1) == count - 1
    turned = jnp.dot(turn.astype(F32), rel[:32], precision=lax.Precision.HIGHEST, preferred_element_type=F32)
    height[...] = turned[:count, :HEAD]
    width_out[...] = rel[32 : 32 + count, :HEAD]
    for i in (3, 2, 0, 1):
        loads[i].wait()
        step = held[i].shape[0] // 5

        @pl.loop(0, 5)
        def _(m):
            at = pl.ds(pl.multiple_of(m * step, step), step)
            full[i][at] = held[i][at].astype(F32)

        stores[i].start()
        for j in {3: (5,), 2: (4,)}.get(i, ()):
            loads[j].wait()
            stores[j].start()
    for copy in stores:
        copy.wait()


def finish_outputs(got, part):
    early, late, rel = got[6:9]
    grads = [value.reshape(-1, value.shape[-1]) for value in got[2:6]]
    width = early.shape[1]
    sds = jax.ShapeDtypeStruct
    any_spec = pl.BlockSpec(memory_space=pl.ANY)
    vmem_spec = pl.BlockSpec(memory_space=pltpu.VMEM)
    out_shape = [sds((2, 2 * part), F32), sds((width,), F32), sds((2 * SIDE - 1, HEAD), F32)]
    out_shape += [sds((2 * SIDE - 1, HEAD), F32), sds((5,), F32)] + [sds((width,), F32)] * 6
    final = [sds(value.shape, F32) for value in grads]
    out_shape += final + [sds(value.shape, value.dtype) for value in got[:2]]
    return pl.pallas_call(
        finish_kernel,
        out_shape=out_shape,
        in_specs=[vmem_spec] * 3 + [any_spec] * 6,
        out_specs=[vmem_spec] * 11 + [any_spec] * 6,
        scratch_shapes=[pltpu.VMEM(value.shape, value.dtype) for value in grads + list(got[:2]) + final]
        + [pltpu.SemaphoreType.DMA((6,))] * 2,
        compiler_params=pltpu.CompilerParams(vmem_limit_bytes=VMEM_LIMIT),
        name="finish",
    )(early, late, rel, *grads, *got[:2])


VMEM_LIMIT = 64 * 1024 * 1024 - 512 * 1024


def over_chips(
    tokens, valid_mask, out_grad, first_gain, first_shift, qkv_weight, qkv_bias, rel_height, rel_width,
    proj_weight, proj_bias, second_gain, second_shift, expand_weight, expand_bias, shrink_weight, shrink_bias,
):
    def turned(value):
        return value.transpose(1, 0, 2)

    rows, _, local_width = qkv_weight.shape
    part = local_width // 2
    hidden = expand_weight.shape[1] // 2
    qkv_src = qkv_weight.transpose(1, 2, 0).reshape(3, 2, part, rows)
    proj_src = proj_weight.reshape(2, 2, part // 2, proj_weight.shape[1])
    expand_src = expand_weight.reshape(2, rows // 2, 2 * hidden)
    shrink_src = shrink_weight.reshape(2, 2, hidden // 2, shrink_weight.shape[1])
    vectors = (first_gain, first_shift, second_gain, second_shift, proj_bias, shrink_bias)
    got = run_kernel(
        turned(tokens), valid_mask, turned(out_grad), vectors, qkv_bias, expand_bias, rel_height, rel_width,
        (qkv_src, proj_src, expand_src, shrink_src),
    )
    outs = finish_outputs(got, part)
    qkv_bias_sum, expand_bias_sum, height_sum, width_sum, rms = outs[:5]
    gain_one, shift_one, gain_two, shift_two, proj_bias_sum, shrink_bias_sum = outs[5:11]
    qkv_sum, proj_sum, expand_sum, shrink_sum, block_out, input_grad = outs[11:]
    return (
        turned(block_out),
        turned(input_grad),
        gain_one,
        shift_one,
        qkv_sum.reshape(3, local_width, rows).transpose(2, 0, 1),
        qkv_bias_sum,
        height_sum,
        width_sum,
        proj_sum.reshape(proj_weight.shape),
        proj_bias_sum,
        gain_two,
        shift_two,
        expand_sum.reshape(expand_weight.shape),
        expand_bias_sum,
        shrink_sum.reshape(shrink_weight.shape),
        shrink_bias_sum,
        rms,
    )


epsilon = 1e-06
highest = lax.Precision.HIGHEST


def layer_norm(values, norm_gain, norm_shift):
    center = values - jnp.mean(values, axis=-1, keepdims=True)
    spread = jnp.mean(center * center, axis=-1, keepdims=True)
    return center * lax.rsqrt(spread + epsilon) * norm_gain + norm_shift


def offset_table(span_size):
    positions = jnp.arange(span_size)
    offset = positions[:, None] - positions[None, :] + span_size - 1
    return (offset[:, :, None] == jnp.arange(2 * span_size - 1)[None, None, :]).astype(jnp.float32)


def attention_scores(
    query_rows, key_rows, rel_rows_table, rel_cols_table, onehot_table, span_size, scaling
):
    window_count, tokens_per, head_count, head_size = query_rows.shape
    rel_count = 2 * span_size - 1
    direct = (
        jnp.einsum("bthc,buhc->bhtu", query_rows, key_rows, preferred_element_type=jnp.float32)
        * scaling
    )
    query_float = query_rows.astype(jnp.float32)
    along_rows = jnp.einsum("bthc,jc->bhtj", query_float, rel_rows_table, precision=highest)
    along_cols = jnp.einsum("bthc,jc->bhtj", query_float, rel_cols_table, precision=highest)
    grid_rows = along_rows.reshape(window_count, head_count, span_size, span_size, rel_count)
    grid_cols = along_cols.reshape(window_count, head_count, span_size, span_size, rel_count)
    rel_rows = jnp.einsum("bhxyj,xkj->bhxyk", grid_rows, onehot_table, precision=highest)
    rel_cols = jnp.einsum("bhxyj,ywj->bhxyw", grid_cols, onehot_table, precision=highest)
    score_sum = direct.reshape(window_count, head_count, span_size, span_size, span_size, span_size)
    score_sum = score_sum + rel_rows[:, :, :, :, :, None] + rel_cols[:, :, :, :, None, :]
    return score_sum.reshape(window_count, head_count, tokens_per, tokens_per)


def relative_back(score_float, onehot_table, span_size):
    window_count, head_count, tokens_per, other_tokens = score_float.shape
    grid = score_float.reshape(window_count, head_count, span_size, span_size, span_size, span_size)
    rows_part = jnp.einsum("bhxykw,xkj->bhxyj", grid, onehot_table, precision=highest)
    cols_part = jnp.einsum("bhxykw,ywj->bhxyj", grid, onehot_table, precision=highest)
    return (
        rows_part.reshape(window_count, head_count, tokens_per, -1),
        cols_part.reshape(window_count, head_count, tokens_per, -1),
    )


def gather_weights(qkv_weight, proj_weight, expand_weight, shrink_weight):
    return (
        lax.all_gather(qkv_weight, "row", axis=0, tiled=True),
        lax.all_gather(proj_weight, "row", axis=1, tiled=True),
        lax.all_gather(expand_weight, "row", axis=0, tiled=True),
        lax.all_gather(shrink_weight, "row", axis=1, tiled=True),
    )


def gather_tokens(normed):
    return lax.all_gather(normed, "col", axis=0, tiled=True)


def gather_grads(grad_low):
    return lax.all_gather(grad_low, "col", axis=0, tiled=True)


def sum_branch(inputs_low, weight_full, own_windows):

    def term(first_row, row_count):
        return jnp.einsum(
            "btk,kd->btd", inputs_low, weight_full, preferred_element_type=jnp.float32
        )

    return lax.psum_scatter(
        term(jnp.int32(0), own_windows * lax.axis_size("col")),
        "col",
        scatter_dimension=0,
        tiled=True,
    )


def sum_input(grads_low, weight_full, own_windows):

    def term(first_row, row_count):
        return jnp.einsum("btk,dk->btd", grads_low, weight_full, preferred_element_type=jnp.float32)

    return lax.psum_scatter(
        term(jnp.int32(0), own_windows * lax.axis_size("col")),
        "col",
        scatter_dimension=0,
        tiled=True,
    )


def activate(values):
    return jax.nn.gelu(values, approximate=False)


def per_device(
    tokens,
    valid_mask,
    out_grad,
    first_gain,
    first_shift,
    qkv_weight,
    qkv_bias,
    rel_height,
    rel_width,
    proj_weight,
    proj_bias,
    second_gain,
    second_shift,
    expand_weight,
    expand_bias,
    shrink_weight,
    shrink_bias,
):
    span_size = (rel_height.shape[0] + 1) // 2
    head_size = rel_height.shape[1]
    local_width = qkv_weight.shape[2]
    head_count = local_width // head_size
    own_windows = tokens.shape[0]
    tokens_per = tokens.shape[1]
    model_width = tokens.shape[2]
    scaling = head_size ** (-0.5)
    onehot_table = offset_table(span_size)
    inputs = tokens.astype(jnp.float32)
    keep_mask = valid_mask.astype(jnp.float32)[:, :, None]

    def first_norm(values, norm_gain, norm_shift):
        return layer_norm(values, norm_gain, norm_shift) * keep_mask

    qkv_full, proj_full, expand_full, shrink_full = gather_weights(
        qkv_weight, proj_weight, expand_weight, shrink_weight
    )
    normed_first, first_back = jax.vjp(first_norm, inputs, first_gain, first_shift)
    first_all = gather_tokens(normed_first.astype(jnp.bfloat16))
    all_windows = first_all.shape[0]
    bias_rows = jnp.stack([qkv_bias[0], jnp.zeros_like(qkv_bias[0]), qkv_bias[1]])
    projected = (
        jnp.einsum("btd,dsk->btsk", first_all, qkv_full, preferred_element_type=jnp.float32)
        + bias_rows
    )
    projected = projected.astype(jnp.bfloat16)
    head_shape = (all_windows, tokens_per, head_count, head_size)
    query_low = projected[:, :, 0].reshape(head_shape)
    key_low = projected[:, :, 1].reshape(head_shape)
    value_low = projected[:, :, 2].reshape(head_shape)
    scores = attention_scores(
        query_low, key_low, rel_height, rel_width, onehot_table, span_size, scaling
    )
    top_score = jnp.max(scores, axis=-1, keepdims=True)
    log_total = top_score + jnp.log(jnp.sum(jnp.exp(scores - top_score), axis=-1, keepdims=True))
    probs_low = jnp.exp(scores - log_total).astype(jnp.bfloat16)
    attended = jnp.einsum(
        "bhtu,buhc->bthc", probs_low, value_low, preferred_element_type=jnp.float32
    )
    attended_low = attended.reshape(all_windows, tokens_per, local_width).astype(jnp.bfloat16)
    attn_out = sum_branch(attended_low, proj_full, own_windows) + proj_bias
    middle = inputs + attn_out
    normed_second, second_back = jax.vjp(layer_norm, middle, second_gain, second_shift)
    second_all = gather_tokens(normed_second.astype(jnp.bfloat16))
    hidden_pre = (
        jnp.einsum("btd,df->btf", second_all, expand_full, preferred_element_type=jnp.float32)
        + expand_bias
    )
    active_value, active_back = jax.vjp(activate, hidden_pre)
    hidden_low = active_value.astype(jnp.bfloat16)
    mlp_out = sum_branch(hidden_low, shrink_full, own_windows) + shrink_bias
    result = middle + mlp_out
    stat_terms = jnp.stack(
        [
            jnp.sum(keep_mask * inputs * inputs),
            jnp.sum(keep_mask * middle * middle),
            jnp.sum(keep_mask * result * result),
            jnp.sum(keep_mask * attn_out * attn_out),
            jnp.sum(keep_mask * mlp_out * mlp_out),
        ]
    )
    valid_count = jnp.sum(keep_mask)
    stat_total, count_total = lax.psum((stat_terms, valid_count), ("dp", "row", "col"))
    out_float = out_grad.astype(jnp.float32)
    qkv_full, proj_full, expand_full, shrink_full = gather_weights(
        qkv_weight, proj_weight, expand_weight, shrink_weight
    )
    mlp_grad_low = out_float.astype(jnp.bfloat16)
    shrink_bias_grad = jnp.sum(mlp_grad_low, axis=(0, 1), dtype=jnp.float32)
    mlp_grad_all = gather_grads(mlp_grad_low)
    shrink_grad_full = jnp.einsum(
        "btf,btd->fd", hidden_low, mlp_grad_all, preferred_element_type=jnp.float32
    )
    hidden_grad = jnp.einsum(
        "btd,fd->btf", mlp_grad_all, shrink_full, preferred_element_type=jnp.float32
    )
    pre_grad_low = active_back(hidden_grad)[0].astype(jnp.bfloat16)
    expand_bias_grad = jnp.sum(pre_grad_low, axis=(0, 1), dtype=jnp.float32)
    expand_grad_full = jnp.einsum(
        "btd,btf->df", second_all, pre_grad_low, preferred_element_type=jnp.float32
    )
    second_grad = sum_input(pre_grad_low, expand_full, own_windows)
    middle_part, second_gain_grad, second_shift_grad = second_back(second_grad)
    middle_grad = out_float + middle_part
    attn_grad_low = middle_grad.astype(jnp.bfloat16)
    proj_bias_grad = jnp.sum(attn_grad_low, axis=(0, 1), dtype=jnp.float32)
    attn_grad_all = gather_grads(attn_grad_low)
    proj_grad_full = jnp.einsum(
        "btk,btd->kd", attended_low, attn_grad_all, preferred_element_type=jnp.float32
    )
    attended_grad = jnp.einsum(
        "btd,kd->btk", attn_grad_all, proj_full, preferred_element_type=jnp.float32
    )
    attended_grad = attended_grad.astype(jnp.bfloat16).reshape(head_shape)
    scores_again = attention_scores(
        query_low, key_low, rel_height, rel_width, onehot_table, span_size, scaling
    )
    probs_float = jnp.exp(scores_again - log_total)
    probs_again = probs_float.astype(jnp.bfloat16)
    prob_grad = jnp.einsum(
        "bthc,buhc->bhtu", attended_grad, value_low, preferred_element_type=jnp.float32
    )
    value_grad = jnp.einsum(
        "bhtu,bthc->buhc", probs_again, attended_grad, preferred_element_type=jnp.float32
    )
    score_grad = probs_float * (
        prob_grad - jnp.sum(probs_float * prob_grad, axis=-1, keepdims=True)
    )
    score_low = score_grad.astype(jnp.bfloat16)
    rows_grad, cols_grad = relative_back(score_low.astype(jnp.float32), onehot_table, span_size)
    query_float = query_low.astype(jnp.float32)
    query_grad = (
        jnp.einsum("bhtu,buhc->bthc", score_low, key_low, preferred_element_type=jnp.float32)
        * scaling
    )
    query_grad = query_grad + jnp.einsum("bhtj,jc->bthc", rows_grad, rel_height, precision=highest)
    query_grad = query_grad + jnp.einsum("bhtj,jc->bthc", cols_grad, rel_width, precision=highest)
    key_grad = (
        jnp.einsum("bhtu,bthc->buhc", score_low, query_low, preferred_element_type=jnp.float32)
        * scaling
    )
    rel_height_grad = jnp.einsum("bhtj,bthc->jc", rows_grad, query_float, precision=highest)
    rel_width_grad = jnp.einsum("bhtj,bthc->jc", cols_grad, query_float, precision=highest)
    flat_shape = (all_windows, tokens_per, local_width)
    qkv_grad_low = jnp.stack(
        [
            query_grad.reshape(flat_shape),
            key_grad.reshape(flat_shape),
            value_grad.reshape(flat_shape),
        ],
        axis=2,
    ).astype(jnp.bfloat16)
    qkv_bias_grad = jnp.sum(qkv_grad_low[:, :, 0::2], axis=(0, 1), dtype=jnp.float32)
    qkv_grad_full = jnp.einsum(
        "btd,btsk->dsk", first_all, qkv_grad_low, preferred_element_type=jnp.float32
    )
    first_grad = sum_input(
        qkv_grad_low.reshape(all_windows, tokens_per, 3 * local_width),
        qkv_full.reshape(qkv_full.shape[0], 3 * local_width),
        own_windows,
    )
    input_part, first_gain_grad, first_shift_grad = first_back(first_grad)
    input_grad = middle_grad + input_part
    qkv_rows, proj_rows, expand_rows, shrink_rows = (
        lax.psum_scatter(qkv_grad_full, "row", scatter_dimension=0, tiled=True),
        lax.psum_scatter(proj_grad_full, "row", scatter_dimension=1, tiled=True),
        lax.psum_scatter(expand_grad_full, "row", scatter_dimension=0, tiled=True),
        lax.psum_scatter(shrink_grad_full, "row", scatter_dimension=1, tiled=True),
    )
    qkv_sum, proj_sum, expand_sum, shrink_sum = lax.psum(
        (qkv_rows, proj_rows, expand_rows, shrink_rows), "dp"
    )
    qkv_bias_sum, expand_bias_sum = lax.psum((qkv_bias_grad, expand_bias_grad), ("dp", "row"))
    (
        gain_one_sum,
        shift_one_sum,
        gain_two_sum,
        shift_two_sum,
        proj_bias_sum,
        shrink_bias_sum,
        height_sum,
        width_sum,
    ) = lax.psum(
        (
            first_gain_grad,
            first_shift_grad,
            second_gain_grad,
            second_shift_grad,
            proj_bias_grad,
            shrink_bias_grad,
            rel_height_grad,
            rel_width_grad,
        ),
        ("dp", "row", "col"),
    )
    rms = jnp.sqrt(stat_total / (count_total * model_width))
    return (
        result.astype(jnp.bfloat16),
        input_grad,
        gain_one_sum,
        shift_one_sum,
        qkv_sum,
        qkv_bias_sum,
        height_sum,
        width_sum,
        proj_sum,
        proj_bias_sum,
        gain_two_sum,
        shift_two_sum,
        expand_sum,
        expand_bias_sum,
        shrink_sum,
        shrink_bias_sum,
        rms,
    )


def choose(mesh):
    fits = tuple(mesh.shape[name] for name in ("dp", "row", "col")) == (4, 2, 4)
    return over_chips if fits else per_device


def solution(mesh):
    in_specs = (
        P(("dp", "row", "col"), None, None),
        P(("dp", "row", "col"), None),
        P(("dp", "row", "col"), None, None),
        P(),
        P(),
        P("row", None, "col"),
        P(None, "col"),
        P(),
        P(),
        P("col", "row"),
        P(),
        P(),
        P(),
        P("row", "col"),
        P("col"),
        P("col", "row"),
        P(),
    )
    out_specs = (
        P(("dp", "row", "col"), None, None),
        P(("dp", "row", "col"), None, None),
        P(),
        P(),
        P("row", None, "col"),
        P(None, "col"),
        P(),
        P(),
        P("col", "row"),
        P(),
        P(),
        P(),
        P("row", "col"),
        P("col"),
        P("col", "row"),
        P(),
        P(),
    )
    return jax.shard_map(
        choose(mesh), mesh=mesh, in_specs=in_specs, out_specs=out_specs, check_vma=False
    )
```
